32 devices in a mesh: dp: 16 (over z, y, x), mp: 2 (over core).
Axes of the slice: x: 2, y: 2, z: 4, core: 2. Of those that a mesh axis runs over, the one named last changes fastest.
Arguments:
- dec_input: bfloat16 [16, 512, 768], P('dp'), may hold values from -6 to 6
- out_grad: bfloat16 [16, 512, 768], P('dp'), may hold values from -8 to 8
- enc_feats: bfloat16 [16, 2, 16, 128, 768], P('dp', 'mp'), may hold values from -16 to 16
- mem_lengths: int32 [16], replicated, may hold values from 256 to 4096, as said below
- dec_lengths: int32 [16], replicated, may hold values from 128 to 512, as said below
- doc_owner: int32 [16], replicated, may hold values from 0 to 15, each once
- group_gain: float32 [768], replicated, may hold values from 0.5 to 1.5
- group_bias: float32 [768], replicated, may hold values from -3 to 3
- conv_weight: bfloat16 [768, 768], replicated, may hold values from -0.21875 to 0.21875
- cross_kv: bfloat16 [768, 2, 768], replicated, may hold values from -0.21875 to 0.21875
- self_gain: float32 [768], replicated, may hold values from 0.5 to 1.5
- self_qkv: bfloat16 [768, 3, 768], P(None, None, 'mp'), may hold values from -0.21875 to 0.21875
- self_out: bfloat16 [768, 768], P('mp'), may hold values from -2 to 2
- cross_gain: float32 [768], replicated, may hold values from 0.5 to 1.5
- cross_query: bfloat16 [768, 768], P(None, 'mp'), may hold values from -0.21875 to 0.21875
- cross_out: bfloat16 [768, 768], P('mp'), may hold values from -6 to 6
- ffn_gain: float32 [768], replicated, may hold values from 0.5 to 1.5
- ffn_in: bfloat16 [768, 3072], P(None, 'mp'), may hold values from -0.21875 to 0.21875
- ffn_out: bfloat16 [3072, 768], P('mp'), may hold values from -0.109375 to 0.109375
Outputs:
- layer_out: bfloat16 [16, 512, 768], P('dp')
- input_grad: float32 [16, 512, 768], P('dp')
- memory_grad: float32 [16, 2, 16, 128, 768], P('dp', 'mp')
- group_gain_grad: float32 [768], P('dp')
- group_bias_grad: float32 [768], P('dp')
- conv_grad: float32 [768, 768], P('dp')
- cross_kv_grad: float32 [768, 2, 768], P('dp')
- self_gain_grad: float32 [768], P('dp')
- self_qkv_grad: float32 [768, 3, 768], P('dp', None, 'mp')
- self_out_grad: float32 [768, 768], P('mp', 'dp')
- cross_gain_grad: float32 [768], P('dp')
- cross_query_grad: float32 [768, 768], P('dp', 'mp')
- cross_out_grad: float32 [768, 768], P('mp', 'dp')
- ffn_gain_grad: float32 [768], P('dp')
- ffn_in_grad: float32 [768, 3072], P('dp', 'mp')
- ffn_out_grad: float32 [3072, 768], P('mp', 'dp')
The draws below stay inside these ranges and needn't reach their ends.
Inputs may be any that keep to these rules, and one draw needn't show every extreme that they name: `mem_lengths`: one document, drawn from the seed, has exactly 4096 memory tokens. `dec_lengths`: one slot, drawn from the seed, has exactly 512 decoder tokens. `doc_owner`: each document is read by exactly one decoder slot.
All inputs are finite; a program needn't handle non-finite values.
Results may differ from the reference program's by a relative error of at most 0.015.
Values may be sent and summed in bfloat16 or wider, within the bound.
No kernel may reach another device: no remote copies, remote signals or barrier semaphores. Data moves between devices by JAX's collectives and lax.ppermute only.
A program may use at most 256 MiB of HBM per device.

```python
import jax
import jax.numpy as jnp
from jax import lax

D = 768
H = 12
HD = 64
FF = 3072
GROUPS = 32
DEC = 512
MEMLEN = 4096
DOC_DEV = 1
DOCS = 16
SUB = 128
N_DP = 16
N_MP = 2


def draw_out_grad(key, part):
    key = jax.random.fold_in(key, 41)
    rough_key, shared_key = jax.random.split(key)
    rough_part = jnp.clip(jax.random.normal(rough_key, (DOCS, DEC, D), jnp.float32), -4.0, 4.0)
    shared = 0.8 * jnp.clip(jax.random.normal(shared_key, (DOCS, 1, D), jnp.float32), -4.0, 4.0)
    return (rough_part + shared).astype(jnp.bfloat16)


def device_scales(chip_count, lowest, highest_scale):
    steps = jnp.arange(chip_count, dtype=jnp.float32) / max(chip_count - 1, 1)
    return lowest * jnp.exp(jnp.log(highest_scale / lowest) * steps)


def draw_enc_feats(key, part):
    key = jax.random.fold_in(key, 11)
    rough_key, shared_key = jax.random.split(key)
    chip_count = DOCS // DOC_DEV
    core_count = MEMLEN // (SUB * chip_count)
    full_shape = (chip_count, core_count, DOCS, SUB, D)
    device_ramp = device_scales(chip_count, 0.6, 1.8)[:, None, None, None, None]
    rough_part = jnp.clip(jax.random.normal(rough_key, full_shape, jnp.float32), -3.0, 3.0)
    shared = 0.6 * jnp.clip(jax.random.normal(shared_key, (1, 1, DOCS, 1, D), jnp.float32), -3.0, 3.0)
    values = (rough_part + shared) * device_ramp
    return values.astype(jnp.bfloat16)


def draw_mem_lengths(key, part):
    key = jax.random.fold_in(key, 23)
    power_key, span_key, jitter_key, pick_key = jax.random.split(key, 4)
    lowest = MEMLEN // 16
    powers = jax.random.randint(power_key, (DOCS,), 2, 6)
    spans_drawn = jax.random.randint(span_key, (DOCS,), 0, jnp.left_shift(1, powers))
    jitter = jax.random.randint(jitter_key, (DOCS,), 0, lowest)
    lengths = jnp.minimum(lowest * (1 + spans_drawn) + jitter, MEMLEN)
    chosen = jax.random.randint(pick_key, (), 0, DOCS)
    return jnp.where(jnp.arange(DOCS) == chosen, MEMLEN, lengths).astype(jnp.int32)


def draw_dec_lengths(key, part):
    key = jax.random.fold_in(key, 37)
    length_key, pick_key = jax.random.split(key)
    lengths = jax.random.randint(length_key, (DOCS,), DEC // 4, DEC + 1)
    chosen = jax.random.randint(pick_key, (), 0, DOCS)
    return jnp.where(jnp.arange(DOCS) == chosen, DEC, lengths).astype(jnp.int32)


def steps_of(own_key, extent, cuts, least, largest):
    loudness, own = 1.0, jax.random.fold_in(own_key, 6)
    for dim, shards_of in cuts:
        steps = jnp.exp(jax.random.uniform(jax.random.fold_in(own, dim), (shards_of,), jnp.float32, least / len(cuts), largest / len(cuts)))
        loudness = loudness * jnp.repeat(steps, extent[dim] // shards_of).reshape([-1 if axis == dim else 1 for axis in range(len(extent))])
    return loudness


def bell_draw(rng, dims, width, bound, pieces=(), kind=jnp.bfloat16):
    array = width * jax.random.normal(rng, dims, jnp.float32)
    if pieces:
        array = array * steps_of(rng, dims, pieces, -0.22, 0.18)
    return jnp.clip(array, -bound, bound).astype(kind)


def setup_inputs(seed: int = 0) -> dict:
    key_of = jax.random.split(jax.random.key(seed), 20)
    dec_input = bell_draw(key_of[0], (DOCS, DEC, D), 1.0, 6.0, ((0, 16),))
    out_grad = draw_out_grad(jax.random.fold_in(key_of[19], 71), 0)
    enc_feats = draw_enc_feats(jax.random.fold_in(key_of[19], 71), 0)
    mem_lengths = draw_mem_lengths(jax.random.fold_in(key_of[19], 71), 0)
    dec_lengths = draw_dec_lengths(jax.random.fold_in(key_of[19], 71), 0)
    doc_owner = jax.random.permutation(key_of[5], DOCS).astype(jnp.int32)
    group_gain = jnp.clip(1.0 + 0.1 * jax.random.normal(key_of[6], (D,), jnp.float32), 0.5, 1.5)
    group_bias = bell_draw(key_of[7], (D,), 0.5, 3.0, (), jnp.float32)
    conv_weight = bell_draw(key_of[8], (D, D), D ** -0.5, 0.21875)
    cross_kv = bell_draw(key_of[9], (D, 2, D), D ** -0.5, 0.21875)
    self_gain = jnp.clip(1.0 + 0.1 * jax.random.normal(key_of[10], (D,), jnp.float32), 0.5, 1.5)
    self_qkv = bell_draw(key_of[11], (D, 3, D), D ** -0.5, 0.21875, ((2, 2),))
    self_out = bell_draw(key_of[12], (D, D), 8 ** -0.5, 2.0, ((0, 2),))
    cross_gain = jnp.clip(1.0 + 0.1 * jax.random.normal(key_of[13], (D,), jnp.float32), 0.5, 1.5)
    cross_query = bell_draw(key_of[14], (D, D), D ** -0.5, 0.21875, ((1, 2),))
    cross_out = bell_draw(key_of[15], (D, D), 1 ** -0.5, 6.0, ((0, 2),))
    ffn_gain = jnp.clip(1.0 + 0.1 * jax.random.normal(key_of[16], (D,), jnp.float32), 0.5, 1.5)
    ffn_in = bell_draw(key_of[17], (D, FF), D ** -0.5, 0.21875, ((1, 2),))
    ffn_out = bell_draw(key_of[18], (FF, D), FF ** -0.5, 0.109375, ((0, 2),))
    return {"dec_input": dec_input, "out_grad": out_grad, "enc_feats": enc_feats, "mem_lengths": mem_lengths, "dec_lengths": dec_lengths, "doc_owner": doc_owner, "group_gain": group_gain, "group_bias": group_bias, "conv_weight": conv_weight, "cross_kv": cross_kv, "self_gain": self_gain, "self_qkv": self_qkv, "self_out": self_out, "cross_gain": cross_gain, "cross_query": cross_query, "cross_out": cross_out, "ffn_gain": ffn_gain, "ffn_in": ffn_in, "ffn_out": ffn_out}


highest = lax.Precision.HIGHEST
norm_eps = 1e-06
group_eps = 1e-05
masked_fill = -1000000000.0

@jax.custom_vjp
def low(v):
    return lax.optimization_barrier(v.astype(jnp.bfloat16)).astype(jnp.float32)

@jax.custom_vjp
def low_back(v):
    return v

def low_keep(v):
    return (low(v), None)

def low_pass(kept, grad):
    return (grad,)

def back_keep(v):
    return (v, None)

def back_low(kept, grad):
    return (low(grad),)
low.defvjp(low_keep, low_pass)
low_back.defvjp(back_keep, back_low)

def matmul(left, right):
    return jnp.dot(left, right, preferred_element_type=jnp.float32, precision=highest)

def scale_rows(values, gain):
    return values * lax.rsqrt(lax.optimization_barrier(jnp.mean(values * values, axis=-1, keepdims=True)) + norm_eps) * gain

def softmax_rows(scores):
    row_max = lax.optimization_barrier(jnp.max(scores, axis=-1, keepdims=True))
    shifted = jnp.exp(scores - row_max)
    return shifted / lax.optimization_barrier(jnp.sum(shifted, axis=-1, keepdims=True))

def self_doc(inputs):
    queries, key_rows, values, length = inputs
    scores = low_back(jnp.einsum('qhe,khe->hqk', queries, key_rows, precision=highest) * 0.125)
    row_pos = lax.broadcasted_iota(jnp.int32, (DEC, DEC), 0)
    col_pos = lax.broadcasted_iota(jnp.int32, (DEC, DEC), 1)
    allowed = (col_pos <= row_pos) & (col_pos < length)
    weights = low(softmax_rows(jnp.where(allowed[None], scores, masked_fill)))
    return jnp.einsum('hqk,khe->qhe', weights, values, precision=highest)

def reference(dec_input, out_grad, enc_feats, mem_lengths, dec_lengths, doc_owner, group_gain, group_bias, conv_weight, cross_kv, self_gain, self_qkv, self_out, cross_gain, cross_query, cross_out, ffn_gain, ffn_in, ffn_out):
    per_group = D // GROUPS
    chip_pos = lax.broadcasted_iota(jnp.int32, (N_DP, N_MP, SUB), 0)
    core_pos = lax.broadcasted_iota(jnp.int32, (N_DP, N_MP, SUB), 1)
    slot_pos = lax.broadcasted_iota(jnp.int32, (N_DP, N_MP, SUB), 2)
    position = (slot_pos * N_MP + core_pos) * N_DP + chip_pos
    live_mask = (position[:, :, None, :] < mem_lengths[None, None, :, None]).astype(jnp.float32)
    entries = (mem_lengths * per_group).astype(jnp.float32)[:, None]
    key_position = position.reshape(MEMLEN)
    row_count = DOCS * DEC

    def forward(dec_input, enc_feats, group_gain, group_bias, conv_weight, cross_kv, self_gain, self_qkv, self_out, cross_gain, cross_query, cross_out, ffn_gain, ffn_in, ffn_out):
        grouped = enc_feats.reshape(N_DP, N_MP, DOCS, SUB, GROUPS, per_group)
        masked = grouped * live_mask[..., None, None]
        first_sum = lax.optimization_barrier(jnp.sum(masked, axis=(0, 1, 3, 5)))
        second_sum = lax.optimization_barrier(jnp.sum(masked * grouped, axis=(0, 1, 3, 5)))
        center = first_sum / entries
        spread = lax.rsqrt(second_sum / entries - center * center + group_eps)
        normed = ((grouped - center[None, None, :, None, :, None]) * spread[None, None, :, None, :, None]).reshape(N_DP, N_MP, DOCS, SUB, D)
        hidden_mem = low(jax.nn.silu(normed * group_gain + group_bias))
        memory = enc_feats + matmul(hidden_mem.reshape(-1, D), conv_weight).reshape(N_DP, N_MP, DOCS, SUB, D)
        memory = low_back(low(memory))
        mem_pairs = low_back(low(matmul(memory.reshape(-1, D), cross_kv.reshape(D, 2 * D))))
        mem_pairs = mem_pairs.reshape(N_DP, N_MP, DOCS, SUB, 2, H, HD)
        flat_in = dec_input.reshape(row_count, D)
        normed_one = low_back(low(scale_rows(flat_in, self_gain)))
        projected = jnp.einsum('td,dkf->tkf', normed_one, self_qkv, precision=highest)
        projected = low_back(low(projected)).reshape(DOCS, DEC, 3, H, HD)
        attended = lax.map(jax.checkpoint(self_doc), (projected[:, :, 0], projected[:, :, 1], projected[:, :, 2], dec_lengths))
        attended = low_back(low(attended.reshape(row_count, D)))
        first_out = flat_in + low_back(matmul(attended, self_out))
        normed_two = low_back(low(scale_rows(first_out, cross_gain)))
        cross_q = low_back(low(matmul(normed_two, cross_query))).reshape(DOCS, DEC, H, HD)

        def cross_doc(inputs):
            queries, document = inputs
            doc_pairs = lax.dynamic_index_in_dim(mem_pairs, document, axis=2, keepdims=False).reshape(MEMLEN, 2, H, HD)
            doc_limit = lax.dynamic_index_in_dim(mem_lengths, document, keepdims=False)
            scores = low_back(jnp.einsum('qhe,khe->hqk', queries, doc_pairs[:, 0], precision=highest) * 0.125)
            weights = low(softmax_rows(jnp.where((key_position < doc_limit)[None, None, :], scores, masked_fill)))
            return jnp.einsum('hqk,khe->qhe', weights, doc_pairs[:, 1], precision=highest)
        crossed = lax.map(jax.checkpoint(cross_doc), (cross_q, doc_owner))
        crossed = low_back(low(crossed.reshape(row_count, D)))
        second_out = first_out + low_back(matmul(crossed, cross_out))
        normed_three = low_back(low(scale_rows(second_out, ffn_gain)))
        lifted = low_back(matmul(normed_three, ffn_in))
        active = low_back(low(jax.nn.gelu(lifted, approximate=True)))
        result = second_out + low_back(matmul(active, ffn_out))
        return result.reshape(DOCS, DEC, D)
    floats = (dec_input.astype(jnp.float32), enc_feats.astype(jnp.float32), group_gain, group_bias, conv_weight.astype(jnp.float32), cross_kv.astype(jnp.float32), self_gain, self_qkv.astype(jnp.float32), self_out.astype(jnp.float32), cross_gain, cross_query.astype(jnp.float32), cross_out.astype(jnp.float32), ffn_gain, ffn_in.astype(jnp.float32), ffn_out.astype(jnp.float32))
    result, pullback = jax.vjp(forward, *floats)
    gradients = pullback(out_grad.astype(jnp.float32))
    return (result.astype(jnp.bfloat16), gradients[0], gradients[1], gradients[2], gradients[3], gradients[4], gradients[5], gradients[6], gradients[7], gradients[8], gradients[9], gradients[10], gradients[11], gradients[12], gradients[13], gradients[14])
```

```python
from functools import partial

import jax
import jax.numpy as jnp
from jax import lax
from jax.experimental import pallas as pl
from jax.experimental.pallas import tpu as pltpu
from jax.sharding import PartitionSpec as P

HD = 64
GROUPS = 32
DEC = 512


norm_eps = 1e-06
group_eps = 1e-05
masked_fill = -1000000000.0
vmem_budget = 48 * 1024 * 1024
low_type = jnp.bfloat16
wide_type = jnp.float32


def dot_wide(left, right):
    return jnp.dot(left, right, preferred_element_type=wide_type)


def dot_rows(left, right):
    return lax.dot_general(left, right, (((0,), (0,)), ((), ())), preferred_element_type=wide_type)


def dot_columns(left, right):
    return lax.dot_general(left, right, (((1,), (1,)), ((), ())), preferred_element_type=wide_type)


def norm_rows(values, gain):
    factor = lax.rsqrt(jnp.mean(values * values, axis=-1, keepdims=True) + norm_eps)
    return (values * factor * gain, factor)


def norm_rows_back(values, factor, gain, incoming):
    scaled = incoming * gain
    inward = factor * scaled - values * factor * factor * factor * jnp.mean(
        scaled * values, axis=-1, keepdims=True
    )
    gain_grad = jnp.sum(incoming * values * factor, axis=0)
    return (inward, gain_grad)


def other_core(values):
    return lax.ppermute(values, "mp", [(0, 1), (1, 0)])


def core_total(partial_sum):
    return partial_sum + other_core(partial_sum)


def scatter_sum(values, order, chip_index, keep_type):
    chips = values.shape[0]
    bits = len(order)
    current = values.reshape((2,) * bits + values.shape[1:])
    left = list(range(bits - 1, -1, -1))
    for bit in order:
        axis = left.index(bit)
        mine = (chip_index >> bit) & 1
        sent = lax.dynamic_index_in_dim(current, 1 - mine, axis, False)
        kept = lax.dynamic_index_in_dim(current, mine, axis, False)
        came = lax.ppermute(sent, "dp", [(chip, chip ^ (1 << bit)) for chip in range(chips)])
        current = kept.astype(wide_type) + came.astype(wide_type)
        left.pop(axis)
        if left:
            current = current.astype(keep_type)
    return current


def gather_kernel(owner, lengths, place, rows, out, sums, *, chips, sub):
    slot = pl.program_id(0)
    block = rows[0]
    out[0] = block
    wide = block.astype(wide_type)
    position = (lax.broadcasted_iota(jnp.int32, wide.shape, 0) * 2 + place[1]) * chips + place[0]
    live = jnp.where(position < lengths[owner[slot]], wide, 0.0)
    sums[0] = jnp.concatenate(
        (
            jnp.sum(live, axis=0, keepdims=True),
            jnp.sum(live * wide, axis=0, keepdims=True),
            jnp.zeros((6, wide.shape[1]), wide_type),
        )
    )


def gather_docs(memory_in, doc_owner, mem_lengths, place, chips):
    docs, sub, width = memory_in.shape
    return pl.pallas_call(
        partial(gather_kernel, chips=chips, sub=sub),
        grid_spec=pltpu.PrefetchScalarGridSpec(
            num_scalar_prefetch=3,
            grid=(docs,),
            in_specs=[pl.BlockSpec((1, sub, width), lambda j, owner, lens, place: (owner[j], 0, 0))],
            out_specs=[
                pl.BlockSpec((1, sub, width), lambda j, owner, lens, place: (j, 0, 0)),
                pl.BlockSpec((1, 8, width), lambda j, owner, lens, place: (j, 0, 0)),
            ],
        ),
        out_shape=[
            jax.ShapeDtypeStruct((docs, sub, width), low_type),
            jax.ShapeDtypeStruct((docs, 8, width), wide_type),
        ],
        compiler_params=pltpu.CompilerParams(vmem_limit_bytes=vmem_budget),
        name="gather_docs",
    )(doc_owner, mem_lengths, place, memory_in)


def spread_kernel(owner, rows, out):
    out[0] = rows[0].astype(wide_type)


def spread_docs(rows, doc_owner):
    docs, sub, width = rows.shape
    return pl.pallas_call(
        spread_kernel,
        grid_spec=pltpu.PrefetchScalarGridSpec(
            num_scalar_prefetch=1,
            grid=(docs,),
            in_specs=[pl.BlockSpec((1, sub, width), lambda j, owner: (j, 0, 0))],
            out_specs=pl.BlockSpec((1, sub, width), lambda j, owner: (owner[j], 0, 0)),
        ),
        out_shape=jax.ShapeDtypeStruct((docs, sub, width), wide_type),
        compiler_params=pltpu.CompilerParams(vmem_limit_bytes=vmem_budget),
        name="spread_docs",
    )(doc_owner, rows)


def chunk_of(chips, sub):
    return min(sub, max(16, 512 // chips))


def live_rows(facts, start, chips, span):
    row = lax.broadcasted_iota(jnp.int32, (chips * span, 1), 0)
    chip, step = row // span, row % span
    return ((start + step) * 2 + facts[1]) * chips + chip < facts[0]


def in_branches(facts, start, chips, span, work, dead=None):
    first = (start * 2 + facts[1]) * chips
    last = ((start + span - 1) * 2 + facts[1]) * chips + chips - 1
    full = last < facts[0]
    none = first >= facts[0]

    @pl.when(full)
    def _():
        work(None)

    @pl.when(jnp.logical_not(full) & jnp.logical_not(none))
    def _():
        work(live_rows(facts, start, chips, span))

    if dead is not None:
        pl.when(none)(dead)


def cross_forward_kernel(
    facts, query_t, rows, weight, top_in, total_in, sum_in, pairs, top, total, gathered, *, chips, span
):
    step = pl.program_id(0)
    half = weight.shape[1] // 2
    width = rows.shape[-1]

    @pl.when(step == 0)
    def _():
        top[...] = top_in[...]
        total[...] = total_in[...]
        gathered[...] = sum_in[...]

    def work(live):
        block = rows[...].reshape(chips * span, width)
        made = dot_wide(block, weight[...]).astype(low_type)
        pairs[...] = made.reshape(chips, span, 2 * half)
        for pair in range(half // 128):
            key_pair = made[:, pair * 128 : pair * 128 + 128]
            value_pair = made[:, half + pair * 128 : half + pair * 128 + 128]
            for side in range(2):
                head = pair * 2 + side
                scores = dot_wide(key_pair, query_t[head])
                if live is not None:
                    scores = jnp.where(live, scores, masked_fill)
                old_top = top[head : head + 1, :]
                new_top = jnp.maximum(old_top, jnp.max(scores, axis=0, keepdims=True))
                weights = jnp.exp(scores - new_top)
                shrink = jnp.exp(old_top - new_top)
                total[head : head + 1, :] = total[head : head + 1, :] * shrink + jnp.sum(
                    weights, axis=0, keepdims=True
                )
                part = dot_rows(value_pair, weights.astype(low_type))
                gathered[head * HD : head * HD + HD, :] = (
                    gathered[head * HD : head * HD + HD, :] * shrink + part[side * HD : side * HD + HD, :]
                )
                top[head : head + 1, :] = new_top

    def dead():
        pairs[...] = jnp.zeros_like(pairs)

    in_branches(facts, step * span, chips, span, work, dead)


def whole(shape):
    return pl.BlockSpec(shape, lambda j, facts: (0,) * len(shape))


def cross_forward(facts, query_t, rows, weight, carry):
    chips, sub, width = rows.shape
    heads, _, queries = query_t.shape
    span = chunk_of(chips, sub)
    stat = (8, queries)
    summed = (heads * HD, queries)
    block = pl.BlockSpec((chips, span, width), lambda j, facts: (0, j, 0))
    pair_block = pl.BlockSpec((chips, span, weight.shape[1]), lambda j, facts: (0, j, 0))
    return pl.pallas_call(
        partial(cross_forward_kernel, chips=chips, span=span),
        grid_spec=pltpu.PrefetchScalarGridSpec(
            num_scalar_prefetch=1,
            grid=(sub // span,),
            in_specs=[
                whole(query_t.shape),
                block,
                whole(weight.shape),
                whole(stat),
                whole(stat),
                whole(summed),
            ],
            out_specs=[pair_block, whole(stat), whole(stat), whole(summed)],
        ),
        out_shape=[
            jax.ShapeDtypeStruct((chips, sub, weight.shape[1]), low_type),
            jax.ShapeDtypeStruct(stat, wide_type),
            jax.ShapeDtypeStruct(stat, wide_type),
            jax.ShapeDtypeStruct(summed, wide_type),
        ],
        compiler_params=pltpu.CompilerParams(vmem_limit_bytes=vmem_budget),
        name="cross_forward",
    )(facts, query_t, rows, weight, *carry)


def cross_backward_kernel(
    facts, query, query_t, grad, grad_t, log_total, inner, pairs, weight_t, pair_grads, row_grads, query_grad,
    held, *, chips, span
):
    step = pl.program_id(0)
    half = weight_t.shape[0] // 2
    width = weight_t.shape[1]

    @pl.when(step == 0)
    def _():
        query_grad[...] = jnp.zeros_like(query_grad)

    def work(live):
        block = pairs[...].reshape(chips * span, 2 * half)
        for pair in range(half // 128):
            key_pair = block[:, pair * 128 : pair * 128 + 128]
            value_pair = block[:, half + pair * 128 : half + pair * 128 + 128]
            key_sum, value_sum = 0.0, 0.0
            for side in range(2):
                head = pair * 2 + side
                scores = dot_wide(key_pair, query_t[head])
                if live is not None:
                    scores = jnp.where(live, scores, masked_fill)
                probs = jnp.exp(scores - log_total[head : head + 1, :])
                grad_probs = dot_wide(value_pair, grad_t[head])
                grad_scores = (probs * (grad_probs - inner[head : head + 1, :])).astype(low_type)
                value_sum = value_sum + dot_wide(probs.astype(low_type), grad[head])
                key_sum = key_sum + dot_wide(grad_scores, query[head])
                part = dot_rows(key_pair, grad_scores)
                query_grad[head * HD : head * HD + HD, :] += part[side * HD : side * HD + HD, :]
            held[:, pair * 128 : pair * 128 + 128] = key_sum.astype(low_type)
            held[:, half + pair * 128 : half + pair * 128 + 128] = value_sum.astype(low_type)
        made = held[...]
        pair_grads[...] = made.reshape(chips, span, 2 * half)
        row_grads[...] = dot_wide(made, weight_t[...]).astype(row_grads.dtype).reshape(chips, span, width)

    def dead():
        pair_grads[...] = jnp.zeros_like(pair_grads)
        row_grads[...] = jnp.zeros_like(row_grads)

    in_branches(facts, step * span, chips, span, work, dead)


def cross_backward(facts, query, query_t, grad, grad_t, log_total, inner, pairs, weight_t, grad_type):
    chips, sub, both = pairs.shape
    width = weight_t.shape[1]
    heads, _, queries = query_t.shape
    span = chunk_of(chips, sub)
    pair_block = pl.BlockSpec((chips, span, both), lambda j, facts: (0, j, 0))
    row_block = pl.BlockSpec((chips, span, width), lambda j, facts: (0, j, 0))
    return pl.pallas_call(
        partial(cross_backward_kernel, chips=chips, span=span),
        grid_spec=pltpu.PrefetchScalarGridSpec(
            num_scalar_prefetch=1,
            grid=(sub // span,),
            in_specs=[
                whole(query.shape),
                whole(query_t.shape),
                whole(grad.shape),
                whole(grad_t.shape),
                whole(log_total.shape),
                whole(inner.shape),
                pair_block,
                whole(weight_t.shape),
            ],
            out_specs=[pair_block, row_block, whole((heads * HD, queries))],
            scratch_shapes=[pltpu.VMEM((chips * span, both), low_type)],
        ),
        out_shape=[
            jax.ShapeDtypeStruct((chips, sub, both), low_type),
            jax.ShapeDtypeStruct((chips, sub, width), grad_type),
            jax.ShapeDtypeStruct((heads * HD, queries), wide_type),
        ],
        compiler_params=pltpu.CompilerParams(vmem_limit_bytes=vmem_budget),
        name="cross_backward",
    )(facts, query, query_t, grad, grad_t, log_total, inner, pairs, weight_t)


def padded_heads(values):
    rows, width = values.shape
    pairs = values.reshape(rows, width // 128, 128).transpose(1, 0, 2)
    left = lax.broadcasted_iota(jnp.int32, (1, 1, 128), 2) < HD
    none = jnp.zeros_like(pairs)
    both = jnp.stack((jnp.where(left, pairs, none), jnp.where(left, none, pairs)), axis=1)
    return both.reshape(width // HD, rows, 128)


def padded_heads_t(values_t):
    width, rows = values_t.shape
    pairs = values_t.reshape(width // 128, 2, HD, rows)
    none = jnp.zeros_like(pairs[:, 0])
    even = jnp.concatenate((pairs[:, 0], none), axis=1)
    odd = jnp.concatenate((none, pairs[:, 1]), axis=1)
    return jnp.stack((even, odd), axis=1).reshape(width // HD, 128, rows)


def attend(queries, key_rows, values, allowed):
    scores = (
        jnp.einsum("hne,hme->hnm", queries, key_rows, preferred_element_type=jnp.float32) * 0.125
    )
    scores = jnp.where(allowed, scores, masked_fill)
    row_max = jnp.max(scores, axis=-1, keepdims=True)
    shifted = jnp.exp(scores - row_max)
    row_total = jnp.sum(shifted, axis=-1, keepdims=True)
    weights = (shifted / row_total).astype(jnp.bfloat16)
    output = jnp.einsum("hnm,hme->hne", weights, values, preferred_element_type=jnp.float32)
    return (output.astype(jnp.bfloat16), (row_max + jnp.log(row_total))[..., 0])


def attend_back(queries, key_rows, values, allowed, log_total, grad_output):
    scores = (
        jnp.einsum("hne,hme->hnm", queries, key_rows, preferred_element_type=jnp.float32) * 0.125
    )
    scores = jnp.where(allowed, scores, masked_fill)
    probs = jnp.exp(scores - log_total[..., None])
    grad_probs = jnp.einsum("hne,hme->hnm", grad_output, values, preferred_element_type=jnp.float32)
    grad_scores = probs * (grad_probs - jnp.sum(probs * grad_probs, axis=-1, keepdims=True))
    grad_low = grad_scores.astype(jnp.bfloat16)
    query_grad = (
        jnp.einsum("hnm,hme->hne", grad_low, key_rows, preferred_element_type=jnp.float32) * 0.125
    )
    key_grad = (
        jnp.einsum("hnm,hne->hme", grad_low, queries, preferred_element_type=jnp.float32) * 0.125
    )
    value_grad = jnp.einsum(
        "hnm,hne->hme", probs.astype(jnp.bfloat16), grad_output, preferred_element_type=jnp.float32
    )
    return (query_grad, key_grad, value_grad)


def shards(
    dec_input,
    out_grad,
    enc_feats,
    mem_lengths,
    dec_lengths,
    doc_owner,
    group_gain,
    group_bias,
    conv_weight,
    cross_kv,
    self_gain,
    self_qkv,
    self_out,
    cross_gain,
    cross_query,
    cross_out,
    ffn_gain,
    ffn_in,
    ffn_out,
):
    chips = lax.axis_size("dp")
    chip_index = lax.axis_index("dp")
    core_index = lax.axis_index("mp")
    memory_in = enc_feats[0, 0]
    docs, sub, width = memory_in.shape
    per_group = width // GROUPS
    half = width // 2
    heads = half // HD
    rows_here = docs * sub
    share = width // chips
    bits = chips.bit_length() - 1
    orders = [
        tuple((bit + turn) % 3 if bit < 3 else bit for bit in range(bits)) if bits >= 3 else tuple(range(bits))
        for turn in range(3)
    ]

    place = jnp.stack((chip_index, core_index)).astype(jnp.int32)
    outgoing, channel_sums = gather_docs(memory_in, doc_owner, mem_lengths, place, chips)
    features = lax.all_to_all(outgoing, "dp", split_axis=0, concat_axis=0, tiled=True)
    group_of = (
        lax.broadcasted_iota(jnp.int32, (width, GROUPS), 0) // per_group
        == lax.broadcasted_iota(jnp.int32, (width, GROUPS), 1)
    ).astype(wide_type)

    def group_sums(channels):
        return jnp.dot(channels, group_of, precision=lax.Precision.HIGHEST)

    def to_channels(groups):
        return jnp.dot(groups, group_of.T, precision=lax.Precision.HIGHEST)

    sums_here = group_sums(channel_sums[:, :2].reshape(docs * 2, width)).reshape(docs, 2 * GROUPS)
    sums_all = core_total(scatter_sum(sums_here, orders[0], chip_index, wide_type))
    document = doc_owner[chip_index]
    length = mem_lengths[document]
    entries = (length * per_group).astype(wide_type)
    center = sums_all[:GROUPS] / entries
    spread = lax.rsqrt(sums_all[GROUPS:] / entries - center * center + group_eps)
    channel_stats = to_channels(jnp.stack((center, spread)))
    center_row, spread_row = channel_stats[0:1], channel_stats[1:2]

    dec_rows = DEC
    input_flat = dec_input.astype(wide_type).reshape(dec_rows, width)
    normed_one, factor_one = norm_rows(input_flat, self_gain)
    normed_one = normed_one.astype(low_type)
    self_weight = self_qkv.reshape(width, 3 * half)
    qkv_self = dot_wide(normed_one, self_weight).astype(low_type)
    qkv_heads = qkv_self.reshape(DEC, 3, heads, HD).transpose(1, 2, 0, 3)
    row_pos = lax.broadcasted_iota(jnp.int32, (DEC, DEC), 0)
    col_pos = lax.broadcasted_iota(jnp.int32, (DEC, DEC), 1)
    allowed = ((col_pos <= row_pos) & (col_pos < dec_lengths[chip_index]))[None]
    output, self_total = attend(qkv_heads[0], qkv_heads[1], qkv_heads[2], allowed)
    attended = output.transpose(1, 0, 2).reshape(dec_rows, half)
    first_out = input_flat + core_total(dot_wide(attended, self_out))
    normed_two, factor_two = norm_rows(first_out, cross_gain)
    normed_two = normed_two.astype(low_type)
    cross_q = dot_wide(normed_two, cross_query).astype(low_type) * jnp.asarray(0.125, low_type)
    query_heads = padded_heads(cross_q)
    query_heads_t = padded_heads_t(cross_q.T)

    features_wide = features.reshape(rows_here, width).astype(wide_type)
    normed = (features_wide - center_row) * spread_row
    activation_in = normed * group_gain + group_bias
    hidden = jax.nn.silu(activation_in).astype(low_type)
    memory_own = (features_wide + dot_wide(hidden, conv_weight)).astype(low_type)
    memory_other = other_core(memory_own)
    pair_weight = lax.dynamic_slice_in_dim(cross_kv, core_index * half, half, axis=2).reshape(width, 2 * half)

    facts_own = jnp.stack((length, core_index)).astype(jnp.int32)
    facts_other = jnp.stack((length, 1 - core_index)).astype(jnp.int32)
    carry = (
        jnp.full((8, dec_rows), -1e30, wide_type),
        jnp.zeros((8, dec_rows), wide_type),
        jnp.zeros((half, dec_rows), wide_type),
    )
    pairs_own, *carry = cross_forward(
        facts_own, query_heads_t, memory_own.reshape(chips, sub, width), pair_weight, carry
    )
    pairs_other, top, total, gathered = cross_forward(
        facts_other, query_heads_t, memory_other.reshape(chips, sub, width), pair_weight, carry
    )
    crossed_t = (gathered.reshape(heads, HD, dec_rows) / total[:heads, None, :]).reshape(half, dec_rows)
    log_total = top + jnp.log(jnp.maximum(total, 1e-30))
    crossed = crossed_t.T.astype(low_type)
    second_out = first_out + core_total(dot_wide(crossed, cross_out))

    normed_three, factor_three = norm_rows(second_out, ffn_gain)
    normed_three = normed_three.astype(low_type)
    lifted = dot_wide(normed_three, ffn_in)
    gelu_value, gelu_back = jax.vjp(partial(jax.nn.gelu, approximate=True), lifted)
    active = gelu_value.astype(low_type)
    grad_low = out_grad.reshape(dec_rows, width)
    grad_result = grad_low.astype(wide_type)
    grad_active = dot_columns(grad_low, ffn_out).astype(low_type)
    grad_lifted = gelu_back(grad_active.astype(wide_type))[0].astype(low_type)
    grad_normed_three = core_total(dot_columns(grad_lifted, ffn_in))
    grad_second, ffn_gain_grad = norm_rows_back(second_out, factor_three, ffn_gain, grad_normed_three)
    grad_second = grad_second + grad_result
    grad_cross = grad_second.astype(low_type)
    grad_crossed = dot_columns(grad_cross, cross_out).astype(low_type)
    grad_crossed_t = grad_crossed.T
    inner = jnp.sum(
        (grad_crossed_t.astype(wide_type) * crossed_t).reshape(heads, HD, dec_rows), axis=1
    )
    inner = jnp.concatenate((inner, jnp.zeros((8 - heads, dec_rows), wide_type)))
    grad_heads = padded_heads(grad_crossed)
    grad_heads_t = padded_heads_t(grad_crossed_t)

    result = second_out + core_total(dot_wide(active, ffn_out))
    layer_out = result.astype(low_type).reshape(1, DEC, width)

    def by_row(grad):
        return grad.astype(low_type).reshape(chips, share, grad.shape[1])

    third = 2 * active.shape[1] // 3
    ffn_parts = (
        scatter_sum(by_row(dot_rows(normed_three, grad_lifted[:, :third])), orders[0], chip_index, low_type),
        scatter_sum(by_row(dot_rows(normed_three, grad_lifted[:, third:])), orders[1], chip_index, low_type),
        scatter_sum(by_row(dot_rows(grad_low, active[:, : third // 2])), orders[1], chip_index, low_type),
        scatter_sum(by_row(dot_rows(grad_low, active[:, third // 2 :])), orders[2], chip_index, low_type),
    )
    ffn_in_grad = jnp.concatenate(ffn_parts[:2], axis=1)
    ffn_out_grad = jnp.concatenate(ffn_parts[2:], axis=1).T

    weight_t = pair_weight.T
    pair_grads_other, row_grads_other, query_grad_other = cross_backward(
        facts_other, query_heads, query_heads_t, grad_heads, grad_heads_t, log_total, inner, pairs_other, weight_t,
        low_type,
    )
    row_grads_came = other_core(row_grads_other)
    pair_grads_own, row_grads_own, query_grad_own = cross_backward(
        facts_own, query_heads, query_heads_t, grad_heads, grad_heads_t, log_total, inner, pairs_own, weight_t,
        wide_type,
    )
    grad_memory = (row_grads_own + row_grads_came.astype(wide_type)).astype(low_type).reshape(rows_here, width)

    grad_hidden = dot_columns(grad_memory, conv_weight)
    gate = jax.nn.sigmoid(activation_in)
    grad_act = grad_hidden * gate * (1.0 + activation_in * (1.0 - gate))
    gain_part = jnp.sum(grad_act * normed, axis=0)
    bias_part = jnp.sum(grad_act, axis=0)
    backs = to_channels(group_sums(core_total(jnp.stack((bias_part, gain_part))) * group_gain)) / entries
    position = (
        (lax.broadcasted_iota(jnp.int32, (chips, sub, 1), 1) * 2 + core_index) * chips
        + lax.broadcasted_iota(jnp.int32, (chips, sub, 1), 0)
    ).reshape(rows_here, 1)
    live = (position < length).astype(wide_type)
    grad_features = grad_memory.astype(wide_type) + spread_row * (
        grad_act * group_gain - live * (backs[0:1] + normed * backs[1:2])
    )
    returned = lax.all_to_all(
        grad_features.astype(low_type).reshape(docs, sub, width), "dp", split_axis=0, concat_axis=0, tiled=True
    )
    memory_grad = spread_docs(returned, doc_owner).reshape(1, 1, docs, sub, width)

    grad_cq = ((query_grad_own + query_grad_other) * 0.125).T.astype(low_type)
    grad_normed_two = core_total(dot_columns(grad_cq, cross_query))
    grad_first, cross_gain_grad = norm_rows_back(first_out, factor_two, cross_gain, grad_normed_two)
    grad_first = grad_first + grad_second
    grad_self = grad_first.astype(low_type)
    grad_attended = dot_columns(grad_self, self_out).astype(low_type)
    grad_attended = grad_attended.reshape(DEC, heads, HD).transpose(1, 0, 2)
    query_grad, key_grad, value_grad = attend_back(
        qkv_heads[0], qkv_heads[1], qkv_heads[2], allowed, self_total, grad_attended
    )
    grad_qkv = (
        jnp.stack((query_grad, key_grad, value_grad))
        .astype(low_type)
        .transpose(2, 0, 1, 3)
        .reshape(dec_rows, 3 * half)
    )
    grad_normed_one = core_total(dot_columns(grad_qkv, self_weight))
    grad_input, self_gain_grad = norm_rows_back(input_flat, factor_one, self_gain, grad_normed_one)
    input_grad = (grad_input + grad_first).reshape(1, DEC, width)

    pair_weight_grad = dot_rows(memory_own, pair_grads_own.reshape(rows_here, 2 * half)) + dot_rows(
        memory_other, pair_grads_other.reshape(rows_here, 2 * half)
    )
    conv_part = dot_rows(hidden, grad_memory)
    conv_keep = lax.dynamic_slice_in_dim(conv_part, core_index * half, half, axis=1)
    conv_send = lax.dynamic_slice_in_dim(conv_part, (1 - core_index) * half, half, axis=1).astype(low_type)
    conv_half = conv_keep + other_core(conv_send).astype(wide_type)
    pair_sum = scatter_sum(by_row(pair_weight_grad), orders[0], chip_index, low_type)
    conv_sum = scatter_sum(by_row(conv_half), orders[1], chip_index, low_type)
    cross_out_sum = scatter_sum(by_row(dot_rows(grad_cross, crossed)), orders[2], chip_index, low_type)
    cross_query_sum = scatter_sum(by_row(dot_rows(normed_two, grad_cq)), orders[2], chip_index, low_type)
    self_out_sum = scatter_sum(by_row(dot_rows(grad_self, attended)), orders[2], chip_index, low_type)
    self_qkv_sum = scatter_sum(by_row(dot_rows(normed_one, grad_qkv)), orders[1], chip_index, low_type)
    gains = jnp.stack((gain_part, bias_part, self_gain_grad, cross_gain_grad, ffn_gain_grad))
    gains = jnp.concatenate((gains, jnp.zeros((3, width), wide_type)))
    gain_sums = scatter_sum(
        gains.reshape(8, chips, share).transpose(1, 0, 2), orders[0], chip_index, wide_type
    )
    group_sums_both = core_total(gain_sums[:2])

    def both_cores(mine):
        theirs = other_core(mine.astype(low_type)).astype(wide_type)
        return jnp.where(core_index == 0, mine, theirs), jnp.where(core_index == 0, theirs, mine)

    conv_grad = jnp.concatenate(both_cores(conv_sum), axis=1)
    pair_left, pair_right = both_cores(pair_sum)
    cross_kv_grad = jnp.concatenate(
        (pair_left.reshape(share, 2, half), pair_right.reshape(share, 2, half)), axis=2
    )
    return (
        layer_out,
        input_grad,
        memory_grad,
        group_sums_both[0],
        group_sums_both[1],
        conv_grad,
        cross_kv_grad,
        gain_sums[2],
        self_qkv_sum.reshape(share, 3, half),
        self_out_sum.T,
        gain_sums[3],
        cross_query_sum,
        cross_out_sum.T,
        gain_sums[4],
        ffn_in_grad,
        ffn_out_grad,
    )


def solution(mesh):
    placed = (
        P("dp", None, None),
        P("dp", None, None),
        P("dp", "mp", None, None, None),
        P(),
        P(),
        P(),
        P(),
        P(),
        P(),
        P(),
        P(),
        P(None, None, "mp"),
        P("mp", None),
        P(),
        P(None, "mp"),
        P("mp", None),
        P(),
        P(None, "mp"),
        P("mp", None),
    )
    return jax.shard_map(
        shards,
        mesh=mesh,
        in_specs=placed,
        out_specs=(
            P("dp", None, None),
            P("dp", None, None),
            P("dp", "mp", None, None, None),
            P("dp"),
            P("dp"),
            P("dp", None),
            P("dp", None, None),
            P("dp"),
            P("dp", None, "mp"),
            P("mp", "dp"),
            P("dp"),
            P("dp", "mp"),
            P("mp", "dp"),
            P("dp"),
            P("dp", "mp"),
            P("mp", "dp"),
        ),
        check_vma=False,
    )
```

```python
from functools import partial

import jax
import jax.numpy as jnp
from jax import lax
from jax.experimental import pallas as pl
from jax.experimental.pallas import tpu as pltpu
from jax.sharding import PartitionSpec as P

HD = 64
GROUPS = 32
DEC = 512


norm_eps = 1e-06
group_eps = 1e-05
masked_fill = -1000000000.0
vmem_budget = 48 * 1024 * 1024
heavy = pl.CostEstimate(flops=10**10, bytes_accessed=10**7, transcendentals=10**7)
low_type = jnp.bfloat16
wide_type = jnp.float32


def dot_wide(left, right):
    return jnp.dot(left, right, preferred_element_type=wide_type)


def dot_rows(left, right):
    return lax.dot_general(left, right, (((0,), (0,)), ((), ())), preferred_element_type=wide_type)


def dot_columns(left, right):
    return lax.dot_general(left, right, (((1,), (1,)), ((), ())), preferred_element_type=wide_type)


def norm_rows(values, gain):
    factor = lax.rsqrt(jnp.mean(values * values, axis=-1, keepdims=True) + norm_eps)
    return (values * factor * gain, factor)


def norm_rows_back(values, factor, gain, incoming):
    scaled = incoming * gain
    inward = factor * scaled - values * factor * factor * factor * jnp.mean(
        scaled * values, axis=-1, keepdims=True
    )
    gain_grad = jnp.sum(incoming * values * factor, axis=0)
    return (inward, gain_grad)


def other_core(values):
    return lax.ppermute(values, "mp", [(0, 1), (1, 0)])


def core_total(partial_sum):
    return partial_sum + other_core(partial_sum)


tie = lax.optimization_barrier


class ScatterSums:
    def __init__(self, arrays, orders, chip_index):
        chips = arrays[0].shape[0]
        self.chip_index = chip_index
        self.bits = chips.bit_length() - 1
        self.orders = [list(order) for order in orders]
        self.left = [list(range(self.bits - 1, -1, -1)) for _ in arrays]
        self.current = [array.reshape((2,) * self.bits + array.shape[1:]) for array in arrays]
        self.kept = self.sent = self.came = None

    def copied(self):
        other = object.__new__(ScatterSums)
        other.chip_index, other.bits = self.chip_index, self.bits
        other.orders = [list(order) for order in self.orders]
        other.left = [list(left) for left in self.left]
        other.current, other.kept, other.sent, other.came = self.current, self.kept, self.sent, self.came
        return other

    def begin(self):
        self.kept, self.sent = [], []
        for number, order in enumerate(self.orders):
            axis = self.left[number].index(order[0])
            mine = (self.chip_index >> order[0]) & 1
            self.sent.append(lax.dynamic_index_in_dim(self.current[number], 1 - mine, axis, False))
            self.kept.append(lax.dynamic_index_in_dim(self.current[number], mine, axis, False))
            self.left[number].pop(axis)

    def ahead_of(self, value):
        self.sent, value = tie((self.sent, value))
        return value

    def send(self):
        chips = 1 << self.bits
        self.came = [
            lax.ppermute(sent, "dp", [(chip, chip ^ (1 << order[0])) for chip in range(chips)])
            for sent, order in zip(self.sent, self.orders)
        ]

    def behind(self, value):
        self.came, value = tie((self.came, value))
        return value

    def merge(self):
        merged = []
        for number, order in enumerate(self.orders):
            total = self.kept[number].astype(wide_type) + self.came[number].astype(wide_type)
            order.pop(0)
            merged.append(total.astype(self.current[number].dtype) if order else total)
        self.current = merged

    def step(self):
        self.begin()
        self.send()
        self.merge()

    def finish(self):
        while self.orders[0]:
            self.step()
        return self.current


def merge_kernel(facts, *refs, plans):
    count = len(plans)
    outs = list(refs[2 * count :])
    for plan, kept, came in zip(plans, refs[:count], refs[count : 2 * count]):
        entries, after, turn = plan["entries"], plan["after"], plan["turn"]

        def total(entry, kept=kept, came=came, after=after):
            own = kept[entry] if after is None else kept[entry >> after, 0, entry & ((1 << after) - 1)]
            return own.astype(wide_type) + came[entry].astype(wide_type)

        if turn is None:
            outs.pop(0)[...] = total(0)
            continue
        sent_out, kept_out = outs.pop(0), outs.pop(0)
        bit, behind = turn
        mine = (facts[0] >> bit) & 1
        for place in range(entries // 2):
            base = (place >> behind << (behind + 1)) | (place & ((1 << behind) - 1))
            kept_out[place] = total(base + (mine << behind)).astype(low_type)
            sent_out[place] = total(base + ((1 - mine) << behind)).astype(low_type)


class Sums:
    def __init__(self, arrays, orders, chip_index):
        self.chip_index = chip_index
        self.chips = arrays[0].shape[0]
        self.bits = self.chips.bit_length() - 1
        self.orders, self.step = orders, 0
        self.left = [tuple(range(self.bits - 1, -1, -1))] * len(arrays)
        self.kept, self.sent, self.came = list(arrays), None, None

    def copied(self):
        other = object.__new__(Sums)
        other.__dict__.update(self.__dict__)
        return other

    @property
    def going(self):
        return self.step < self.bits

    def start(self, value):
        views = []
        self.sent = []
        for array, order in zip(self.kept, self.orders):
            behind = order[0]
            ahead = self.bits - 1 - behind
            view = array.reshape((1 << ahead, 2, 1 << behind) + array.shape[1:])
            mine = (self.chip_index >> order[0]) & 1
            sent = lax.dynamic_index_in_dim(view, 1 - mine, 1, False)
            self.sent.append(sent.reshape((self.chips // 2,) + array.shape[1:]))
            views.append(view)
        self.kept = views
        return self.leave(value)

    def leave(self, value):
        self.sent, value = tie((self.sent, value))
        self.came = [
            lax.ppermute(sent, "dp", [(chip, chip ^ (1 << order[self.step])) for chip in range(self.chips)])
            for sent, order in zip(self.sent, self.orders)
        ]
        return value

    def round(self, value, leave_last=False):
        self.came, value = tie((self.came, value))
        if self.step == self.bits - 1 and leave_last:
            self.step += 1
            return value
        plans, in_specs, out_specs, out_shape, left = [], [], [], [], []
        for kept, came, order, bits in zip(self.kept, self.came, self.orders, self.left):
            entries, rows, columns = came.shape
            bit = order[self.step]
            if self.step == 0:
                in_specs.append(
                    pl.BlockSpec(
                        (kept.shape[0], 1) + kept.shape[2:],
                        lambda j, facts, bit=bit: (0, (facts[0] >> bit) & 1, 0, 0, 0),
                    )
                )
            else:
                in_specs.append(whole(kept.shape))
            bits = tuple(other for other in bits if other != bit)
            left.append(bits)
            plan = {"entries": entries, "after": bit if self.step == 0 else None, "turn": None}
            if bits:
                following = order[self.step + 1]
                plan["turn"] = (following, len(bits) - 1 - bits.index(following))
                half = (entries // 2, rows, columns)
                out_specs += [whole(half)] * 2
                out_shape += [jax.ShapeDtypeStruct(half, low_type)] * 2
            else:
                out_specs.append(whole((rows, columns)))
                out_shape.append(jax.ShapeDtypeStruct((rows, columns), wide_type))
            plans.append(plan)
        in_specs += [whole(came.shape) for came in self.came]
        made = pl.pallas_call(
            partial(merge_kernel, plans=plans),
            grid_spec=pltpu.PrefetchScalarGridSpec(
                num_scalar_prefetch=1, grid=(1,), in_specs=in_specs, out_specs=out_specs
            ),
            out_shape=out_shape,
            compiler_params=pltpu.CompilerParams(vmem_limit_bytes=vmem_budget),
            cost_estimate=heavy,
            name="merge_sums",
        )(self.chip_index[None].astype(jnp.int32), *self.kept, *self.came)
        self.left = left
        self.step += 1
        if not self.going:
            self.kept = made
            return value
        self.sent, self.kept = made[0::2], made[1::2]
        return self.leave(value)


def gather_kernel(owner, rows, out, held, came, gone, *, docs):
    loads = [pltpu.make_async_copy(rows.at[owner[slot]], held.at[slot], came.at[slot]) for slot in range(docs)]
    stores = [pltpu.make_async_copy(held.at[slot], out.at[slot], gone.at[slot]) for slot in range(docs)]
    for load in loads:
        load.start()
    for load, store in zip(loads, stores):
        load.wait()
        store.start()
    for store in stores:
        store.wait()


def gather_docs(memory_in, doc_owner):
    docs = memory_in.shape[0]
    return pl.pallas_call(
        partial(gather_kernel, docs=docs),
        grid_spec=pltpu.PrefetchScalarGridSpec(
            num_scalar_prefetch=1,
            grid=(),
            in_specs=[pl.BlockSpec(memory_space=pl.ANY)],
            out_specs=pl.BlockSpec(memory_space=pl.ANY),
            scratch_shapes=[
                pltpu.VMEM(memory_in.shape, low_type),
                pltpu.SemaphoreType.DMA((docs,)),
                pltpu.SemaphoreType.DMA((docs,)),
            ],
        ),
        out_shape=jax.ShapeDtypeStruct(memory_in.shape, low_type),
        compiler_params=pltpu.CompilerParams(vmem_limit_bytes=vmem_budget),
        cost_estimate=heavy,
        name="gather_docs",
    )(doc_owner, memory_in)


def prepare_kernel(
    cross_kv, conv, cross_out, ffn_in, self_qkv, cross_query, self_out,
    pair, pair_t, conv_t, cross_out_t, ffn_in_t, own, own_t, cross_query_t, self_out_t,
):
    width = conv.shape[0]
    half = cross_out.shape[0]
    for side in range(2):
        part = cross_kv[:, side, :]
        pair[:, side * width : side * width + width] = part
        pair_t[side * width : side * width + width, :] = part.T
    for side in range(3):
        part = self_qkv[:, side, :]
        own[:, side * half : side * half + half] = part
        own_t[side * half : side * half + half, :] = part.T
    conv_t[...] = conv[...].T
    cross_out_t[...] = cross_out[...].T
    ffn_in_t[...] = ffn_in[...].T
    cross_query_t[...] = cross_query[...].T
    self_out_t[...] = self_out[...].T


def prepare_weights(cross_kv, conv, cross_out, ffn_in, self_qkv, cross_query, self_out):
    half, width = cross_out.shape
    shapes = (
        (width, 2 * width),
        (2 * width, width),
        (width, width),
        (width, half),
        ffn_in.shape[::-1],
        (width, 3 * half),
        (3 * half, width),
        (half, width),
        (width, half),
    )
    return pl.pallas_call(
        prepare_kernel,
        out_shape=[jax.ShapeDtypeStruct(shape, low_type) for shape in shapes],
        compiler_params=pltpu.CompilerParams(vmem_limit_bytes=vmem_budget),
        cost_estimate=heavy,
        name="prepare_weights",
    )(cross_kv, conv, cross_out, ffn_in, self_qkv, cross_query, self_out)


def moved_kernel(owner, facts, features, groups, out, stats, *, chips):
    slot = pl.program_id(0)
    sub, width = features.shape[1:]

    @pl.when(slot == 0)
    def _():
        own_group = (
            lax.broadcasted_iota(jnp.int32, (128, width), 1) // (width // GROUPS)
            == lax.broadcasted_iota(jnp.int32, (128, width), 0)
        ).astype(wide_type)
        stats[...] = jnp.dot(
            groups[...].reshape(chips * 8, 128), own_group, precision=lax.Precision.HIGHEST
        ).reshape(chips, 8, width)

    position = (lax.broadcasted_iota(jnp.int32, (sub, 1), 0) * 2 + facts[1]) * chips + facts[0]
    normed = (features[0].astype(wide_type) - stats[slot, 0:1, :]) * stats[slot, 1:2, :]
    moved = stats[slot, 1:2, :] * (stats[slot, 2:3, :] + normed * stats[slot, 3:4, :])
    out[0] = jnp.where(position < facts[2 + owner[slot]], moved, 0.0).astype(low_type)


def moved_rows(doc_owner, facts, features, groups):
    docs, sub, width = features.shape
    return pl.pallas_call(
        partial(moved_kernel, chips=docs),
        grid_spec=pltpu.PrefetchScalarGridSpec(
            num_scalar_prefetch=2,
            grid=(docs,),
            in_specs=[
                pl.BlockSpec((1, sub, width), lambda j, owner, facts: (owner[j], 0, 0)),
                pl.BlockSpec(groups.shape, lambda j, owner, facts: (0, 0, 0)),
            ],
            out_specs=pl.BlockSpec((1, sub, width), lambda j, owner, facts: (j, 0, 0)),
            scratch_shapes=[pltpu.VMEM((docs, 8, width), wide_type)],
        ),
        out_shape=jax.ShapeDtypeStruct(features.shape, low_type),
        compiler_params=pltpu.CompilerParams(vmem_limit_bytes=vmem_budget),
        cost_estimate=heavy,
        name="moved_rows",
    )(doc_owner, facts, features, groups)


def spread_kernel(owner, rows, moved, out, held, taken, wide, came, also, gone, *, docs):
    loads = [pltpu.make_async_copy(rows.at[slot], held.at[slot], came.at[slot]) for slot in range(docs)]
    takes = [pltpu.make_async_copy(moved.at[slot], taken.at[slot], also.at[slot]) for slot in range(docs)]
    stores = [pltpu.make_async_copy(wide.at[slot], out.at[owner[slot]], gone.at[slot]) for slot in range(docs)]
    for load, take in zip(loads, takes):
        load.start()
        take.start()
    for slot in range(docs):
        loads[slot].wait()
        takes[slot].wait()
        wide[slot] = held[slot].astype(wide_type) - taken[slot].astype(wide_type)
        stores[slot].start()
    for store in stores:
        store.wait()


def spread_docs(rows, moved, doc_owner):
    docs = rows.shape[0]
    return pl.pallas_call(
        partial(spread_kernel, docs=docs),
        grid_spec=pltpu.PrefetchScalarGridSpec(
            num_scalar_prefetch=1,
            grid=(),
            in_specs=[pl.BlockSpec(memory_space=pl.ANY), pl.BlockSpec(memory_space=pl.ANY)],
            out_specs=pl.BlockSpec(memory_space=pl.ANY),
            scratch_shapes=[
                pltpu.VMEM(rows.shape, low_type),
                pltpu.VMEM(rows.shape, low_type),
                pltpu.VMEM(rows.shape, wide_type),
                pltpu.SemaphoreType.DMA((docs,)),
                pltpu.SemaphoreType.DMA((docs,)),
                pltpu.SemaphoreType.DMA((docs,)),
            ],
        ),
        out_shape=jax.ShapeDtypeStruct(rows.shape, wide_type),
        compiler_params=pltpu.CompilerParams(vmem_limit_bytes=vmem_budget),
        cost_estimate=heavy,
        name="spread_docs",
    )(doc_owner, rows, moved)


def chunk_of(chips, sub):
    return min(sub, max(16, 512 // chips))


def live_rows(facts, start, chips, span):
    row = lax.broadcasted_iota(jnp.int32, (chips * span, 1), 0)
    chip, step = row // span, row % span
    return ((start + step) * 2 + facts[1]) * chips + chip < facts[0]


def in_branches(facts, start, chips, span, work, dead=None):
    first = (start * 2 + facts[1]) * chips
    last = ((start + span - 1) * 2 + facts[1]) * chips + chips - 1
    full = last < facts[0]
    none = first >= facts[0]

    @pl.when(full)
    def _():
        work(None)

    @pl.when(jnp.logical_not(full) & jnp.logical_not(none))
    def _():
        work(live_rows(facts, start, chips, span))

    if dead is not None:
        pl.when(none)(dead)


def whole(shape):
    return pl.BlockSpec(shape, lambda j, facts: (0,) * len(shape))


def slab(shape, span):
    return pl.BlockSpec((shape[0], span, shape[2]), lambda j, facts: (0, j, 0))


def memory_forward_kernel(facts, rows, stats, weight, out, *, chips, span):
    width = rows.shape[-1]
    wide = rows[...].reshape(chips * span, width).astype(wide_type)
    drive = (wide - stats[0:1, :]) * stats[1:2, :] * stats[2:3, :] + stats[3:4, :]
    hidden = (drive / (1.0 + jnp.exp(-drive))).astype(low_type)
    made = wide + dot_wide(hidden, weight[...])
    out[...] = made.astype(low_type).reshape(chips, span, width)


def memory_forward(facts, rows, stats, weight):
    chips, sub, width = rows.shape
    span = chunk_of(chips, sub)
    return pl.pallas_call(
        partial(memory_forward_kernel, chips=chips, span=span),
        grid_spec=pltpu.PrefetchScalarGridSpec(
            num_scalar_prefetch=1,
            grid=(sub // span,),
            in_specs=[slab(rows.shape, span), whole(stats.shape), whole(weight.shape)],
            out_specs=slab(rows.shape, span),
        ),
        out_shape=jax.ShapeDtypeStruct(rows.shape, low_type),
        compiler_params=pltpu.CompilerParams(vmem_limit_bytes=vmem_budget),
        cost_estimate=heavy,
        name="memory_forward",
    )(facts, rows, stats, weight)


def memory_backward_kernel(
    facts, rows, own, came, stats, weight_t, grad_out, hidden_out, base_out, sums, groups, *, chips, span, steps
):
    step = pl.program_id(0)
    width = rows.shape[-1]
    count = chips * span

    @pl.when(step == 0)
    def _():
        sums[...] = jnp.zeros_like(sums)

    wide = rows[...].reshape(count, width).astype(wide_type)
    normed = (wide - stats[0:1, :]) * stats[1:2, :]
    drive = normed * stats[2:3, :] + stats[3:4, :]
    gate = 1.0 / (1.0 + jnp.exp(-drive))
    hidden_out[...] = (drive * gate).astype(low_type).reshape(chips, span, width)
    grad = (own[...].reshape(count, width) + came[...].reshape(count, width).astype(wide_type)).astype(low_type)
    grad_out[...] = grad.reshape(chips, span, width)
    grad_act = dot_wide(grad, weight_t[...]) * (gate * (1.0 + drive * (1.0 - gate)))
    sums[0:1, :] += jnp.sum(grad_act, axis=0, keepdims=True)
    sums[1:2, :] += jnp.sum(grad_act * normed, axis=0, keepdims=True)
    base = grad.astype(wide_type) + grad_act * (stats[1:2, :] * stats[2:3, :])
    base_out[...] = base.astype(low_type).reshape(chips, span, width)

    @pl.when(step == steps - 1)
    def _():
        per_group = width // GROUPS
        group_of = (
            lax.broadcasted_iota(jnp.int32, (width, 128), 0) // per_group
            == lax.broadcasted_iota(jnp.int32, (width, 128), 1)
        ).astype(wide_type)
        entries = (facts[0] * per_group).astype(wide_type)
        rows_of = jnp.concatenate(
            (
                stats[0:2, :] * (0.5 / per_group),
                sums[0:2, :] * stats[2:3, :] / entries,
                jnp.zeros((4, width), wide_type),
            )
        )
        groups[...] = jnp.dot(rows_of, group_of, precision=lax.Precision.HIGHEST)


def memory_backward(facts, rows, own, came, stats, weight_t):
    chips, sub, width = rows.shape
    span = chunk_of(chips, sub)
    block = slab(rows.shape, span)
    return pl.pallas_call(
        partial(memory_backward_kernel, chips=chips, span=span, steps=sub // span),
        grid_spec=pltpu.PrefetchScalarGridSpec(
            num_scalar_prefetch=1,
            grid=(sub // span,),
            in_specs=[block, block, block, whole(stats.shape), whole(weight_t.shape)],
            out_specs=[block, block, block, whole(stats.shape), whole((8, 128))],
        ),
        out_shape=[
            jax.ShapeDtypeStruct(rows.shape, low_type),
            jax.ShapeDtypeStruct(rows.shape, low_type),
            jax.ShapeDtypeStruct(rows.shape, low_type),
            jax.ShapeDtypeStruct(stats.shape, wide_type),
            jax.ShapeDtypeStruct((8, 128), wide_type),
        ],
        compiler_params=pltpu.CompilerParams(vmem_limit_bytes=vmem_budget),
        cost_estimate=heavy,
        name="memory_backward",
    )(facts, rows, own, came, stats, weight_t)


def cross_forward_kernel(
    facts, query_t, rows, key_weight, value_weight, top_in, total_in, sum_in, pairs, top, total, gathered,
    *, chips, span
):
    step = pl.program_id(0)
    half = key_weight.shape[1]
    width = rows.shape[-1]

    @pl.when(step == 0)
    def _():
        top[...] = top_in[...]
        total[...] = total_in[...]
        gathered[...] = sum_in[...]

    def work(live):
        block = rows[...].reshape(chips * span, width)
        keys = dot_wide(block, key_weight[...]).astype(low_type)
        values = dot_wide(block, value_weight[...]).astype(low_type)
        pairs[:, :, :half] = keys.reshape(chips, span, half)
        pairs[:, :, half:] = values.reshape(chips, span, half)
        for pair in range(half // 128):
            key_pair = keys[:, pair * 128 : pair * 128 + 128]
            value_pair = values[:, pair * 128 : pair * 128 + 128]
            for side in range(2):
                head = pair * 2 + side
                scores = dot_wide(key_pair, query_t[head])
                if live is not None:
                    scores = jnp.where(live, scores, masked_fill)
                old_top = top[head : head + 1, :]
                new_top = jnp.maximum(old_top, jnp.max(scores, axis=0, keepdims=True))
                weights = jnp.exp(scores - new_top)
                shrink = jnp.exp(old_top - new_top)
                total[head : head + 1, :] = total[head : head + 1, :] * shrink + jnp.sum(
                    weights, axis=0, keepdims=True
                )
                part = dot_rows(value_pair, weights.astype(low_type))
                gathered[head * HD : head * HD + HD, :] = (
                    gathered[head * HD : head * HD + HD, :] * shrink + part[side * HD : side * HD + HD, :]
                )
                top[head : head + 1, :] = new_top

    def dead():
        pairs[...] = jnp.zeros_like(pairs)

    in_branches(facts, step * span, chips, span, work, dead)


def cross_forward(facts, query_t, rows, weight, carry):
    chips, sub, width = rows.shape
    heads, _, queries = query_t.shape
    half = heads * HD
    span = chunk_of(chips, sub)
    stat = (8, queries)
    summed = (half, queries)
    return pl.pallas_call(
        partial(cross_forward_kernel, chips=chips, span=span),
        grid_spec=pltpu.PrefetchScalarGridSpec(
            num_scalar_prefetch=1,
            grid=(sub // span,),
            in_specs=[
                whole(query_t.shape),
                slab(rows.shape, span),
                pl.BlockSpec((width, half), lambda j, facts: (0, facts[2])),
                pl.BlockSpec((width, half), lambda j, facts: (0, 2 + facts[2])),
                whole(stat),
                whole(stat),
                whole(summed),
            ],
            out_specs=[slab((chips, sub, 2 * half), span), whole(stat), whole(stat), whole(summed)],
        ),
        out_shape=[
            jax.ShapeDtypeStruct((chips, sub, 2 * half), low_type),
            jax.ShapeDtypeStruct(stat, wide_type),
            jax.ShapeDtypeStruct(stat, wide_type),
            jax.ShapeDtypeStruct(summed, wide_type),
        ],
        compiler_params=pltpu.CompilerParams(vmem_limit_bytes=vmem_budget),
        cost_estimate=heavy,
        name="cross_forward",
    )(facts, query_t, rows, weight, weight, *carry)


def cross_close_kernel(gathered, top, total, weight, crossed, crossed_t, log_total, part, *, heads):
    log_total[...] = top[...] + jnp.log(jnp.maximum(total[...], 1e-30))
    for head in range(heads):
        rows = slice(head * HD, head * HD + HD)
        crossed_t[rows, :] = gathered[rows, :] / total[head : head + 1, :]
    low = crossed_t[...].T.astype(low_type)
    crossed[...] = low
    part[...] = dot_wide(low, weight[...])


def cross_close(gathered, top, total, weight):
    half, queries = gathered.shape
    return pl.pallas_call(
        partial(cross_close_kernel, heads=half // HD),
        out_shape=[
            jax.ShapeDtypeStruct((queries, half), low_type),
            jax.ShapeDtypeStruct((half, queries), wide_type),
            jax.ShapeDtypeStruct(top.shape, wide_type),
            jax.ShapeDtypeStruct((queries, weight.shape[1]), wide_type),
        ],
        compiler_params=pltpu.CompilerParams(vmem_limit_bytes=vmem_budget),
        cost_estimate=heavy,
        name="cross_close",
    )(gathered, top, total, weight)


gelu_scale = 0.7978845608028654
gelu_cubic = 0.044715


def feed_forward_kernel(
    first, own, came, gain, weight, weight_t, grad_active, second, normed, both_grad, both_active, grad_normed
):
    step = pl.program_id(0)

    @pl.when(step == 0)
    def _():
        total = first[...] + (own[...] + came[...])
        second[...] = total
        factor = lax.rsqrt(jnp.mean(total * total, axis=-1, keepdims=True) + norm_eps)
        normed[...] = (total * factor * gain[...]).astype(low_type)
        grad_normed[...] = jnp.zeros_like(grad_normed)

    lifted = dot_wide(normed[...], weight[...])
    square = lifted * lifted
    bent = jnp.tanh(gelu_scale * (lifted * (1.0 + gelu_cubic * square)))
    half_up = 0.5 * (1.0 + bent)
    both_active[...] = (lifted * half_up).astype(low_type)
    slope = half_up + (0.5 * gelu_scale) * lifted * (1.0 - bent * bent) * (1.0 + 3.0 * gelu_cubic * square)
    grad_lifted = (grad_active[...].astype(wide_type) * slope).astype(low_type)
    both_grad[...] = grad_lifted
    grad_normed[...] += dot_wide(grad_lifted, weight_t[...])


def feed_forward(first, own, came, gain, weight, weight_t, grad_active):
    rows, width = first.shape
    hidden = weight.shape[1]
    block = 512
    still = pl.BlockSpec((rows, width), lambda j: (0, 0))
    moving = pl.BlockSpec((rows, block), lambda j: (0, j))
    return pl.pallas_call(
        feed_forward_kernel,
        grid=(hidden // block,),
        in_specs=[
            still,
            still,
            still,
            pl.BlockSpec((1, width), lambda j: (0, 0)),
            pl.BlockSpec((width, block), lambda j: (0, j)),
            pl.BlockSpec((block, width), lambda j: (j, 0)),
            moving,
        ],
        out_specs=[still, still, moving, moving, still],
        out_shape=[
            jax.ShapeDtypeStruct((rows, width), wide_type),
            jax.ShapeDtypeStruct((rows, width), low_type),
            jax.ShapeDtypeStruct((rows, hidden), low_type),
            jax.ShapeDtypeStruct((rows, hidden), low_type),
            jax.ShapeDtypeStruct((rows, width), wide_type),
        ],
        compiler_params=pltpu.CompilerParams(vmem_limit_bytes=vmem_budget),
        cost_estimate=heavy,
        name="feed_forward",
    )(first, own, came, gain, weight, weight_t, grad_active)


def feed_close_kernel(
    second, own, came, gain, grad_out, weight_t, crossed_t, grad_second, gain_grad, grad_cross, heads_out,
    heads_out_t, inner, *, heads,
):
    values = second[...]
    incoming = (own[...] + came[...]).astype(low_type).astype(wide_type)
    factor = lax.rsqrt(jnp.mean(values * values, axis=-1, keepdims=True) + norm_eps)
    scaled = incoming * gain[...]
    inward = factor * scaled - values * (factor * factor * factor) * jnp.mean(
        scaled * values, axis=-1, keepdims=True
    )
    gain_grad[...] = jnp.broadcast_to(
        jnp.sum(incoming * values * factor, axis=0, keepdims=True), gain_grad.shape
    )
    total = inward + grad_out[...].astype(wide_type)
    grad_second[...] = total
    low = total.astype(low_type)
    grad_cross[...] = low
    made = dot_wide(low, weight_t[...])
    made_low = made.astype(low_type)
    made_t = made_low.astype(wide_type).T
    low_t = made_t.astype(low_type)
    left = lax.broadcasted_iota(jnp.int32, (made.shape[0], 128), 1) < HD
    inner[...] = jnp.zeros_like(inner)
    for head in range(heads):
        pair = made_low[:, head // 2 * 128 : head // 2 * 128 + 128]
        keep = left if head % 2 == 0 else jnp.logical_not(left)
        heads_out[head] = jnp.where(keep, pair, jnp.zeros_like(pair))
        rows = slice(head * HD, head * HD + HD)
        own_rows = slice(head % 2 * HD, head % 2 * HD + HD)
        other_rows = slice((1 - head % 2) * HD, (1 - head % 2) * HD + HD)
        heads_out_t[head, own_rows, :] = low_t[rows, :]
        heads_out_t[head, other_rows, :] = jnp.zeros_like(low_t[rows, :])
        inner[head : head + 1, :] = jnp.sum(made_t[rows, :] * crossed_t[rows, :], axis=0, keepdims=True)


def feed_close(second, own, came, gain, grad_out, weight_t, crossed_t):
    rows, width = second.shape
    half = weight_t.shape[1]
    heads = half // HD
    return pl.pallas_call(
        partial(feed_close_kernel, heads=heads),
        out_shape=[
            jax.ShapeDtypeStruct((rows, width), wide_type),
            jax.ShapeDtypeStruct((8, width), wide_type),
            jax.ShapeDtypeStruct((rows, width), low_type),
            jax.ShapeDtypeStruct((heads, rows, 128), low_type),
            jax.ShapeDtypeStruct((heads, 128, rows), low_type),
            jax.ShapeDtypeStruct((8, rows), wide_type),
        ],
        compiler_params=pltpu.CompilerParams(vmem_limit_bytes=vmem_budget),
        cost_estimate=heavy,
        name="feed_close",
    )(second, own, came, gain, grad_out, weight_t, crossed_t)


def feed_weights_kernel(
    normed, grad_out, grad_cross, both_grad, both_active, crossed, left, middle, right, turned, *, steps
):
    step = pl.program_id(0)
    third = (2 * steps + 1) // 3

    @pl.when(step == 0)
    def _():
        turned[...] = normed[...].T

    @pl.when(step == steps)
    def _():
        turned[...] = grad_out[...].T

    @pl.when(step == 2 * steps)
    def _():
        turned[...] = grad_cross[...].T

    for number, out in enumerate((left, middle, right)):
        inside = (step >= number * third) & (step < number * third + third)

        @pl.when(inside & (step < steps))
        def _(out=out):
            out[...] = dot_wide(turned[...], both_grad[...]).astype(low_type)

        @pl.when(inside & (step >= steps) & (step < 2 * steps))
        def _(out=out):
            out[...] = dot_wide(turned[...], both_active[...]).astype(low_type)

        @pl.when(inside & (step == 2 * steps))
        def _(out=out):
            out[...] = dot_wide(turned[...], crossed[...]).astype(low_type)


def feed_weights(normed, grad_out, grad_cross, grad_lifted, active, crossed):
    rows, width = normed.shape
    hidden = active.shape[1]
    block = crossed.shape[1]
    steps = hidden // block
    third = (2 * steps + 1) // 3

    def piece(number):
        return pl.BlockSpec((width, block), lambda j: (0, jnp.clip(j - number * third, 0, third - 1)))

    still = pl.BlockSpec((rows, width), lambda j: (0, 0))
    return pl.pallas_call(
        partial(feed_weights_kernel, steps=steps),
        grid=(2 * steps + 1,),
        in_specs=[
            still,
            still,
            still,
            pl.BlockSpec((rows, block), lambda j: (0, jnp.minimum(j, steps - 1))),
            pl.BlockSpec((rows, block), lambda j: (0, jnp.clip(j - steps, 0, steps - 1))),
            pl.BlockSpec((rows, block), lambda j: (0, 0)),
        ],
        out_specs=[piece(number) for number in range(3)],
        out_shape=[jax.ShapeDtypeStruct((width, third * block), low_type)] * 3,
        scratch_shapes=[pltpu.VMEM((width, rows), low_type)],
        compiler_params=pltpu.CompilerParams(vmem_limit_bytes=vmem_budget),
        cost_estimate=heavy,
        name="feed_weights",
    )(normed, grad_out, grad_cross, grad_lifted, active, crossed)


def cross_backward_kernel(
    facts, query, query_t, grad, grad_t, log_total, inner, pairs, key_weight_t, value_weight_t, pair_grads,
    row_grads, query_grad, held, *, chips, span
):
    step = pl.program_id(0)
    half, width = key_weight_t.shape

    @pl.when(step == 0)
    def _():
        query_grad[...] = jnp.zeros_like(query_grad)

    def work(live):
        block = pairs[...].reshape(chips * span, 2 * half)
        for pair in range(half // 128):
            key_pair = block[:, pair * 128 : pair * 128 + 128]
            value_pair = block[:, half + pair * 128 : half + pair * 128 + 128]
            key_sum, value_sum = 0.0, 0.0
            for side in range(2):
                head = pair * 2 + side
                scores = dot_wide(key_pair, query_t[head])
                if live is not None:
                    scores = jnp.where(live, scores, masked_fill)
                probs = jnp.exp(scores - log_total[head : head + 1, :])
                grad_probs = dot_wide(value_pair, grad_t[head])
                grad_scores = (probs * (grad_probs - inner[head : head + 1, :])).astype(low_type)
                value_sum = value_sum + dot_wide(probs.astype(low_type), grad[head])
                key_sum = key_sum + dot_wide(grad_scores, query[head])
                part = dot_rows(key_pair, grad_scores)
                query_grad[head * HD : head * HD + HD, :] += part[side * HD : side * HD + HD, :]
            held[:, pair * 128 : pair * 128 + 128] = key_sum.astype(low_type)
            held[:, half + pair * 128 : half + pair * 128 + 128] = value_sum.astype(low_type)
        made = held[...]
        pair_grads[...] = made.reshape(chips, span, 2 * half)
        back = dot_wide(made[:, :half], key_weight_t[...]) + dot_wide(made[:, half:], value_weight_t[...])
        row_grads[...] = back.astype(row_grads.dtype).reshape(chips, span, width)

    def dead():
        pair_grads[...] = jnp.zeros_like(pair_grads)
        row_grads[...] = jnp.zeros_like(row_grads)

    in_branches(facts, step * span, chips, span, work, dead)


def cross_backward(facts, query, query_t, grad, grad_t, log_total, inner, pairs, weight_t, grad_type):
    chips, sub, both = pairs.shape
    width = weight_t.shape[1]
    heads, _, queries = query_t.shape
    span = chunk_of(chips, sub)
    half = both // 2
    pair_block = slab(pairs.shape, span)
    row_block = slab((chips, sub, width), span)
    return pl.pallas_call(
        partial(cross_backward_kernel, chips=chips, span=span),
        grid_spec=pltpu.PrefetchScalarGridSpec(
            num_scalar_prefetch=1,
            grid=(sub // span,),
            in_specs=[
                whole(query.shape),
                whole(query_t.shape),
                whole(grad.shape),
                whole(grad_t.shape),
                whole(log_total.shape),
                whole(inner.shape),
                pair_block,
                pl.BlockSpec((half, width), lambda j, facts: (facts[2], 0)),
                pl.BlockSpec((half, width), lambda j, facts: (2 + facts[2], 0)),
            ],
            out_specs=[pair_block, row_block, whole((heads * HD, queries))],
            scratch_shapes=[pltpu.VMEM((chips * span, both), low_type)],
        ),
        out_shape=[
            jax.ShapeDtypeStruct((chips, sub, both), low_type),
            jax.ShapeDtypeStruct((chips, sub, width), grad_type),
            jax.ShapeDtypeStruct((heads * HD, queries), wide_type),
        ],
        compiler_params=pltpu.CompilerParams(vmem_limit_bytes=vmem_budget),
        cost_estimate=heavy,
        name="cross_backward",
    )(facts, query, query_t, grad, grad_t, log_total, inner, pairs, weight_t, weight_t)


def query_back_kernel(own, other, weight_t, grad, part):
    low = ((own[...] + other[...]) * 0.125).T.astype(low_type)
    grad[...] = low
    part[...] = dot_wide(low, weight_t[...])


def query_back(own, other, weight_t):
    half, rows = own.shape
    return pl.pallas_call(
        query_back_kernel,
        out_shape=[
            jax.ShapeDtypeStruct((rows, half), low_type),
            jax.ShapeDtypeStruct((rows, weight_t.shape[1]), wide_type),
        ],
        compiler_params=pltpu.CompilerParams(vmem_limit_bytes=vmem_budget),
        cost_estimate=heavy,
        name="query_back",
    )(own, other, weight_t)


def memory_weights_kernel(
    rows, hidden, other, pair_grads, row_grads, other_grads, pair_out, conv_out, pair_sum, conv_sum,
    *, chips, span, steps
):
    step = pl.program_id(0)
    count = chips * span

    def flat(ref):
        return ref[...].reshape(count, ref.shape[-1])

    @pl.when(step == 0)
    def _():
        pair_sum[...] = jnp.zeros_like(pair_sum)
        conv_sum[...] = jnp.zeros_like(conv_sum)

    pair_sum[...] += dot_rows(flat(rows), flat(pair_grads)) + dot_rows(flat(other), flat(other_grads))
    conv_sum[...] += dot_rows(flat(hidden), flat(row_grads))

    @pl.when(step == steps - 1)
    def _():
        pair_out[...] = pair_sum[...].astype(low_type)
        conv_out[...] = conv_sum[...].astype(low_type)


def memory_weights(rows, hidden, other, pair_grads, row_grads, other_grads):
    chips, sub, width = rows.shape
    span = chunk_of(chips, sub)
    both = pair_grads.shape[2]
    steps = sub // span
    block = pl.BlockSpec((chips, span, width), lambda j: (0, j, 0))
    pair_block = pl.BlockSpec((chips, span, both), lambda j: (0, j, 0))
    return pl.pallas_call(
        partial(memory_weights_kernel, chips=chips, span=span, steps=steps),
        grid=(steps,),
        in_specs=[block, block, block, pair_block, block, pair_block],
        out_specs=[pl.BlockSpec((width, both), lambda j: (0, 0)), pl.BlockSpec((width, width), lambda j: (0, 0))],
        out_shape=[
            jax.ShapeDtypeStruct((width, both), low_type),
            jax.ShapeDtypeStruct((width, width), low_type),
        ],
        scratch_shapes=[pltpu.VMEM((width, both), wide_type), pltpu.VMEM((width, width), wide_type)],
        compiler_params=pltpu.CompilerParams(vmem_limit_bytes=vmem_budget),
        cost_estimate=heavy,
        name="memory_weights",
    )(rows, hidden, other, pair_grads, row_grads, other_grads)


def side_weights_kernel(normed_one, grad_qkv, normed_two, grad_cq, grad_self, attended, own, others):
    half = attended.shape[1]
    own[...] = dot_rows(normed_one[...], grad_qkv[...]).astype(low_type)
    others[:, :half] = dot_rows(normed_two[...], grad_cq[...]).astype(low_type)
    others[:, half:] = dot_rows(grad_self[...], attended[...]).astype(low_type)


def side_weights(*args):
    width = args[0].shape[1]
    half = args[-1].shape[1]
    return pl.pallas_call(
        side_weights_kernel,
        out_shape=[
            jax.ShapeDtypeStruct((width, 3 * half), low_type),
            jax.ShapeDtypeStruct((width, 2 * half), low_type),
        ],
        compiler_params=pltpu.CompilerParams(vmem_limit_bytes=vmem_budget),
        cost_estimate=heavy,
        name="side_weights",
    )(*args)


def product_kernel(left, right, out):
    @pl.when(pl.program_id(0) == 0)
    def _():
        out[...] = jnp.zeros_like(out)

    out[...] += dot_wide(left[...], right[...])


def product(left, right):
    rows, depth = left.shape
    width = right.shape[1]
    block = 512
    return pl.pallas_call(
        product_kernel,
        grid=(depth // block,),
        in_specs=[
            pl.BlockSpec((rows, block), lambda j: (0, j)),
            pl.BlockSpec((block, width), lambda j: (j, 0)),
        ],
        out_specs=pl.BlockSpec((rows, width), lambda j: (0, 0)),
        out_shape=jax.ShapeDtypeStruct((rows, width), wide_type),
        compiler_params=pltpu.CompilerParams(vmem_limit_bytes=vmem_budget),
        cost_estimate=heavy,
        name="product",
    )(left, right)


def back_through_norm(values, incoming, gain):
    factor = lax.rsqrt(jnp.mean(values * values, axis=-1, keepdims=True) + norm_eps)
    scaled = incoming * gain
    inward = factor * scaled - values * (factor * factor * factor) * jnp.mean(
        scaled * values, axis=-1, keepdims=True
    )
    return inward, jnp.sum(incoming * values * factor, axis=0, keepdims=True)


def self_backward_kernel(
    facts, values, own, came, gain, grad_second, out_weight_t, triple, log_total, weight_t,
    grad_first, grad_low, gain_grad, triple_grad, part, *, heads,
):
    rows = triple.shape[0]
    half = heads * HD
    incoming = (own[...] + came[...]).astype(low_type).astype(wide_type)
    inward, gain_row = back_through_norm(values[...], incoming, gain[...])
    gain_grad[...] = jnp.broadcast_to(gain_row, gain_grad.shape)
    total = inward + grad_second[...]
    grad_first[...] = total
    grad_low[...] = total.astype(low_type)
    grad = dot_wide(grad_low[...], out_weight_t[...]).astype(low_type)
    key_pos = lax.broadcasted_iota(jnp.int32, (rows, rows), 0)
    query_pos = lax.broadcasted_iota(jnp.int32, (rows, rows), 1)
    allowed = (key_pos <= query_pos) & (key_pos < facts[0])
    left = lax.broadcasted_iota(jnp.int32, (rows, 128), 1) < HD
    for pair in range(heads // 2):
        lanes = slice(pair * 128, pair * 128 + 128)
        query_pair = triple[:, lanes]
        key_pair = triple[:, half + pair * 128 : half + pair * 128 + 128]
        value_pair = triple[:, 2 * half + pair * 128 : 2 * half + pair * 128 + 128]
        grad_pair = grad[:, lanes]
        key_sum, value_sum, query_parts = 0.0, 0.0, []
        for side in range(2):
            head = pair * 2 + side
            keep = left if side == 0 else jnp.logical_not(left)
            query = jnp.where(keep, query_pair, jnp.zeros_like(query_pair))
            grad_head = jnp.where(keep, grad_pair, jnp.zeros_like(grad_pair))
            scores = dot_columns(key_pair, query) * 0.125
            probs = jnp.exp(jnp.where(allowed, scores, masked_fill) - log_total[head : head + 1, :])
            grad_probs = dot_columns(value_pair, grad_head)
            inner = jnp.sum(probs * grad_probs, axis=0, keepdims=True)
            grad_scores = (probs * (grad_probs - inner)).astype(low_type)
            value_sum = value_sum + dot_wide(probs.astype(low_type), grad_head)
            key_sum = key_sum + dot_wide(grad_scores, query)
            query_parts.append(dot_rows(key_pair, grad_scores)[side * HD : side * HD + HD, :])
        triple_grad[:, lanes] = (jnp.concatenate(query_parts) * 0.125).T.astype(low_type)
        triple_grad[:, half + pair * 128 : half + pair * 128 + 128] = (key_sum * 0.125).astype(low_type)
        triple_grad[:, 2 * half + pair * 128 : 2 * half + pair * 128 + 128] = value_sum.astype(low_type)
    part[...] = dot_wide(triple_grad[...], weight_t[...])


def self_backward(facts, values, own, came, gain, grad_second, out_weight_t, triple, log_total, weight_t):
    rows, wide = triple.shape
    width = weight_t.shape[1]
    args = (values, own, came, gain, grad_second, out_weight_t, triple, log_total, weight_t)
    outs = (
        ((rows, width), wide_type),
        ((rows, width), low_type),
        ((8, width), wide_type),
        ((rows, wide), low_type),
        ((rows, width), wide_type),
    )
    return pl.pallas_call(
        partial(self_backward_kernel, heads=wide // (3 * HD)),
        grid_spec=pltpu.PrefetchScalarGridSpec(
            num_scalar_prefetch=1,
            grid=(1,),
            in_specs=[whole(arg.shape) for arg in args],
            out_specs=[whole(shape) for shape, _ in outs],
        ),
        out_shape=[jax.ShapeDtypeStruct(shape, kind) for shape, kind in outs],
        compiler_params=pltpu.CompilerParams(vmem_limit_bytes=vmem_budget),
        cost_estimate=heavy,
        name="self_backward",
    )(facts, *args)


def input_back_kernel(
    values, own, came, gain, grad_first, second, result_own, result_came, act_sums, cross_gain_grad,
    ffn_gain_grad, input_grad, layer_out, gains_out,
):
    incoming = (own[...] + came[...]).astype(low_type).astype(wide_type)
    inward, gain_row = back_through_norm(values[...].astype(wide_type), incoming, gain[...])
    input_grad[...] = inward + grad_first[...]
    layer_out[...] = (second[...] + (result_own[...] + result_came[...])).astype(low_type)
    width = values.shape[1]
    gains = jnp.concatenate(
        (
            act_sums[1:2, :],
            act_sums[0:1, :],
            0.5 * gain_row,
            0.5 * cross_gain_grad[0:1, :],
            0.5 * ffn_gain_grad[0:1, :],
            jnp.zeros((3, width), wide_type),
        )
    )
    for tile in range(width // 128):
        gains_out[tile] = gains[:, tile * 128 : tile * 128 + 128]


def input_back(*args):
    rows, width = args[0].shape
    outs = (((rows, width), wide_type), ((rows, width), low_type), ((width // 128, 8, 128), wide_type))
    return pl.pallas_call(
        input_back_kernel,
        out_shape=[jax.ShapeDtypeStruct(shape, kind) for shape, kind in outs],
        compiler_params=pltpu.CompilerParams(vmem_limit_bytes=vmem_budget),
        cost_estimate=heavy,
        name="input_back",
    )(*args)


def assemble_kernel(
    facts, pair, conv_part, pair_came, conv_came, own_kept, own_came, other_kept, other_came, left, middle, right, conv, cross_kv, cross_out,
    self_qkv, cross_query, self_out, ffn_in, ffn_out,
):
    width = conv.shape[1]
    half = width // 2
    third = left.shape[1]
    hidden = ffn_in.shape[1]
    first = facts[1] == 0
    conv[...] = conv_part[...] + conv_came[...]
    for side in range(2):
        mine = pair[:, side * half : side * half + half]
        theirs = pair_came[:, side * half : side * half + half]
        cross_kv[:, side, :half] = jnp.where(first, mine, theirs)
        cross_kv[:, side, half:] = jnp.where(first, theirs, mine)
    own = own_kept[0].astype(wide_type) + own_came[0].astype(wide_type)
    for side in range(3):
        self_qkv[:, side, :] = own[:, side * half : side * half + half]
    other = other_kept[0].astype(wide_type) + other_came[0].astype(wide_type)
    cross_query[...] = other[:, :half]
    self_out[...] = other[:, half:].T
    ffn_in[:, :third] = left[...]
    ffn_in[:, third:] = middle[:, : hidden - third]
    ffn_out[: 2 * third - hidden, :] = middle[:, hidden - third :].T
    ffn_out[2 * third - hidden :, :] = right[:, : 2 * hidden - 2 * third].T
    cross_out[...] = right[:, 2 * hidden - 2 * third :].T


def assemble(facts, *args):
    share, width = args[0].shape
    left = args[-1]
    half = width // 2
    hidden = (3 * left.shape[1] - half) // 2
    outs = (
        (share, width),
        (share, 2, width),
        (half, share),
        (share, 3, half),
        (share, half),
        (half, share),
        (share, hidden),
        (hidden, share),
    )
    return pl.pallas_call(
        assemble_kernel,
        grid_spec=pltpu.PrefetchScalarGridSpec(
            num_scalar_prefetch=1,
            grid=(1,),
            in_specs=[whole(arg.shape) for arg in args],
            out_specs=[whole(shape) for shape in outs],
        ),
        out_shape=[jax.ShapeDtypeStruct(shape, wide_type) for shape in outs],
        compiler_params=pltpu.CompilerParams(vmem_limit_bytes=vmem_budget),
        cost_estimate=heavy,
        name="assemble",
    )(facts, *args)


def padded_heads(values):
    rows, width = values.shape
    pairs = values.reshape(rows, width // 128, 128).transpose(1, 0, 2)
    left = lax.broadcasted_iota(jnp.int32, (1, 1, 128), 2) < HD
    none = jnp.zeros_like(pairs)
    both = jnp.stack((jnp.where(left, pairs, none), jnp.where(left, none, pairs)), axis=1)
    return both.reshape(width // HD, rows, 128)


def padded_heads_t(values_t):
    width, rows = values_t.shape
    pairs = values_t.reshape(width // 128, 2, HD, rows)
    none = jnp.zeros_like(pairs[:, 0])
    even = jnp.concatenate((pairs[:, 0], none), axis=1)
    odd = jnp.concatenate((none, pairs[:, 1]), axis=1)
    return jnp.stack((even, odd), axis=1).reshape(width // HD, 128, rows)


def attend(queries, key_rows, values, allowed):
    scores = (
        jnp.einsum("hne,hme->hnm", queries, key_rows, preferred_element_type=jnp.float32) * 0.125
    )
    scores = jnp.where(allowed, scores, masked_fill)
    row_max = jnp.max(scores, axis=-1, keepdims=True)
    shifted = jnp.exp(scores - row_max)
    row_total = jnp.sum(shifted, axis=-1, keepdims=True)
    weights = (shifted / row_total).astype(jnp.bfloat16)
    output = jnp.einsum("hnm,hme->hne", weights, values, preferred_element_type=jnp.float32)
    return (output.astype(jnp.bfloat16), (row_max + jnp.log(row_total))[..., 0])


def shards(
    dec_input,
    out_grad,
    enc_feats,
    mem_lengths,
    dec_lengths,
    doc_owner,
    group_gain,
    group_bias,
    conv_weight,
    cross_kv,
    self_gain,
    self_qkv,
    self_out,
    cross_gain,
    cross_query,
    cross_out,
    ffn_gain,
    ffn_in,
    ffn_out,
):
    chips = lax.axis_size("dp")
    chip_index = lax.axis_index("dp")
    core_index = lax.axis_index("mp")
    memory_in = enc_feats[0, 0]
    docs, sub, width = memory_in.shape
    per_group = width // GROUPS
    half = width // 2
    heads = half // HD
    rows_here = docs * sub
    share = width // chips
    bits = chips.bit_length() - 1
    rest = tuple(range(4, bits))
    order_sets = {
        "stats": (0, 1, 2, 3),
        "left": (2, 3, 0, 1),
        "middle": (0, 2, 3, 1),
        "right": (1, 2, 3, 0),
        "along": (0, 1, 2, 3),
        "across": (1, 0, 2, 3),
    }
    orders = {
        name: order + rest if bits >= 4 else tuple(range(bits)) for name, order in order_sets.items()
    }

    outgoing = gather_docs(memory_in, doc_owner)
    features = lax.all_to_all(outgoing, "dp", split_axis=0, concat_axis=0, tiled=True)
    outgoing, memory_here, dec_input = tie((outgoing, memory_in, dec_input))
    wide_in = memory_here.astype(wide_type)
    slot_pos = lax.broadcasted_iota(jnp.int32, (docs, sub), 1)
    live_in = ((slot_pos * 2 + core_index) * chips + chip_index < mem_lengths[:, None])[:, :, None]
    masked_in = jnp.where(live_in, wide_in, 0.0)
    channel_sums = jnp.stack((jnp.sum(masked_in, axis=1), jnp.sum(masked_in * wide_in, axis=1)), axis=1)
    group_of = (
        lax.broadcasted_iota(jnp.int32, (width, GROUPS), 0) // per_group
        == lax.broadcasted_iota(jnp.int32, (width, GROUPS), 1)
    ).astype(wide_type)

    def group_sums(channels):
        return jnp.dot(channels, group_of, precision=lax.Precision.HIGHEST)

    def to_channels(groups):
        return jnp.dot(groups, group_of.T, precision=lax.Precision.HIGHEST)

    sums_here = group_sums(channel_sums.reshape(docs * 2, width)).reshape(docs, 2 * GROUPS)
    sums_here = jnp.take(sums_here, doc_owner, axis=0, mode="clip")
    stat_sums = ScatterSums([core_total(sums_here)], [orders["stats"]], chip_index)
    stat_sums.begin()

    dec_rows = DEC
    dec_rows_in = dec_input.reshape(dec_rows, width)
    input_flat = dec_rows_in.astype(wide_type)
    input_flat = stat_sums.ahead_of(input_flat)
    stat_sums.send()
    normed_one, factor_one = norm_rows(input_flat, self_gain)
    normed_one = normed_one.astype(low_type)
    grad_low = out_grad.reshape(DEC, width)
    grad_active = dot_columns(grad_low, ffn_out).astype(low_type)
    prepared = (
        *prepare_weights(cross_kv, conv_weight, cross_out, ffn_in, self_qkv, cross_query, self_out), grad_active
    )
    normed_one, prepared = tie((normed_one, prepared))
    pair_weight, weight_t, conv_weight_t, cross_out_t, ffn_in_t = prepared[:5]
    self_weight, self_weight_t, cross_query_t, self_out_t, grad_active = prepared[5:]

    def next_step(sums, value):
        value = sums.behind(value)
        sums.merge()
        if sums.orders[0]:
            sums.begin()
            value = sums.ahead_of(value)
            sums.send()
        return value

    qkv_self = dot_wide(normed_one, self_weight).astype(low_type)
    qkv_self = next_step(stat_sums, qkv_self)
    qkv_heads = qkv_self.reshape(DEC, 3, heads, HD).transpose(1, 2, 0, 3)
    row_pos = lax.broadcasted_iota(jnp.int32, (DEC, DEC), 0)
    col_pos = lax.broadcasted_iota(jnp.int32, (DEC, DEC), 1)
    allowed = ((col_pos <= row_pos) & (col_pos < dec_lengths[chip_index]))[None]
    output, self_total = attend(qkv_heads[0], qkv_heads[1], qkv_heads[2], allowed)
    self_totals = jnp.concatenate((self_total, jnp.zeros((8 - heads, DEC), wide_type)))
    attended = output.transpose(1, 0, 2).reshape(dec_rows, half)
    attended = next_step(stat_sums, attended)
    first_out = input_flat + core_total(dot_wide(attended, self_out))
    normed_two, factor_two = norm_rows(first_out, cross_gain)
    normed_two = normed_two.astype(low_type)
    normed_two = next_step(stat_sums, normed_two)
    cross_q = dot_wide(normed_two, cross_query).astype(low_type) * jnp.asarray(0.125, low_type)
    query_heads = padded_heads(cross_q)
    query_heads_t = padded_heads_t(cross_q.T)
    while stat_sums.orders[0]:
        query_heads = next_step(stat_sums, query_heads)
    sums_all = stat_sums.current[0]

    document = doc_owner[chip_index]
    length = mem_lengths[document]
    entries = (length * per_group).astype(wide_type)
    center = sums_all[:GROUPS] / entries
    spread = lax.rsqrt(sums_all[GROUPS:] / entries - center * center + group_eps)
    channel_stats = to_channels(jnp.stack((center, spread)))
    stats = jnp.concatenate(
        (channel_stats, group_gain[None], group_bias[None], jnp.zeros((4, width), wide_type))
    )

    facts_own = jnp.stack((length, core_index, core_index)).astype(jnp.int32)
    facts_other = jnp.stack((length, 1 - core_index, core_index)).astype(jnp.int32)
    features, stats, query_heads, query_heads_t = tie((features, stats, query_heads, query_heads_t))
    memory_own = memory_forward(facts_own, features, stats, conv_weight)
    memory_other = other_core(memory_own)

    carry = (
        jnp.full((8, dec_rows), -1e30, wide_type),
        jnp.zeros((8, dec_rows), wide_type),
        jnp.zeros((half, dec_rows), wide_type),
    )
    pairs_own, *carry = cross_forward(
        facts_own, query_heads_t, memory_own, pair_weight, carry
    )
    pairs_other, top, total, gathered = cross_forward(
        facts_other, query_heads_t, memory_other, pair_weight, carry
    )
    crossed, crossed_t, log_total, part = cross_close(gathered, top, total, cross_out)

    second_out, normed_three, grad_lifted, active, part = feed_forward(
        first_out, part, other_core(part), ffn_gain[None], ffn_in, ffn_in_t, grad_active
    )
    part_came = other_core(part)
    result_part = product(active, ffn_out)
    part_came, result_part = tie((part_came, result_part))
    result_came = other_core(result_part)
    grad_second, ffn_gain_grad, grad_cross, grad_heads, grad_heads_t, inner = feed_close(
        second_out, part, part_came, ffn_gain[None], grad_low, cross_out_t, crossed_t
    )
    feed_grads = feed_weights(normed_three, grad_low, grad_cross, grad_lifted, active, crossed)
    feed_sums = Sums(
        [grad.reshape(chips, share, grad.shape[1]) for grad in feed_grads],
        [orders["left"], orders["middle"], orders["right"]],
        chip_index,
    )
    inner = feed_sums.start(inner)

    pair_grads_other, row_grads_other, query_grad_other = cross_backward(
        facts_other, query_heads, query_heads_t, grad_heads, grad_heads_t, log_total, inner, pairs_other, weight_t,
        low_type,
    )
    facts_two, query_grad_other = feed_sums.round((facts_own, query_grad_other))
    row_grads_came = other_core(row_grads_other)
    pair_grads_own, row_grads_own, query_grad_own = cross_backward(
        facts_two, query_heads, query_heads_t, grad_heads, grad_heads_t, log_total, inner, pairs_own, weight_t,
        wide_type,
    )

    facts_three, query_grad_own = feed_sums.round((facts_own, query_grad_own))
    grad_memory, hidden, base, act_sums, groups = memory_backward(
        facts_three, features, row_grads_own, row_grads_came, stats, conv_weight_t
    )
    place = jnp.concatenate((jnp.stack((chip_index, core_index)).astype(jnp.int32), mem_lengths))
    self_facts = dec_lengths[chip_index][None]

    def late_gradients(late):
        query_grad_own, query_grad_other, pair_grads_own, pair_grads_other, hidden, grad_memory = late
        late_feed = feed_sums.copied()

        memory_parts = memory_weights(memory_own, hidden, memory_other, pair_grads_own, grad_memory, pair_grads_other)
        memory_sums = Sums(
            [part.reshape(chips, share, -1) for part in memory_parts], [orders["along"], orders["across"]], chip_index
        )
        query_grad_own = memory_sums.start(query_grad_own)
        own_slot = lax.broadcasted_iota(jnp.int32, (chips, 1, 1), 0) == chip_index
        document_groups = jnp.where(own_slot, core_total(groups)[None], 0.0)

        def round_with(sums, small, value, leave_last=False):
            pairs = [(chip, chip ^ (1 << sums.step)) for chip in range(chips)]
            small_came = lax.ppermute(small, "dp", pairs)
            small_came, value = sums.round((small_came, value), leave_last)
            return small + small_came, value

        grad_cq, part = query_back(query_grad_own, query_grad_other, cross_query_t)
        part_came = other_core(part)
        part_came = late_feed.round(part_came)
        grad_first, grad_self, cross_gain_grad, grad_qkv, part_one = self_backward(
            self_facts, first_out, part, part_came, cross_gain[None], grad_second, self_out_t, qkv_self, self_totals,
            self_weight_t,
        )
        part_one_came = other_core(part_one)
        own_part, other_part = side_weights(normed_one, grad_qkv, normed_two, grad_cq, grad_self, attended)
        late_sums = Sums(
            [own_part.reshape(chips, share, -1), other_part.reshape(chips, share, -1)],
            [orders["along"], orders["across"]],
            chip_index,
        )
        part_one_came = late_sums.start(part_one_came)
        input_grad, layer_out, gains = input_back(
            dec_rows_in, part_one, part_one_came, self_gain[None], grad_first, second_out, result_part, result_came,
            act_sums, cross_gain_grad, ffn_gain_grad,
        )
        gains = core_total(gains)
        while late_feed.going:
            input_grad = late_feed.round(input_grad)
        document_groups, input_grad = round_with(memory_sums, document_groups, input_grad)
        gains, input_grad = round_with(late_sums, gains, input_grad)
        while memory_sums.going:
            document_groups, input_grad = round_with(memory_sums, document_groups, input_grad)
            if memory_sums.going:
                gains, input_grad = round_with(late_sums, gains, input_grad)
        memory_came = [other_core(kept) for kept in memory_sums.kept]
        while late_sums.step < bits - 1:
            gains, input_grad = round_with(late_sums, gains, input_grad)
        moved = moved_rows(doc_owner, place, memory_in, document_groups)
        gains, moved = round_with(late_sums, gains, moved, True)
        weight_grads = assemble(
            place, *memory_sums.kept, *memory_came, late_sums.kept[0], late_sums.came[0], late_sums.kept[1], late_sums.came[1],
            *late_feed.kept,
        )
        gains = gains.transpose(1, 0, 2).reshape(8, width)
        gains = lax.dynamic_slice_in_dim(gains, chip_index * share, share, axis=1)
        return moved, layer_out, input_grad, gains, weight_grads

    late = (query_grad_own, query_grad_other, pair_grads_own, pair_grads_other, hidden, grad_memory)
    base, late, act_sums, groups, came = tie((base, late, act_sums, groups, feed_sums.came))
    feed_sums.came = came
    returned = lax.all_to_all(base, "dp", split_axis=0, concat_axis=0, tiled=True)

    def late_work():
        return late_gradients(late)

    def no_work():
        return jax.tree.map(lambda leaf: jnp.zeros(leaf.shape, leaf.dtype), jax.eval_shape(late_work))

    moved, layer_out, input_grad, gains, weight_grads = lax.cond(length > 0, late_work, no_work)
    memory_grad = spread_docs(returned, moved, doc_owner)
    conv_grad, cross_kv_grad, cross_out_grad, self_qkv_grad, cross_query_grad, self_out_grad = weight_grads[:6]
    ffn_in_grad, ffn_out_grad = weight_grads[6:]
    return (
        layer_out.reshape(1, DEC, width),
        input_grad.reshape(1, DEC, width),
        memory_grad.reshape(1, 1, docs, sub, width),
        gains[0],
        gains[1],
        conv_grad,
        cross_kv_grad,
        gains[2],
        self_qkv_grad,
        self_out_grad,
        gains[3],
        cross_query_grad,
        cross_out_grad,
        gains[4],
        ffn_in_grad,
        ffn_out_grad,
    )


def solution(mesh):
    placed = (
        P("dp", None, None),
        P("dp", None, None),
        P("dp", "mp", None, None, None),
        P(),
        P(),
        P(),
        P(),
        P(),
        P(),
        P(),
        P(),
        P(None, None, "mp"),
        P("mp", None),
        P(),
        P(None, "mp"),
        P("mp", None),
        P(),
        P(None, "mp"),
        P("mp", None),
    )
    return jax.shard_map(
        shards,
        mesh=mesh,
        in_specs=placed,
        out_specs=(
            P("dp", None, None),
            P("dp", None, None),
            P("dp", "mp", None, None, None),
            P("dp"),
            P("dp"),
            P("dp", None),
            P("dp", None, None),
            P("dp"),
            P("dp", None, "mp"),
            P("mp", "dp"),
            P("dp"),
            P("dp", "mp"),
            P("mp", "dp"),
            P("dp"),
            P("dp", "mp"),
            P("mp", "dp"),
        ),
        check_vma=False,
    )
```

```python
from functools import partial

import jax
import jax.numpy as jnp
from jax import lax
from jax.experimental import pallas as pl
from jax.experimental.pallas import tpu as pltpu
from jax.sharding import PartitionSpec as P

HD = 64
GROUPS = 32
DEC = 512


norm_eps = 1e-06
group_eps = 1e-05
masked_fill = -1000000000.0
largest_sum = 1e17
vmem_budget = 48 * 1024 * 1024
heavy = pl.CostEstimate(flops=10**10, bytes_accessed=10**7, transcendentals=10**7)
low_type = jnp.bfloat16
wide_type = jnp.float32


def dot_wide(left, right):
    return jnp.dot(left, right, preferred_element_type=wide_type)


def dot_rows(left, right):
    return lax.dot_general(left, right, (((0,), (0,)), ((), ())), preferred_element_type=wide_type)


def dot_columns(left, right):
    return lax.dot_general(left, right, (((1,), (1,)), ((), ())), preferred_element_type=wide_type)


def norm_rows(values, gain):
    factor = lax.rsqrt(jnp.mean(values * values, axis=-1, keepdims=True) + norm_eps)
    return (values * factor * gain, factor)


def norm_rows_back(values, factor, gain, incoming):
    scaled = incoming * gain
    inward = factor * scaled - values * factor * factor * factor * jnp.mean(
        scaled * values, axis=-1, keepdims=True
    )
    gain_grad = jnp.sum(incoming * values * factor, axis=0)
    return (inward, gain_grad)


def other_core(values):
    return lax.ppermute(values, "mp", [(0, 1), (1, 0)])


def core_total(partial_sum):
    return partial_sum + other_core(partial_sum)


tie = lax.optimization_barrier


class ScatterSums:
    def __init__(self, arrays, orders, chip_index):
        chips = arrays[0].shape[0]
        self.chip_index = chip_index
        self.bits = chips.bit_length() - 1
        self.orders = [list(order) for order in orders]
        self.left = [list(range(self.bits - 1, -1, -1)) for _ in arrays]
        self.current = [array.reshape((2,) * self.bits + array.shape[1:]) for array in arrays]
        self.kept = self.sent = self.came = None

    def copied(self):
        other = object.__new__(ScatterSums)
        other.chip_index, other.bits = self.chip_index, self.bits
        other.orders = [list(order) for order in self.orders]
        other.left = [list(left) for left in self.left]
        other.current, other.kept, other.sent, other.came = self.current, self.kept, self.sent, self.came
        return other

    def begin(self):
        self.kept, self.sent = [], []
        for number, order in enumerate(self.orders):
            axis = self.left[number].index(order[0])
            mine = (self.chip_index >> order[0]) & 1
            self.sent.append(lax.dynamic_index_in_dim(self.current[number], 1 - mine, axis, False))
            self.kept.append(lax.dynamic_index_in_dim(self.current[number], mine, axis, False))
            self.left[number].pop(axis)

    def ahead_of(self, value):
        self.sent, value = tie((self.sent, value))
        return value

    def send(self):
        chips = 1 << self.bits
        self.came = [
            lax.ppermute(sent, "dp", [(chip, chip ^ (1 << order[0])) for chip in range(chips)])
            for sent, order in zip(self.sent, self.orders)
        ]

    def behind(self, value):
        self.came, value = tie((self.came, value))
        return value

    def merge(self):
        merged = []
        for number, order in enumerate(self.orders):
            total = self.kept[number].astype(wide_type) + self.came[number].astype(wide_type)
            order.pop(0)
            merged.append(total.astype(self.current[number].dtype) if order else total)
        self.current = merged

    def step(self):
        self.begin()
        self.send()
        self.merge()

    def finish(self):
        while self.orders[0]:
            self.step()
        return self.current


def merge_kernel(facts, *refs, plans):
    count = len(plans)
    outs = list(refs[2 * count :])
    for plan, kept, came in zip(plans, refs[:count], refs[count : 2 * count]):
        entries, after, turn = plan["entries"], plan["after"], plan["turn"]

        def total(entry, kept=kept, came=came, after=after):
            own = kept[entry] if after is None else kept[entry >> after, 0, entry & ((1 << after) - 1)]
            return own.astype(wide_type) + came[entry].astype(wide_type)

        if turn is None:
            outs.pop(0)[...] = total(0)
            continue
        sent_out, kept_out = outs.pop(0), outs.pop(0)
        bit, behind = turn
        mine = (facts[0] >> bit) & 1
        for place in range(entries // 2):
            base = (place >> behind << (behind + 1)) | (place & ((1 << behind) - 1))
            kept_out[place] = total(base + (mine << behind)).astype(low_type)
            sent_out[place] = total(base + ((1 - mine) << behind)).astype(low_type)


class Part:
    def __init__(self, array, order):
        self.kept, self.order = array, order
        self.sent = self.came = self.total = None
        self.step = 0
        self.left = tuple(range(len(order) - 1, -1, -1))

    def copied(self):
        other = object.__new__(Part)
        other.__dict__.update(self.__dict__)
        return other


class Sums:
    def __init__(self, parts, chip_index):
        self.parts, self.chip_index = parts, chip_index

    @staticmethod
    def of(arrays, orders, chip_index):
        return Sums([Part(array, order) for array, order in zip(arrays, orders)], chip_index)

    def copied(self):
        return Sums([part.copied() for part in self.parts], self.chip_index)

    def joined(self, *others):
        return Sums([part for sums in (self, *others) for part in sums.parts], self.chip_index)

    @property
    def going(self):
        return [part for part in self.parts if part.total is None]

    @property
    def totals(self):
        return [part.total for part in self.parts]

    def start(self, value):
        for part in self.parts:
            chips = part.kept.shape[0]
            behind = part.order[0]
            ahead = len(part.order) - 1 - behind
            view = part.kept.reshape((1 << ahead, 2, 1 << behind) + part.kept.shape[1:])
            mine = (self.chip_index >> behind) & 1
            sent = lax.dynamic_index_in_dim(view, 1 - mine, 1, False)
            part.sent = sent.reshape((chips // 2,) + part.kept.shape[1:])
            part.kept = view
        return self.leave(self.parts, value)

    def leave(self, parts, value):
        sent, value = tie(([part.sent for part in parts], value))
        for part, leaving in zip(parts, sent):
            chips = 1 << len(part.order)
            bit = part.order[part.step]
            part.came = lax.ppermute(leaving, "dp", [(chip, chip ^ (1 << bit)) for chip in range(chips)])
        return value

    def round(self, value):
        parts = self.going
        came, value = tie(([part.came for part in parts], value))
        plans, in_specs, out_specs, out_shape = [], [], [], []
        for part, arrived in zip(parts, came):
            part.came = arrived
            entries, rows, columns = arrived.shape
            kept, bit = part.kept, part.order[part.step]
            if part.step == 0:
                in_specs.append(
                    pl.BlockSpec(
                        (kept.shape[0], 1) + kept.shape[2:],
                        lambda j, facts, bit=bit: (0, (facts[0] >> bit) & 1, 0, 0, 0),
                    )
                )
            else:
                in_specs.append(whole(kept.shape))
            plan = {"entries": entries, "after": bit if part.step == 0 else None, "turn": None}
            part.left = tuple(other for other in part.left if other != bit)
            if part.left:
                following = part.order[part.step + 1]
                plan["turn"] = (following, len(part.left) - 1 - part.left.index(following))
                half = (entries // 2, rows, columns)
                out_specs += [whole(half)] * 2
                out_shape += [jax.ShapeDtypeStruct(half, low_type)] * 2
            else:
                out_specs.append(whole((rows, columns)))
                out_shape.append(jax.ShapeDtypeStruct((rows, columns), wide_type))
            plans.append(plan)
        in_specs += [whole(part.came.shape) for part in parts]
        made = pl.pallas_call(
            partial(merge_kernel, plans=plans),
            grid_spec=pltpu.PrefetchScalarGridSpec(
                num_scalar_prefetch=1, grid=(1,), in_specs=in_specs, out_specs=out_specs
            ),
            out_shape=out_shape,
            compiler_params=pltpu.CompilerParams(vmem_limit_bytes=vmem_budget),
            cost_estimate=heavy,
            name="merge_sums",
        )(
            self.chip_index[None].astype(jnp.int32),
            *[part.kept for part in parts],
            *[part.came for part in parts],
        )
        made = list(made)
        for part in parts:
            part.step += 1
            if part.left:
                part.sent, part.kept = made.pop(0), made.pop(0)
            else:
                part.total = made.pop(0)
        parts = [part for part in parts if part.left]
        return self.leave(parts, value) if parts else value


def nothing_like(work):
    def nothing():
        return jax.tree.map(lambda leaf: jnp.zeros(leaf.shape, leaf.dtype), jax.eval_shape(work))

    return nothing


def gather_kernel(owner, rows, out, held, came, gone, *, docs):
    loads = [pltpu.make_async_copy(rows.at[owner[slot]], held.at[slot], came.at[slot]) for slot in range(docs)]
    stores = [pltpu.make_async_copy(held.at[slot], out.at[slot], gone.at[slot]) for slot in range(docs)]
    for load in loads:
        load.start()
    for load, store in zip(loads, stores):
        load.wait()
        store.start()
    for store in stores:
        store.wait()


def gather_docs(memory_in, doc_owner):
    docs = memory_in.shape[0]
    return pl.pallas_call(
        partial(gather_kernel, docs=docs),
        grid_spec=pltpu.PrefetchScalarGridSpec(
            num_scalar_prefetch=1,
            grid=(),
            in_specs=[pl.BlockSpec(memory_space=pl.ANY)],
            out_specs=pl.BlockSpec(memory_space=pl.ANY),
            scratch_shapes=[
                pltpu.VMEM(memory_in.shape, low_type),
                pltpu.SemaphoreType.DMA((docs,)),
                pltpu.SemaphoreType.DMA((docs,)),
            ],
        ),
        out_shape=jax.ShapeDtypeStruct(memory_in.shape, low_type),
        compiler_params=pltpu.CompilerParams(vmem_limit_bytes=vmem_budget),
        cost_estimate=heavy,
        name="gather_docs",
    )(doc_owner, memory_in)


def prepare_kernel(cross_kv, pair):
    width = cross_kv.shape[0]
    for side in range(2):
        pair[:, side * width : side * width + width] = cross_kv[:, side, :]


def prepare_weights(cross_kv):
    width = cross_kv.shape[0]
    return pl.pallas_call(
        prepare_kernel,
        out_shape=jax.ShapeDtypeStruct((width, 2 * width), low_type),
        compiler_params=pltpu.CompilerParams(vmem_limit_bytes=vmem_budget),
        cost_estimate=heavy,
        name="prepare_weights",
    )(cross_kv)


def moved_kernel(owner, facts, features, groups, out, stats, *, chips, count):
    step = pl.program_id(0)
    sub, width = features.shape[1:]

    @pl.when(step == 0)
    def _():
        own_group = (
            lax.broadcasted_iota(jnp.int32, (128, width), 1) // (width // GROUPS)
            == lax.broadcasted_iota(jnp.int32, (128, width), 0)
        ).astype(wide_type)
        stats[...] = jnp.dot(
            groups[0:chips].reshape(chips * 8, 128), own_group, precision=lax.Precision.HIGHEST
        ).reshape(chips, 8, width)

    position = (lax.broadcasted_iota(jnp.int32, (sub, 1), 0) * 2 + facts[1]) * chips + facts[0]

    def one(place, carry):
        slot = step * count + place
        document = owner[slot]
        normed = (features[document].astype(wide_type) - stats[slot, 0:1, :]) * stats[slot, 1:2, :]
        moved = stats[slot, 1:2, :] * (stats[slot, 2:3, :] + normed * stats[slot, 3:4, :])
        out[place] = jnp.where(position < facts[2 + document], moved, 0.0).astype(low_type)
        return carry

    lax.fori_loop(0, count, one, 0)


def moved_rows(doc_owner, facts, features, groups):
    docs, sub, width = features.shape
    count = max(docs // 4, 1)
    return pl.pallas_call(
        partial(moved_kernel, chips=docs, count=count),
        grid_spec=pltpu.PrefetchScalarGridSpec(
            num_scalar_prefetch=2,
            grid=(docs // count,),
            in_specs=[
                pl.BlockSpec(features.shape, lambda j, owner, facts: (0, 0, 0)),
                pl.BlockSpec(groups.shape, lambda j, owner, facts: (0, 0, 0)),
            ],
            out_specs=pl.BlockSpec((count, sub, width), lambda j, owner, facts: (j, 0, 0)),
            scratch_shapes=[pltpu.VMEM((docs, 8, width), wide_type)],
        ),
        out_shape=jax.ShapeDtypeStruct(features.shape, low_type),
        compiler_params=pltpu.CompilerParams(vmem_limit_bytes=vmem_budget),
        cost_estimate=heavy,
        name="moved_rows",
    )(doc_owner, facts, features, groups)


def spread_kernel(owner, rows, moved, out, held, taken, wide, came, also, gone, *, docs):
    loads = [pltpu.make_async_copy(rows.at[slot], held.at[slot], came.at[slot]) for slot in range(docs)]
    takes = [pltpu.make_async_copy(moved.at[slot], taken.at[slot], also.at[slot]) for slot in range(docs)]
    stores = [pltpu.make_async_copy(wide.at[slot], out.at[owner[slot]], gone.at[slot]) for slot in range(docs)]
    for load, take in zip(loads, takes):
        load.start()
        take.start()
    for slot in range(docs):
        loads[slot].wait()
        takes[slot].wait()
        wide[slot] = held[slot].astype(wide_type) - taken[slot].astype(wide_type)
        stores[slot].start()
    for store in stores:
        store.wait()


def spread_docs(rows, moved, doc_owner):
    docs = rows.shape[0]
    return pl.pallas_call(
        partial(spread_kernel, docs=docs),
        grid_spec=pltpu.PrefetchScalarGridSpec(
            num_scalar_prefetch=1,
            grid=(),
            in_specs=[pl.BlockSpec(memory_space=pl.ANY), pl.BlockSpec(memory_space=pl.ANY)],
            out_specs=pl.BlockSpec(memory_space=pl.ANY),
            scratch_shapes=[
                pltpu.VMEM(rows.shape, low_type),
                pltpu.VMEM(rows.shape, low_type),
                pltpu.VMEM(rows.shape, wide_type),
                pltpu.SemaphoreType.DMA((docs,)),
                pltpu.SemaphoreType.DMA((docs,)),
                pltpu.SemaphoreType.DMA((docs,)),
            ],
        ),
        out_shape=jax.ShapeDtypeStruct(rows.shape, wide_type),
        compiler_params=pltpu.CompilerParams(vmem_limit_bytes=vmem_budget),
        cost_estimate=heavy,
        name="spread_docs",
    )(doc_owner, rows, moved)


def chunk_of(chips, sub):
    return min(sub, max(16, 512 // chips))


def live_rows(facts, start, chips, span):
    row = lax.broadcasted_iota(jnp.int32, (chips * span, 1), 0)
    chip, step = row // span, row % span
    return ((start + step) * 2 + facts[1]) * chips + chip < facts[0]


def in_branches(facts, start, chips, span, work, dead=None):
    first = (start * 2 + facts[1]) * chips
    last = ((start + span - 1) * 2 + facts[1]) * chips + chips - 1
    full = last < facts[0]
    none = first >= facts[0]

    @pl.when(full)
    def _():
        work(None)

    @pl.when(jnp.logical_not(full) & jnp.logical_not(none))
    def _():
        work(live_rows(facts, start, chips, span))

    if dead is not None:
        pl.when(none)(dead)


def whole(shape):
    return pl.BlockSpec(shape, lambda j, facts: (0,) * len(shape))


def slab(shape, span):
    return pl.BlockSpec((shape[0], span, shape[2]), lambda j, facts: (0, j, 0))


def memory_forward_kernel(facts, rows, stats, weight, out, *, chips, span):
    width = rows.shape[-1]
    wide = rows[...].reshape(chips * span, width).astype(wide_type)
    drive = (wide - stats[0:1, :]) * stats[1:2, :] * stats[2:3, :] + stats[3:4, :]
    hidden = (drive * (0.5 + 0.5 * jnp.tanh(0.5 * drive))).astype(low_type)
    made = wide + dot_wide(hidden, weight[...])
    out[...] = made.astype(low_type).reshape(chips, span, width)


def memory_forward(facts, rows, stats, weight):
    chips, sub, width = rows.shape
    span = chunk_of(chips, sub)
    return pl.pallas_call(
        partial(memory_forward_kernel, chips=chips, span=span),
        grid_spec=pltpu.PrefetchScalarGridSpec(
            num_scalar_prefetch=1,
            grid=(sub // span,),
            in_specs=[slab(rows.shape, span), whole(stats.shape), whole(weight.shape)],
            out_specs=slab(rows.shape, span),
        ),
        out_shape=jax.ShapeDtypeStruct(rows.shape, low_type),
        compiler_params=pltpu.CompilerParams(vmem_limit_bytes=vmem_budget),
        cost_estimate=heavy,
        name="memory_forward",
    )(facts, rows, stats, weight)


def memory_backward_kernel(
    facts, rows, own, came, stats, weight, grad_out, hidden_out, base_out, sums, groups, *, chips, span, steps
):
    step = pl.program_id(0)
    width = rows.shape[-1]
    count = chips * span

    @pl.when(step == 0)
    def _():
        sums[...] = jnp.zeros_like(sums)

    wide = rows[...].reshape(count, width).astype(wide_type)
    normed = (wide - stats[0:1, :]) * stats[1:2, :]
    drive = normed * stats[2:3, :] + stats[3:4, :]
    gate = 0.5 + 0.5 * jnp.tanh(0.5 * drive)
    hidden_out[...] = (drive * gate).astype(low_type).reshape(chips, span, width)
    grad = (own[...].reshape(count, width) + came[...].reshape(count, width).astype(wide_type)).astype(low_type)
    grad_out[...] = grad.reshape(chips, span, width)
    grad_act = dot_columns(grad, weight[...]) * (gate * (1.0 + drive * (1.0 - gate)))
    sums[0:1, :] += jnp.sum(grad_act, axis=0, keepdims=True)
    sums[1:2, :] += jnp.sum(grad_act * normed, axis=0, keepdims=True)
    base = grad.astype(wide_type) + grad_act * (stats[1:2, :] * stats[2:3, :])
    base_out[...] = base.astype(low_type).reshape(chips, span, width)

    @pl.when(step == steps - 1)
    def _():
        per_group = width // GROUPS
        group_of = (
            lax.broadcasted_iota(jnp.int32, (width, 128), 0) // per_group
            == lax.broadcasted_iota(jnp.int32, (width, 128), 1)
        ).astype(wide_type)
        entries = (facts[0] * per_group).astype(wide_type)
        rows_of = jnp.concatenate(
            (
                stats[0:2, :] * (0.5 / per_group),
                sums[0:2, :] * stats[2:3, :] / entries,
                jnp.zeros((4, width), wide_type),
            )
        )
        groups[...] = jnp.dot(rows_of, group_of, precision=lax.Precision.HIGHEST)


def memory_backward(facts, rows, own, came, stats, weight):
    chips, sub, width = rows.shape
    span = chunk_of(chips, sub)
    block = slab(rows.shape, span)
    return pl.pallas_call(
        partial(memory_backward_kernel, chips=chips, span=span, steps=sub // span),
        grid_spec=pltpu.PrefetchScalarGridSpec(
            num_scalar_prefetch=1,
            grid=(sub // span,),
            in_specs=[block, block, block, whole(stats.shape), whole(weight.shape)],
            out_specs=[block, block, block, whole(stats.shape), whole((8, 128))],
        ),
        out_shape=[
            jax.ShapeDtypeStruct(rows.shape, low_type),
            jax.ShapeDtypeStruct(rows.shape, low_type),
            jax.ShapeDtypeStruct(rows.shape, low_type),
            jax.ShapeDtypeStruct(stats.shape, wide_type),
            jax.ShapeDtypeStruct((8, 128), wide_type),
        ],
        compiler_params=pltpu.CompilerParams(vmem_limit_bytes=vmem_budget),
        cost_estimate=heavy,
        name="memory_backward",
    )(facts, rows, own, came, stats, weight)


def cross_forward_kernel(
    facts, query_t, rows, key_weight, value_weight, top_in, total_in, sum_in, pairs, top, total, gathered,
    total_here, sum_here, held, *, chips, span
):
    step = pl.program_id(0)
    half = key_weight.shape[1]
    width = rows.shape[-1]

    @pl.when(step == 0)
    def _():
        top[...] = top_in[...]
        total[...] = total_in[...]
        gathered[...] = sum_in[...]

    def work(live):
        block = rows[...].reshape(chips * span, width)
        keys = dot_wide(block, key_weight[...]).astype(low_type)
        values = dot_wide(block, value_weight[...]).astype(low_type)
        pairs[:, :, :half] = keys.reshape(chips, span, half)
        pairs[:, :, half:] = values.reshape(chips, span, half)
        heads = half // HD

        def score(head):
            made = dot_wide(keys[:, head // 2 * 128 : head // 2 * 128 + 128], query_t[head])
            return made if live is None else jnp.where(live, made, masked_fill)

        def part_of(head, weights):
            part = dot_rows(values[:, head // 2 * 128 : head // 2 * 128 + 128], weights.astype(low_type))
            return part[head % 2 * HD : head % 2 * HD + HD, :]

        def plain():
            following = score(0)
            for head in range(heads):
                scores = following
                if head + 1 < heads:
                    following = score(head + 1)
                weights = jnp.exp(scores - top[head : head + 1, :])
                total_here[head : head + 1, :] = jnp.sum(weights, axis=0, keepdims=True)
                sum_here[head * HD : head * HD + HD, :] = part_of(head, weights)

        def shifted():
            following = score(0)
            for head in range(heads):
                scores = following
                if head + 1 < heads:
                    following = score(head + 1)
                old_top = top[head : head + 1, :]
                new_top = jnp.maximum(old_top, jnp.max(scores, axis=0, keepdims=True))
                weights = jnp.exp(scores - new_top)
                shrink = jnp.exp(old_top - new_top)
                total[head : head + 1, :] = total[head : head + 1, :] * shrink + jnp.sum(
                    weights, axis=0, keepdims=True
                )
                rows_of = slice(head * HD, head * HD + HD)
                gathered[rows_of, :] = gathered[rows_of, :] * shrink + part_of(head, weights)
                top[head : head + 1, :] = new_top

        fresh = (facts[3] == 1) & (step == 0)
        held[0] = jnp.where(fresh, 1, 0)

        @pl.when(jnp.logical_not(fresh))
        def _():
            plain()
            small = jnp.max(total_here[0:heads, :]) < largest_sum
            held[0] = jnp.where(small, 0, 1)

            @pl.when(small)
            def _():
                total[0:heads, :] += total_here[0:heads, :]
                gathered[...] += sum_here[...]

        pl.when(held[0] == 1)(shifted)

    def dead():
        pairs[...] = jnp.zeros_like(pairs)

    in_branches(facts, step * span, chips, span, work, dead)


def cross_forward(facts, query_t, rows, weight, carry):
    chips, sub, width = rows.shape
    heads, _, queries = query_t.shape
    half = heads * HD
    span = chunk_of(chips, sub)
    stat = (8, queries)
    summed = (half, queries)
    return pl.pallas_call(
        partial(cross_forward_kernel, chips=chips, span=span),
        grid_spec=pltpu.PrefetchScalarGridSpec(
            num_scalar_prefetch=1,
            grid=(sub // span,),
            in_specs=[
                whole(query_t.shape),
                slab(rows.shape, span),
                pl.BlockSpec((width, half), lambda j, facts: (0, facts[2])),
                pl.BlockSpec((width, half), lambda j, facts: (0, 2 + facts[2])),
                whole(stat),
                whole(stat),
                whole(summed),
            ],
            out_specs=[slab((chips, sub, 2 * half), span), whole(stat), whole(stat), whole(summed)],
            scratch_shapes=[
                pltpu.VMEM(stat, wide_type),
                pltpu.VMEM(summed, wide_type),
                pltpu.SMEM((1,), jnp.int32),
            ],
        ),
        out_shape=[
            jax.ShapeDtypeStruct((chips, sub, 2 * half), low_type),
            jax.ShapeDtypeStruct(stat, wide_type),
            jax.ShapeDtypeStruct(stat, wide_type),
            jax.ShapeDtypeStruct(summed, wide_type),
        ],
        compiler_params=pltpu.CompilerParams(vmem_limit_bytes=vmem_budget),
        cost_estimate=heavy,
        name="cross_forward",
    )(facts, query_t, rows, weight, weight, *carry)


def cross_close_kernel(gathered, top, total, weight, crossed, crossed_t, log_total, part, *, heads):
    log_total[...] = top[...] + jnp.log(jnp.maximum(total[...], 1e-30))
    for head in range(heads):
        rows = slice(head * HD, head * HD + HD)
        crossed_t[rows, :] = gathered[rows, :] / total[head : head + 1, :]
    low = crossed_t[...].T.astype(low_type)
    crossed[...] = low
    part[...] = dot_wide(low, weight[...])


def cross_close(gathered, top, total, weight):
    half, queries = gathered.shape
    return pl.pallas_call(
        partial(cross_close_kernel, heads=half // HD),
        out_shape=[
            jax.ShapeDtypeStruct((queries, half), low_type),
            jax.ShapeDtypeStruct((half, queries), wide_type),
            jax.ShapeDtypeStruct(top.shape, wide_type),
            jax.ShapeDtypeStruct((queries, weight.shape[1]), wide_type),
        ],
        compiler_params=pltpu.CompilerParams(vmem_limit_bytes=vmem_budget),
        cost_estimate=heavy,
        name="cross_close",
    )(gathered, top, total, weight)


gelu_scale = 0.7978845608028654
gelu_cubic = 0.044715


def feed_forward_kernel(
    first, own, came, gain, weight, grad_active, second, normed, both_grad, both_active, grad_normed
):
    step = pl.program_id(0)

    @pl.when(step == 0)
    def _():
        total = first[...] + (own[...] + came[...])
        second[...] = total
        factor = lax.rsqrt(jnp.mean(total * total, axis=-1, keepdims=True) + norm_eps)
        normed[...] = (total * factor * gain[...]).astype(low_type)
        grad_normed[...] = jnp.zeros_like(grad_normed)

    lifted = dot_wide(normed[...], weight[...])
    square = lifted * lifted
    bent = jnp.tanh(gelu_scale * (lifted * (1.0 + gelu_cubic * square)))
    half_up = 0.5 * (1.0 + bent)
    both_active[...] = (lifted * half_up).astype(low_type)
    slope = half_up + (0.5 * gelu_scale) * lifted * (1.0 - bent * bent) * (1.0 + 3.0 * gelu_cubic * square)
    grad_lifted = (grad_active[...].astype(wide_type) * slope).astype(low_type)
    both_grad[...] = grad_lifted
    grad_normed[...] += dot_columns(grad_lifted, weight[...])


def feed_forward(first, own, came, gain, weight, grad_active):
    rows, width = first.shape
    hidden = weight.shape[1]
    block = 512
    still = pl.BlockSpec((rows, width), lambda j: (0, 0))
    moving = pl.BlockSpec((rows, block), lambda j: (0, j))
    return pl.pallas_call(
        feed_forward_kernel,
        grid=(hidden // block,),
        in_specs=[
            still,
            still,
            still,
            pl.BlockSpec((1, width), lambda j: (0, 0)),
            pl.BlockSpec((width, block), lambda j: (0, j)),
            moving,
        ],
        out_specs=[still, still, moving, moving, still],
        out_shape=[
            jax.ShapeDtypeStruct((rows, width), wide_type),
            jax.ShapeDtypeStruct((rows, width), low_type),
            jax.ShapeDtypeStruct((rows, hidden), low_type),
            jax.ShapeDtypeStruct((rows, hidden), low_type),
            jax.ShapeDtypeStruct((rows, width), wide_type),
        ],
        compiler_params=pltpu.CompilerParams(vmem_limit_bytes=vmem_budget),
        cost_estimate=heavy,
        name="feed_forward",
    )(first, own, came, gain, weight, grad_active)


def feed_close_kernel(
    second, own, came, gain, grad_out, weight, crossed_t, grad_second, gain_grad, grad_cross, heads_out,
    heads_out_t, inner, *, heads,
):
    values = second[...]
    incoming = (own[...] + came[...]).astype(low_type).astype(wide_type)
    factor = lax.rsqrt(jnp.mean(values * values, axis=-1, keepdims=True) + norm_eps)
    scaled = incoming * gain[...]
    inward = factor * scaled - values * (factor * factor * factor) * jnp.mean(
        scaled * values, axis=-1, keepdims=True
    )
    gain_grad[...] = jnp.broadcast_to(
        jnp.sum(incoming * values * factor, axis=0, keepdims=True), gain_grad.shape
    )
    total = inward + grad_out[...].astype(wide_type)
    grad_second[...] = total
    low = total.astype(low_type)
    grad_cross[...] = low
    made = dot_columns(low, weight[...])
    made_low = made.astype(low_type)
    made_t = made_low.astype(wide_type).T
    low_t = made_t.astype(low_type)
    left = lax.broadcasted_iota(jnp.int32, (made.shape[0], 128), 1) < HD
    inner[...] = jnp.zeros_like(inner)
    for head in range(heads):
        pair = made_low[:, head // 2 * 128 : head // 2 * 128 + 128]
        keep = left if head % 2 == 0 else jnp.logical_not(left)
        heads_out[head] = jnp.where(keep, pair, jnp.zeros_like(pair))
        rows = slice(head * HD, head * HD + HD)
        own_rows = slice(head % 2 * HD, head % 2 * HD + HD)
        other_rows = slice((1 - head % 2) * HD, (1 - head % 2) * HD + HD)
        heads_out_t[head, own_rows, :] = low_t[rows, :]
        heads_out_t[head, other_rows, :] = jnp.zeros_like(low_t[rows, :])
        inner[head : head + 1, :] = jnp.sum(made_t[rows, :] * crossed_t[rows, :], axis=0, keepdims=True)


def feed_close(second, own, came, gain, grad_out, weight, crossed_t):
    rows, width = second.shape
    half = weight.shape[0]
    heads = half // HD
    return pl.pallas_call(
        partial(feed_close_kernel, heads=heads),
        out_shape=[
            jax.ShapeDtypeStruct((rows, width), wide_type),
            jax.ShapeDtypeStruct((8, width), wide_type),
            jax.ShapeDtypeStruct((rows, width), low_type),
            jax.ShapeDtypeStruct((heads, rows, 128), low_type),
            jax.ShapeDtypeStruct((heads, 128, rows), low_type),
            jax.ShapeDtypeStruct((8, rows), wide_type),
        ],
        compiler_params=pltpu.CompilerParams(vmem_limit_bytes=vmem_budget),
        cost_estimate=heavy,
        name="feed_close",
    )(second, own, came, gain, grad_out, weight, crossed_t)


def feed_weights_kernel(
    normed, grad_out, grad_cross, both_grad, both_active, crossed, left, middle, right, turned, *, steps
):
    step = pl.program_id(0)
    third = (2 * steps + 1) // 3

    @pl.when(step == 0)
    def _():
        turned[...] = normed[...].T

    @pl.when(step == steps)
    def _():
        turned[...] = grad_out[...].T

    @pl.when(step == 2 * steps)
    def _():
        turned[...] = grad_cross[...].T

    for number, out in enumerate((left, middle, right)):
        inside = (step >= number * third) & (step < number * third + third)

        @pl.when(inside & (step < steps))
        def _(out=out):
            out[...] = dot_wide(turned[...], both_grad[...]).astype(low_type)

        @pl.when(inside & (step >= steps) & (step < 2 * steps))
        def _(out=out):
            out[...] = dot_wide(turned[...], both_active[...]).astype(low_type)

        @pl.when(inside & (step == 2 * steps))
        def _(out=out):
            out[...] = dot_wide(turned[...], crossed[...]).astype(low_type)


def feed_weights(normed, grad_out, grad_cross, grad_lifted, active, crossed):
    rows, width = normed.shape
    hidden = active.shape[1]
    block = crossed.shape[1]
    steps = hidden // block
    third = (2 * steps + 1) // 3

    def piece(number):
        return pl.BlockSpec((width, block), lambda j: (0, jnp.clip(j - number * third, 0, third - 1)))

    still = pl.BlockSpec((rows, width), lambda j: (0, 0))
    return pl.pallas_call(
        partial(feed_weights_kernel, steps=steps),
        grid=(2 * steps + 1,),
        in_specs=[
            still,
            still,
            still,
            pl.BlockSpec((rows, block), lambda j: (0, jnp.minimum(j, steps - 1))),
            pl.BlockSpec((rows, block), lambda j: (0, jnp.clip(j - steps, 0, steps - 1))),
            pl.BlockSpec((rows, block), lambda j: (0, 0)),
        ],
        out_specs=[piece(number) for number in range(3)],
        out_shape=[jax.ShapeDtypeStruct((width, third * block), low_type)] * 3,
        scratch_shapes=[pltpu.VMEM((width, rows), low_type)],
        compiler_params=pltpu.CompilerParams(vmem_limit_bytes=vmem_budget),
        cost_estimate=heavy,
        name="feed_weights",
    )(normed, grad_out, grad_cross, grad_lifted, active, crossed)


def cross_backward_kernel(
    facts, query, query_t, grad, grad_t, log_total, inner, pairs, key_weight, value_weight, pair_grads,
    row_grads, query_grad, held, *, chips, span
):
    step = pl.program_id(0)
    width, half = key_weight.shape

    @pl.when(step == 0)
    def _():
        query_grad[...] = jnp.zeros_like(query_grad)

    def work(live):
        block = pairs[...].reshape(chips * span, 2 * half)
        heads = half // HD

        def lanes(head, shift=0):
            return block[:, shift + head // 2 * 128 : shift + head // 2 * 128 + 128]

        def products(head):
            scores = dot_wide(lanes(head), query_t[head])
            if live is not None:
                scores = jnp.where(live, scores, masked_fill)
            return scores, dot_wide(lanes(head, half), grad_t[head])

        following = products(0)
        for pair in range(heads // 2):
            lows, low_grads = [], []
            for side in range(2):
                head = pair * 2 + side
                scores, grad_probs = following
                if head + 1 < heads:
                    following = products(head + 1)
                probs = jnp.exp(scores - log_total[head : head + 1, :])
                low_grads.append((probs * (grad_probs - inner[head : head + 1, :])).astype(low_type))
                lows.append(probs.astype(low_type))
                part = dot_rows(lanes(head), low_grads[-1])
                query_grad[head * HD : head * HD + HD, :] += part[side * HD : side * HD + HD, :]
            at = pair * 128
            both = slice(pair * 2, pair * 2 + 2)
            queries = query.shape[1]
            held[:, at : at + 128] = dot_wide(
                jnp.concatenate(low_grads, axis=1), query[both].reshape(2 * queries, 128)
            ).astype(low_type)
            held[:, half + at : half + at + 128] = dot_wide(
                jnp.concatenate(lows, axis=1), grad[both].reshape(2 * queries, 128)
            ).astype(low_type)
        made = held[...]
        pair_grads[...] = made.reshape(chips, span, 2 * half)
        back = dot_columns(made[:, :half], key_weight[...]) + dot_columns(made[:, half:], value_weight[...])
        row_grads[...] = back.astype(row_grads.dtype).reshape(chips, span, width)

    def dead():
        pair_grads[...] = jnp.zeros_like(pair_grads)
        row_grads[...] = jnp.zeros_like(row_grads)

    in_branches(facts, step * span, chips, span, work, dead)


def cross_backward(facts, query, query_t, grad, grad_t, log_total, inner, pairs, weight, grad_type):
    chips, sub, both = pairs.shape
    width = weight.shape[0]
    heads, _, queries = query_t.shape
    span = chunk_of(chips, sub)
    half = both // 2
    pair_block = slab(pairs.shape, span)
    row_block = slab((chips, sub, width), span)
    return pl.pallas_call(
        partial(cross_backward_kernel, chips=chips, span=span),
        grid_spec=pltpu.PrefetchScalarGridSpec(
            num_scalar_prefetch=1,
            grid=(sub // span,),
            in_specs=[
                whole(query.shape),
                whole(query_t.shape),
                whole(grad.shape),
                whole(grad_t.shape),
                whole(log_total.shape),
                whole(inner.shape),
                pair_block,
                pl.BlockSpec((width, half), lambda j, facts: (0, facts[2])),
                pl.BlockSpec((width, half), lambda j, facts: (0, 2 + facts[2])),
            ],
            out_specs=[pair_block, row_block, whole((heads * HD, queries))],
            scratch_shapes=[pltpu.VMEM((chips * span, both), low_type)],
        ),
        out_shape=[
            jax.ShapeDtypeStruct((chips, sub, both), low_type),
            jax.ShapeDtypeStruct((chips, sub, width), grad_type),
            jax.ShapeDtypeStruct((heads * HD, queries), wide_type),
        ],
        compiler_params=pltpu.CompilerParams(vmem_limit_bytes=vmem_budget),
        cost_estimate=heavy,
        name="cross_backward",
    )(facts, query, query_t, grad, grad_t, log_total, inner, pairs, weight, weight)


def query_back_kernel(own, other, weight, grad, part):
    low = ((own[...] + other[...]) * 0.125).T.astype(low_type)
    grad[...] = low
    part[...] = dot_columns(low, weight[...])


def query_back(own, other, weight):
    half, rows = own.shape
    return pl.pallas_call(
        query_back_kernel,
        out_shape=[
            jax.ShapeDtypeStruct((rows, half), low_type),
            jax.ShapeDtypeStruct((rows, weight.shape[0]), wide_type),
        ],
        compiler_params=pltpu.CompilerParams(vmem_limit_bytes=vmem_budget),
        cost_estimate=heavy,
        name="query_back",
    )(own, other, weight)


def memory_weights_kernel(
    facts, rows, hidden, other, pair_grads, row_grads, other_grads, pair_out, keep_out, send_out, pair_sum, conv_sum,
    *, chips, span, steps
):
    step = pl.program_id(0)
    count = chips * span

    def flat(ref):
        return ref[...].reshape(count, ref.shape[-1])

    @pl.when(step == 0)
    def _():
        pair_sum[...] = jnp.zeros_like(pair_sum)
        conv_sum[...] = jnp.zeros_like(conv_sum)

    pair_sum[...] += dot_rows(flat(rows), flat(pair_grads)) + dot_rows(flat(other), flat(other_grads))
    conv_sum[...] += dot_rows(flat(hidden), flat(row_grads))

    @pl.when(step == steps - 1)
    def _():
        pair_out[...] = pair_sum[...].astype(low_type)
        half = keep_out.shape[1]
        first = facts[1] == 0
        keep_out[...] = jnp.where(first, conv_sum[:, :half], conv_sum[:, half:])
        send_out[...] = jnp.where(first, conv_sum[:, half:], conv_sum[:, :half]).astype(low_type)


def memory_weights(facts, rows, hidden, other, pair_grads, row_grads, other_grads):
    chips, sub, width = rows.shape
    span = chunk_of(chips, sub)
    both = pair_grads.shape[2]
    steps = sub // span
    block = slab(rows.shape, span)
    pair_block = slab(pair_grads.shape, span)
    outs = (((width, both), low_type), ((width, width // 2), wide_type), ((width, width // 2), low_type))
    return pl.pallas_call(
        partial(memory_weights_kernel, chips=chips, span=span, steps=steps),
        grid_spec=pltpu.PrefetchScalarGridSpec(
            num_scalar_prefetch=1,
            grid=(steps,),
            in_specs=[block, block, block, pair_block, block, pair_block],
            out_specs=[whole(shape) for shape, _ in outs],
            scratch_shapes=[pltpu.VMEM((width, both), wide_type), pltpu.VMEM((width, width), wide_type)],
        ),
        out_shape=[jax.ShapeDtypeStruct(shape, kind) for shape, kind in outs],
        compiler_params=pltpu.CompilerParams(vmem_limit_bytes=vmem_budget),
        cost_estimate=heavy,
        name="memory_weights",
    )(facts, rows, hidden, other, pair_grads, row_grads, other_grads)


def side_weights_kernel(normed_one, grad_qkv, normed_two, grad_cq, grad_self, attended, own, others):
    half = attended.shape[1]
    own[...] = dot_rows(normed_one[...], grad_qkv[...]).astype(low_type)
    others[:, :half] = dot_rows(normed_two[...], grad_cq[...]).astype(low_type)
    others[:, half:] = dot_rows(grad_self[...], attended[...]).astype(low_type)


def side_weights(*args):
    width = args[0].shape[1]
    half = args[-1].shape[1]
    return pl.pallas_call(
        side_weights_kernel,
        out_shape=[
            jax.ShapeDtypeStruct((width, 3 * half), low_type),
            jax.ShapeDtypeStruct((width, 2 * half), low_type),
        ],
        compiler_params=pltpu.CompilerParams(vmem_limit_bytes=vmem_budget),
        cost_estimate=heavy,
        name="side_weights",
    )(*args)


def product_kernel(left, right, out):
    @pl.when(pl.program_id(0) == 0)
    def _():
        out[...] = jnp.zeros_like(out)

    out[...] += dot_wide(left[...], right[...])


def product(left, right):
    rows, depth = left.shape
    width = right.shape[1]
    block = 512
    return pl.pallas_call(
        product_kernel,
        grid=(depth // block,),
        in_specs=[
            pl.BlockSpec((rows, block), lambda j: (0, j)),
            pl.BlockSpec((block, width), lambda j: (j, 0)),
        ],
        out_specs=pl.BlockSpec((rows, width), lambda j: (0, 0)),
        out_shape=jax.ShapeDtypeStruct((rows, width), wide_type),
        compiler_params=pltpu.CompilerParams(vmem_limit_bytes=vmem_budget),
        cost_estimate=heavy,
        name="product",
    )(left, right)


def back_through_norm(values, incoming, gain):
    factor = lax.rsqrt(jnp.mean(values * values, axis=-1, keepdims=True) + norm_eps)
    scaled = incoming * gain
    inward = factor * scaled - values * (factor * factor * factor) * jnp.mean(
        scaled * values, axis=-1, keepdims=True
    )
    return inward, jnp.sum(incoming * values * factor, axis=0, keepdims=True)


def self_forward_kernel(
    facts, rows_in, gain, weight, out_weight, normed_out, triple, attended, log_total, part, *, heads
):
    values = rows_in[...].astype(wide_type)
    factor = lax.rsqrt(jnp.mean(values * values, axis=-1, keepdims=True) + norm_eps)
    normed = (values * factor * gain[...]).astype(low_type)
    normed_out[...] = normed
    rows = values.shape[0]
    half = heads * HD
    for side in range(3):
        triple[:, side * half : side * half + half] = dot_wide(normed, weight[side]).astype(low_type)
    key_pos = lax.broadcasted_iota(jnp.int32, (rows, rows), 0)
    query_pos = lax.broadcasted_iota(jnp.int32, (rows, rows), 1)
    allowed = (key_pos <= query_pos) & (key_pos < facts[0])
    left = lax.broadcasted_iota(jnp.int32, (rows, 128), 1) < HD
    log_total[...] = jnp.zeros_like(log_total)
    for pair in range(heads // 2):
        lanes = slice(pair * 128, pair * 128 + 128)
        query_pair = triple[:, lanes]
        key_pair = triple[:, half + pair * 128 : half + pair * 128 + 128]
        value_pair = triple[:, 2 * half + pair * 128 : 2 * half + pair * 128 + 128]
        parts = []
        for side in range(2):
            head = pair * 2 + side
            keep = left if side == 0 else jnp.logical_not(left)
            query = jnp.where(keep, query_pair, jnp.zeros_like(query_pair))
            scores = jnp.where(allowed, dot_columns(key_pair, query) * 0.125, masked_fill)
            top = jnp.max(scores, axis=0, keepdims=True)
            weights = jnp.exp(scores - top)
            total = jnp.sum(weights, axis=0, keepdims=True)
            log_total[head : head + 1, :] = top + jnp.log(total)
            made = dot_rows(value_pair, (weights / total).astype(low_type))
            parts.append(made[side * HD : side * HD + HD, :])
        attended[:, lanes] = jnp.concatenate(parts).T.astype(low_type)
    part[...] = dot_wide(attended[...], out_weight[...])


def self_forward(facts, rows_in, gain, weight, out_weight):
    rows, width = rows_in.shape
    half = out_weight.shape[0]
    args = (rows_in, gain, weight, out_weight)
    outs = (
        ((rows, width), low_type),
        ((rows, 3 * half), low_type),
        ((rows, half), low_type),
        ((8, rows), wide_type),
        ((rows, width), wide_type),
    )
    return pl.pallas_call(
        partial(self_forward_kernel, heads=half // HD),
        grid_spec=pltpu.PrefetchScalarGridSpec(
            num_scalar_prefetch=1,
            grid=(1,),
            in_specs=[whole(arg.shape) for arg in args],
            out_specs=[whole(shape) for shape, _ in outs],
        ),
        out_shape=[jax.ShapeDtypeStruct(shape, kind) for shape, kind in outs],
        compiler_params=pltpu.CompilerParams(vmem_limit_bytes=vmem_budget),
        cost_estimate=heavy,
        name="self_forward",
    )(facts, *args)


def query_forward_kernel(rows_in, own, came, gain, weight, first, normed_out, heads_out, heads_out_t, *, heads):
    total = rows_in[...].astype(wide_type) + (own[...] + came[...])
    first[...] = total
    factor = lax.rsqrt(jnp.mean(total * total, axis=-1, keepdims=True) + norm_eps)
    normed = (total * factor * gain[...]).astype(low_type)
    normed_out[...] = normed
    query = (dot_wide(normed, weight[...]).astype(low_type).astype(wide_type) * 0.125).astype(low_type)
    turned = query.T
    left = lax.broadcasted_iota(jnp.int32, (query.shape[0], 128), 1) < HD
    for head in range(heads):
        pair = query[:, head // 2 * 128 : head // 2 * 128 + 128]
        keep = left if head % 2 == 0 else jnp.logical_not(left)
        heads_out[head] = jnp.where(keep, pair, jnp.zeros_like(pair))
        own_rows = slice(head % 2 * HD, head % 2 * HD + HD)
        other_rows = slice((1 - head % 2) * HD, (1 - head % 2) * HD + HD)
        mine = turned[head * HD : head * HD + HD, :]
        heads_out_t[head, own_rows, :] = mine
        heads_out_t[head, other_rows, :] = jnp.zeros_like(mine)


def query_forward(rows_in, own, came, gain, weight):
    rows, width = rows_in.shape
    heads = weight.shape[1] // HD
    outs = (
        ((rows, width), wide_type),
        ((rows, width), low_type),
        ((heads, rows, 128), low_type),
        ((heads, 128, rows), low_type),
    )
    return pl.pallas_call(
        partial(query_forward_kernel, heads=heads),
        out_shape=[jax.ShapeDtypeStruct(shape, kind) for shape, kind in outs],
        compiler_params=pltpu.CompilerParams(vmem_limit_bytes=vmem_budget),
        cost_estimate=heavy,
        name="query_forward",
    )(rows_in, own, came, gain, weight)


def self_backward_kernel(
    facts, values, own, came, gain, grad_second, out_weight, triple, log_total, weight,
    grad_first, grad_low, gain_grad, triple_grad, part, *, heads,
):
    rows = triple.shape[0]
    half = heads * HD
    incoming = (own[...] + came[...]).astype(low_type).astype(wide_type)
    inward, gain_row = back_through_norm(values[...], incoming, gain[...])
    gain_grad[...] = jnp.broadcast_to(gain_row, gain_grad.shape)
    total = inward + grad_second[...]
    grad_first[...] = total
    grad_low[...] = total.astype(low_type)
    grad = dot_columns(grad_low[...], out_weight[...]).astype(low_type)
    key_pos = lax.broadcasted_iota(jnp.int32, (rows, rows), 0)
    query_pos = lax.broadcasted_iota(jnp.int32, (rows, rows), 1)
    allowed = (key_pos <= query_pos) & (key_pos < facts[0])
    left = lax.broadcasted_iota(jnp.int32, (rows, 128), 1) < HD
    for pair in range(heads // 2):
        lanes = slice(pair * 128, pair * 128 + 128)
        query_pair = triple[:, lanes]
        key_pair = triple[:, half + pair * 128 : half + pair * 128 + 128]
        value_pair = triple[:, 2 * half + pair * 128 : 2 * half + pair * 128 + 128]
        grad_pair = grad[:, lanes]
        key_sum, value_sum, query_parts = 0.0, 0.0, []
        for side in range(2):
            head = pair * 2 + side
            keep = left if side == 0 else jnp.logical_not(left)
            query = jnp.where(keep, query_pair, jnp.zeros_like(query_pair))
            grad_head = jnp.where(keep, grad_pair, jnp.zeros_like(grad_pair))
            scores = dot_columns(key_pair, query) * 0.125
            probs = jnp.exp(jnp.where(allowed, scores, masked_fill) - log_total[head : head + 1, :])
            grad_probs = dot_columns(value_pair, grad_head)
            inner = jnp.sum(probs * grad_probs, axis=0, keepdims=True)
            grad_scores = (probs * (grad_probs - inner)).astype(low_type)
            value_sum = value_sum + dot_wide(probs.astype(low_type), grad_head)
            key_sum = key_sum + dot_wide(grad_scores, query)
            query_parts.append(dot_rows(key_pair, grad_scores)[side * HD : side * HD + HD, :])
        triple_grad[:, lanes] = (jnp.concatenate(query_parts) * 0.125).T.astype(low_type)
        triple_grad[:, half + pair * 128 : half + pair * 128 + 128] = (key_sum * 0.125).astype(low_type)
        triple_grad[:, 2 * half + pair * 128 : 2 * half + pair * 128 + 128] = value_sum.astype(low_type)
    part[...] = (
        dot_columns(triple_grad[:, :half], weight[0])
        + dot_columns(triple_grad[:, half : 2 * half], weight[1])
        + dot_columns(triple_grad[:, 2 * half :], weight[2])
    )


def self_backward(facts, values, own, came, gain, grad_second, out_weight, triple, log_total, weight):
    rows, wide = triple.shape
    width = weight.shape[1]
    args = (values, own, came, gain, grad_second, out_weight, triple, log_total, weight)
    outs = (
        ((rows, width), wide_type),
        ((rows, width), low_type),
        ((8, width), wide_type),
        ((rows, wide), low_type),
        ((rows, width), wide_type),
    )
    return pl.pallas_call(
        partial(self_backward_kernel, heads=wide // (3 * HD)),
        grid_spec=pltpu.PrefetchScalarGridSpec(
            num_scalar_prefetch=1,
            grid=(1,),
            in_specs=[whole(arg.shape) for arg in args],
            out_specs=[whole(shape) for shape, _ in outs],
        ),
        out_shape=[jax.ShapeDtypeStruct(shape, kind) for shape, kind in outs],
        compiler_params=pltpu.CompilerParams(vmem_limit_bytes=vmem_budget),
        cost_estimate=heavy,
        name="self_backward",
    )(facts, *args)


def input_back_kernel(
    facts, values, own, came, gain, grad_first, second, result_own, result_came, act_sums, cross_gain_grad,
    ffn_gain_grad, groups, input_grad, layer_out, small, *, chips,
):
    incoming = (own[...] + came[...]).astype(low_type).astype(wide_type)
    inward, gain_row = back_through_norm(values[...].astype(wide_type), incoming, gain[...])
    input_grad[...] = inward + grad_first[...]
    layer_out[...] = (second[...] + (result_own[...] + result_came[...])).astype(low_type)
    width = values.shape[1]
    gains = jnp.concatenate(
        (
            act_sums[1:2, :],
            act_sums[0:1, :],
            0.5 * gain_row,
            0.5 * cross_gain_grad[0:1, :],
            0.5 * ffn_gain_grad[0:1, :],
            jnp.zeros((3, width), wide_type),
        )
    )
    small[...] = jnp.zeros_like(small)
    small[facts[0]] = groups[...]
    for tile in range(width // 128):
        small[chips + tile] = gains[:, tile * 128 : tile * 128 + 128]


def input_back(facts, chips, *args):
    rows, width = args[0].shape
    outs = (((rows, width), wide_type), ((rows, width), low_type), ((chips + width // 128, 8, 128), wide_type))
    return pl.pallas_call(
        partial(input_back_kernel, chips=chips),
        grid_spec=pltpu.PrefetchScalarGridSpec(
            num_scalar_prefetch=1,
            grid=(1,),
            in_specs=[whole(arg.shape) for arg in args],
            out_specs=[whole(shape) for shape, _ in outs],
        ),
        out_shape=[jax.ShapeDtypeStruct(shape, kind) for shape, kind in outs],
        compiler_params=pltpu.CompilerParams(vmem_limit_bytes=vmem_budget),
        cost_estimate=heavy,
        name="input_back",
    )(facts, *args)


def assemble_kernel(
    facts, pair, conv_part, pair_came, conv_came, own, other, left, middle, right, gains, conv, cross_kv,
    cross_out, self_qkv, cross_query, self_out, ffn_in, ffn_out, *gain_outs,
):
    width = conv.shape[1]
    half = width // 2
    third = left.shape[1]
    hidden = ffn_in.shape[1]
    first = facts[1] == 0
    conv[:, :half] = jnp.where(first, conv_part[...], conv_came[...])
    conv[:, half:] = jnp.where(first, conv_came[...], conv_part[...])
    for side in range(2):
        mine = pair[:, side * half : side * half + half]
        theirs = pair_came[:, side * half : side * half + half]
        cross_kv[:, side, :half] = jnp.where(first, mine, theirs)
        cross_kv[:, side, half:] = jnp.where(first, theirs, mine)
    for side in range(3):
        self_qkv[side] = own[:, side * half : side * half + half]
    cross_query[...] = other[:, :half]
    self_out[...] = other[:, half:]
    ffn_in[:, :third] = left[...]
    ffn_in[:, third:] = middle[:, : hidden - third]
    ffn_out[:, : 2 * third - hidden] = middle[:, hidden - third :]
    ffn_out[:, 2 * third - hidden :] = right[:, : 2 * hidden - 2 * third]
    cross_out[...] = right[:, 2 * hidden - 2 * third :]
    share = conv.shape[0]
    picked = (
        lax.broadcasted_iota(jnp.int32, (width, share), 0)
        == lax.broadcasted_iota(jnp.int32, (width, share), 1) + facts[0] * share
    ).astype(wide_type)
    first_tile = gains.shape[0] - width // 128
    rows_of = jnp.concatenate([gains[first_tile + tile] for tile in range(width // 128)], axis=1)
    mine = jnp.dot(rows_of, picked, precision=lax.Precision.HIGHEST)
    for number, out in enumerate(gain_outs):
        out[...] = mine[number : number + 1, :]


def assemble(facts, *args):
    share, width = args[0].shape
    left = args[-2]
    half = width // 2
    hidden = (3 * left.shape[1] - half) // 2
    outs = (
        (share, width),
        (share, 2, width),
        (share, half),
        (3, share, half),
        (share, half),
        (share, half),
        (share, hidden),
        (share, hidden),
    ) + ((1, share),) * 5
    return pl.pallas_call(
        assemble_kernel,
        grid_spec=pltpu.PrefetchScalarGridSpec(
            num_scalar_prefetch=1,
            grid=(1,),
            in_specs=[whole(arg.shape) for arg in args],
            out_specs=[whole(shape) for shape in outs],
        ),
        out_shape=[jax.ShapeDtypeStruct(shape, wide_type) for shape in outs],
        compiler_params=pltpu.CompilerParams(vmem_limit_bytes=vmem_budget),
        cost_estimate=heavy,
        name="assemble",
    )(facts, *args)


def shards(
    dec_input,
    out_grad,
    enc_feats,
    mem_lengths,
    dec_lengths,
    doc_owner,
    group_gain,
    group_bias,
    conv_weight,
    cross_kv,
    self_gain,
    self_qkv,
    self_out,
    cross_gain,
    cross_query,
    cross_out,
    ffn_gain,
    ffn_in,
    ffn_out,
):
    chips = lax.axis_size("dp")
    chip_index = lax.axis_index("dp")
    core_index = lax.axis_index("mp")
    memory_in = enc_feats[0, 0]
    docs, sub, width = memory_in.shape
    per_group = width // GROUPS
    half = width // 2
    heads = half // HD
    rows_here = docs * sub
    share = width // chips
    bits = chips.bit_length() - 1
    rest = tuple(range(4, bits))
    order_sets = {
        "stats": (0, 1, 2, 3),
        "left": (2, 3, 0, 1),
        "middle": (0, 2, 3, 1),
        "right": (1, 0, 2, 3),
        "own": (1, 2, 0, 3),
        "other": (0, 1, 3, 2),
        "pair": (2, 0, 1, 3),
        "along": (0, 1, 2, 3),
        "across": (1, 0, 2, 3),
    }
    orders = {
        name: order + rest if bits >= 4 else tuple(range(bits)) for name, order in order_sets.items()
    }

    outgoing = gather_docs(memory_in, doc_owner)
    features = lax.all_to_all(outgoing, "dp", split_axis=0, concat_axis=0, tiled=True)
    outgoing, memory_here, dec_input = tie((outgoing, memory_in, dec_input))
    wide_in = memory_here.astype(wide_type)
    slot_pos = lax.broadcasted_iota(jnp.int32, (docs, sub), 1)
    live_in = ((slot_pos * 2 + core_index) * chips + chip_index < mem_lengths[:, None])[:, :, None]
    masked_in = jnp.where(live_in, wide_in, 0.0)
    channel_sums = jnp.stack((jnp.sum(masked_in, axis=1), jnp.sum(masked_in * wide_in, axis=1)), axis=1)
    group_of = (
        lax.broadcasted_iota(jnp.int32, (width, GROUPS), 0) // per_group
        == lax.broadcasted_iota(jnp.int32, (width, GROUPS), 1)
    ).astype(wide_type)

    def group_sums(channels):
        return jnp.dot(channels, group_of, precision=lax.Precision.HIGHEST)

    def to_channels(groups):
        return jnp.dot(groups, group_of.T, precision=lax.Precision.HIGHEST)

    sums_here = group_sums(channel_sums.reshape(docs * 2, width)).reshape(docs, 2 * GROUPS)
    sums_here = jnp.take(sums_here, doc_owner, axis=0, mode="clip")
    stat_sums = ScatterSums([core_total(sums_here)], [orders["stats"]], chip_index)
    stat_sums.begin()

    def next_step(sums, value):
        value = sums.behind(value)
        sums.merge()
        if sums.orders[0]:
            sums.begin()
            value = sums.ahead_of(value)
            sums.send()
        return value

    dec_rows = DEC
    dec_rows_in = stat_sums.ahead_of(dec_input.reshape(dec_rows, width))
    stat_sums.send()
    self_facts = dec_lengths[chip_index][None]
    self_weight = self_qkv.transpose(1, 0, 2)
    normed_one, qkv_self, attended, self_totals, part = self_forward(
        self_facts, dec_rows_in, self_gain[None], self_weight, self_out
    )
    part_came = other_core(part)
    part_came = next_step(stat_sums, part_came)
    first_out, normed_two, query_heads, query_heads_t = query_forward(
        dec_rows_in, part, part_came, cross_gain[None], cross_query
    )
    cross_kv, query_heads = next_step(stat_sums, (cross_kv, query_heads))
    pair_weight = prepare_weights(cross_kv)
    pair_weight, query_heads = next_step(stat_sums, (pair_weight, query_heads))
    grad_low, query_heads, pair_weight = tie((out_grad.reshape(DEC, width), query_heads, pair_weight))
    grad_active = dot_columns(grad_low, ffn_out).astype(low_type)
    grad_active, query_heads = tie((grad_active, query_heads))
    while stat_sums.orders[0]:
        query_heads = next_step(stat_sums, query_heads)
    sums_all = stat_sums.current[0]

    document = doc_owner[chip_index]
    length = mem_lengths[document]
    entries = (length * per_group).astype(wide_type)
    center = sums_all[:GROUPS] / entries
    spread = lax.rsqrt(sums_all[GROUPS:] / entries - center * center + group_eps)
    channel_stats = to_channels(jnp.stack((center, spread)))
    stats = jnp.concatenate(
        (channel_stats, group_gain[None], group_bias[None], jnp.zeros((4, width), wide_type))
    )

    facts_own = jnp.stack((length, core_index, core_index, 1)).astype(jnp.int32)
    facts_other = jnp.stack((length, 1 - core_index, core_index, 0)).astype(jnp.int32)
    features, stats, query_heads, query_heads_t = tie((features, stats, query_heads, query_heads_t))
    memory_own = memory_forward(facts_own, features, stats, conv_weight)
    memory_other = other_core(memory_own)

    carry = (
        jnp.full((8, dec_rows), -1e30, wide_type),
        jnp.zeros((8, dec_rows), wide_type),
        jnp.zeros((half, dec_rows), wide_type),
    )
    pairs_own, *carry = cross_forward(
        facts_own, query_heads_t, memory_own, pair_weight, carry
    )
    pairs_other, top, total, gathered = cross_forward(
        facts_other, query_heads_t, memory_other, pair_weight, carry
    )
    crossed, crossed_t, log_total, part = cross_close(gathered, top, total, cross_out)

    second_out, normed_three, grad_lifted, active, part = feed_forward(
        first_out, part, other_core(part), ffn_gain[None], ffn_in, grad_active
    )
    part_came = other_core(part)
    result_part = product(active, ffn_out)
    part_came, result_part = tie((part_came, result_part))
    result_came = other_core(result_part)
    grad_second, ffn_gain_grad, grad_cross, grad_heads, grad_heads_t, inner = feed_close(
        second_out, part, part_came, ffn_gain[None], grad_low, cross_out, crossed_t
    )
    feed_grads = feed_weights(normed_three, grad_low, grad_cross, grad_lifted, active, crossed)
    feed_sums = Sums.of(
        [grad.reshape(chips, share, grad.shape[1]) for grad in feed_grads],
        [orders["left"], orders["middle"], orders["right"]],
        chip_index,
    )
    inner = feed_sums.start(inner)

    pair_grads_other, row_grads_other, query_grad_other = cross_backward(
        facts_other, query_heads, query_heads_t, grad_heads, grad_heads_t, log_total, inner, pairs_other, pair_weight,
        low_type,
    )
    facts_two, query_grad_other = feed_sums.round((facts_own, query_grad_other))
    row_grads_came = other_core(row_grads_other)
    pair_grads_own, row_grads_own, query_grad_own = cross_backward(
        facts_two, query_heads, query_heads_t, grad_heads, grad_heads_t, log_total, inner, pairs_own, pair_weight,
        wide_type,
    )

    facts_three, query_grad_own = feed_sums.round((facts_own, query_grad_own))
    grad_memory, hidden, base, act_sums, groups = memory_backward(
        facts_three, features, row_grads_own, row_grads_came, stats, conv_weight
    )
    place = jnp.concatenate((jnp.stack((chip_index, core_index)).astype(jnp.int32), mem_lengths))

    def late_gradients(late):
        query_grad_own, query_grad_other, pair_grads_own, pair_grads_other, hidden, grad_memory = late
        late_feed = feed_sums.copied()

        grad_cq, part = query_back(query_grad_own, query_grad_other, cross_query)
        part_came = other_core(part)
        grad_first, grad_self, cross_gain_grad, grad_qkv, part_one = self_backward(
            self_facts, first_out, part, part_came, cross_gain[None], grad_second, self_out, qkv_self, self_totals,
            self_weight,
        )
        part_one_came = other_core(part_one)
        own_part, other_part = side_weights(normed_one, grad_qkv, normed_two, grad_cq, grad_self, attended)
        late_sums = Sums.of(
            [own_part.reshape(chips, share, -1), other_part.reshape(chips, share, -1)],
            [orders["own"], orders["other"]],
            chip_index,
        )
        grad_memory, part_one_came = late_sums.start((grad_memory, part_one_came))

        def beside():
            pair_part, conv_keep, conv_send = memory_weights(
                place, memory_own, hidden, memory_other, pair_grads_own, grad_memory, pair_grads_other
            )
            conv_came = other_core(conv_send)
            came, conv_keep = tie((part_one_came, conv_keep))
            results = input_back(
                place, chips, dec_rows_in, part_one, came, self_gain[None], grad_first, second_out, result_part,
                result_came, act_sums, cross_gain_grad, ffn_gain_grad, groups,
            )
            results, conv_came = tie((results, conv_came))
            small = core_total(results[2])
            return (pair_part, (conv_keep + conv_came.astype(wide_type)).astype(low_type)), (*results[:2], small)

        memory_parts, (input_grad, layer_out, small) = lax.cond(length > 0, beside, nothing_like(beside))
        memory_sums = Sums.of(
            [part.reshape(chips, share, -1) for part in memory_parts], [orders["pair"], orders["other"]], chip_index
        )
        input_grad, small = memory_sums.start((input_grad, small))
        all_sums = late_feed.joined(late_sums, memory_sums)
        for hop in range(bits):
            small_came = lax.ppermute(small, "dp", [(chip, chip ^ (1 << hop)) for chip in range(chips)])
            small_came, input_grad = all_sums.round((small_came, input_grad))
            small = small + small_came
        feed_totals, late_totals, memory_totals = late_feed.totals, late_sums.totals, memory_sums.totals
        memory_came = [other_core(total) for total in memory_totals]
        moved = moved_rows(doc_owner, place, memory_in, small)
        weight_grads = assemble(
            place, *memory_totals, *memory_came, *late_totals, *feed_totals, small,
        )
        return moved, layer_out, input_grad, weight_grads

    late = (query_grad_own, query_grad_other, pair_grads_own, pair_grads_other, hidden, grad_memory)
    base, late, act_sums, groups, came = tie(
        (base, late, act_sums, groups, [part.came for part in feed_sums.parts])
    )
    for part, arrived in zip(feed_sums.parts, came):
        part.came = arrived
    returned = lax.all_to_all(base, "dp", split_axis=0, concat_axis=0, tiled=True)

    def late_work():
        return late_gradients(late)

    moved, layer_out, input_grad, weight_grads = lax.cond(length > 0, late_work, nothing_like(late_work))
    memory_grad = spread_docs(returned, moved, doc_owner)
    conv_grad, cross_kv_grad, cross_out_grad, self_qkv_grad, cross_query_grad, self_out_grad = weight_grads[:6]
    ffn_in_grad, ffn_out_grad = weight_grads[6:8]
    gains = [gain.reshape(share) for gain in weight_grads[8:]]
    return (
        layer_out.reshape(1, DEC, width),
        input_grad.reshape(1, DEC, width),
        memory_grad.reshape(1, 1, docs, sub, width),
        gains[0],
        gains[1],
        conv_grad,
        cross_kv_grad,
        gains[2],
        self_qkv_grad.transpose(1, 0, 2),
        self_out_grad.T,
        gains[3],
        cross_query_grad,
        cross_out_grad.T,
        gains[4],
        ffn_in_grad,
        ffn_out_grad.T,
    )


def solution(mesh):
    placed = (
        P("dp", None, None),
        P("dp", None, None),
        P("dp", "mp", None, None, None),
        P(),
        P(),
        P(),
        P(),
        P(),
        P(),
        P(),
        P(),
        P(None, None, "mp"),
        P("mp", None),
        P(),
        P(None, "mp"),
        P("mp", None),
        P(),
        P(None, "mp"),
        P("mp", None),
    )
    return jax.shard_map(
        shards,
        mesh=mesh,
        in_specs=placed,
        out_specs=(
            P("dp", None, None),
            P("dp", None, None),
            P("dp", "mp", None, None, None),
            P("dp"),
            P("dp"),
            P("dp", None),
            P("dp", None, None),
            P("dp"),
            P("dp", None, "mp"),
            P("mp", "dp"),
            P("dp"),
            P("dp", "mp"),
            P("mp", "dp"),
            P("dp"),
            P("dp", "mp"),
            P("mp", "dp"),
        ),
        check_vma=False,
    )
```

```python
from functools import partial

import jax
import jax.numpy as jnp
from jax import lax
from jax.experimental import pallas as pl
from jax.experimental.pallas import tpu as pltpu
from jax.sharding import PartitionSpec as P

HD = 64
GROUPS = 32
DEC = 512


norm_eps = 1e-06
group_eps = 1e-05
masked_fill = -1000000000.0
largest_sum = 1e17
vmem_budget = 16 * 1024 * 1024
vmem_large = 48 * 1024 * 1024


def room(chips):
    return vmem_budget if chips <= 16 else vmem_large


heavy = pl.CostEstimate(flops=10**10, bytes_accessed=10**7, transcendentals=10**7)
low_type = jnp.bfloat16
wide_type = jnp.float32


def dot_wide(left, right):
    return jnp.dot(left, right, preferred_element_type=wide_type)


def dot_rows(left, right):
    return lax.dot_general(left, right, (((0,), (0,)), ((), ())), preferred_element_type=wide_type)


def dot_columns(left, right):
    return lax.dot_general(left, right, (((1,), (1,)), ((), ())), preferred_element_type=wide_type)


def norm_rows(values, gain):
    factor = lax.rsqrt(jnp.mean(values * values, axis=-1, keepdims=True) + norm_eps)
    return (values * factor * gain, factor)


def norm_rows_back(values, factor, gain, incoming):
    scaled = incoming * gain
    inward = factor * scaled - values * factor * factor * factor * jnp.mean(
        scaled * values, axis=-1, keepdims=True
    )
    gain_grad = jnp.sum(incoming * values * factor, axis=0)
    return (inward, gain_grad)


def other_core(values):
    return lax.ppermute(values, "mp", [(0, 1), (1, 0)])


def core_total(partial_sum):
    return partial_sum + other_core(partial_sum)


tie = lax.optimization_barrier


class ScatterSums:
    def __init__(self, arrays, orders, chip_index):
        chips = arrays[0].shape[0]
        self.chip_index = chip_index
        self.bits = chips.bit_length() - 1
        self.orders = [list(order) for order in orders]
        self.left = [list(range(self.bits - 1, -1, -1)) for _ in arrays]
        self.current = [array.reshape((2,) * self.bits + array.shape[1:]) for array in arrays]
        self.kept = self.sent = self.came = None

    def copied(self):
        other = object.__new__(ScatterSums)
        other.chip_index, other.bits = self.chip_index, self.bits
        other.orders = [list(order) for order in self.orders]
        other.left = [list(left) for left in self.left]
        other.current, other.kept, other.sent, other.came = self.current, self.kept, self.sent, self.came
        return other

    def begin(self):
        self.kept, self.sent = [], []
        for number, order in enumerate(self.orders):
            axis = self.left[number].index(order[0])
            mine = (self.chip_index >> order[0]) & 1
            self.sent.append(lax.dynamic_index_in_dim(self.current[number], 1 - mine, axis, False))
            self.kept.append(lax.dynamic_index_in_dim(self.current[number], mine, axis, False))
            self.left[number].pop(axis)

    def ahead_of(self, value):
        self.sent, value = tie((self.sent, value))
        return value

    def send(self):
        chips = 1 << self.bits
        self.came = [
            lax.ppermute(sent, "dp", [(chip, chip ^ (1 << order[0])) for chip in range(chips)])
            for sent, order in zip(self.sent, self.orders)
        ]

    def behind(self, value):
        self.came, value = tie((self.came, value))
        return value

    def merge(self):
        merged = []
        for number, order in enumerate(self.orders):
            total = self.kept[number].astype(wide_type) + self.came[number].astype(wide_type)
            order.pop(0)
            merged.append(total.astype(self.current[number].dtype) if order else total)
        self.current = merged

    def step(self):
        self.begin()
        self.send()
        self.merge()

    def finish(self):
        while self.orders[0]:
            self.step()
        return self.current


def merge_kernel(facts, *refs, plans):
    count = len(plans)
    outs = list(refs[2 * count :])
    for plan, kept, came in zip(plans, refs[:count], refs[count : 2 * count]):
        entries, after, turn = plan["entries"], plan["after"], plan["turn"]

        def total(entry, kept=kept, came=came, after=after):
            own = kept[entry] if after is None else kept[entry >> after, 0, entry & ((1 << after) - 1)]
            return own.astype(wide_type) + came[entry].astype(wide_type)

        if turn is None:
            outs.pop(0)[...] = total(0)
            continue
        sent_out, kept_out = outs.pop(0), outs.pop(0)
        bit, behind = turn
        mine = (facts[0] >> bit) & 1
        for place in range(entries // 2):
            base = (place >> behind << (behind + 1)) | (place & ((1 << behind) - 1))
            kept_out[place] = total(base + (mine << behind)).astype(low_type)
            sent_out[place] = total(base + ((1 - mine) << behind)).astype(low_type)


class Part:
    def __init__(self, array, order):
        self.kept, self.order = array, order
        self.sent = self.came = self.total = None
        self.step = 0
        self.left = tuple(range(len(order) - 1, -1, -1))

    def copied(self):
        other = object.__new__(Part)
        other.__dict__.update(self.__dict__)
        return other


class Sums:
    def __init__(self, parts, chip_index):
        self.parts, self.chip_index = parts, chip_index

    @staticmethod
    def of(arrays, orders, chip_index):
        return Sums([Part(array, order) for array, order in zip(arrays, orders)], chip_index)

    def copied(self):
        return Sums([part.copied() for part in self.parts], self.chip_index)

    def joined(self, *others):
        return Sums([part for sums in (self, *others) for part in sums.parts], self.chip_index)

    def state(self):
        return [(part.kept, part.came) for part in self.parts]

    def stepped(self):
        other = self.copied()
        for part in other.parts:
            part.left = tuple(bit for bit in part.left if bit != part.order[part.step])
            part.step += 1
        return other

    def with_state(self, state):
        other = self.copied()
        for part, (kept, came) in zip(other.parts, state):
            part.kept, part.came = kept, came
        return other

    @property
    def going(self):
        return [part for part in self.parts if part.total is None]

    @property
    def totals(self):
        return [part.total for part in self.parts]

    def start(self, value):
        for part in self.parts:
            chips = part.kept.shape[0]
            behind = part.order[0]
            ahead = len(part.order) - 1 - behind
            view = part.kept.reshape((1 << ahead, 2, 1 << behind) + part.kept.shape[1:])
            mine = (self.chip_index >> behind) & 1
            sent = lax.dynamic_index_in_dim(view, 1 - mine, 1, False)
            part.sent = sent.reshape((chips // 2,) + part.kept.shape[1:])
            part.kept = view
        return self.leave(self.parts, value)

    def leave(self, parts, value):
        sent, value = tie(([part.sent for part in parts], value))
        for part, leaving in zip(parts, sent):
            chips = 1 << len(part.order)
            bit = part.order[part.step]
            part.came = lax.ppermute(leaving, "dp", [(chip, chip ^ (1 << bit)) for chip in range(chips)])
        return value

    def round(self, value):
        parts = self.going
        came, value = tie(([part.came for part in parts], value))
        plans, in_specs, out_specs, out_shape = [], [], [], []
        for part, arrived in zip(parts, came):
            part.came = arrived
            entries, rows, columns = arrived.shape
            kept, bit = part.kept, part.order[part.step]
            if part.step == 0:
                in_specs.append(
                    pl.BlockSpec(
                        (kept.shape[0], 1) + kept.shape[2:],
                        lambda j, facts, bit=bit: (0, (facts[0] >> bit) & 1, 0, 0, 0),
                    )
                )
            else:
                in_specs.append(whole(kept.shape))
            plan = {"entries": entries, "after": bit if part.step == 0 else None, "turn": None}
            part.left = tuple(other for other in part.left if other != bit)
            if part.left:
                following = part.order[part.step + 1]
                plan["turn"] = (following, len(part.left) - 1 - part.left.index(following))
                half = (entries // 2, rows, columns)
                out_specs += [whole(half)] * 2
                out_shape += [jax.ShapeDtypeStruct(half, low_type)] * 2
            else:
                out_specs.append(whole((rows, columns)))
                out_shape.append(jax.ShapeDtypeStruct((rows, columns), wide_type))
            plans.append(plan)
        in_specs += [whole(part.came.shape) for part in parts]
        made = pl.pallas_call(
            partial(merge_kernel, plans=plans),
            grid_spec=pltpu.PrefetchScalarGridSpec(
                num_scalar_prefetch=1, grid=(1,), in_specs=in_specs, out_specs=out_specs
            ),
            out_shape=out_shape,
            compiler_params=pltpu.CompilerParams(vmem_limit_bytes=room(1 << len(parts[0].order))),
            cost_estimate=heavy,
            name="merge_sums",
        )(
            self.chip_index[None].astype(jnp.int32),
            *[part.kept for part in parts],
            *[part.came for part in parts],
        )
        made = list(made)
        for part in parts:
            part.step += 1
            if part.left:
                part.sent, part.kept = made.pop(0), made.pop(0)
            else:
                part.total = made.pop(0)
        parts = [part for part in parts if part.left]
        return self.leave(parts, value) if parts else value


def nothing_like(work):
    def nothing():
        return jax.tree.map(lambda leaf: jnp.zeros(leaf.shape, leaf.dtype), jax.eval_shape(work))

    return nothing


def gather_kernel(owner, rows, out, held, came, gone, *, docs):
    loads = [pltpu.make_async_copy(rows.at[owner[slot]], held.at[slot], came.at[slot]) for slot in range(docs)]
    stores = [pltpu.make_async_copy(held.at[slot], out.at[slot], gone.at[slot]) for slot in range(docs)]
    for load in loads:
        load.start()
    for load, store in zip(loads, stores):
        load.wait()
        store.start()
    for store in stores:
        store.wait()


def gather_docs(memory_in, doc_owner):
    docs = memory_in.shape[0]
    return pl.pallas_call(
        partial(gather_kernel, docs=docs),
        grid_spec=pltpu.PrefetchScalarGridSpec(
            num_scalar_prefetch=1,
            grid=(),
            in_specs=[pl.BlockSpec(memory_space=pl.ANY)],
            out_specs=pl.BlockSpec(memory_space=pltpu.HBM),
            scratch_shapes=[
                pltpu.VMEM(memory_in.shape, low_type),
                pltpu.SemaphoreType.DMA((docs,)),
                pltpu.SemaphoreType.DMA((docs,)),
            ],
        ),
        out_shape=jax.ShapeDtypeStruct(memory_in.shape, low_type),
        compiler_params=pltpu.CompilerParams(vmem_limit_bytes=vmem_large),
        cost_estimate=heavy,
        name="gather_docs",
    )(doc_owner, memory_in)


def prepare_kernel(cross_kv, pair):
    width = cross_kv.shape[0]
    for side in range(2):
        pair[:, side * width : side * width + width] = cross_kv[:, side, :]


def prepare_weights(cross_kv):
    width = cross_kv.shape[0]
    return pl.pallas_call(
        prepare_kernel,
        out_shape=jax.ShapeDtypeStruct((width, 2 * width), low_type),
        compiler_params=pltpu.CompilerParams(vmem_limit_bytes=vmem_budget),
        cost_estimate=heavy,
        name="prepare_weights",
    )(cross_kv)


def moved_kernel(owner, facts, features, groups, out, stats, *, chips, count):
    step = pl.program_id(0)
    sub, width = features.shape[1:]

    @pl.when(step == 0)
    def _():
        own_group = (
            lax.broadcasted_iota(jnp.int32, (128, width), 1) // (width // GROUPS)
            == lax.broadcasted_iota(jnp.int32, (128, width), 0)
        ).astype(wide_type)
        stats[...] = jnp.dot(
            groups[0:chips].reshape(chips * 8, 128), own_group, precision=lax.Precision.HIGHEST
        ).reshape(chips, 8, width)

    position = (lax.broadcasted_iota(jnp.int32, (sub, 1), 0) * 2 + facts[1]) * chips + facts[0]

    def one(place, carry):
        slot = step * count + place
        document = owner[slot]
        normed = (features[document].astype(wide_type) - stats[slot, 0:1, :]) * stats[slot, 1:2, :]
        moved = stats[slot, 1:2, :] * (stats[slot, 2:3, :] + normed * stats[slot, 3:4, :])
        out[place] = jnp.where(position < facts[2 + document], moved, 0.0).astype(low_type)
        return carry

    lax.fori_loop(0, count, one, 0)


def moved_rows(doc_owner, facts, features, groups):
    docs, sub, width = features.shape
    count = max(docs // 4, 1)
    return pl.pallas_call(
        partial(moved_kernel, chips=docs, count=count),
        grid_spec=pltpu.PrefetchScalarGridSpec(
            num_scalar_prefetch=2,
            grid=(docs // count,),
            in_specs=[
                pl.BlockSpec(features.shape, lambda j, owner, facts: (0, 0, 0)),
                pl.BlockSpec(groups.shape, lambda j, owner, facts: (0, 0, 0)),
            ],
            out_specs=pl.BlockSpec((count, sub, width), lambda j, owner, facts: (j, 0, 0)),
            scratch_shapes=[pltpu.VMEM((docs, 8, width), wide_type)],
        ),
        out_shape=jax.ShapeDtypeStruct(features.shape, low_type),
        compiler_params=pltpu.CompilerParams(vmem_limit_bytes=room(docs)),
        cost_estimate=heavy,
        name="moved_rows",
    )(doc_owner, facts, features, groups)


def spread_kernel(owner, *refs, docs, pieces):
    rows = refs[:pieces]
    moved, out, held, taken, wide, came, also, gone = refs[pieces:]
    each = rows[0].shape[1]
    loads = [
        [
            pltpu.make_async_copy(
                piece.at[slot], held.at[slot, pl.ds(number * each, each)], came.at[slot * pieces + number]
            )
            for number, piece in enumerate(rows)
        ]
        for slot in range(docs)
    ]
    takes = [pltpu.make_async_copy(moved.at[slot], taken.at[slot], also.at[slot]) for slot in range(docs)]
    stores = [pltpu.make_async_copy(wide.at[slot], out.at[owner[slot]], gone.at[slot]) for slot in range(docs)]
    for slot in range(docs):
        for load in loads[slot]:
            load.start()
        takes[slot].start()
    for slot in range(docs):
        for load in loads[slot]:
            load.wait()
        takes[slot].wait()
        wide[slot] = held[slot].astype(wide_type) - taken[slot].astype(wide_type)
        stores[slot].start()
    for store in stores:
        store.wait()


def spread_docs(rows, moved, doc_owner):
    docs = moved.shape[0]
    pieces = len(rows)
    return pl.pallas_call(
        partial(spread_kernel, docs=docs, pieces=pieces),
        grid_spec=pltpu.PrefetchScalarGridSpec(
            num_scalar_prefetch=1,
            grid=(),
            in_specs=[pl.BlockSpec(memory_space=pl.ANY)] * (pieces + 1),
            out_specs=pl.BlockSpec(memory_space=pl.ANY),
            scratch_shapes=[
                pltpu.VMEM(moved.shape, low_type),
                pltpu.VMEM(moved.shape, low_type),
                pltpu.VMEM(moved.shape, wide_type),
                pltpu.SemaphoreType.DMA((docs * pieces,)),
                pltpu.SemaphoreType.DMA((docs,)),
                pltpu.SemaphoreType.DMA((docs,)),
            ],
        ),
        out_shape=jax.ShapeDtypeStruct(moved.shape, wide_type),
        compiler_params=pltpu.CompilerParams(vmem_limit_bytes=vmem_large),
        cost_estimate=heavy,
        name="spread_docs",
    )(doc_owner, *rows, moved)


def chunk_of(chips, sub):
    return min(sub, max(16, 512 // chips))


def live_rows(facts, start, chips, span):
    row = lax.broadcasted_iota(jnp.int32, (chips * span, 1), 0)
    chip, step = row // span, row % span
    return ((start + step) * 2 + facts[1]) * chips + chip < facts[0]


def in_branches(facts, start, chips, span, work, dead=None):
    first = (start * 2 + facts[1]) * chips
    last = ((start + span - 1) * 2 + facts[1]) * chips + chips - 1
    full = last < facts[0]
    none = first >= facts[0]

    @pl.when(full)
    def _():
        work(None)

    @pl.when(jnp.logical_not(full) & jnp.logical_not(none))
    def _():
        work(live_rows(facts, start, chips, span))

    if dead is not None:
        pl.when(none)(dead)


def whole(shape):
    return pl.BlockSpec(shape, lambda j, facts: (0,) * len(shape))


def slab(shape, span, first=0):
    return pl.BlockSpec((shape[0], span, shape[2]), lambda j, facts: (0, j + first, 0))


def memory_forward_kernel(facts, rows, stats, weight, out, *, chips, span):
    width = rows.shape[-1]
    wide = rows[...].reshape(chips * span, width).astype(wide_type)
    drive = (wide - stats[0:1, :]) * stats[1:2, :] * stats[2:3, :] + stats[3:4, :]
    hidden = (drive * (0.5 + 0.5 * jnp.tanh(0.5 * drive))).astype(low_type)
    made = wide + dot_wide(hidden, weight[...])
    out[...] = made.astype(low_type).reshape(chips, span, width)


def memory_forward(facts, rows, stats, weight):
    chips, sub, width = rows.shape
    span = chunk_of(chips, sub)
    return pl.pallas_call(
        partial(memory_forward_kernel, chips=chips, span=span),
        grid_spec=pltpu.PrefetchScalarGridSpec(
            num_scalar_prefetch=1,
            grid=(sub // span,),
            in_specs=[slab(rows.shape, span), whole(stats.shape), whole(weight.shape)],
            out_specs=slab(rows.shape, span),
        ),
        out_shape=jax.ShapeDtypeStruct(rows.shape, low_type),
        compiler_params=pltpu.CompilerParams(vmem_limit_bytes=room(chips)),
        cost_estimate=heavy,
        name="memory_forward",
    )(facts, rows, stats, weight)


def memory_backward_kernel(
    facts, rows, own, came, stats, weight, sums_in, grad_out, hidden_out, base_out, sums, groups, *, chips, span, steps
):
    step = pl.program_id(0)
    width = rows.shape[-1]
    count = chips * span

    @pl.when(step == 0)
    def _():
        sums[...] = sums_in[...]

    wide = rows[...].reshape(count, width).astype(wide_type)
    normed = (wide - stats[0:1, :]) * stats[1:2, :]
    drive = normed * stats[2:3, :] + stats[3:4, :]
    gate = 0.5 + 0.5 * jnp.tanh(0.5 * drive)
    hidden_out[...] = (drive * gate).astype(low_type).reshape(chips, span, width)
    grad = (own[...].reshape(count, width) + came[...].reshape(count, width).astype(wide_type)).astype(low_type)
    grad_out[...] = grad.reshape(chips, span, width)
    grad_act = dot_columns(grad, weight[...]) * (gate * (1.0 + drive * (1.0 - gate)))
    sums[0:1, :] += jnp.sum(grad_act, axis=0, keepdims=True)
    sums[1:2, :] += jnp.sum(grad_act * normed, axis=0, keepdims=True)
    base = grad.astype(wide_type) + grad_act * (stats[1:2, :] * stats[2:3, :])
    base_out[...] = base.astype(low_type).reshape(chips, span, width)

    @pl.when(step == steps - 1)
    def _():
        per_group = width // GROUPS
        group_of = (
            lax.broadcasted_iota(jnp.int32, (width, 128), 0) // per_group
            == lax.broadcasted_iota(jnp.int32, (width, 128), 1)
        ).astype(wide_type)
        entries = (facts[0] * per_group).astype(wide_type)
        rows_of = jnp.concatenate(
            (
                stats[0:2, :] * (0.5 / per_group),
                sums[0:2, :] * stats[2:3, :] / entries,
                jnp.zeros((4, width), wide_type),
            )
        )
        groups[...] = jnp.dot(rows_of, group_of, precision=lax.Precision.HIGHEST)


def memory_backward(facts, rows, own, came, stats, weight, sums_in, first):
    chips, sub, width = own.shape
    span = chunk_of(chips, rows.shape[1])
    block = slab(own.shape, span)
    return pl.pallas_call(
        partial(memory_backward_kernel, chips=chips, span=span, steps=sub // span),
        grid_spec=pltpu.PrefetchScalarGridSpec(
            num_scalar_prefetch=1,
            grid=(sub // span,),
            in_specs=[
                slab(rows.shape, span, first),
                block,
                block,
                whole(stats.shape),
                whole(weight.shape),
                whole(sums_in.shape),
            ],
            out_specs=[block, block, block, whole(stats.shape), whole((8, 128))],
        ),
        out_shape=[
            jax.ShapeDtypeStruct(own.shape, low_type),
            jax.ShapeDtypeStruct(own.shape, low_type),
            pltpu.HBM(own.shape, low_type),
            jax.ShapeDtypeStruct(stats.shape, wide_type),
            jax.ShapeDtypeStruct((8, 128), wide_type),
        ],
        compiler_params=pltpu.CompilerParams(vmem_limit_bytes=room(chips)),
        cost_estimate=heavy,
        name="memory_backward",
    )(facts, rows, own, came, stats, weight, sums_in)


def cross_forward_kernel(
    facts, query_t, rows, key_weight, value_weight, top_in, total_in, sum_in, pairs, top, total, gathered,
    total_here, sum_here, held, *, chips, span
):
    step = pl.program_id(0)
    half = key_weight.shape[1]
    width = rows.shape[-1]

    @pl.when(step == 0)
    def _():
        top[...] = top_in[...]
        total[...] = total_in[...]
        gathered[...] = sum_in[...]

    def work(live):
        block = rows[...].reshape(chips * span, width)
        keys = dot_wide(block, key_weight[...]).astype(low_type)
        values = dot_wide(block, value_weight[...]).astype(low_type)
        pairs[:, :, :half] = keys.reshape(chips, span, half)
        pairs[:, :, half:] = values.reshape(chips, span, half)
        heads = half // HD

        def score(head):
            made = dot_wide(keys[:, head // 2 * 128 : head // 2 * 128 + 128], query_t[head])
            return made if live is None else jnp.where(live, made, masked_fill)

        def part_of(head, weights):
            part = dot_rows(values[:, head // 2 * 128 : head // 2 * 128 + 128], weights.astype(low_type))
            return part[head % 2 * HD : head % 2 * HD + HD, :]

        def plain():
            following = score(0)
            for head in range(heads):
                scores = following
                if head + 1 < heads:
                    following = score(head + 1)
                weights = jnp.exp(scores - top[head : head + 1, :])
                total_here[head : head + 1, :] = jnp.sum(weights, axis=0, keepdims=True)
                sum_here[head * HD : head * HD + HD, :] = part_of(head, weights)

        def shifted():
            following = score(0)
            for head in range(heads):
                scores = following
                if head + 1 < heads:
                    following = score(head + 1)
                old_top = top[head : head + 1, :]
                new_top = jnp.maximum(old_top, jnp.max(scores, axis=0, keepdims=True))
                weights = jnp.exp(scores - new_top)
                shrink = jnp.exp(old_top - new_top)
                total[head : head + 1, :] = total[head : head + 1, :] * shrink + jnp.sum(
                    weights, axis=0, keepdims=True
                )
                rows_of = slice(head * HD, head * HD + HD)
                gathered[rows_of, :] = gathered[rows_of, :] * shrink + part_of(head, weights)
                top[head : head + 1, :] = new_top

        fresh = (facts[3] == 1) & (step == 0)
        held[0] = jnp.where(fresh, 1, 0)

        @pl.when(jnp.logical_not(fresh))
        def _():
            plain()
            small = jnp.max(total_here[0:heads, :]) < largest_sum
            held[0] = jnp.where(small, 0, 1)

            @pl.when(small)
            def _():
                total[0:heads, :] += total_here[0:heads, :]
                gathered[...] += sum_here[...]

        pl.when(held[0] == 1)(shifted)

    def dead():
        pairs[...] = jnp.zeros_like(pairs)

    in_branches(facts, step * span, chips, span, work, dead)


def cross_forward(facts, query_t, rows, weight, carry):
    chips, sub, width = rows.shape
    heads, _, queries = query_t.shape
    half = heads * HD
    span = chunk_of(chips, sub)
    stat = (8, queries)
    summed = (half, queries)
    return pl.pallas_call(
        partial(cross_forward_kernel, chips=chips, span=span),
        grid_spec=pltpu.PrefetchScalarGridSpec(
            num_scalar_prefetch=1,
            grid=(sub // span,),
            in_specs=[
                whole(query_t.shape),
                slab(rows.shape, span),
                pl.BlockSpec((width, half), lambda j, facts: (0, facts[2])),
                pl.BlockSpec((width, half), lambda j, facts: (0, 2 + facts[2])),
                whole(stat),
                whole(stat),
                whole(summed),
            ],
            out_specs=[slab((chips, sub, 2 * half), span), whole(stat), whole(stat), whole(summed)],
            scratch_shapes=[
                pltpu.VMEM(stat, wide_type),
                pltpu.VMEM(summed, wide_type),
                pltpu.SMEM((1,), jnp.int32),
            ],
        ),
        out_shape=[
            jax.ShapeDtypeStruct((chips, sub, 2 * half), low_type),
            jax.ShapeDtypeStruct(stat, wide_type),
            jax.ShapeDtypeStruct(stat, wide_type),
            jax.ShapeDtypeStruct(summed, wide_type),
        ],
        compiler_params=pltpu.CompilerParams(vmem_limit_bytes=room(chips)),
        cost_estimate=heavy,
        name="cross_forward",
    )(facts, query_t, rows, weight, weight, *carry)


def cross_close_kernel(gathered, top, total, weight, crossed, crossed_t, log_total, part, *, heads):
    log_total[...] = top[...] + jnp.log(jnp.maximum(total[...], 1e-30))
    for head in range(heads):
        rows = slice(head * HD, head * HD + HD)
        crossed_t[rows, :] = gathered[rows, :] / total[head : head + 1, :]
    low = crossed_t[...].T.astype(low_type)
    crossed[...] = low
    part[...] = dot_wide(low, weight[...])


def cross_close(gathered, top, total, weight):
    half, queries = gathered.shape
    return pl.pallas_call(
        partial(cross_close_kernel, heads=half // HD),
        out_shape=[
            jax.ShapeDtypeStruct((queries, half), low_type),
            jax.ShapeDtypeStruct((half, queries), wide_type),
            jax.ShapeDtypeStruct(top.shape, wide_type),
            jax.ShapeDtypeStruct((queries, weight.shape[1]), wide_type),
        ],
        compiler_params=pltpu.CompilerParams(vmem_limit_bytes=vmem_budget),
        cost_estimate=heavy,
        name="cross_close",
    )(gathered, top, total, weight)


gelu_scale = 0.7978845608028654
gelu_cubic = 0.044715


def feed_forward_kernel(
    first, own, came, gain, weight, grad_active, second, normed, both_grad, both_active, grad_normed
):
    step = pl.program_id(0)

    @pl.when(step == 0)
    def _():
        total = first[...] + (own[...] + came[...])
        second[...] = total
        factor = lax.rsqrt(jnp.mean(total * total, axis=-1, keepdims=True) + norm_eps)
        normed[...] = (total * factor * gain[...]).astype(low_type)
        grad_normed[...] = jnp.zeros_like(grad_normed)

    lifted = dot_wide(normed[...], weight[...])
    square = lifted * lifted
    bent = jnp.tanh(gelu_scale * (lifted * (1.0 + gelu_cubic * square)))
    half_up = 0.5 * (1.0 + bent)
    both_active[...] = (lifted * half_up).astype(low_type)
    slope = half_up + (0.5 * gelu_scale) * lifted * (1.0 - bent * bent) * (1.0 + 3.0 * gelu_cubic * square)
    grad_lifted = (grad_active[...].astype(wide_type) * slope).astype(low_type)
    both_grad[...] = grad_lifted
    grad_normed[...] += dot_columns(grad_lifted, weight[...])


def feed_forward(first, own, came, gain, weight, grad_active):
    rows, width = first.shape
    hidden = weight.shape[1]
    block = 512
    still = pl.BlockSpec((rows, width), lambda j: (0, 0))
    moving = pl.BlockSpec((rows, block), lambda j: (0, j))
    return pl.pallas_call(
        feed_forward_kernel,
        grid=(hidden // block,),
        in_specs=[
            still,
            still,
            still,
            pl.BlockSpec((1, width), lambda j: (0, 0)),
            pl.BlockSpec((width, block), lambda j: (0, j)),
            moving,
        ],
        out_specs=[still, still, moving, moving, still],
        out_shape=[
            jax.ShapeDtypeStruct((rows, width), wide_type),
            jax.ShapeDtypeStruct((rows, width), low_type),
            jax.ShapeDtypeStruct((rows, hidden), low_type),
            jax.ShapeDtypeStruct((rows, hidden), low_type),
            jax.ShapeDtypeStruct((rows, width), wide_type),
        ],
        compiler_params=pltpu.CompilerParams(vmem_limit_bytes=vmem_budget),
        cost_estimate=heavy,
        name="feed_forward",
    )(first, own, came, gain, weight, grad_active)


def feed_close_kernel(
    second, own, came, gain, grad_out, weight, crossed_t, grad_second, gain_grad, grad_cross, heads_out,
    heads_out_t, inner, *, heads,
):
    values = second[...]
    incoming = (own[...] + came[...]).astype(low_type).astype(wide_type)
    factor = lax.rsqrt(jnp.mean(values * values, axis=-1, keepdims=True) + norm_eps)
    scaled = incoming * gain[...]
    inward = factor * scaled - values * (factor * factor * factor) * jnp.mean(
        scaled * values, axis=-1, keepdims=True
    )
    gain_grad[...] = jnp.broadcast_to(
        jnp.sum(incoming * values * factor, axis=0, keepdims=True), gain_grad.shape
    )
    total = inward + grad_out[...].astype(wide_type)
    grad_second[...] = total
    low = total.astype(low_type)
    grad_cross[...] = low
    made = dot_columns(low, weight[...])
    made_low = made.astype(low_type)
    made_t = made_low.astype(wide_type).T
    low_t = made_t.astype(low_type)
    left = lax.broadcasted_iota(jnp.int32, (made.shape[0], 128), 1) < HD
    inner[...] = jnp.zeros_like(inner)
    for head in range(heads):
        pair = made_low[:, head // 2 * 128 : head // 2 * 128 + 128]
        keep = left if head % 2 == 0 else jnp.logical_not(left)
        heads_out[head] = jnp.where(keep, pair, jnp.zeros_like(pair))
        rows = slice(head * HD, head * HD + HD)
        own_rows = slice(head % 2 * HD, head % 2 * HD + HD)
        other_rows = slice((1 - head % 2) * HD, (1 - head % 2) * HD + HD)
        heads_out_t[head, own_rows, :] = low_t[rows, :]
        heads_out_t[head, other_rows, :] = jnp.zeros_like(low_t[rows, :])
        inner[head : head + 1, :] = jnp.sum(made_t[rows, :] * crossed_t[rows, :], axis=0, keepdims=True)


def feed_close(second, own, came, gain, grad_out, weight, crossed_t):
    rows, width = second.shape
    half = weight.shape[0]
    heads = half // HD
    return pl.pallas_call(
        partial(feed_close_kernel, heads=heads),
        out_shape=[
            jax.ShapeDtypeStruct((rows, width), wide_type),
            jax.ShapeDtypeStruct((8, width), wide_type),
            jax.ShapeDtypeStruct((rows, width), low_type),
            jax.ShapeDtypeStruct((heads, rows, 128), low_type),
            jax.ShapeDtypeStruct((heads, 128, rows), low_type),
            jax.ShapeDtypeStruct((8, rows), wide_type),
        ],
        compiler_params=pltpu.CompilerParams(vmem_limit_bytes=vmem_budget),
        cost_estimate=heavy,
        name="feed_close",
    )(second, own, came, gain, grad_out, weight, crossed_t)


def feed_weights_kernel(
    normed, grad_out, grad_cross, both_grad, both_active, crossed, left, middle, right, turned, *, steps
):
    step = pl.program_id(0)
    third = (2 * steps + 1) // 3

    @pl.when(step == 0)
    def _():
        turned[...] = normed[...].T

    @pl.when(step == steps)
    def _():
        turned[...] = grad_out[...].T

    @pl.when(step == 2 * steps)
    def _():
        turned[...] = grad_cross[...].T

    for number, out in enumerate((left, middle, right)):
        inside = (step >= number * third) & (step < number * third + third)

        @pl.when(inside & (step < steps))
        def _(out=out):
            out[...] = dot_wide(turned[...], both_grad[...]).astype(low_type)

        @pl.when(inside & (step >= steps) & (step < 2 * steps))
        def _(out=out):
            out[...] = dot_wide(turned[...], both_active[...]).astype(low_type)

        @pl.when(inside & (step == 2 * steps))
        def _(out=out):
            out[...] = dot_wide(turned[...], crossed[...]).astype(low_type)


def feed_weights(normed, grad_out, grad_cross, grad_lifted, active, crossed):
    rows, width = normed.shape
    hidden = active.shape[1]
    block = crossed.shape[1]
    steps = hidden // block
    third = (2 * steps + 1) // 3

    def piece(number):
        return pl.BlockSpec((width, block), lambda j: (0, jnp.clip(j - number * third, 0, third - 1)))

    still = pl.BlockSpec((rows, width), lambda j: (0, 0))
    return pl.pallas_call(
        partial(feed_weights_kernel, steps=steps),
        grid=(2 * steps + 1,),
        in_specs=[
            still,
            still,
            still,
            pl.BlockSpec((rows, block), lambda j: (0, jnp.minimum(j, steps - 1))),
            pl.BlockSpec((rows, block), lambda j: (0, jnp.clip(j - steps, 0, steps - 1))),
            pl.BlockSpec((rows, block), lambda j: (0, 0)),
        ],
        out_specs=[piece(number) for number in range(3)],
        out_shape=[jax.ShapeDtypeStruct((width, third * block), low_type)] * 3,
        scratch_shapes=[pltpu.VMEM((width, rows), low_type)],
        compiler_params=pltpu.CompilerParams(vmem_limit_bytes=vmem_budget),
        cost_estimate=heavy,
        name="feed_weights",
    )(normed, grad_out, grad_cross, grad_lifted, active, crossed)


def cross_backward_kernel(
    facts, query, query_t, grad, grad_t, log_total, inner, pairs, key_weight, value_weight, pair_grads,
    row_grads, query_grad, held, *, chips, span, first
):
    step = pl.program_id(0)
    width, half = key_weight.shape

    @pl.when(step == 0)
    def _():
        query_grad[...] = jnp.zeros_like(query_grad)

    def work(live):
        block = pairs[...].reshape(chips * span, 2 * half)
        heads = half // HD

        def lanes(head, shift=0):
            return block[:, shift + head // 2 * 128 : shift + head // 2 * 128 + 128]

        def products(head):
            scores = dot_wide(lanes(head), query_t[head])
            if live is not None:
                scores = jnp.where(live, scores, masked_fill)
            return scores, dot_wide(lanes(head, half), grad_t[head])

        following = products(0)
        for pair in range(heads // 2):
            lows, low_grads = [], []
            for side in range(2):
                head = pair * 2 + side
                scores, grad_probs = following
                if head + 1 < heads:
                    following = products(head + 1)
                probs = jnp.exp(scores - log_total[head : head + 1, :])
                low_grads.append((probs * (grad_probs - inner[head : head + 1, :])).astype(low_type))
                lows.append(probs.astype(low_type))
                part = dot_rows(lanes(head), low_grads[-1])
                query_grad[head * HD : head * HD + HD, :] += part[side * HD : side * HD + HD, :]
            at = pair * 128
            both = slice(pair * 2, pair * 2 + 2)
            queries = query.shape[1]
            held[:, at : at + 128] = dot_wide(
                jnp.concatenate(low_grads, axis=1), query[both].reshape(2 * queries, 128)
            ).astype(low_type)
            held[:, half + at : half + at + 128] = dot_wide(
                jnp.concatenate(lows, axis=1), grad[both].reshape(2 * queries, 128)
            ).astype(low_type)
        made = held[...]
        pair_grads[...] = made.reshape(chips, span, 2 * half)
        back = dot_columns(made[:, :half], key_weight[...]) + dot_columns(made[:, half:], value_weight[...])
        row_grads[...] = back.astype(row_grads.dtype).reshape(chips, span, width)

    def dead():
        pair_grads[...] = jnp.zeros_like(pair_grads)
        row_grads[...] = jnp.zeros_like(row_grads)

    in_branches(facts, (step + first) * span, chips, span, work, dead)


def cross_backward(facts, query, query_t, grad, grad_t, log_total, inner, pairs, weight, grad_type, first, steps):
    chips, sub, both = pairs.shape
    width = weight.shape[0]
    heads, _, queries = query_t.shape
    span = chunk_of(chips, sub)
    half = both // 2
    rows = steps * span
    pair_block = slab((chips, rows, both), span)
    row_block = slab((chips, rows, width), span)
    return pl.pallas_call(
        partial(cross_backward_kernel, chips=chips, span=span, first=first),
        grid_spec=pltpu.PrefetchScalarGridSpec(
            num_scalar_prefetch=1,
            grid=(steps,),
            in_specs=[
                whole(query.shape),
                whole(query_t.shape),
                whole(grad.shape),
                whole(grad_t.shape),
                whole(log_total.shape),
                whole(inner.shape),
                slab(pairs.shape, span, first),
                pl.BlockSpec((width, half), lambda j, facts: (0, facts[2])),
                pl.BlockSpec((width, half), lambda j, facts: (0, 2 + facts[2])),
            ],
            out_specs=[pair_block, row_block, whole((heads * HD, queries))],
            scratch_shapes=[pltpu.VMEM((chips * span, both), low_type)],
        ),
        out_shape=[
            jax.ShapeDtypeStruct((chips, rows, both), low_type),
            jax.ShapeDtypeStruct((chips, rows, width), grad_type),
            jax.ShapeDtypeStruct((heads * HD, queries), wide_type),
        ],
        compiler_params=pltpu.CompilerParams(vmem_limit_bytes=room(chips)),
        cost_estimate=heavy,
        name="cross_backward",
    )(facts, query, query_t, grad, grad_t, log_total, inner, pairs, weight, weight)


def query_back_kernel(*refs):
    *parts, weight, grad, part = refs
    total = parts[0][...]
    for other in parts[1:]:
        total = total + other[...]
    low = (total * 0.125).T.astype(low_type)
    grad[...] = low
    part[...] = dot_columns(low, weight[...])


def query_back(parts, weight):
    half, rows = parts[0].shape
    return pl.pallas_call(
        query_back_kernel,
        out_shape=[
            jax.ShapeDtypeStruct((rows, half), low_type),
            jax.ShapeDtypeStruct((rows, weight.shape[0]), wide_type),
        ],
        compiler_params=pltpu.CompilerParams(vmem_limit_bytes=vmem_budget),
        cost_estimate=heavy,
        name="query_back",
    )(*parts, weight)


def memory_weights_kernel(facts, *refs, pieces, chips, span, steps):
    rows, other = refs[:2]
    sets = [refs[2 + 4 * piece : 6 + 4 * piece] for piece in range(pieces)]
    pair_out, keep_out, send_out, pair_sum, conv_sum = refs[2 + 4 * pieces :]
    step = pl.program_id(0)
    count = chips * span
    each = steps // pieces

    def flat(ref):
        return ref[...].reshape(count, ref.shape[-1])

    @pl.when(step == 0)
    def _():
        pair_sum[...] = jnp.zeros_like(pair_sum)
        conv_sum[...] = jnp.zeros_like(conv_sum)

    for piece, (hidden, pair_grads, row_grads, other_grads) in enumerate(sets):

        @pl.when((step >= piece * each) & (step < piece * each + each))
        def _(hidden=hidden, pair_grads=pair_grads, row_grads=row_grads, other_grads=other_grads):
            pair_sum[...] += dot_rows(flat(rows), flat(pair_grads)) + dot_rows(flat(other), flat(other_grads))
            conv_sum[...] += dot_rows(flat(hidden), flat(row_grads))

    @pl.when(step == steps - 1)
    def _():
        pair_out[...] = pair_sum[...].astype(low_type)
        half = keep_out.shape[1]
        first = facts[1] == 0
        keep_out[...] = jnp.where(first, conv_sum[:, :half], conv_sum[:, half:])
        send_out[...] = jnp.where(first, conv_sum[:, half:], conv_sum[:, :half]).astype(low_type)


def memory_weights(facts, rows, other, sets):
    chips, sub, width = rows.shape
    span = chunk_of(chips, sub)
    both = sets[0][1].shape[2]
    steps = sub // span
    pieces = len(sets)
    each = steps // pieces

    def piece_block(piece, columns):
        return pl.BlockSpec(
            (chips, span, columns), lambda j, facts: (0, jnp.clip(j - piece * each, 0, each - 1), 0)
        )

    in_specs = [slab(rows.shape, span), slab(other.shape, span)]
    for piece, arrays in enumerate(sets):
        in_specs += [piece_block(piece, array.shape[2]) for array in arrays]
    outs = (((width, both), low_type), ((width, width // 2), wide_type), ((width, width // 2), low_type))
    return pl.pallas_call(
        partial(memory_weights_kernel, pieces=pieces, chips=chips, span=span, steps=steps),
        grid_spec=pltpu.PrefetchScalarGridSpec(
            num_scalar_prefetch=1,
            grid=(steps,),
            in_specs=in_specs,
            out_specs=[whole(shape) for shape, _ in outs],
            scratch_shapes=[pltpu.VMEM((width, both), wide_type), pltpu.VMEM((width, width), wide_type)],
        ),
        out_shape=[jax.ShapeDtypeStruct(shape, kind) for shape, kind in outs],
        compiler_params=pltpu.CompilerParams(vmem_limit_bytes=room(chips)),
        cost_estimate=heavy,
        name="memory_weights",
    )(facts, rows, other, *[array for arrays in sets for array in arrays])


def side_weights_kernel(normed_one, grad_qkv, normed_two, grad_cq, grad_self, attended, first, second):
    half = attended.shape[1]
    cut = first.shape[1]
    first[...] = dot_rows(normed_one[...], grad_qkv[:, :cut]).astype(low_type)
    rest = 3 * half - cut
    second[:, :rest] = dot_rows(normed_one[...], grad_qkv[:, cut:]).astype(low_type)
    second[:, rest : rest + half] = dot_rows(normed_two[...], grad_cq[...]).astype(low_type)
    second[:, rest + half :] = dot_rows(grad_self[...], attended[...]).astype(low_type)


def side_weights(*args):
    width = args[0].shape[1]
    half = args[-1].shape[1]
    cut = 3 * half - 128
    return pl.pallas_call(
        side_weights_kernel,
        out_shape=[
            jax.ShapeDtypeStruct((width, cut), low_type),
            jax.ShapeDtypeStruct((width, 5 * half - cut), low_type),
        ],
        compiler_params=pltpu.CompilerParams(vmem_limit_bytes=vmem_budget),
        cost_estimate=heavy,
        name="side_weights",
    )(*args)


def product_kernel(left, right, out):
    @pl.when(pl.program_id(0) == 0)
    def _():
        out[...] = jnp.zeros_like(out)

    out[...] += dot_wide(left[...], right[...])


def product(left, right):
    rows, depth = left.shape
    width = right.shape[1]
    block = 512
    return pl.pallas_call(
        product_kernel,
        grid=(depth // block,),
        in_specs=[
            pl.BlockSpec((rows, block), lambda j: (0, j)),
            pl.BlockSpec((block, width), lambda j: (j, 0)),
        ],
        out_specs=pl.BlockSpec((rows, width), lambda j: (0, 0)),
        out_shape=jax.ShapeDtypeStruct((rows, width), wide_type),
        compiler_params=pltpu.CompilerParams(vmem_limit_bytes=vmem_budget),
        cost_estimate=heavy,
        name="product",
    )(left, right)


def back_through_norm(values, incoming, gain):
    factor = lax.rsqrt(jnp.mean(values * values, axis=-1, keepdims=True) + norm_eps)
    scaled = incoming * gain
    inward = factor * scaled - values * (factor * factor * factor) * jnp.mean(
        scaled * values, axis=-1, keepdims=True
    )
    return inward, jnp.sum(incoming * values * factor, axis=0, keepdims=True)


def self_forward_kernel(
    facts, rows_in, gain, weight, out_weight, normed_out, triple, attended, log_total, part, *, heads
):
    values = rows_in[...].astype(wide_type)
    factor = lax.rsqrt(jnp.mean(values * values, axis=-1, keepdims=True) + norm_eps)
    normed = (values * factor * gain[...]).astype(low_type)
    normed_out[...] = normed
    rows = values.shape[0]
    half = heads * HD
    for side in range(3):
        triple[:, side * half : side * half + half] = dot_wide(normed, weight[side]).astype(low_type)
    key_pos = lax.broadcasted_iota(jnp.int32, (rows, rows), 0)
    query_pos = lax.broadcasted_iota(jnp.int32, (rows, rows), 1)
    allowed = (key_pos <= query_pos) & (key_pos < facts[0])
    left = lax.broadcasted_iota(jnp.int32, (rows, 128), 1) < HD
    log_total[...] = jnp.zeros_like(log_total)
    for pair in range(heads // 2):
        lanes = slice(pair * 128, pair * 128 + 128)
        query_pair = triple[:, lanes]
        key_pair = triple[:, half + pair * 128 : half + pair * 128 + 128]
        value_pair = triple[:, 2 * half + pair * 128 : 2 * half + pair * 128 + 128]
        parts = []
        for side in range(2):
            head = pair * 2 + side
            keep = left if side == 0 else jnp.logical_not(left)
            query = jnp.where(keep, query_pair, jnp.zeros_like(query_pair))
            scores = jnp.where(allowed, dot_columns(key_pair, query) * 0.125, masked_fill)
            top = jnp.max(scores, axis=0, keepdims=True)
            weights = jnp.exp(scores - top)
            total = jnp.sum(weights, axis=0, keepdims=True)
            log_total[head : head + 1, :] = top + jnp.log(total)
            made = dot_rows(value_pair, (weights / total).astype(low_type))
            parts.append(made[side * HD : side * HD + HD, :])
        attended[:, lanes] = jnp.concatenate(parts).T.astype(low_type)
    part[...] = dot_wide(attended[...], out_weight[...])


def self_forward(facts, rows_in, gain, weight, out_weight):
    rows, width = rows_in.shape
    half = out_weight.shape[0]
    args = (rows_in, gain, weight, out_weight)
    outs = (
        ((rows, width), low_type),
        ((rows, 3 * half), low_type),
        ((rows, half), low_type),
        ((8, rows), wide_type),
        ((rows, width), wide_type),
    )
    return pl.pallas_call(
        partial(self_forward_kernel, heads=half // HD),
        grid_spec=pltpu.PrefetchScalarGridSpec(
            num_scalar_prefetch=1,
            grid=(1,),
            in_specs=[whole(arg.shape) for arg in args],
            out_specs=[whole(shape) for shape, _ in outs],
        ),
        out_shape=[jax.ShapeDtypeStruct(shape, kind) for shape, kind in outs],
        compiler_params=pltpu.CompilerParams(vmem_limit_bytes=vmem_budget),
        cost_estimate=heavy,
        name="self_forward",
    )(facts, *args)


def query_forward_kernel(rows_in, own, came, gain, weight, first, normed_out, heads_out, heads_out_t, *, heads):
    total = rows_in[...].astype(wide_type) + (own[...] + came[...])
    first[...] = total
    factor = lax.rsqrt(jnp.mean(total * total, axis=-1, keepdims=True) + norm_eps)
    normed = (total * factor * gain[...]).astype(low_type)
    normed_out[...] = normed
    query = (dot_wide(normed, weight[...]).astype(low_type).astype(wide_type) * 0.125).astype(low_type)
    turned = query.T
    left = lax.broadcasted_iota(jnp.int32, (query.shape[0], 128), 1) < HD
    for head in range(heads):
        pair = query[:, head // 2 * 128 : head // 2 * 128 + 128]
        keep = left if head % 2 == 0 else jnp.logical_not(left)
        heads_out[head] = jnp.where(keep, pair, jnp.zeros_like(pair))
        own_rows = slice(head % 2 * HD, head % 2 * HD + HD)
        other_rows = slice((1 - head % 2) * HD, (1 - head % 2) * HD + HD)
        mine = turned[head * HD : head * HD + HD, :]
        heads_out_t[head, own_rows, :] = mine
        heads_out_t[head, other_rows, :] = jnp.zeros_like(mine)


def query_forward(rows_in, own, came, gain, weight):
    rows, width = rows_in.shape
    heads = weight.shape[1] // HD
    outs = (
        ((rows, width), wide_type),
        ((rows, width), low_type),
        ((heads, rows, 128), low_type),
        ((heads, 128, rows), low_type),
    )
    return pl.pallas_call(
        partial(query_forward_kernel, heads=heads),
        out_shape=[jax.ShapeDtypeStruct(shape, kind) for shape, kind in outs],
        compiler_params=pltpu.CompilerParams(vmem_limit_bytes=vmem_budget),
        cost_estimate=heavy,
        name="query_forward",
    )(rows_in, own, came, gain, weight)


def self_backward_kernel(
    facts, values, own, came, gain, grad_second, out_weight, triple, log_total, weight,
    grad_first, grad_low, gain_grad, triple_grad, part, *, heads,
):
    rows = triple.shape[0]
    half = heads * HD
    incoming = (own[...] + came[...]).astype(low_type).astype(wide_type)
    inward, gain_row = back_through_norm(values[...], incoming, gain[...])
    gain_grad[...] = jnp.broadcast_to(gain_row, gain_grad.shape)
    total = inward + grad_second[...]
    grad_first[...] = total
    grad_low[...] = total.astype(low_type)
    grad = dot_columns(grad_low[...], out_weight[...]).astype(low_type)
    key_pos = lax.broadcasted_iota(jnp.int32, (rows, rows), 0)
    query_pos = lax.broadcasted_iota(jnp.int32, (rows, rows), 1)
    allowed = (key_pos <= query_pos) & (key_pos < facts[0])
    left = lax.broadcasted_iota(jnp.int32, (rows, 128), 1) < HD
    for pair in range(heads // 2):
        lanes = slice(pair * 128, pair * 128 + 128)
        query_pair = triple[:, lanes]
        key_pair = triple[:, half + pair * 128 : half + pair * 128 + 128]
        value_pair = triple[:, 2 * half + pair * 128 : 2 * half + pair * 128 + 128]
        grad_pair = grad[:, lanes]
        key_sum, value_sum, query_parts = 0.0, 0.0, []
        for side in range(2):
            head = pair * 2 + side
            keep = left if side == 0 else jnp.logical_not(left)
            query = jnp.where(keep, query_pair, jnp.zeros_like(query_pair))
            grad_head = jnp.where(keep, grad_pair, jnp.zeros_like(grad_pair))
            scores = dot_columns(key_pair, query) * 0.125
            probs = jnp.exp(jnp.where(allowed, scores, masked_fill) - log_total[head : head + 1, :])
            grad_probs = dot_columns(value_pair, grad_head)
            inner = jnp.sum(probs * grad_probs, axis=0, keepdims=True)
            grad_scores = (probs * (grad_probs - inner)).astype(low_type)
            value_sum = value_sum + dot_wide(probs.astype(low_type), grad_head)
            key_sum = key_sum + dot_wide(grad_scores, query)
            query_parts.append(dot_rows(key_pair, grad_scores)[side * HD : side * HD + HD, :])
        triple_grad[:, lanes] = (jnp.concatenate(query_parts) * 0.125).T.astype(low_type)
        triple_grad[:, half + pair * 128 : half + pair * 128 + 128] = (key_sum * 0.125).astype(low_type)
        triple_grad[:, 2 * half + pair * 128 : 2 * half + pair * 128 + 128] = value_sum.astype(low_type)
    part[...] = (
        dot_columns(triple_grad[:, :half], weight[0])
        + dot_columns(triple_grad[:, half : 2 * half], weight[1])
        + dot_columns(triple_grad[:, 2 * half :], weight[2])
    )


def self_backward(facts, values, own, came, gain, grad_second, out_weight, triple, log_total, weight):
    rows, wide = triple.shape
    width = weight.shape[1]
    args = (values, own, came, gain, grad_second, out_weight, triple, log_total, weight)
    outs = (
        ((rows, width), wide_type),
        ((rows, width), low_type),
        ((8, width), wide_type),
        ((rows, wide), low_type),
        ((rows, width), wide_type),
    )
    return pl.pallas_call(
        partial(self_backward_kernel, heads=wide // (3 * HD)),
        grid_spec=pltpu.PrefetchScalarGridSpec(
            num_scalar_prefetch=1,
            grid=(1,),
            in_specs=[whole(arg.shape) for arg in args],
            out_specs=[whole(shape) for shape, _ in outs],
        ),
        out_shape=[jax.ShapeDtypeStruct(shape, kind) for shape, kind in outs],
        compiler_params=pltpu.CompilerParams(vmem_limit_bytes=vmem_budget),
        cost_estimate=heavy,
        name="self_backward",
    )(facts, *args)


def input_back_kernel(
    values, own, came, gain, grad_first, second, result_own, result_came, act_sums, cross_gain_grad,
    ffn_gain_grad, input_grad, layer_out, gains_out,
):
    incoming = (own[...] + came[...]).astype(low_type).astype(wide_type)
    inward, gain_row = back_through_norm(values[...].astype(wide_type), incoming, gain[...])
    input_grad[...] = inward + grad_first[...]
    layer_out[...] = (second[...] + (result_own[...] + result_came[...])).astype(low_type)
    width = values.shape[1]
    gains = jnp.concatenate(
        (
            act_sums[1:2, :],
            act_sums[0:1, :],
            0.5 * gain_row,
            0.5 * cross_gain_grad[0:1, :],
            0.5 * ffn_gain_grad[0:1, :],
            jnp.zeros((3, width), wide_type),
        )
    )
    for tile in range(width // 128):
        gains_out[tile] = gains[:, tile * 128 : tile * 128 + 128]


def input_back(*args):
    rows, width = args[0].shape
    outs = (((rows, width), wide_type), ((rows, width), low_type), ((width // 128, 8, 128), wide_type))
    return pl.pallas_call(
        input_back_kernel,
        out_shape=[jax.ShapeDtypeStruct(shape, kind) for shape, kind in outs],
        compiler_params=pltpu.CompilerParams(vmem_limit_bytes=vmem_budget),
        cost_estimate=heavy,
        name="input_back",
    )(*args)


def assemble_kernel(
    facts, memory, memory_came, own, other, left, middle, right, gains, conv, cross_kv,
    cross_out, self_qkv, cross_query, self_out, ffn_in, ffn_out, *gain_outs,
):
    width = conv.shape[1]
    half = width // 2
    third = left.shape[1]
    hidden = ffn_in.shape[1]
    first = facts[1] == 0
    conv[:, :half] = jnp.where(first, memory[:, width:], memory_came[:, width:])
    conv[:, half:] = jnp.where(first, memory_came[:, width:], memory[:, width:])
    for side in range(2):
        mine = memory[:, side * half : side * half + half]
        theirs = memory_came[:, side * half : side * half + half]
        cross_kv[:, side, :half] = jnp.where(first, mine, theirs)
        cross_kv[:, side, half:] = jnp.where(first, theirs, mine)
    rest = 3 * half - own.shape[1]
    self_qkv[0] = own[:, :half]
    self_qkv[1] = own[:, half : 2 * half]
    self_qkv[2, :, : half - rest] = own[:, 2 * half :]
    self_qkv[2, :, half - rest :] = other[:, :rest]
    cross_query[...] = other[:, rest : rest + half]
    self_out[...] = other[:, rest + half :]
    ffn_in[:, :third] = left[...]
    ffn_in[:, third:] = middle[:, : hidden - third]
    ffn_out[:, : 2 * third - hidden] = middle[:, hidden - third :]
    ffn_out[:, 2 * third - hidden :] = right[:, : 2 * hidden - 2 * third]
    cross_out[...] = right[:, 2 * hidden - 2 * third :]
    share = conv.shape[0]
    picked = (
        lax.broadcasted_iota(jnp.int32, (width, share), 0)
        == lax.broadcasted_iota(jnp.int32, (width, share), 1) + facts[0] * share
    ).astype(wide_type)
    first_tile = gains.shape[0] - width // 128
    rows_of = jnp.concatenate([gains[first_tile + tile] for tile in range(width // 128)], axis=1)
    mine = jnp.dot(rows_of, picked, precision=lax.Precision.HIGHEST)
    for number, out in enumerate(gain_outs):
        out[...] = mine[number : number + 1, :]


def assemble(facts, *args):
    share = args[0].shape[0]
    width = 2 * args[0].shape[1] // 3
    half = width // 2
    hidden = (3 * args[4].shape[1] - half) // 2
    outs = (
        (share, width),
        (share, 2, width),
        (share, half),
        (3, share, half),
        (share, half),
        (share, half),
        (share, hidden),
        (share, hidden),
    ) + ((1, share),) * 5
    return pl.pallas_call(
        assemble_kernel,
        grid_spec=pltpu.PrefetchScalarGridSpec(
            num_scalar_prefetch=1,
            grid=(1,),
            in_specs=[whole(arg.shape) for arg in args],
            out_specs=[whole(shape) for shape in outs],
        ),
        out_shape=[jax.ShapeDtypeStruct(shape, wide_type) for shape in outs],
        compiler_params=pltpu.CompilerParams(vmem_limit_bytes=vmem_budget),
        cost_estimate=heavy,
        name="assemble",
    )(facts, *args)


def shards(
    dec_input,
    out_grad,
    enc_feats,
    mem_lengths,
    dec_lengths,
    doc_owner,
    group_gain,
    group_bias,
    conv_weight,
    cross_kv,
    self_gain,
    self_qkv,
    self_out,
    cross_gain,
    cross_query,
    cross_out,
    ffn_gain,
    ffn_in,
    ffn_out,
):
    chips = lax.axis_size("dp")
    chip_index = lax.axis_index("dp")
    core_index = lax.axis_index("mp")
    memory_in = enc_feats[0, 0]
    docs, sub, width = memory_in.shape
    per_group = width // GROUPS
    half = width // 2
    heads = half // HD
    rows_here = docs * sub
    share = width // chips
    bits = chips.bit_length() - 1
    rest = tuple(range(4, bits))
    order_sets = {
        "stats": (0, 1, 2, 3),
        "left": (2, 3, 0, 1),
        "middle": (0, 2, 3, 1),
        "right": (1, 0, 2, 3),
        "first": (0, 1, 2, 3),
        "second": (1, 0, 2, 3),
        "memory": (1, 2, 3, 0),
    }
    orders = {
        name: order + rest if bits >= 4 else tuple(range(bits)) for name, order in order_sets.items()
    }

    outgoing = gather_docs(memory_in, doc_owner)
    features = lax.all_to_all(outgoing, "dp", split_axis=0, concat_axis=0, tiled=True)
    outgoing, dec_input = tie((outgoing, dec_input))
    dec_rows = DEC
    dec_rows_in = dec_input.reshape(dec_rows, width)
    self_facts = dec_lengths[chip_index][None]
    self_weight = self_qkv.transpose(1, 0, 2)
    normed_one, qkv_self, attended, self_totals, part = self_forward(
        self_facts, dec_rows_in, self_gain[None], self_weight, self_out
    )
    part_came = other_core(part)
    memory_here, part = tie((memory_in, part))
    wide_in = memory_here.astype(wide_type)
    slot_pos = lax.broadcasted_iota(jnp.int32, (docs, sub), 1)
    live_in = ((slot_pos * 2 + core_index) * chips + chip_index < mem_lengths[:, None])[:, :, None]
    masked_in = jnp.where(live_in, wide_in, 0.0)
    channel_sums = jnp.stack((jnp.sum(masked_in, axis=1), jnp.sum(masked_in * wide_in, axis=1)), axis=1)
    group_of = (
        lax.broadcasted_iota(jnp.int32, (width, GROUPS), 0) // per_group
        == lax.broadcasted_iota(jnp.int32, (width, GROUPS), 1)
    ).astype(wide_type)

    def group_sums(channels):
        return jnp.dot(channels, group_of, precision=lax.Precision.HIGHEST)

    def to_channels(groups):
        return jnp.dot(groups, group_of.T, precision=lax.Precision.HIGHEST)

    sums_here = group_sums(channel_sums.reshape(docs * 2, width)).reshape(docs, 2 * GROUPS)
    sums_here = jnp.take(sums_here, doc_owner, axis=0, mode="clip")
    stat_sums = ScatterSums([core_total(sums_here)], [orders["stats"]], chip_index)
    stat_sums.begin()

    def next_step(sums, value):
        value = sums.behind(value)
        sums.merge()
        if sums.orders[0]:
            sums.begin()
            value = sums.ahead_of(value)
            sums.send()
        return value

    part_came = stat_sums.ahead_of(part_came)
    stat_sums.send()
    first_out, normed_two, query_heads, query_heads_t = query_forward(
        dec_rows_in, part, part_came, cross_gain[None], cross_query
    )
    cross_kv, query_heads = next_step(stat_sums, (cross_kv, query_heads))
    pair_weight = prepare_weights(cross_kv)
    pair_weight, query_heads = next_step(stat_sums, (pair_weight, query_heads))
    grad_low, query_heads, pair_weight = tie((out_grad.reshape(DEC, width), query_heads, pair_weight))
    grad_active = dot_columns(grad_low, ffn_out).astype(low_type)
    grad_active, query_heads = tie((grad_active, query_heads))
    while stat_sums.orders[0]:
        query_heads = next_step(stat_sums, query_heads)
    sums_all = stat_sums.current[0]

    document = doc_owner[chip_index]
    length = mem_lengths[document]
    entries = (length * per_group).astype(wide_type)
    center = sums_all[:GROUPS] / entries
    spread = lax.rsqrt(sums_all[GROUPS:] / entries - center * center + group_eps)
    channel_stats = to_channels(jnp.stack((center, spread)))
    stats = jnp.concatenate(
        (channel_stats, group_gain[None], group_bias[None], jnp.zeros((4, width), wide_type))
    )

    facts_own = jnp.stack((length, core_index, core_index, 1)).astype(jnp.int32)
    facts_other = jnp.stack((length, 1 - core_index, core_index, 0)).astype(jnp.int32)
    features, stats, query_heads, query_heads_t = tie((features, stats, query_heads, query_heads_t))
    memory_own = memory_forward(facts_own, features, stats, conv_weight)
    memory_other = other_core(memory_own)

    carry = (
        jnp.full((8, dec_rows), -1e30, wide_type),
        jnp.zeros((8, dec_rows), wide_type),
        jnp.zeros((half, dec_rows), wide_type),
    )
    pairs_own, *carry = cross_forward(
        facts_own, query_heads_t, memory_own, pair_weight, carry
    )
    pairs_other, top, total, gathered = cross_forward(
        facts_other, query_heads_t, memory_other, pair_weight, carry
    )
    crossed, crossed_t, log_total, part = cross_close(gathered, top, total, cross_out)

    second_out, normed_three, grad_lifted, active, part = feed_forward(
        first_out, part, other_core(part), ffn_gain[None], ffn_in, grad_active
    )
    part_came = other_core(part)
    result_part = product(active, ffn_out)
    part_came, result_part = tie((part_came, result_part))
    result_came = other_core(result_part)
    grad_second, ffn_gain_grad, grad_cross, grad_heads, grad_heads_t, inner = feed_close(
        second_out, part, part_came, ffn_gain[None], grad_low, cross_out, crossed_t
    )
    feed_grads = feed_weights(normed_three, grad_low, grad_cross, grad_lifted, active, crossed)
    feed_sums = Sums.of(
        [grad.reshape(chips, share, grad.shape[1]) for grad in feed_grads],
        [orders["left"], orders["middle"], orders["right"]],
        chip_index,
    )
    inner = feed_sums.start(inner)

    steps = sub // chunk_of(chips, sub)
    place = jnp.concatenate((jnp.stack((chip_index, core_index)).astype(jnp.int32), mem_lengths))
    pair_other, row_other, query_other = cross_backward(
        facts_other, query_heads, query_heads_t, grad_heads, grad_heads_t, log_total, inner, pairs_other, pair_weight,
        low_type, 0, steps,
    )
    facts_two, query_other = feed_sums.round((facts_own, query_other))
    row_came = other_core(row_other)
    pair_own, row_own, query_own = cross_backward(
        facts_two, query_heads, query_heads_t, grad_heads, grad_heads_t, log_total, inner, pairs_own, pair_weight,
        wide_type, 0, steps,
    )

    facts_three, query_own = feed_sums.round((facts_own, query_own))
    grad_memory, hidden, base, act_sums, groups = memory_backward(
        facts_three, features, row_own, row_came, stats, conv_weight, jnp.zeros((8, width), wide_type), 0
    )
    queries, sets = (query_other, query_own), [(hidden, pair_own, grad_memory, pair_other)]

    def dp_hop(value, bit):
        return lax.ppermute(value, "dp", [(chip, chip ^ (1 << bit)) for chip in range(chips)])

    feed_came, base, queries = tie(([part.came for part in feed_sums.parts], base, queries))
    for part, arrived in zip(feed_sums.parts, feed_came):
        part.came = arrived
    returned = [lax.all_to_all(base, "dp", split_axis=0, concat_axis=0, tiled=True)]

    def when_live(work):
        return lax.cond(length > 0, work, nothing_like(work))

    def self_work():
        own_slot = lax.broadcasted_iota(jnp.int32, (chips, 1, 1), 0) == chip_index
        document_groups = jnp.where(own_slot, core_total(groups)[None], 0.0)

        grad_cq, part = query_back(queries, cross_query)
        part_came = other_core(part)
        grad_first, grad_self, cross_gain_grad, grad_qkv, part_one = self_backward(
            self_facts, first_out, part, part_came, cross_gain[None], grad_second, self_out, qkv_self, self_totals,
            self_weight,
        )
        part_one_came = other_core(part_one)
        first_part, second_part = side_weights(normed_one, grad_qkv, normed_two, grad_cq, grad_self, attended)
        part_one_came, first_part = tie((part_one_came, first_part))
        return grad_first, cross_gain_grad, part_one, part_one_came, document_groups, (first_part, second_part)

    queries = feed_sums.round(queries)
    early_feed, late_feed = Sums(feed_sums.parts[:2], chip_index), Sums(feed_sums.parts[2:], chip_index)
    grad_first, cross_gain_grad, part_one, part_one_came, document_groups, late_parts = when_live(self_work)
    while early_feed.going:
        document_groups = early_feed.round(document_groups)
    late_sums = Sums.of(
        [part.reshape(chips, share, -1) for part in late_parts], [orders["first"], orders["second"]], chip_index
    )
    document_groups = late_sums.start(document_groups)

    def memory_work():
        pair_part, conv_keep, conv_send = memory_weights(place, memory_own, memory_other, sets)
        conv_came = other_core(conv_send)
        came, conv_keep = tie((part_one_came, conv_keep))
        input_grad, layer_out, gains = input_back(
            dec_rows_in, part_one, came, self_gain[None], grad_first, second_out, result_part, result_came, act_sums,
            cross_gain_grad, ffn_gain_grad,
        )
        gains, conv_came = tie((gains, conv_came))
        conv_part = (conv_keep + conv_came.astype(wide_type)).astype(low_type)
        return input_grad, layer_out, core_total(gains), jnp.concatenate((pair_part, conv_part), axis=1)

    input_grad, layer_out, small, memory_part = when_live(memory_work)

    memory_sums = Sums.of([memory_part.reshape(chips, share, -1)], [orders["memory"]], chip_index)
    small = memory_sums.start(small)
    late_sums = late_sums.joined(memory_sums)
    all_sums = late_feed.joined(late_sums)
    hop = 0
    moved = memory_grad = None
    while all_sums.going:
        small_came = dp_hop(small, hop) if hop < bits else None
        for bit in ((0,), (1, 2), range(3, bits))[hop] if hop < 3 else ():
            document_groups = document_groups + dp_hop(document_groups, bit)
        value = (small_came, document_groups)
        if hop == 2:
            moved = moved_rows(doc_owner, place, memory_in, document_groups)
            value = (small_came, moved)
        if hop == 3:
            memory_grad = spread_docs(returned, moved, doc_owner)
            value = (small_came, memory_grad)
        if hop == 0:
            returned, small_came = tie((returned, small_came))
            value = (small_came, document_groups)
        small_came, value = all_sums.round(value)
        if hop < bits:
            small = small + small_came
        if hop < 2:
            document_groups = value
        elif hop == 2:
            moved = value
        elif hop == 3:
            memory_grad = value
        hop += 1
    while hop < bits:
        small = small + dp_hop(small, hop)
        hop += 1
    if moved is None:
        moved = moved_rows(doc_owner, place, memory_in, document_groups)
    if memory_grad is None:
        memory_grad = spread_docs(returned, moved, doc_owner)
    first_total, second_total, memory_total = late_sums.totals
    memory_came = other_core(memory_total)
    weight_grads = assemble(
        place, memory_total, memory_came, first_total, second_total, *feed_sums.totals, small
    )
    conv_grad, cross_kv_grad, cross_out_grad, self_qkv_grad, cross_query_grad, self_out_grad = weight_grads[:6]
    ffn_in_grad, ffn_out_grad = weight_grads[6:8]
    gains = [gain.reshape(share) for gain in weight_grads[8:]]
    return (
        layer_out.reshape(1, DEC, width),
        input_grad.reshape(1, DEC, width),
        memory_grad.reshape(1, 1, docs, sub, width),
        gains[0],
        gains[1],
        conv_grad,
        cross_kv_grad,
        gains[2],
        self_qkv_grad.transpose(1, 0, 2),
        self_out_grad.T,
        gains[3],
        cross_query_grad,
        cross_out_grad.T,
        gains[4],
        ffn_in_grad,
        ffn_out_grad.T,
    )


def solution(mesh):
    placed = (
        P("dp", None, None),
        P("dp", None, None),
        P("dp", "mp", None, None, None),
        P(),
        P(),
        P(),
        P(),
        P(),
        P(),
        P(),
        P(),
        P(None, None, "mp"),
        P("mp", None),
        P(),
        P(None, "mp"),
        P("mp", None),
        P(),
        P(None, "mp"),
        P("mp", None),
    )
    return jax.shard_map(
        shards,
        mesh=mesh,
        in_specs=placed,
        out_specs=(
            P("dp", None, None),
            P("dp", None, None),
            P("dp", "mp", None, None, None),
            P("dp"),
            P("dp"),
            P("dp", None),
            P("dp", None, None),
            P("dp"),
            P("dp", None, "mp"),
            P("mp", "dp"),
            P("dp"),
            P("dp", "mp"),
            P("mp", "dp"),
            P("dp"),
            P("dp", "mp"),
            P("mp", "dp"),
        ),
        check_vma=False,
    )
```

```python
from functools import partial

import jax
import jax.numpy as jnp
from jax import lax
from jax.experimental import pallas as pl
from jax.experimental.pallas import tpu as pltpu
from jax.sharding import PartitionSpec as P

HD = 64
GROUPS = 32
DEC = 512


norm_eps = 1e-06
group_eps = 1e-05
masked_fill = -1000000000.0
largest_sum = 1e17
vmem_budget = 16 * 1024 * 1024
vmem_large = 48 * 1024 * 1024


def room(chips):
    return vmem_budget if chips <= 16 else vmem_large


heavy = pl.CostEstimate(flops=10**10, bytes_accessed=10**7, transcendentals=10**7)
low_type = jnp.bfloat16
wide_type = jnp.float32


def dot_wide(left, right):
    return jnp.dot(left, right, preferred_element_type=wide_type)


def dot_rows(left, right):
    return lax.dot_general(left, right, (((0,), (0,)), ((), ())), preferred_element_type=wide_type)


def dot_columns(left, right):
    return lax.dot_general(left, right, (((1,), (1,)), ((), ())), preferred_element_type=wide_type)


def norm_rows(values, gain):
    factor = lax.rsqrt(jnp.mean(values * values, axis=-1, keepdims=True) + norm_eps)
    return (values * factor * gain, factor)


def norm_rows_back(values, factor, gain, incoming):
    scaled = incoming * gain
    inward = factor * scaled - values * factor * factor * factor * jnp.mean(
        scaled * values, axis=-1, keepdims=True
    )
    gain_grad = jnp.sum(incoming * values * factor, axis=0)
    return (inward, gain_grad)


def other_core(values):
    return lax.ppermute(values, "mp", [(0, 1), (1, 0)])


def core_total(partial_sum):
    return partial_sum + other_core(partial_sum)


tie = lax.optimization_barrier


class ScatterSums:
    def __init__(self, arrays, orders, chip_index):
        chips = arrays[0].shape[0]
        self.chip_index = chip_index
        self.bits = chips.bit_length() - 1
        self.orders = [list(order) for order in orders]
        self.left = [list(range(self.bits - 1, -1, -1)) for _ in arrays]
        self.current = [array.reshape((2,) * self.bits + array.shape[1:]) for array in arrays]
        self.kept = self.sent = self.came = None

    def copied(self):
        other = object.__new__(ScatterSums)
        other.chip_index, other.bits = self.chip_index, self.bits
        other.orders = [list(order) for order in self.orders]
        other.left = [list(left) for left in self.left]
        other.current, other.kept, other.sent, other.came = self.current, self.kept, self.sent, self.came
        return other

    def begin(self):
        self.kept, self.sent = [], []
        for number, order in enumerate(self.orders):
            axis = self.left[number].index(order[0])
            mine = (self.chip_index >> order[0]) & 1
            self.sent.append(lax.dynamic_index_in_dim(self.current[number], 1 - mine, axis, False))
            self.kept.append(lax.dynamic_index_in_dim(self.current[number], mine, axis, False))
            self.left[number].pop(axis)

    def ahead_of(self, value):
        self.sent, value = tie((self.sent, value))
        return value

    def send(self):
        chips = 1 << self.bits
        self.came = [
            lax.ppermute(sent, "dp", [(chip, chip ^ (1 << order[0])) for chip in range(chips)])
            for sent, order in zip(self.sent, self.orders)
        ]

    def behind(self, value):
        self.came, value = tie((self.came, value))
        return value

    def merge(self):
        merged = []
        for number, order in enumerate(self.orders):
            total = self.kept[number].astype(wide_type) + self.came[number].astype(wide_type)
            order.pop(0)
            merged.append(total.astype(self.current[number].dtype) if order else total)
        self.current = merged

    def step(self):
        self.begin()
        self.send()
        self.merge()

    def finish(self):
        while self.orders[0]:
            self.step()
        return self.current


def merge_kernel(facts, *refs, plans):
    count = len(plans)
    outs = list(refs[2 * count :])
    for plan, kept, came in zip(plans, refs[:count], refs[count : 2 * count]):
        entries, after, turn = plan["entries"], plan["after"], plan["turn"]

        def total(entry, kept=kept, came=came, after=after):
            own = kept[entry] if after is None else kept[entry >> after, 0, entry & ((1 << after) - 1)]
            return own.astype(wide_type) + came[entry].astype(wide_type)

        if turn is None:
            outs.pop(0)[...] = total(0)
            continue
        sent_out, kept_out = outs.pop(0), outs.pop(0)
        bit, behind = turn
        mine = (facts[0] >> bit) & 1
        for place in range(entries // 2):
            base = (place >> behind << (behind + 1)) | (place & ((1 << behind) - 1))
            kept_out[place] = total(base + (mine << behind)).astype(low_type)
            sent_out[place] = total(base + ((1 - mine) << behind)).astype(low_type)


class Part:
    def __init__(self, array, order):
        self.kept, self.order = array, order
        self.sent = self.came = self.total = None
        self.step = 0
        self.left = tuple(range(len(order) - 1, -1, -1))

    def copied(self):
        other = object.__new__(Part)
        other.__dict__.update(self.__dict__)
        return other


class Sums:
    def __init__(self, parts, chip_index):
        self.parts, self.chip_index = parts, chip_index

    @staticmethod
    def of(arrays, orders, chip_index):
        return Sums([Part(array, order) for array, order in zip(arrays, orders)], chip_index)

    def copied(self):
        return Sums([part.copied() for part in self.parts], self.chip_index)

    def joined(self, *others):
        return Sums([part for sums in (self, *others) for part in sums.parts], self.chip_index)

    def state(self):
        return [(part.kept, part.came) for part in self.parts]

    def stepped(self):
        other = self.copied()
        for part in other.parts:
            part.left = tuple(bit for bit in part.left if bit != part.order[part.step])
            part.step += 1
        return other

    def with_state(self, state):
        other = self.copied()
        for part, (kept, came) in zip(other.parts, state):
            part.kept, part.came = kept, came
        return other

    @property
    def going(self):
        return [part for part in self.parts if part.total is None]

    @property
    def totals(self):
        return [part.total for part in self.parts]

    def start(self, value):
        for part in self.parts:
            chips = part.kept.shape[0]
            behind = part.order[0]
            ahead = len(part.order) - 1 - behind
            view = part.kept.reshape((1 << ahead, 2, 1 << behind) + part.kept.shape[1:])
            mine = (self.chip_index >> behind) & 1
            sent = lax.dynamic_index_in_dim(view, 1 - mine, 1, False)
            part.sent = sent.reshape((chips // 2,) + part.kept.shape[1:])
            part.kept = view
        return self.leave(self.parts, value)

    def leave(self, parts, value):
        sent, value = tie(([part.sent for part in parts], value))
        for part, leaving in zip(parts, sent):
            chips = 1 << len(part.order)
            bit = part.order[part.step]
            part.came = lax.ppermute(leaving, "dp", [(chip, chip ^ (1 << bit)) for chip in range(chips)])
        return value

    def round(self, value):
        parts = self.going
        came, value = tie(([part.came for part in parts], value))
        plans, in_specs, out_specs, out_shape = [], [], [], []
        for part, arrived in zip(parts, came):
            part.came = arrived
            entries, rows, columns = arrived.shape
            kept, bit = part.kept, part.order[part.step]
            if part.step == 0:
                in_specs.append(
                    pl.BlockSpec(
                        (kept.shape[0], 1) + kept.shape[2:],
                        lambda j, facts, bit=bit: (0, (facts[0] >> bit) & 1, 0, 0, 0),
                    )
                )
            else:
                in_specs.append(whole(kept.shape))
            plan = {"entries": entries, "after": bit if part.step == 0 else None, "turn": None}
            part.left = tuple(other for other in part.left if other != bit)
            if part.left:
                following = part.order[part.step + 1]
                plan["turn"] = (following, len(part.left) - 1 - part.left.index(following))
                half = (entries // 2, rows, columns)
                out_specs += [whole(half)] * 2
                out_shape += [jax.ShapeDtypeStruct(half, low_type)] * 2
            else:
                out_specs.append(whole((rows, columns)))
                out_shape.append(jax.ShapeDtypeStruct((rows, columns), wide_type))
            plans.append(plan)
        in_specs += [whole(part.came.shape) for part in parts]
        made = pl.pallas_call(
            partial(merge_kernel, plans=plans),
            grid_spec=pltpu.PrefetchScalarGridSpec(
                num_scalar_prefetch=1, grid=(1,), in_specs=in_specs, out_specs=out_specs
            ),
            out_shape=out_shape,
            compiler_params=pltpu.CompilerParams(vmem_limit_bytes=room(1 << len(parts[0].order))),
            cost_estimate=heavy,
            name="merge_sums",
        )(
            self.chip_index[None].astype(jnp.int32),
            *[part.kept for part in parts],
            *[part.came for part in parts],
        )
        made = list(made)
        for part in parts:
            part.step += 1
            if part.left:
                part.sent, part.kept = made.pop(0), made.pop(0)
            else:
                part.total = made.pop(0)
        parts = [part for part in parts if part.left]
        return self.leave(parts, value) if parts else value


def nothing_like(work):
    def nothing():
        return jax.tree.map(lambda leaf: jnp.zeros(leaf.shape, leaf.dtype), jax.eval_shape(work))

    return nothing


def gather_kernel(owner, rows, out, held, came, gone, *, docs):
    loads = [pltpu.make_async_copy(rows.at[owner[slot]], held.at[slot], came.at[slot]) for slot in range(docs)]
    stores = [pltpu.make_async_copy(held.at[slot], out.at[slot], gone.at[slot]) for slot in range(docs)]
    for load in loads:
        load.start()
    for load, store in zip(loads, stores):
        load.wait()
        store.start()
    for store in stores:
        store.wait()


def gather_docs(memory_in, doc_owner):
    docs = memory_in.shape[0]
    return pl.pallas_call(
        partial(gather_kernel, docs=docs),
        grid_spec=pltpu.PrefetchScalarGridSpec(
            num_scalar_prefetch=1,
            grid=(),
            in_specs=[pl.BlockSpec(memory_space=pl.ANY)],
            out_specs=pl.BlockSpec(memory_space=pl.ANY),
            scratch_shapes=[
                pltpu.VMEM(memory_in.shape, low_type),
                pltpu.SemaphoreType.DMA((docs,)),
                pltpu.SemaphoreType.DMA((docs,)),
            ],
        ),
        out_shape=pltpu.HBM(memory_in.shape, low_type),
        compiler_params=pltpu.CompilerParams(vmem_limit_bytes=vmem_large),
        cost_estimate=heavy,
        name="gather_docs",
    )(doc_owner, memory_in)


def prepare_kernel(cross_kv, pair):
    width = cross_kv.shape[0]
    for side in range(2):
        pair[:, side * width : side * width + width] = cross_kv[:, side, :]


def prepare_weights(cross_kv):
    width = cross_kv.shape[0]
    return pl.pallas_call(
        prepare_kernel,
        out_shape=jax.ShapeDtypeStruct((width, 2 * width), low_type),
        compiler_params=pltpu.CompilerParams(vmem_limit_bytes=vmem_budget),
        cost_estimate=heavy,
        name="prepare_weights",
    )(cross_kv)


def moved_kernel(owner, facts, features, groups, out, stats, *, chips, count):
    step = pl.program_id(0)
    sub, width = features.shape[1:]

    @pl.when(step == 0)
    def _():
        own_group = (
            lax.broadcasted_iota(jnp.int32, (128, width), 1) // (width // GROUPS)
            == lax.broadcasted_iota(jnp.int32, (128, width), 0)
        ).astype(wide_type)
        stats[...] = jnp.dot(
            groups[0:chips].reshape(chips * 8, 128), own_group, precision=lax.Precision.HIGHEST
        ).reshape(chips, 8, width)

    position = (lax.broadcasted_iota(jnp.int32, (sub, 1), 0) * 2 + facts[1]) * chips + facts[0]

    def one(place, carry):
        slot = step * count + place
        document = owner[slot]
        normed = (features[document].astype(wide_type) - stats[slot, 0:1, :]) * stats[slot, 1:2, :]
        moved = stats[slot, 1:2, :] * (stats[slot, 2:3, :] + normed * stats[slot, 3:4, :])
        out[place] = jnp.where(position < facts[2 + document], moved, 0.0).astype(low_type)
        return carry

    lax.fori_loop(0, count, one, 0)


def moved_rows(doc_owner, facts, features, groups):
    docs, sub, width = features.shape
    count = max(docs // 4, 1)
    return pl.pallas_call(
        partial(moved_kernel, chips=docs, count=count),
        grid_spec=pltpu.PrefetchScalarGridSpec(
            num_scalar_prefetch=2,
            grid=(docs // count,),
            in_specs=[
                pl.BlockSpec(features.shape, lambda j, owner, facts: (0, 0, 0)),
                pl.BlockSpec(groups.shape, lambda j, owner, facts: (0, 0, 0)),
            ],
            out_specs=pl.BlockSpec((count, sub, width), lambda j, owner, facts: (j, 0, 0)),
            scratch_shapes=[pltpu.VMEM((docs, 8, width), wide_type)],
        ),
        out_shape=jax.ShapeDtypeStruct(features.shape, low_type),
        compiler_params=pltpu.CompilerParams(vmem_limit_bytes=room(docs)),
        cost_estimate=heavy,
        name="moved_rows",
    )(doc_owner, facts, features, groups)


def spread_kernel(owner, *refs, docs, pieces):
    rows = refs[:pieces]
    moved, out, held, taken, wide, came, also, gone = refs[pieces:]
    each = rows[0].shape[1]
    loads = [
        [
            pltpu.make_async_copy(
                piece.at[slot], held.at[slot, pl.ds(number * each, each)], came.at[slot * pieces + number]
            )
            for number, piece in enumerate(rows)
        ]
        for slot in range(docs)
    ]
    takes = [pltpu.make_async_copy(moved.at[slot], taken.at[slot], also.at[slot]) for slot in range(docs)]
    stores = [pltpu.make_async_copy(wide.at[slot], out.at[owner[slot]], gone.at[slot]) for slot in range(docs)]
    for slot in range(docs):
        for load in loads[slot]:
            load.start()
        takes[slot].start()
    for slot in range(docs):
        for load in loads[slot]:
            load.wait()
        takes[slot].wait()
        wide[slot] = held[slot].astype(wide_type) - taken[slot].astype(wide_type)
        stores[slot].start()
    for store in stores:
        store.wait()


def spread_docs(rows, moved, doc_owner):
    docs = moved.shape[0]
    pieces = len(rows)
    return pl.pallas_call(
        partial(spread_kernel, docs=docs, pieces=pieces),
        grid_spec=pltpu.PrefetchScalarGridSpec(
            num_scalar_prefetch=1,
            grid=(),
            in_specs=[pl.BlockSpec(memory_space=pl.ANY)] * (pieces + 1),
            out_specs=pl.BlockSpec(memory_space=pl.ANY),
            scratch_shapes=[
                pltpu.VMEM(moved.shape, low_type),
                pltpu.VMEM(moved.shape, low_type),
                pltpu.VMEM(moved.shape, wide_type),
                pltpu.SemaphoreType.DMA((docs * pieces,)),
                pltpu.SemaphoreType.DMA((docs,)),
                pltpu.SemaphoreType.DMA((docs,)),
            ],
        ),
        out_shape=jax.ShapeDtypeStruct(moved.shape, wide_type),
        compiler_params=pltpu.CompilerParams(vmem_limit_bytes=vmem_large),
        cost_estimate=heavy,
        name="spread_docs",
    )(doc_owner, *rows, moved)


def chunk_of(chips, sub):
    return min(sub, max(16, 512 // chips))


def live_rows(facts, start, chips, span):
    row = lax.broadcasted_iota(jnp.int32, (chips * span, 1), 0)
    chip, step = row // span, row % span
    return ((start + step) * 2 + facts[1]) * chips + chip < facts[0]


def in_branches(facts, start, chips, span, work, dead=None):
    first = (start * 2 + facts[1]) * chips
    last = ((start + span - 1) * 2 + facts[1]) * chips + chips - 1
    full = last < facts[0]
    none = first >= facts[0]

    @pl.when(full)
    def _():
        work(None)

    @pl.when(jnp.logical_not(full) & jnp.logical_not(none))
    def _():
        work(live_rows(facts, start, chips, span))

    if dead is not None:
        pl.when(none)(dead)


def whole(shape):
    return pl.BlockSpec(shape, lambda j, facts: (0,) * len(shape))


def slab(shape, span, first=0):
    return pl.BlockSpec((shape[0], span, shape[2]), lambda j, facts: (0, j + first, 0))


def memory_forward_kernel(facts, rows, stats, weight, out, *, chips, span):
    width = rows.shape[-1]
    wide = rows[...].reshape(chips * span, width).astype(wide_type)
    drive = (wide - stats[0:1, :]) * stats[1:2, :] * stats[2:3, :] + stats[3:4, :]
    hidden = (drive * (0.5 + 0.5 * jnp.tanh(0.5 * drive))).astype(low_type)
    made = wide + dot_wide(hidden, weight[...])
    out[...] = made.astype(low_type).reshape(chips, span, width)


def memory_forward(facts, rows, stats, weight):
    chips, sub, width = rows.shape
    span = chunk_of(chips, sub)
    return pl.pallas_call(
        partial(memory_forward_kernel, chips=chips, span=span),
        grid_spec=pltpu.PrefetchScalarGridSpec(
            num_scalar_prefetch=1,
            grid=(sub // span,),
            in_specs=[slab(rows.shape, span), whole(stats.shape), whole(weight.shape)],
            out_specs=slab(rows.shape, span),
        ),
        out_shape=pltpu.HBM(rows.shape, low_type),
        compiler_params=pltpu.CompilerParams(vmem_limit_bytes=room(chips)),
        cost_estimate=heavy,
        name="memory_forward",
    )(facts, rows, stats, weight)


def memory_backward_kernel(
    facts, rows, own, came, stats, weight, sums_in, grad_out, hidden_out, base_out, sums, groups, *, chips, span, steps
):
    step = pl.program_id(0)
    width = rows.shape[-1]
    count = chips * span

    @pl.when(step == 0)
    def _():
        sums[...] = sums_in[...]

    wide = rows[...].reshape(count, width).astype(wide_type)
    normed = (wide - stats[0:1, :]) * stats[1:2, :]
    drive = normed * stats[2:3, :] + stats[3:4, :]
    gate = 0.5 + 0.5 * jnp.tanh(0.5 * drive)
    hidden_out[...] = (drive * gate).astype(low_type).reshape(chips, span, width)
    grad = (own[...].reshape(count, width) + came[...].reshape(count, width).astype(wide_type)).astype(low_type)
    grad_out[...] = grad.reshape(chips, span, width)
    grad_act = dot_columns(grad, weight[...]) * (gate * (1.0 + drive * (1.0 - gate)))
    sums[0:1, :] += jnp.sum(grad_act, axis=0, keepdims=True)
    sums[1:2, :] += jnp.sum(grad_act * normed, axis=0, keepdims=True)
    base = grad.astype(wide_type) + grad_act * (stats[1:2, :] * stats[2:3, :])
    base_out[...] = base.astype(low_type).reshape(chips, span, width)

    @pl.when(step == steps - 1)
    def _():
        per_group = width // GROUPS
        group_of = (
            lax.broadcasted_iota(jnp.int32, (width, 128), 0) // per_group
            == lax.broadcasted_iota(jnp.int32, (width, 128), 1)
        ).astype(wide_type)
        entries = (facts[0] * per_group).astype(wide_type)
        rows_of = jnp.concatenate(
            (
                stats[0:2, :] * (0.5 / per_group),
                sums[0:2, :] * stats[2:3, :] / entries,
                jnp.zeros((4, width), wide_type),
            )
        )
        groups[...] = jnp.dot(rows_of, group_of, precision=lax.Precision.HIGHEST)


def memory_backward(facts, rows, own, came, stats, weight, sums_in, first):
    chips, sub, width = own.shape
    span = chunk_of(chips, rows.shape[1])
    block = slab(own.shape, span)
    return pl.pallas_call(
        partial(memory_backward_kernel, chips=chips, span=span, steps=sub // span),
        grid_spec=pltpu.PrefetchScalarGridSpec(
            num_scalar_prefetch=1,
            grid=(sub // span,),
            in_specs=[
                slab(rows.shape, span, first),
                block,
                block,
                whole(stats.shape),
                whole(weight.shape),
                whole(sums_in.shape),
            ],
            out_specs=[block, block, block, whole(stats.shape), whole((8, 128))],
        ),
        out_shape=[
            jax.ShapeDtypeStruct(own.shape, low_type),
            jax.ShapeDtypeStruct(own.shape, low_type),
            pltpu.HBM(own.shape, low_type),
            jax.ShapeDtypeStruct(stats.shape, wide_type),
            jax.ShapeDtypeStruct((8, 128), wide_type),
        ],
        compiler_params=pltpu.CompilerParams(vmem_limit_bytes=room(chips)),
        cost_estimate=heavy,
        name="memory_backward",
    )(facts, rows, own, came, stats, weight, sums_in)


def cross_forward_kernel(
    facts, query_t, rows, key_weight, value_weight, top_in, total_in, sum_in, pairs, top, total, gathered,
    total_here, sum_here, held, *, chips, span
):
    step = pl.program_id(0)
    half = key_weight.shape[1]
    width = rows.shape[-1]

    @pl.when(step == 0)
    def _():
        top[...] = top_in[...]
        total[...] = total_in[...]
        gathered[...] = sum_in[...]

    def work(live):
        block = rows[...].reshape(chips * span, width)
        keys = dot_wide(block, key_weight[...]).astype(low_type)
        values = dot_wide(block, value_weight[...]).astype(low_type)
        pairs[:, :, :half] = keys.reshape(chips, span, half)
        pairs[:, :, half:] = values.reshape(chips, span, half)
        heads = half // HD

        def score(head):
            made = dot_wide(keys[:, head // 2 * 128 : head // 2 * 128 + 128], query_t[head])
            return made if live is None else jnp.where(live, made, masked_fill)

        def part_of(head, weights):
            part = dot_rows(values[:, head // 2 * 128 : head // 2 * 128 + 128], weights.astype(low_type))
            return part[head % 2 * HD : head % 2 * HD + HD, :]

        def plain():
            following = score(0)
            for head in range(heads):
                scores = following
                if head + 1 < heads:
                    following = score(head + 1)
                weights = jnp.exp(scores - top[head : head + 1, :])
                total_here[head : head + 1, :] = jnp.sum(weights, axis=0, keepdims=True)
                sum_here[head * HD : head * HD + HD, :] = part_of(head, weights)

        def shifted():
            following = score(0)
            for head in range(heads):
                scores = following
                if head + 1 < heads:
                    following = score(head + 1)
                old_top = top[head : head + 1, :]
                new_top = jnp.maximum(old_top, jnp.max(scores, axis=0, keepdims=True))
                weights = jnp.exp(scores - new_top)
                shrink = jnp.exp(old_top - new_top)
                total[head : head + 1, :] = total[head : head + 1, :] * shrink + jnp.sum(
                    weights, axis=0, keepdims=True
                )
                rows_of = slice(head * HD, head * HD + HD)
                gathered[rows_of, :] = gathered[rows_of, :] * shrink + part_of(head, weights)
                top[head : head + 1, :] = new_top

        fresh = (facts[3] == 1) & (step == 0)
        held[0] = jnp.where(fresh, 1, 0)

        @pl.when(jnp.logical_not(fresh))
        def _():
            plain()
            small = jnp.max(total_here[0:heads, :]) < largest_sum
            held[0] = jnp.where(small, 0, 1)

            @pl.when(small)
            def _():
                total[0:heads, :] += total_here[0:heads, :]
                gathered[...] += sum_here[...]

        pl.when(held[0] == 1)(shifted)

    def dead():
        pairs[...] = jnp.zeros_like(pairs)

    in_branches(facts, step * span, chips, span, work, dead)


def cross_forward(facts, query_t, rows, weight, carry):
    chips, sub, width = rows.shape
    heads, _, queries = query_t.shape
    half = heads * HD
    span = chunk_of(chips, sub)
    stat = (8, queries)
    summed = (half, queries)
    return pl.pallas_call(
        partial(cross_forward_kernel, chips=chips, span=span),
        grid_spec=pltpu.PrefetchScalarGridSpec(
            num_scalar_prefetch=1,
            grid=(sub // span,),
            in_specs=[
                whole(query_t.shape),
                slab(rows.shape, span),
                pl.BlockSpec((width, half), lambda j, facts: (0, facts[2])),
                pl.BlockSpec((width, half), lambda j, facts: (0, 2 + facts[2])),
                whole(stat),
                whole(stat),
                whole(summed),
            ],
            out_specs=[slab((chips, sub, 2 * half), span), whole(stat), whole(stat), whole(summed)],
            scratch_shapes=[
                pltpu.VMEM(stat, wide_type),
                pltpu.VMEM(summed, wide_type),
                pltpu.SMEM((1,), jnp.int32),
            ],
        ),
        out_shape=[
            jax.ShapeDtypeStruct((chips, sub, 2 * half), low_type),
            jax.ShapeDtypeStruct(stat, wide_type),
            jax.ShapeDtypeStruct(stat, wide_type),
            jax.ShapeDtypeStruct(summed, wide_type),
        ],
        compiler_params=pltpu.CompilerParams(vmem_limit_bytes=room(chips)),
        cost_estimate=heavy,
        name="cross_forward",
    )(facts, query_t, rows, weight, weight, *carry)


def cross_close_kernel(gathered, top, total, weight, crossed, crossed_t, log_total, part, *, heads):
    log_total[...] = top[...] + jnp.log(jnp.maximum(total[...], 1e-30))
    for head in range(heads):
        rows = slice(head * HD, head * HD + HD)
        crossed_t[rows, :] = gathered[rows, :] / total[head : head + 1, :]
    low = crossed_t[...].T.astype(low_type)
    crossed[...] = low
    part[...] = dot_wide(low, weight[...])


def cross_close(gathered, top, total, weight):
    half, queries = gathered.shape
    return pl.pallas_call(
        partial(cross_close_kernel, heads=half // HD),
        out_shape=[
            jax.ShapeDtypeStruct((queries, half), low_type),
            jax.ShapeDtypeStruct((half, queries), wide_type),
            jax.ShapeDtypeStruct(top.shape, wide_type),
            jax.ShapeDtypeStruct((queries, weight.shape[1]), wide_type),
        ],
        compiler_params=pltpu.CompilerParams(vmem_limit_bytes=vmem_budget),
        cost_estimate=heavy,
        name="cross_close",
    )(gathered, top, total, weight)


gelu_scale = 0.7978845608028654
gelu_cubic = 0.044715


def feed_forward_kernel(
    first, own, came, gain, weight, grad_active, second, normed, both_grad, both_active, grad_normed
):
    step = pl.program_id(0)

    @pl.when(step == 0)
    def _():
        total = first[...] + (own[...] + came[...])
        second[...] = total
        factor = lax.rsqrt(jnp.mean(total * total, axis=-1, keepdims=True) + norm_eps)
        normed[...] = (total * factor * gain[...]).astype(low_type)
        grad_normed[...] = jnp.zeros_like(grad_normed)

    lifted = dot_wide(normed[...], weight[...])
    square = lifted * lifted
    bent = jnp.tanh(gelu_scale * (lifted * (1.0 + gelu_cubic * square)))
    half_up = 0.5 * (1.0 + bent)
    both_active[...] = (lifted * half_up).astype(low_type)
    slope = half_up + (0.5 * gelu_scale) * lifted * (1.0 - bent * bent) * (1.0 + 3.0 * gelu_cubic * square)
    grad_lifted = (grad_active[...].astype(wide_type) * slope).astype(low_type)
    both_grad[...] = grad_lifted
    grad_normed[...] += dot_columns(grad_lifted, weight[...])


def feed_forward(first, own, came, gain, weight, grad_active):
    rows, width = first.shape
    hidden = weight.shape[1]
    block = 512
    still = pl.BlockSpec((rows, width), lambda j: (0, 0))
    moving = pl.BlockSpec((rows, block), lambda j: (0, j))
    return pl.pallas_call(
        feed_forward_kernel,
        grid=(hidden // block,),
        in_specs=[
            still,
            still,
            still,
            pl.BlockSpec((1, width), lambda j: (0, 0)),
            pl.BlockSpec((width, block), lambda j: (0, j)),
            moving,
        ],
        out_specs=[still, still, moving, moving, still],
        out_shape=[
            jax.ShapeDtypeStruct((rows, width), wide_type),
            jax.ShapeDtypeStruct((rows, width), low_type),
            jax.ShapeDtypeStruct((rows, hidden), low_type),
            jax.ShapeDtypeStruct((rows, hidden), low_type),
            jax.ShapeDtypeStruct((rows, width), wide_type),
        ],
        compiler_params=pltpu.CompilerParams(vmem_limit_bytes=vmem_budget),
        cost_estimate=heavy,
        name="feed_forward",
    )(first, own, came, gain, weight, grad_active)


def feed_close_kernel(
    second, own, came, gain, grad_out, weight, crossed_t, grad_second, gain_grad, grad_cross, heads_out,
    heads_out_t, inner, *, heads,
):
    values = second[...]
    incoming = (own[...] + came[...]).astype(low_type).astype(wide_type)
    factor = lax.rsqrt(jnp.mean(values * values, axis=-1, keepdims=True) + norm_eps)
    scaled = incoming * gain[...]
    inward = factor * scaled - values * (factor * factor * factor) * jnp.mean(
        scaled * values, axis=-1, keepdims=True
    )
    gain_grad[...] = jnp.broadcast_to(
        jnp.sum(incoming * values * factor, axis=0, keepdims=True), gain_grad.shape
    )
    total = inward + grad_out[...].astype(wide_type)
    grad_second[...] = total
    low = total.astype(low_type)
    grad_cross[...] = low
    made = dot_columns(low, weight[...])
    made_low = made.astype(low_type)
    made_t = made_low.astype(wide_type).T
    low_t = made_t.astype(low_type)
    left = lax.broadcasted_iota(jnp.int32, (made.shape[0], 128), 1) < HD
    inner[...] = jnp.zeros_like(inner)
    for head in range(heads):
        pair = made_low[:, head // 2 * 128 : head // 2 * 128 + 128]
        keep = left if head % 2 == 0 else jnp.logical_not(left)
        heads_out[head] = jnp.where(keep, pair, jnp.zeros_like(pair))
        rows = slice(head * HD, head * HD + HD)
        own_rows = slice(head % 2 * HD, head % 2 * HD + HD)
        other_rows = slice((1 - head % 2) * HD, (1 - head % 2) * HD + HD)
        heads_out_t[head, own_rows, :] = low_t[rows, :]
        heads_out_t[head, other_rows, :] = jnp.zeros_like(low_t[rows, :])
        inner[head : head + 1, :] = jnp.sum(made_t[rows, :] * crossed_t[rows, :], axis=0, keepdims=True)


def feed_close(second, own, came, gain, grad_out, weight, crossed_t):
    rows, width = second.shape
    half = weight.shape[0]
    heads = half // HD
    return pl.pallas_call(
        partial(feed_close_kernel, heads=heads),
        out_shape=[
            jax.ShapeDtypeStruct((rows, width), wide_type),
            jax.ShapeDtypeStruct((8, width), wide_type),
            jax.ShapeDtypeStruct((rows, width), low_type),
            jax.ShapeDtypeStruct((heads, rows, 128), low_type),
            jax.ShapeDtypeStruct((heads, 128, rows), low_type),
            jax.ShapeDtypeStruct((8, rows), wide_type),
        ],
        compiler_params=pltpu.CompilerParams(vmem_limit_bytes=vmem_budget),
        cost_estimate=heavy,
        name="feed_close",
    )(second, own, came, gain, grad_out, weight, crossed_t)


def feed_weights_kernel(normed, grad_out, grad_cross, grad_lifted, active, crossed, left, middle, right):
    third = left.shape[1]
    rest = grad_lifted.shape[1] - third
    left[...] = dot_rows(normed[...], grad_lifted[:, :third]).astype(low_type)
    middle[:, :rest] = dot_rows(normed[...], grad_lifted[:, third:]).astype(low_type)
    middle[:, rest:] = dot_rows(grad_out[...], active[:, : third - rest]).astype(low_type)
    right[:, : 2 * rest] = dot_rows(grad_out[...], active[:, third - rest :]).astype(low_type)
    right[:, 2 * rest :] = dot_rows(grad_cross[...], crossed[...]).astype(low_type)


def feed_weights(*args):
    width = args[0].shape[1]
    third = (2 * args[3].shape[1] + args[5].shape[1]) // 3
    return pl.pallas_call(
        feed_weights_kernel,
        out_shape=[jax.ShapeDtypeStruct((width, third), low_type)] * 3,
        compiler_params=pltpu.CompilerParams(vmem_limit_bytes=vmem_budget),
        cost_estimate=heavy,
        name="feed_weights",
    )(*args)


def cross_backward_kernel(
    facts, query, query_t, grad, grad_t, log_total, inner, pairs, key_weight, value_weight, pair_grads,
    row_grads, query_grad, held, *, chips, span, first
):
    step = pl.program_id(0)
    width, half = key_weight.shape

    @pl.when(step == 0)
    def _():
        query_grad[...] = jnp.zeros_like(query_grad)

    def work(live):
        block = pairs[...].reshape(chips * span, 2 * half)
        heads = half // HD

        def lanes(head, shift=0):
            return block[:, shift + head // 2 * 128 : shift + head // 2 * 128 + 128]

        def products(head):
            scores = dot_wide(lanes(head), query_t[head])
            if live is not None:
                scores = jnp.where(live, scores, masked_fill)
            return scores, dot_wide(lanes(head, half), grad_t[head])

        following = products(0)
        for pair in range(heads // 2):
            lows, low_grads = [], []
            for side in range(2):
                head = pair * 2 + side
                scores, grad_probs = following
                if head + 1 < heads:
                    following = products(head + 1)
                probs = jnp.exp(scores - log_total[head : head + 1, :])
                low_grads.append((probs * (grad_probs - inner[head : head + 1, :])).astype(low_type))
                lows.append(probs.astype(low_type))
                part = dot_rows(lanes(head), low_grads[-1])
                query_grad[head * HD : head * HD + HD, :] += part[side * HD : side * HD + HD, :]
            at = pair * 128
            both = slice(pair * 2, pair * 2 + 2)
            queries = query.shape[1]
            held[:, at : at + 128] = dot_wide(
                jnp.concatenate(low_grads, axis=1), query[both].reshape(2 * queries, 128)
            ).astype(low_type)
            held[:, half + at : half + at + 128] = dot_wide(
                jnp.concatenate(lows, axis=1), grad[both].reshape(2 * queries, 128)
            ).astype(low_type)
        made = held[...]
        pair_grads[...] = made.reshape(chips, span, 2 * half)
        back = dot_columns(made[:, :half], key_weight[...]) + dot_columns(made[:, half:], value_weight[...])
        row_grads[...] = back.astype(row_grads.dtype).reshape(chips, span, width)

    def dead():
        pair_grads[...] = jnp.zeros_like(pair_grads)
        row_grads[...] = jnp.zeros_like(row_grads)

    in_branches(facts, (step + first) * span, chips, span, work, dead)


def cross_backward(facts, query, query_t, grad, grad_t, log_total, inner, pairs, weight, grad_type, first, steps):
    chips, sub, both = pairs.shape
    width = weight.shape[0]
    heads, _, queries = query_t.shape
    span = chunk_of(chips, sub)
    half = both // 2
    rows = steps * span
    pair_block = slab((chips, rows, both), span)
    row_block = slab((chips, rows, width), span)
    return pl.pallas_call(
        partial(cross_backward_kernel, chips=chips, span=span, first=first),
        grid_spec=pltpu.PrefetchScalarGridSpec(
            num_scalar_prefetch=1,
            grid=(steps,),
            in_specs=[
                whole(query.shape),
                whole(query_t.shape),
                whole(grad.shape),
                whole(grad_t.shape),
                whole(log_total.shape),
                whole(inner.shape),
                slab(pairs.shape, span, first),
                pl.BlockSpec((width, half), lambda j, facts: (0, facts[2])),
                pl.BlockSpec((width, half), lambda j, facts: (0, 2 + facts[2])),
            ],
            out_specs=[pair_block, row_block, whole((heads * HD, queries))],
            scratch_shapes=[pltpu.VMEM((chips * span, both), low_type)],
        ),
        out_shape=[
            jax.ShapeDtypeStruct((chips, rows, both), low_type),
            jax.ShapeDtypeStruct((chips, rows, width), grad_type),
            jax.ShapeDtypeStruct((heads * HD, queries), wide_type),
        ],
        compiler_params=pltpu.CompilerParams(vmem_limit_bytes=room(chips)),
        cost_estimate=heavy,
        name="cross_backward",
    )(facts, query, query_t, grad, grad_t, log_total, inner, pairs, weight, weight)


def query_back_kernel(*refs):
    *parts, weight, grad, part = refs
    total = parts[0][...]
    for other in parts[1:]:
        total = total + other[...]
    low = (total * 0.125).T.astype(low_type)
    grad[...] = low
    part[...] = dot_columns(low, weight[...])


def query_back(parts, weight):
    half, rows = parts[0].shape
    return pl.pallas_call(
        query_back_kernel,
        out_shape=[
            jax.ShapeDtypeStruct((rows, half), low_type),
            jax.ShapeDtypeStruct((rows, weight.shape[0]), wide_type),
        ],
        compiler_params=pltpu.CompilerParams(vmem_limit_bytes=vmem_budget),
        cost_estimate=heavy,
        name="query_back",
    )(*parts, weight)


def memory_weights_kernel(facts, *refs, pieces, chips, span, steps):
    rows, other = refs[:2]
    sets = [refs[2 + 4 * piece : 6 + 4 * piece] for piece in range(pieces)]
    pair_out, keep_out, send_out, pair_sum, conv_sum = refs[2 + 4 * pieces :]
    step = pl.program_id(0)
    count = chips * span
    each = steps // pieces

    def flat(ref):
        return ref[...].reshape(count, ref.shape[-1])

    @pl.when(step == 0)
    def _():
        pair_sum[...] = jnp.zeros_like(pair_sum)
        conv_sum[...] = jnp.zeros_like(conv_sum)

    for piece, (hidden, pair_grads, row_grads, other_grads) in enumerate(sets):

        @pl.when((step >= piece * each) & (step < piece * each + each))
        def _(hidden=hidden, pair_grads=pair_grads, row_grads=row_grads, other_grads=other_grads):
            pair_sum[...] += dot_rows(flat(rows), flat(pair_grads)) + dot_rows(flat(other), flat(other_grads))
            conv_sum[...] += dot_rows(flat(hidden), flat(row_grads))

    @pl.when(step == steps - 1)
    def _():
        pair_out[...] = pair_sum[...].astype(low_type)
        half = keep_out.shape[1]
        first = facts[1] == 0
        keep_out[...] = jnp.where(first, conv_sum[:, :half], conv_sum[:, half:])
        send_out[...] = jnp.where(first, conv_sum[:, half:], conv_sum[:, :half]).astype(low_type)


def memory_weights(facts, rows, other, sets):
    chips, sub, width = rows.shape
    span = chunk_of(chips, sub)
    both = sets[0][1].shape[2]
    steps = sub // span
    pieces = len(sets)
    each = steps // pieces

    def piece_block(piece, columns):
        return pl.BlockSpec(
            (chips, span, columns), lambda j, facts: (0, jnp.clip(j - piece * each, 0, each - 1), 0)
        )

    in_specs = [slab(rows.shape, span), slab(other.shape, span)]
    for piece, arrays in enumerate(sets):
        in_specs += [piece_block(piece, array.shape[2]) for array in arrays]
    outs = (((width, both), low_type), ((width, width // 2), wide_type), ((width, width // 2), low_type))
    return pl.pallas_call(
        partial(memory_weights_kernel, pieces=pieces, chips=chips, span=span, steps=steps),
        grid_spec=pltpu.PrefetchScalarGridSpec(
            num_scalar_prefetch=1,
            grid=(steps,),
            in_specs=in_specs,
            out_specs=[whole(shape) for shape, _ in outs],
            scratch_shapes=[pltpu.VMEM((width, both), wide_type), pltpu.VMEM((width, width), wide_type)],
        ),
        out_shape=[jax.ShapeDtypeStruct(shape, kind) for shape, kind in outs],
        compiler_params=pltpu.CompilerParams(vmem_limit_bytes=room(chips)),
        cost_estimate=heavy,
        name="memory_weights",
    )(facts, rows, other, *[array for arrays in sets for array in arrays])


def side_weights_kernel(normed_one, grad_qkv, normed_two, grad_cq, grad_self, attended, first, second):
    half = attended.shape[1]
    cut = first.shape[1]
    first[...] = dot_rows(normed_one[...], grad_qkv[:, :cut]).astype(low_type)
    rest = 3 * half - cut
    second[:, :rest] = dot_rows(normed_one[...], grad_qkv[:, cut:]).astype(low_type)
    second[:, rest : rest + half] = dot_rows(normed_two[...], grad_cq[...]).astype(low_type)
    second[:, rest + half :] = dot_rows(grad_self[...], attended[...]).astype(low_type)


def side_weights(*args):
    width = args[0].shape[1]
    half = args[-1].shape[1]
    cut = 3 * half - 128
    return pl.pallas_call(
        side_weights_kernel,
        out_shape=[
            jax.ShapeDtypeStruct((width, cut), low_type),
            jax.ShapeDtypeStruct((width, 5 * half - cut), low_type),
        ],
        compiler_params=pltpu.CompilerParams(vmem_limit_bytes=vmem_budget),
        cost_estimate=heavy,
        name="side_weights",
    )(*args)


def product_kernel(left, right, out):
    @pl.when(pl.program_id(0) == 0)
    def _():
        out[...] = jnp.zeros_like(out)

    out[...] += dot_wide(left[...], right[...])


def product(left, right):
    rows, depth = left.shape
    width = right.shape[1]
    block = 512
    return pl.pallas_call(
        product_kernel,
        grid=(depth // block,),
        in_specs=[
            pl.BlockSpec((rows, block), lambda j: (0, j)),
            pl.BlockSpec((block, width), lambda j: (j, 0)),
        ],
        out_specs=pl.BlockSpec((rows, width), lambda j: (0, 0)),
        out_shape=jax.ShapeDtypeStruct((rows, width), wide_type),
        compiler_params=pltpu.CompilerParams(vmem_limit_bytes=vmem_budget),
        cost_estimate=heavy,
        name="product",
    )(left, right)


def back_through_norm(values, incoming, gain):
    factor = lax.rsqrt(jnp.mean(values * values, axis=-1, keepdims=True) + norm_eps)
    scaled = incoming * gain
    inward = factor * scaled - values * (factor * factor * factor) * jnp.mean(
        scaled * values, axis=-1, keepdims=True
    )
    return inward, jnp.sum(incoming * values * factor, axis=0, keepdims=True)


def self_forward_kernel(
    facts, rows_in, gain, weight, out_weight, normed_out, triple, attended, log_total, part, *, heads
):
    values = rows_in[...].astype(wide_type)
    factor = lax.rsqrt(jnp.mean(values * values, axis=-1, keepdims=True) + norm_eps)
    normed = (values * factor * gain[...]).astype(low_type)
    normed_out[...] = normed
    rows = values.shape[0]
    half = heads * HD
    for side in range(3):
        triple[:, side * half : side * half + half] = dot_wide(normed, weight[side]).astype(low_type)
    key_pos = lax.broadcasted_iota(jnp.int32, (rows, rows), 0)
    query_pos = lax.broadcasted_iota(jnp.int32, (rows, rows), 1)
    allowed = (key_pos <= query_pos) & (key_pos < facts[0])
    left = lax.broadcasted_iota(jnp.int32, (rows, 128), 1) < HD
    log_total[...] = jnp.zeros_like(log_total)
    for pair in range(heads // 2):
        lanes = slice(pair * 128, pair * 128 + 128)
        query_pair = triple[:, lanes]
        key_pair = triple[:, half + pair * 128 : half + pair * 128 + 128]
        value_pair = triple[:, 2 * half + pair * 128 : 2 * half + pair * 128 + 128]
        parts = []
        for side in range(2):
            head = pair * 2 + side
            keep = left if side == 0 else jnp.logical_not(left)
            query = jnp.where(keep, query_pair, jnp.zeros_like(query_pair))
            scores = jnp.where(allowed, dot_columns(key_pair, query) * 0.125, masked_fill)
            top = jnp.max(scores, axis=0, keepdims=True)
            weights = jnp.exp(scores - top)
            total = jnp.sum(weights, axis=0, keepdims=True)
            log_total[head : head + 1, :] = top + jnp.log(total)
            made = dot_rows(value_pair, (weights / total).astype(low_type))
            parts.append(made[side * HD : side * HD + HD, :])
        attended[:, lanes] = jnp.concatenate(parts).T.astype(low_type)
    part[...] = dot_wide(attended[...], out_weight[...])


def self_forward(facts, rows_in, gain, weight, out_weight):
    rows, width = rows_in.shape
    half = out_weight.shape[0]
    args = (rows_in, gain, weight, out_weight)
    outs = (
        ((rows, width), low_type),
        ((rows, 3 * half), low_type),
        ((rows, half), low_type),
        ((8, rows), wide_type),
        ((rows, width), wide_type),
    )
    return pl.pallas_call(
        partial(self_forward_kernel, heads=half // HD),
        grid_spec=pltpu.PrefetchScalarGridSpec(
            num_scalar_prefetch=1,
            grid=(1,),
            in_specs=[whole(arg.shape) for arg in args],
            out_specs=[whole(shape) for shape, _ in outs],
        ),
        out_shape=[jax.ShapeDtypeStruct(shape, kind) for shape, kind in outs],
        compiler_params=pltpu.CompilerParams(vmem_limit_bytes=vmem_budget),
        cost_estimate=heavy,
        name="self_forward",
    )(facts, *args)


def query_forward_kernel(rows_in, own, came, gain, weight, first, normed_out, heads_out, heads_out_t, *, heads):
    total = rows_in[...].astype(wide_type) + (own[...] + came[...])
    first[...] = total
    factor = lax.rsqrt(jnp.mean(total * total, axis=-1, keepdims=True) + norm_eps)
    normed = (total * factor * gain[...]).astype(low_type)
    normed_out[...] = normed
    query = (dot_wide(normed, weight[...]).astype(low_type).astype(wide_type) * 0.125).astype(low_type)
    turned = query.T
    left = lax.broadcasted_iota(jnp.int32, (query.shape[0], 128), 1) < HD
    for head in range(heads):
        pair = query[:, head // 2 * 128 : head // 2 * 128 + 128]
        keep = left if head % 2 == 0 else jnp.logical_not(left)
        heads_out[head] = jnp.where(keep, pair, jnp.zeros_like(pair))
        own_rows = slice(head % 2 * HD, head % 2 * HD + HD)
        other_rows = slice((1 - head % 2) * HD, (1 - head % 2) * HD + HD)
        mine = turned[head * HD : head * HD + HD, :]
        heads_out_t[head, own_rows, :] = mine
        heads_out_t[head, other_rows, :] = jnp.zeros_like(mine)


def query_forward(rows_in, own, came, gain, weight):
    rows, width = rows_in.shape
    heads = weight.shape[1] // HD
    outs = (
        ((rows, width), wide_type),
        ((rows, width), low_type),
        ((heads, rows, 128), low_type),
        ((heads, 128, rows), low_type),
    )
    return pl.pallas_call(
        partial(query_forward_kernel, heads=heads),
        out_shape=[jax.ShapeDtypeStruct(shape, kind) for shape, kind in outs],
        compiler_params=pltpu.CompilerParams(vmem_limit_bytes=vmem_budget),
        cost_estimate=heavy,
        name="query_forward",
    )(rows_in, own, came, gain, weight)


def self_backward_kernel(
    facts, values, own, came, gain, grad_second, out_weight, triple, log_total, weight,
    grad_first, grad_low, gain_grad, triple_grad, part, *, heads,
):
    rows = triple.shape[0]
    half = heads * HD
    incoming = (own[...] + came[...]).astype(low_type).astype(wide_type)
    inward, gain_row = back_through_norm(values[...], incoming, gain[...])
    gain_grad[...] = jnp.broadcast_to(gain_row, gain_grad.shape)
    total = inward + grad_second[...]
    grad_first[...] = total
    grad_low[...] = total.astype(low_type)
    grad = dot_columns(grad_low[...], out_weight[...]).astype(low_type)
    key_pos = lax.broadcasted_iota(jnp.int32, (rows, rows), 0)
    query_pos = lax.broadcasted_iota(jnp.int32, (rows, rows), 1)
    allowed = (key_pos <= query_pos) & (key_pos < facts[0])
    left = lax.broadcasted_iota(jnp.int32, (rows, 128), 1) < HD
    for pair in range(heads // 2):
        lanes = slice(pair * 128, pair * 128 + 128)
        query_pair = triple[:, lanes]
        key_pair = triple[:, half + pair * 128 : half + pair * 128 + 128]
        value_pair = triple[:, 2 * half + pair * 128 : 2 * half + pair * 128 + 128]
        grad_pair = grad[:, lanes]
        key_sum, value_sum, query_parts = 0.0, 0.0, []
        for side in range(2):
            head = pair * 2 + side
            keep = left if side == 0 else jnp.logical_not(left)
            query = jnp.where(keep, query_pair, jnp.zeros_like(query_pair))
            grad_head = jnp.where(keep, grad_pair, jnp.zeros_like(grad_pair))
            scores = dot_columns(key_pair, query) * 0.125
            probs = jnp.exp(jnp.where(allowed, scores, masked_fill) - log_total[head : head + 1, :])
            grad_probs = dot_columns(value_pair, grad_head)
            inner = jnp.sum(probs * grad_probs, axis=0, keepdims=True)
            grad_scores = (probs * (grad_probs - inner)).astype(low_type)
            value_sum = value_sum + dot_wide(probs.astype(low_type), grad_head)
            key_sum = key_sum + dot_wide(grad_scores, query)
            query_parts.append(dot_rows(key_pair, grad_scores)[side * HD : side * HD + HD, :])
        triple_grad[:, lanes] = (jnp.concatenate(query_parts) * 0.125).T.astype(low_type)
        triple_grad[:, half + pair * 128 : half + pair * 128 + 128] = (key_sum * 0.125).astype(low_type)
        triple_grad[:, 2 * half + pair * 128 : 2 * half + pair * 128 + 128] = value_sum.astype(low_type)
    part[...] = (
        dot_columns(triple_grad[:, :half], weight[0])
        + dot_columns(triple_grad[:, half : 2 * half], weight[1])
        + dot_columns(triple_grad[:, 2 * half :], weight[2])
    )


def self_backward(facts, values, own, came, gain, grad_second, out_weight, triple, log_total, weight):
    rows, wide = triple.shape
    width = weight.shape[1]
    args = (values, own, came, gain, grad_second, out_weight, triple, log_total, weight)
    outs = (
        ((rows, width), wide_type),
        ((rows, width), low_type),
        ((8, width), wide_type),
        ((rows, wide), low_type),
        ((rows, width), wide_type),
    )
    return pl.pallas_call(
        partial(self_backward_kernel, heads=wide // (3 * HD)),
        grid_spec=pltpu.PrefetchScalarGridSpec(
            num_scalar_prefetch=1,
            grid=(1,),
            in_specs=[whole(arg.shape) for arg in args],
            out_specs=[whole(shape) for shape, _ in outs],
        ),
        out_shape=[jax.ShapeDtypeStruct(shape, kind) for shape, kind in outs],
        compiler_params=pltpu.CompilerParams(vmem_limit_bytes=vmem_budget),
        cost_estimate=heavy,
        name="self_backward",
    )(facts, *args)


def input_back_kernel(
    values, own, came, gain, grad_first, second, result_own, result_came, act_sums, cross_gain_grad,
    ffn_gain_grad, input_grad, layer_out, gains_out,
):
    incoming = (own[...] + came[...]).astype(low_type).astype(wide_type)
    inward, gain_row = back_through_norm(values[...].astype(wide_type), incoming, gain[...])
    input_grad[...] = inward + grad_first[...]
    layer_out[...] = (second[...] + (result_own[...] + result_came[...])).astype(low_type)
    width = values.shape[1]
    gains = jnp.concatenate(
        (
            act_sums[1:2, :],
            act_sums[0:1, :],
            0.5 * gain_row,
            0.5 * cross_gain_grad[0:1, :],
            0.5 * ffn_gain_grad[0:1, :],
            jnp.zeros((3, width), wide_type),
        )
    )
    for tile in range(width // 128):
        gains_out[tile] = gains[:, tile * 128 : tile * 128 + 128]


def input_back(*args):
    rows, width = args[0].shape
    outs = (((rows, width), wide_type), ((rows, width), low_type), ((width // 128, 8, 128), wide_type))
    return pl.pallas_call(
        input_back_kernel,
        out_shape=[jax.ShapeDtypeStruct(shape, kind) for shape, kind in outs],
        compiler_params=pltpu.CompilerParams(vmem_limit_bytes=vmem_budget),
        cost_estimate=heavy,
        name="input_back",
    )(*args)


def assemble_kernel(
    facts, memory, memory_came, own, other, left, middle, right, gains, conv, cross_kv,
    cross_out, self_qkv, cross_query, self_out, ffn_in, ffn_out, *gain_outs,
):
    width = conv.shape[1]
    half = width // 2
    third = left.shape[1]
    hidden = ffn_in.shape[1]
    first = facts[1] == 0
    conv[:, :half] = jnp.where(first, memory[:, width:], memory_came[:, width:])
    conv[:, half:] = jnp.where(first, memory_came[:, width:], memory[:, width:])
    for side in range(2):
        mine = memory[:, side * half : side * half + half]
        theirs = memory_came[:, side * half : side * half + half]
        cross_kv[:, side, :half] = jnp.where(first, mine, theirs)
        cross_kv[:, side, half:] = jnp.where(first, theirs, mine)
    rest = 3 * half - own.shape[1]
    self_qkv[0] = own[:, :half]
    self_qkv[1] = own[:, half : 2 * half]
    self_qkv[2, :, : half - rest] = own[:, 2 * half :]
    self_qkv[2, :, half - rest :] = other[:, :rest]
    cross_query[...] = other[:, rest : rest + half]
    self_out[...] = other[:, rest + half :]
    ffn_in[:, :third] = left[...]
    ffn_in[:, third:] = middle[:, : hidden - third]
    ffn_out[:, : 2 * third - hidden] = middle[:, hidden - third :]
    ffn_out[:, 2 * third - hidden :] = right[:, : 2 * hidden - 2 * third]
    cross_out[...] = right[:, 2 * hidden - 2 * third :]
    share = conv.shape[0]
    picked = (
        lax.broadcasted_iota(jnp.int32, (width, share), 0)
        == lax.broadcasted_iota(jnp.int32, (width, share), 1) + facts[0] * share
    ).astype(wide_type)
    first_tile = gains.shape[0] - width // 128
    rows_of = jnp.concatenate([gains[first_tile + tile] for tile in range(width // 128)], axis=1)
    mine = jnp.dot(rows_of, picked, precision=lax.Precision.HIGHEST)
    for number, out in enumerate(gain_outs):
        out[...] = mine[number : number + 1, :]


def assemble(facts, *args):
    share = args[0].shape[0]
    width = 2 * args[0].shape[1] // 3
    half = width // 2
    hidden = (3 * args[4].shape[1] - half) // 2
    outs = (
        (share, width),
        (share, 2, width),
        (share, half),
        (3, share, half),
        (share, half),
        (share, half),
        (share, hidden),
        (share, hidden),
    ) + ((1, share),) * 5
    return pl.pallas_call(
        assemble_kernel,
        grid_spec=pltpu.PrefetchScalarGridSpec(
            num_scalar_prefetch=1,
            grid=(1,),
            in_specs=[whole(arg.shape) for arg in args],
            out_specs=[whole(shape) for shape in outs],
        ),
        out_shape=[jax.ShapeDtypeStruct(shape, wide_type) for shape in outs],
        compiler_params=pltpu.CompilerParams(vmem_limit_bytes=vmem_budget),
        cost_estimate=heavy,
        name="assemble",
    )(facts, *args)


def shards(
    dec_input,
    out_grad,
    enc_feats,
    mem_lengths,
    dec_lengths,
    doc_owner,
    group_gain,
    group_bias,
    conv_weight,
    cross_kv,
    self_gain,
    self_qkv,
    self_out,
    cross_gain,
    cross_query,
    cross_out,
    ffn_gain,
    ffn_in,
    ffn_out,
):
    chips = lax.axis_size("dp")
    chip_index = lax.axis_index("dp")
    core_index = lax.axis_index("mp")
    memory_in = enc_feats[0, 0]
    docs, sub, width = memory_in.shape
    per_group = width // GROUPS
    half = width // 2
    heads = half // HD
    rows_here = docs * sub
    share = width // chips
    bits = chips.bit_length() - 1
    rest = tuple(range(4, bits))
    order_sets = {
        "stats": (0, 1, 2, 3),
        "left": (2, 3, 0, 1),
        "middle": (0, 2, 3, 1),
        "right": (1, 0, 2, 3),
        "first": (0, 1, 2, 3),
        "second": (2, 0, 1, 3),
        "memory": (1, 2, 0, 3),
    }
    orders = {
        name: order + rest if bits >= 4 else tuple(range(bits)) for name, order in order_sets.items()
    }

    outgoing = gather_docs(memory_in, doc_owner)
    features = lax.all_to_all(outgoing, "dp", split_axis=0, concat_axis=0, tiled=True)
    outgoing, dec_input = tie((outgoing, dec_input))
    dec_rows = DEC
    dec_rows_in = dec_input.reshape(dec_rows, width)
    self_facts = dec_lengths[chip_index][None]
    self_weight = self_qkv.transpose(1, 0, 2)
    normed_one, qkv_self, attended, self_totals, part = self_forward(
        self_facts, dec_rows_in, self_gain[None], self_weight, self_out
    )
    part_came = other_core(part)
    memory_here, part = tie((memory_in, part))
    wide_in = memory_here.astype(wide_type)
    slot_pos = lax.broadcasted_iota(jnp.int32, (docs, sub), 1)
    live_in = ((slot_pos * 2 + core_index) * chips + chip_index < mem_lengths[:, None])[:, :, None]
    masked_in = jnp.where(live_in, wide_in, 0.0)
    channel_sums = jnp.stack((jnp.sum(masked_in, axis=1), jnp.sum(masked_in * wide_in, axis=1)), axis=1)
    group_of = (
        lax.broadcasted_iota(jnp.int32, (width, GROUPS), 0) // per_group
        == lax.broadcasted_iota(jnp.int32, (width, GROUPS), 1)
    ).astype(wide_type)

    def group_sums(channels):
        return jnp.dot(channels, group_of, precision=lax.Precision.HIGHEST)

    def to_channels(groups):
        return jnp.dot(groups, group_of.T, precision=lax.Precision.HIGHEST)

    sums_here = group_sums(channel_sums.reshape(docs * 2, width)).reshape(docs, 2 * GROUPS)
    sums_here = jnp.take(sums_here, doc_owner, axis=0, mode="clip")
    stat_sums = ScatterSums([core_total(sums_here)], [orders["stats"]], chip_index)
    stat_sums.begin()

    def next_step(sums, value):
        value = sums.behind(value)
        sums.merge()
        if sums.orders[0]:
            sums.begin()
            value = sums.ahead_of(value)
            sums.send()
        return value

    part_came = stat_sums.ahead_of(part_came)
    stat_sums.send()
    first_out, normed_two, query_heads, query_heads_t = query_forward(
        dec_rows_in, part, part_came, cross_gain[None], cross_query
    )
    cross_kv, query_heads = next_step(stat_sums, (cross_kv, query_heads))
    pair_weight = prepare_weights(cross_kv)
    pair_weight, query_heads = next_step(stat_sums, (pair_weight, query_heads))
    grad_low, query_heads, pair_weight = tie((out_grad.reshape(DEC, width), query_heads, pair_weight))
    grad_active = dot_columns(grad_low, ffn_out).astype(low_type)
    document = doc_owner[chip_index]
    length = mem_lengths[document]
    facts_own = jnp.stack((length, core_index, core_index, 1)).astype(jnp.int32)
    facts_other = jnp.stack((length, 1 - core_index, core_index, 0)).astype(jnp.int32)
    grad_active, query_heads, facts_own, facts_other = tie((grad_active, query_heads, facts_own, facts_other))
    while stat_sums.orders[0]:
        query_heads = next_step(stat_sums, query_heads)
    sums_all = stat_sums.current[0]

    entries = (length * per_group).astype(wide_type)
    center = sums_all[:GROUPS] / entries
    spread = lax.rsqrt(sums_all[GROUPS:] / entries - center * center + group_eps)
    channel_stats = to_channels(jnp.stack((center, spread)))
    stats = jnp.concatenate(
        (channel_stats, group_gain[None], group_bias[None], jnp.zeros((4, width), wide_type))
    )

    features, stats, query_heads, query_heads_t = tie((features, stats, query_heads, query_heads_t))
    memory_own = memory_forward(facts_own, features, stats, conv_weight)
    memory_other = other_core(memory_own)

    carry = (
        jnp.full((8, dec_rows), -1e30, wide_type),
        jnp.zeros((8, dec_rows), wide_type),
        jnp.zeros((half, dec_rows), wide_type),
    )
    pairs_own, *carry = cross_forward(
        facts_own, query_heads_t, memory_own, pair_weight, carry
    )
    pairs_other, top, total, gathered = cross_forward(
        facts_other, query_heads_t, memory_other, pair_weight, carry
    )
    crossed, crossed_t, log_total, part = cross_close(gathered, top, total, cross_out)

    second_out, normed_three, grad_lifted, active, part = feed_forward(
        first_out, part, other_core(part), ffn_gain[None], ffn_in, grad_active
    )
    part_came = other_core(part)
    result_part = product(active, ffn_out)
    part_came, result_part = tie((part_came, result_part))
    result_came = other_core(result_part)
    grad_second, ffn_gain_grad, grad_cross, grad_heads, grad_heads_t, inner = feed_close(
        second_out, part, part_came, ffn_gain[None], grad_low, cross_out, crossed_t
    )
    feed_grads = feed_weights(normed_three, grad_low, grad_cross, grad_lifted, active, crossed)
    feed_sums = Sums.of(
        [grad.reshape(chips, share, grad.shape[1]) for grad in feed_grads],
        [orders["left"], orders["middle"], orders["right"]],
        chip_index,
    )
    inner = feed_sums.start(inner)

    steps = sub // chunk_of(chips, sub)
    place = jnp.concatenate((jnp.stack((chip_index, core_index)).astype(jnp.int32), mem_lengths))
    pair_other, row_other, query_other = cross_backward(
        facts_other, query_heads, query_heads_t, grad_heads, grad_heads_t, log_total, inner, pairs_other, pair_weight,
        low_type, 0, steps,
    )
    facts_two, query_other = feed_sums.round((facts_own, query_other))
    row_came = other_core(row_other)
    pair_own, row_own, query_own = cross_backward(
        facts_two, query_heads, query_heads_t, grad_heads, grad_heads_t, log_total, inner, pairs_own, pair_weight,
        wide_type, 0, steps,
    )

    facts_three, query_own = feed_sums.round((facts_own, query_own))
    grad_memory, hidden, base, act_sums, groups = memory_backward(
        facts_three, features, row_own, row_came, stats, conv_weight, jnp.zeros((8, width), wide_type), 0
    )
    queries, sets = (query_other, query_own), [(hidden, pair_own, grad_memory, pair_other)]

    def dp_hop(value, bit):
        return lax.ppermute(value, "dp", [(chip, chip ^ (1 << bit)) for chip in range(chips)])

    feed_came, base, queries = tie(([part.came for part in feed_sums.parts], base, queries))
    for part, arrived in zip(feed_sums.parts, feed_came):
        part.came = arrived
    returned = [lax.all_to_all(base, "dp", split_axis=0, concat_axis=0, tiled=True)]

    def when_live(work):
        return lax.cond(length > 0, work, nothing_like(work))

    def self_work():
        own_slot = lax.broadcasted_iota(jnp.int32, (chips, 1, 1), 0) == chip_index
        document_groups = jnp.where(own_slot, core_total(groups)[None], 0.0)

        grad_cq, part = query_back(queries, cross_query)
        part_came = other_core(part)
        grad_first, grad_self, cross_gain_grad, grad_qkv, part_one = self_backward(
            self_facts, first_out, part, part_came, cross_gain[None], grad_second, self_out, qkv_self, self_totals,
            self_weight,
        )
        part_one_came = other_core(part_one)
        first_part, second_part = side_weights(normed_one, grad_qkv, normed_two, grad_cq, grad_self, attended)
        part_one_came, first_part = tie((part_one_came, first_part))
        return grad_first, cross_gain_grad, part_one, part_one_came, document_groups, (first_part, second_part)

    queries = feed_sums.round(queries)
    early_feed, late_feed = Sums(feed_sums.parts[:2], chip_index), Sums(feed_sums.parts[2:], chip_index)
    grad_first, cross_gain_grad, part_one, part_one_came, document_groups, late_parts = when_live(self_work)
    while early_feed.going:
        document_groups = early_feed.round(document_groups)
    late_sums = Sums.of(
        [part.reshape(chips, share, -1) for part in late_parts], [orders["first"], orders["second"]], chip_index
    )
    document_groups = late_sums.start(document_groups)

    def memory_work():
        pair_part, conv_keep, conv_send = memory_weights(place, memory_own, memory_other, sets)
        conv_came = other_core(conv_send)
        came, conv_keep = tie((part_one_came, conv_keep))
        input_grad, layer_out, gains = input_back(
            dec_rows_in, part_one, came, self_gain[None], grad_first, second_out, result_part, result_came, act_sums,
            cross_gain_grad, ffn_gain_grad,
        )
        gains, conv_came = tie((gains, conv_came))
        conv_part = (conv_keep + conv_came.astype(wide_type)).astype(low_type)
        return input_grad, layer_out, core_total(gains), jnp.concatenate((pair_part, conv_part), axis=1)

    input_grad, layer_out, small, memory_part = when_live(memory_work)

    memory_sums = Sums.of([memory_part.reshape(chips, share, -1)], [orders["memory"]], chip_index)
    small = memory_sums.start(small)
    late_sums = late_sums.joined(memory_sums)
    all_sums = late_feed.joined(late_sums)
    hop = 0
    moved = memory_grad = None
    while all_sums.going:
        small_came = dp_hop(small, hop) if hop < bits else None
        for bit in ((0,), (1, 2), range(3, bits))[hop] if hop < 3 else ():
            document_groups = document_groups + dp_hop(document_groups, bit)
        value = (small_came, document_groups)
        if hop == 2:
            moved = moved_rows(doc_owner, place, memory_in, document_groups)
            value = (small_came, moved)
        if hop == 3:
            memory_grad = spread_docs(returned, moved, doc_owner)
            value = (small_came, memory_grad)
        if hop == 0:
            returned, small_came = tie((returned, small_came))
            value = (small_came, document_groups)
        small_came, value = all_sums.round(value)
        if hop < bits:
            small = small + small_came
        if hop < 2:
            document_groups = value
        elif hop == 2:
            moved = value
        elif hop == 3:
            memory_grad = value
        hop += 1
    while hop < bits:
        small = small + dp_hop(small, hop)
        hop += 1
    if moved is None:
        moved = moved_rows(doc_owner, place, memory_in, document_groups)
    if memory_grad is None:
        memory_grad = spread_docs(returned, moved, doc_owner)
    first_total, second_total, memory_total = late_sums.totals
    memory_came = other_core(memory_total)
    weight_grads = assemble(
        place, memory_total, memory_came, first_total, second_total, *feed_sums.totals, small
    )
    conv_grad, cross_kv_grad, cross_out_grad, self_qkv_grad, cross_query_grad, self_out_grad = weight_grads[:6]
    ffn_in_grad, ffn_out_grad = weight_grads[6:8]
    gains = [gain.reshape(share) for gain in weight_grads[8:]]
    return (
        layer_out.reshape(1, DEC, width),
        input_grad.reshape(1, DEC, width),
        memory_grad.reshape(1, 1, docs, sub, width),
        gains[0],
        gains[1],
        conv_grad,
        cross_kv_grad,
        gains[2],
        self_qkv_grad.transpose(1, 0, 2),
        self_out_grad.T,
        gains[3],
        cross_query_grad,
        cross_out_grad.T,
        gains[4],
        ffn_in_grad,
        ffn_out_grad.T,
    )


def solution(mesh):
    placed = (
        P("dp", None, None),
        P("dp", None, None),
        P("dp", "mp", None, None, None),
        P(),
        P(),
        P(),
        P(),
        P(),
        P(),
        P(),
        P(),
        P(None, None, "mp"),
        P("mp", None),
        P(),
        P(None, "mp"),
        P("mp", None),
        P(),
        P(None, "mp"),
        P("mp", None),
    )
    return jax.shard_map(
        shards,
        mesh=mesh,
        in_specs=placed,
        out_specs=(
            P("dp", None, None),
            P("dp", None, None),
            P("dp", "mp", None, None, None),
            P("dp"),
            P("dp"),
            P("dp", None),
            P("dp", None, None),
            P("dp"),
            P("dp", None, "mp"),
            P("mp", "dp"),
            P("dp"),
            P("dp", "mp"),
            P("mp", "dp"),
            P("dp"),
            P("dp", "mp"),
            P("mp", "dp"),
        ),
        check_vma=False,
    )
```

```python
from functools import partial

import jax
import jax.numpy as jnp
from jax import lax
from jax.experimental import pallas as pl
from jax.experimental.pallas import tpu as pltpu
from jax.sharding import PartitionSpec as P

HD = 64
GROUPS = 32
DEC = 512


norm_eps = 1e-06
group_eps = 1e-05
masked_fill = -1000000000.0
largest_sum = 1e17
vmem_budget = 16 * 1024 * 1024
vmem_large = 48 * 1024 * 1024


def room(chips):
    return vmem_budget if chips <= 16 else vmem_large


heavy = pl.CostEstimate(flops=10**10, bytes_accessed=10**7, transcendentals=10**7)
low_type = jnp.bfloat16
wide_type = jnp.float32


def dot_wide(left, right):
    return jnp.dot(left, right, preferred_element_type=wide_type)


def dot_rows(left, right):
    return lax.dot_general(left, right, (((0,), (0,)), ((), ())), preferred_element_type=wide_type)


def dot_columns(left, right):
    return lax.dot_general(left, right, (((1,), (1,)), ((), ())), preferred_element_type=wide_type)


def norm_rows(values, gain):
    factor = lax.rsqrt(jnp.mean(values * values, axis=-1, keepdims=True) + norm_eps)
    return (values * factor * gain, factor)


def norm_rows_back(values, factor, gain, incoming):
    scaled = incoming * gain
    inward = factor * scaled - values * factor * factor * factor * jnp.mean(
        scaled * values, axis=-1, keepdims=True
    )
    gain_grad = jnp.sum(incoming * values * factor, axis=0)
    return (inward, gain_grad)


def other_core(values):
    return lax.ppermute(values, "mp", [(0, 1), (1, 0)])


def core_total(partial_sum):
    return partial_sum + other_core(partial_sum)


tie = lax.optimization_barrier


class ScatterSums:
    def __init__(self, arrays, orders, chip_index):
        chips = arrays[0].shape[0]
        self.chip_index = chip_index
        self.bits = chips.bit_length() - 1
        self.orders = [list(order) for order in orders]
        self.left = [list(range(self.bits - 1, -1, -1)) for _ in arrays]
        self.current = [array.reshape((2,) * self.bits + array.shape[1:]) for array in arrays]
        self.kept = self.sent = self.came = None

    def copied(self):
        other = object.__new__(ScatterSums)
        other.chip_index, other.bits = self.chip_index, self.bits
        other.orders = [list(order) for order in self.orders]
        other.left = [list(left) for left in self.left]
        other.current, other.kept, other.sent, other.came = self.current, self.kept, self.sent, self.came
        return other

    def begin(self):
        self.kept, self.sent = [], []
        for number, order in enumerate(self.orders):
            axis = self.left[number].index(order[0])
            mine = (self.chip_index >> order[0]) & 1
            self.sent.append(lax.dynamic_index_in_dim(self.current[number], 1 - mine, axis, False))
            self.kept.append(lax.dynamic_index_in_dim(self.current[number], mine, axis, False))
            self.left[number].pop(axis)

    def ahead_of(self, value):
        self.sent, value = tie((self.sent, value))
        return value

    def send(self):
        chips = 1 << self.bits
        self.came = [
            lax.ppermute(sent, "dp", [(chip, chip ^ (1 << order[0])) for chip in range(chips)])
            for sent, order in zip(self.sent, self.orders)
        ]

    def behind(self, value):
        self.came, value = tie((self.came, value))
        return value

    def merge(self):
        merged = []
        for number, order in enumerate(self.orders):
            total = self.kept[number].astype(wide_type) + self.came[number].astype(wide_type)
            order.pop(0)
            merged.append(total.astype(self.current[number].dtype) if order else total)
        self.current = merged

    def step(self):
        self.begin()
        self.send()
        self.merge()

    def finish(self):
        while self.orders[0]:
            self.step()
        return self.current


def merge_kernel(facts, *refs, plans):
    count = len(plans)
    outs = list(refs[2 * count :])
    for plan, kept, came in zip(plans, refs[:count], refs[count : 2 * count]):
        entries, after, turn = plan["entries"], plan["after"], plan["turn"]

        def total(entry, kept=kept, came=came, after=after):
            own = kept[entry] if after is None else kept[entry >> after, 0, entry & ((1 << after) - 1)]
            return own.astype(wide_type) + came[entry].astype(wide_type)

        if turn is None:
            outs.pop(0)[...] = total(0)
            continue
        sent_out, kept_out = outs.pop(0), outs.pop(0)
        bit, behind = turn
        mine = (facts[0] >> bit) & 1
        for place in range(entries // 2):
            base = (place >> behind << (behind + 1)) | (place & ((1 << behind) - 1))
            kept_out[place] = total(base + (mine << behind)).astype(low_type)
            sent_out[place] = total(base + ((1 - mine) << behind)).astype(low_type)


class Part:
    def __init__(self, array, order):
        self.kept, self.order = array, order
        self.sent = self.came = self.total = None
        self.step = 0
        self.left = tuple(range(len(order) - 1, -1, -1))

    def copied(self):
        other = object.__new__(Part)
        other.__dict__.update(self.__dict__)
        return other


class Sums:
    def __init__(self, parts, chip_index):
        self.parts, self.chip_index = parts, chip_index

    @staticmethod
    def of(arrays, orders, chip_index):
        return Sums([Part(array, order) for array, order in zip(arrays, orders)], chip_index)

    def copied(self):
        return Sums([part.copied() for part in self.parts], self.chip_index)

    def joined(self, *others):
        return Sums([part for sums in (self, *others) for part in sums.parts], self.chip_index)

    def state(self):
        return [(part.kept, part.came) for part in self.parts]

    def stepped(self):
        other = self.copied()
        for part in other.parts:
            part.left = tuple(bit for bit in part.left if bit != part.order[part.step])
            part.step += 1
        return other

    def with_state(self, state):
        other = self.copied()
        for part, (kept, came) in zip(other.parts, state):
            part.kept, part.came = kept, came
        return other

    @property
    def going(self):
        return [part for part in self.parts if part.total is None]

    @property
    def totals(self):
        return [part.total for part in self.parts]

    def start(self, value):
        for part in self.parts:
            chips = part.kept.shape[0]
            behind = part.order[0]
            ahead = len(part.order) - 1 - behind
            view = part.kept.reshape((1 << ahead, 2, 1 << behind) + part.kept.shape[1:])
            mine = (self.chip_index >> behind) & 1
            sent = lax.dynamic_index_in_dim(view, 1 - mine, 1, False)
            part.sent = sent.reshape((chips // 2,) + part.kept.shape[1:])
            part.kept = view
        return self.leave(self.parts, value)

    def leave(self, parts, value):
        sent, value = tie(([part.sent for part in parts], value))
        for part, leaving in zip(parts, sent):
            chips = 1 << len(part.order)
            bit = part.order[part.step]
            part.came = lax.ppermute(leaving, "dp", [(chip, chip ^ (1 << bit)) for chip in range(chips)])
        return value

    def round(self, value):
        parts = self.going
        came, value = tie(([part.came for part in parts], value))
        plans, in_specs, out_specs, out_shape = [], [], [], []
        for part, arrived in zip(parts, came):
            part.came = arrived
            entries, rows, columns = arrived.shape
            kept, bit = part.kept, part.order[part.step]
            if part.step == 0:
                in_specs.append(
                    pl.BlockSpec(
                        (kept.shape[0], 1) + kept.shape[2:],
                        lambda j, facts, bit=bit: (0, (facts[0] >> bit) & 1, 0, 0, 0),
                    )
                )
            else:
                in_specs.append(whole(kept.shape))
            plan = {"entries": entries, "after": bit if part.step == 0 else None, "turn": None}
            part.left = tuple(other for other in part.left if other != bit)
            if part.left:
                following = part.order[part.step + 1]
                plan["turn"] = (following, len(part.left) - 1 - part.left.index(following))
                half = (entries // 2, rows, columns)
                out_specs += [whole(half)] * 2
                out_shape += [jax.ShapeDtypeStruct(half, low_type)] * 2
            else:
                out_specs.append(whole((rows, columns)))
                out_shape.append(jax.ShapeDtypeStruct((rows, columns), wide_type))
            plans.append(plan)
        in_specs += [whole(part.came.shape) for part in parts]
        made = pl.pallas_call(
            partial(merge_kernel, plans=plans),
            grid_spec=pltpu.PrefetchScalarGridSpec(
                num_scalar_prefetch=1, grid=(1,), in_specs=in_specs, out_specs=out_specs
            ),
            out_shape=out_shape,
            compiler_params=pltpu.CompilerParams(vmem_limit_bytes=room(1 << len(parts[0].order))),
            cost_estimate=heavy,
            name="merge_sums",
        )(
            self.chip_index[None].astype(jnp.int32),
            *[part.kept for part in parts],
            *[part.came for part in parts],
        )
        made = list(made)
        for part in parts:
            part.step += 1
            if part.left:
                part.sent, part.kept = made.pop(0), made.pop(0)
            else:
                part.total = made.pop(0)
        parts = [part for part in parts if part.left]
        return self.leave(parts, value) if parts else value


def nothing_like(work):
    def nothing():
        return jax.tree.map(lambda leaf: jnp.zeros(leaf.shape, leaf.dtype), jax.eval_shape(work))

    return nothing


def gather_kernel(owner, rows, out, done, *, docs):
    copies = [pltpu.make_async_copy(rows.at[owner[slot]], out.at[slot], done.at[slot]) for slot in range(docs)]
    for copy in copies:
        copy.start()
    for copy in copies:
        copy.wait()


def gather_docs(memory_in, doc_owner):
    docs = memory_in.shape[0]
    return pl.pallas_call(
        partial(gather_kernel, docs=docs),
        grid_spec=pltpu.PrefetchScalarGridSpec(
            num_scalar_prefetch=1,
            grid=(),
            in_specs=[pl.BlockSpec(memory_space=pltpu.VMEM)],
            out_specs=pl.BlockSpec(memory_space=pl.ANY),
            scratch_shapes=[pltpu.SemaphoreType.DMA((docs,))],
        ),
        out_shape=pltpu.HBM(memory_in.shape, low_type),
        compiler_params=pltpu.CompilerParams(vmem_limit_bytes=vmem_budget),
        cost_estimate=heavy,
        name="gather_docs",
    )(doc_owner, memory_in)


def prepare_kernel(cross_kv, pair):
    width = cross_kv.shape[0]
    for side in range(2):
        pair[:, side * width : side * width + width] = cross_kv[:, side, :]


def prepare_weights(cross_kv):
    width = cross_kv.shape[0]
    return pl.pallas_call(
        prepare_kernel,
        out_shape=jax.ShapeDtypeStruct((width, 2 * width), low_type),
        compiler_params=pltpu.CompilerParams(vmem_limit_bytes=vmem_budget),
        cost_estimate=heavy,
        name="prepare_weights",
    )(cross_kv)


def moved_kernel(owner, facts, features, groups, out, stats, *, chips, count):
    step = pl.program_id(0)
    sub, width = features.shape[1:]

    @pl.when(step == 0)
    def _():
        own_group = (
            lax.broadcasted_iota(jnp.int32, (128, width), 1) // (width // GROUPS)
            == lax.broadcasted_iota(jnp.int32, (128, width), 0)
        ).astype(wide_type)
        stats[...] = jnp.dot(
            groups[0:chips].reshape(chips * 8, 128), own_group, precision=lax.Precision.HIGHEST
        ).reshape(chips, 8, width)

    position = (lax.broadcasted_iota(jnp.int32, (sub, 1), 0) * 2 + facts[1]) * chips + facts[0]

    def one(place, carry):
        slot = step * count + place
        document = owner[slot]
        normed = (features[document].astype(wide_type) - stats[slot, 0:1, :]) * stats[slot, 1:2, :]
        moved = stats[slot, 1:2, :] * (stats[slot, 2:3, :] + normed * stats[slot, 3:4, :])
        out[place] = jnp.where(position < facts[2 + document], moved, 0.0).astype(low_type)
        return carry

    lax.fori_loop(0, count, one, 0)


def moved_rows(doc_owner, facts, features, groups):
    docs, sub, width = features.shape
    count = max(docs // 4, 1)
    return pl.pallas_call(
        partial(moved_kernel, chips=docs, count=count),
        grid_spec=pltpu.PrefetchScalarGridSpec(
            num_scalar_prefetch=2,
            grid=(docs // count,),
            in_specs=[
                pl.BlockSpec(features.shape, lambda j, owner, facts: (0, 0, 0)),
                pl.BlockSpec(groups.shape, lambda j, owner, facts: (0, 0, 0)),
            ],
            out_specs=pl.BlockSpec((count, sub, width), lambda j, owner, facts: (j, 0, 0)),
            scratch_shapes=[pltpu.VMEM((docs, 8, width), wide_type)],
        ),
        out_shape=jax.ShapeDtypeStruct(features.shape, low_type),
        compiler_params=pltpu.CompilerParams(vmem_limit_bytes=room(docs)),
        cost_estimate=heavy,
        name="moved_rows",
    )(doc_owner, facts, features, groups)


def spread_kernel(owner, *refs, docs, pieces):
    rows = refs[:pieces]
    moved, out, held, taken, wide, came, also, gone = refs[pieces:]
    each = rows[0].shape[1]
    loads = [
        [
            pltpu.make_async_copy(
                piece.at[slot], held.at[slot, pl.ds(number * each, each)], came.at[slot * pieces + number]
            )
            for number, piece in enumerate(rows)
        ]
        for slot in range(docs)
    ]
    takes = [pltpu.make_async_copy(moved.at[slot], taken.at[slot], also.at[slot]) for slot in range(docs)]
    stores = [pltpu.make_async_copy(wide.at[slot], out.at[owner[slot]], gone.at[slot]) for slot in range(docs)]
    for slot in range(docs):
        for load in loads[slot]:
            load.start()
        takes[slot].start()
    for slot in range(docs):
        for load in loads[slot]:
            load.wait()
        takes[slot].wait()
        wide[slot] = held[slot].astype(wide_type) - taken[slot].astype(wide_type)
        stores[slot].start()
    for store in stores:
        store.wait()


def spread_docs(rows, moved, doc_owner):
    docs = moved.shape[0]
    pieces = len(rows)
    return pl.pallas_call(
        partial(spread_kernel, docs=docs, pieces=pieces),
        grid_spec=pltpu.PrefetchScalarGridSpec(
            num_scalar_prefetch=1,
            grid=(),
            in_specs=[pl.BlockSpec(memory_space=pl.ANY)] * (pieces + 1),
            out_specs=pl.BlockSpec(memory_space=pl.ANY),
            scratch_shapes=[
                pltpu.VMEM(moved.shape, low_type),
                pltpu.VMEM(moved.shape, low_type),
                pltpu.VMEM(moved.shape, wide_type),
                pltpu.SemaphoreType.DMA((docs * pieces,)),
                pltpu.SemaphoreType.DMA((docs,)),
                pltpu.SemaphoreType.DMA((docs,)),
            ],
        ),
        out_shape=jax.ShapeDtypeStruct(moved.shape, wide_type),
        compiler_params=pltpu.CompilerParams(vmem_limit_bytes=vmem_large),
        cost_estimate=heavy,
        name="spread_docs",
    )(doc_owner, *rows, moved)


def chunk_of(chips, sub):
    return min(sub, max(16, 512 // chips))


def live_rows(facts, start, chips, span):
    row = lax.broadcasted_iota(jnp.int32, (chips * span, 1), 0)
    chip, step = row // span, row % span
    return ((start + step) * 2 + facts[1]) * chips + chip < facts[0]


def in_branches(facts, start, chips, span, work, dead=None):
    first = (start * 2 + facts[1]) * chips
    last = ((start + span - 1) * 2 + facts[1]) * chips + chips - 1
    full = last < facts[0]
    none = first >= facts[0]

    @pl.when(full)
    def _():
        work(None)

    @pl.when(jnp.logical_not(full) & jnp.logical_not(none))
    def _():
        work(live_rows(facts, start, chips, span))

    if dead is not None:
        pl.when(none)(dead)


def whole(shape):
    return pl.BlockSpec(shape, lambda j, facts: (0,) * len(shape))


def slab(shape, span, first=0):
    return pl.BlockSpec((shape[0], span, shape[2]), lambda j, facts: (0, j + first, 0))


def memory_forward_kernel(facts, rows, stats, weight, out, *, chips, span):
    width = rows.shape[-1]
    wide = rows[...].reshape(chips * span, width).astype(wide_type)
    drive = (wide - stats[0:1, :]) * stats[1:2, :] * stats[2:3, :] + stats[3:4, :]
    hidden = (drive * (0.5 + 0.5 * jnp.tanh(0.5 * drive))).astype(low_type)
    made = wide + dot_wide(hidden, weight[...])
    out[...] = made.astype(low_type).reshape(chips, span, width)


def memory_forward(facts, rows, stats, weight):
    chips, sub, width = rows.shape
    span = chunk_of(chips, sub)
    return pl.pallas_call(
        partial(memory_forward_kernel, chips=chips, span=span),
        grid_spec=pltpu.PrefetchScalarGridSpec(
            num_scalar_prefetch=1,
            grid=(sub // span,),
            in_specs=[slab(rows.shape, span), whole(stats.shape), whole(weight.shape)],
            out_specs=slab(rows.shape, span),
        ),
        out_shape=pltpu.HBM(rows.shape, low_type),
        compiler_params=pltpu.CompilerParams(vmem_limit_bytes=room(chips)),
        cost_estimate=heavy,
        name="memory_forward",
    )(facts, rows, stats, weight)


def memory_backward_kernel(
    facts, rows, own, came, stats, weight, sums_in, grad_out, hidden_out, base_out, sums, groups, *, chips, span, steps
):
    step = pl.program_id(0)
    width = rows.shape[-1]
    count = chips * span

    @pl.when(step == 0)
    def _():
        sums[...] = sums_in[...]

    wide = rows[...].reshape(count, width).astype(wide_type)
    normed = (wide - stats[0:1, :]) * stats[1:2, :]
    drive = normed * stats[2:3, :] + stats[3:4, :]
    gate = 0.5 + 0.5 * jnp.tanh(0.5 * drive)
    hidden_out[...] = (drive * gate).astype(low_type).reshape(chips, span, width)
    grad = (own[...].reshape(count, width) + came[...].reshape(count, width).astype(wide_type)).astype(low_type)
    grad_out[...] = grad.reshape(chips, span, width)
    grad_act = dot_columns(grad, weight[...]) * (gate * (1.0 + drive * (1.0 - gate)))
    sums[0:1, :] += jnp.sum(grad_act, axis=0, keepdims=True)
    sums[1:2, :] += jnp.sum(grad_act * normed, axis=0, keepdims=True)
    base = grad.astype(wide_type) + grad_act * (stats[1:2, :] * stats[2:3, :])
    base_out[...] = base.astype(low_type).reshape(chips, span, width)

    @pl.when(step == steps - 1)
    def _():
        per_group = width // GROUPS
        group_of = (
            lax.broadcasted_iota(jnp.int32, (width, 128), 0) // per_group
            == lax.broadcasted_iota(jnp.int32, (width, 128), 1)
        ).astype(wide_type)
        entries = (facts[0] * per_group).astype(wide_type)
        rows_of = jnp.concatenate(
            (
                stats[0:2, :] * (0.5 / per_group),
                sums[0:2, :] * stats[2:3, :] / entries,
                jnp.zeros((4, width), wide_type),
            )
        )
        groups[...] = jnp.dot(rows_of, group_of, precision=lax.Precision.HIGHEST)


def memory_backward(facts, rows, own, came, stats, weight, sums_in, first):
    chips, sub, width = own.shape
    span = chunk_of(chips, rows.shape[1])
    block = slab(own.shape, span)
    return pl.pallas_call(
        partial(memory_backward_kernel, chips=chips, span=span, steps=sub // span),
        grid_spec=pltpu.PrefetchScalarGridSpec(
            num_scalar_prefetch=1,
            grid=(sub // span,),
            in_specs=[
                slab(rows.shape, span, first),
                block,
                block,
                whole(stats.shape),
                whole(weight.shape),
                whole(sums_in.shape),
            ],
            out_specs=[block, block, block, whole(stats.shape), whole((8, 128))],
        ),
        out_shape=[
            jax.ShapeDtypeStruct(own.shape, low_type),
            jax.ShapeDtypeStruct(own.shape, low_type),
            pltpu.HBM(own.shape, low_type),
            jax.ShapeDtypeStruct(stats.shape, wide_type),
            jax.ShapeDtypeStruct((8, 128), wide_type),
        ],
        compiler_params=pltpu.CompilerParams(vmem_limit_bytes=room(chips)),
        cost_estimate=heavy,
        name="memory_backward",
    )(facts, rows, own, came, stats, weight, sums_in)


def cross_forward_kernel(
    facts, query_t, rows, key_weight, value_weight, top_in, total_in, sum_in, pairs, top, total, gathered,
    total_here, sum_here, held, *, chips, span
):
    step = pl.program_id(0)
    half = key_weight.shape[1]
    width = rows.shape[-1]

    @pl.when(step == 0)
    def _():
        top[...] = top_in[...]
        total[...] = total_in[...]
        gathered[...] = sum_in[...]

    def work(live):
        block = rows[...].reshape(chips * span, width)
        keys = dot_wide(block, key_weight[...]).astype(low_type)
        values = dot_wide(block, value_weight[...]).astype(low_type)
        pairs[:, :, :half] = keys.reshape(chips, span, half)
        pairs[:, :, half:] = values.reshape(chips, span, half)
        heads = half // HD

        def score(head):
            made = dot_wide(keys[:, head // 2 * 128 : head // 2 * 128 + 128], query_t[head])
            return made if live is None else jnp.where(live, made, masked_fill)

        def part_of(head, weights):
            part = dot_rows(values[:, head // 2 * 128 : head // 2 * 128 + 128], weights.astype(low_type))
            return part[head % 2 * HD : head % 2 * HD + HD, :]

        def plain():
            following = score(0)
            for head in range(heads):
                scores = following
                if head + 1 < heads:
                    following = score(head + 1)
                weights = jnp.exp(scores - top[head : head + 1, :])
                total_here[head : head + 1, :] = jnp.sum(weights, axis=0, keepdims=True)
                sum_here[head * HD : head * HD + HD, :] = part_of(head, weights)

        def shifted():
            following = score(0)
            for head in range(heads):
                scores = following
                if head + 1 < heads:
                    following = score(head + 1)
                old_top = top[head : head + 1, :]
                new_top = jnp.maximum(old_top, jnp.max(scores, axis=0, keepdims=True))
                weights = jnp.exp(scores - new_top)
                shrink = jnp.exp(old_top - new_top)
                total[head : head + 1, :] = total[head : head + 1, :] * shrink + jnp.sum(
                    weights, axis=0, keepdims=True
                )
                rows_of = slice(head * HD, head * HD + HD)
                gathered[rows_of, :] = gathered[rows_of, :] * shrink + part_of(head, weights)
                top[head : head + 1, :] = new_top

        fresh = (facts[3] == 1) & (step == 0)
        held[0] = jnp.where(fresh, 1, 0)

        @pl.when(jnp.logical_not(fresh))
        def _():
            plain()
            small = jnp.max(total_here[0:heads, :]) < largest_sum
            held[0] = jnp.where(small, 0, 1)

            @pl.when(small)
            def _():
                total[0:heads, :] += total_here[0:heads, :]
                gathered[...] += sum_here[...]

        pl.when(held[0] == 1)(shifted)

    def dead():
        pairs[...] = jnp.zeros_like(pairs)

    in_branches(facts, step * span, chips, span, work, dead)


def cross_forward(facts, query_t, rows, weight, carry):
    chips, sub, width = rows.shape
    heads, _, queries = query_t.shape
    half = heads * HD
    span = chunk_of(chips, sub)
    stat = (8, queries)
    summed = (half, queries)
    return pl.pallas_call(
        partial(cross_forward_kernel, chips=chips, span=span),
        grid_spec=pltpu.PrefetchScalarGridSpec(
            num_scalar_prefetch=1,
            grid=(sub // span,),
            in_specs=[
                whole(query_t.shape),
                slab(rows.shape, span),
                pl.BlockSpec((width, half), lambda j, facts: (0, facts[2])),
                pl.BlockSpec((width, half), lambda j, facts: (0, 2 + facts[2])),
                whole(stat),
                whole(stat),
                whole(summed),
            ],
            out_specs=[slab((chips, sub, 2 * half), span), whole(stat), whole(stat), whole(summed)],
            scratch_shapes=[
                pltpu.VMEM(stat, wide_type),
                pltpu.VMEM(summed, wide_type),
                pltpu.SMEM((1,), jnp.int32),
            ],
        ),
        out_shape=[
            jax.ShapeDtypeStruct((chips, sub, 2 * half), low_type),
            jax.ShapeDtypeStruct(stat, wide_type),
            jax.ShapeDtypeStruct(stat, wide_type),
            jax.ShapeDtypeStruct(summed, wide_type),
        ],
        compiler_params=pltpu.CompilerParams(vmem_limit_bytes=room(chips)),
        cost_estimate=heavy,
        name="cross_forward",
    )(facts, query_t, rows, weight, weight, *carry)


def cross_close_kernel(gathered, top, total, weight, crossed, crossed_t, log_total, part, *, heads):
    log_total[...] = top[...] + jnp.log(jnp.maximum(total[...], 1e-30))
    for head in range(heads):
        rows = slice(head * HD, head * HD + HD)
        crossed_t[rows, :] = gathered[rows, :] / total[head : head + 1, :]
    low = crossed_t[...].T.astype(low_type)
    crossed[...] = low
    part[...] = dot_wide(low, weight[...])


def cross_close(gathered, top, total, weight):
    half, queries = gathered.shape
    return pl.pallas_call(
        partial(cross_close_kernel, heads=half // HD),
        out_shape=[
            jax.ShapeDtypeStruct((queries, half), low_type),
            jax.ShapeDtypeStruct((half, queries), wide_type),
            jax.ShapeDtypeStruct(top.shape, wide_type),
            jax.ShapeDtypeStruct((queries, weight.shape[1]), wide_type),
        ],
        compiler_params=pltpu.CompilerParams(vmem_limit_bytes=vmem_budget),
        cost_estimate=heavy,
        name="cross_close",
    )(gathered, top, total, weight)


gelu_scale = 0.7978845608028654
gelu_cubic = 0.044715


def feed_forward_kernel(
    first, own, came, gain, weight, grad_active, second, normed, both_grad, both_active, grad_normed
):
    step = pl.program_id(0)

    @pl.when(step == 0)
    def _():
        total = first[...] + (own[...] + came[...])
        second[...] = total
        factor = lax.rsqrt(jnp.mean(total * total, axis=-1, keepdims=True) + norm_eps)
        normed[...] = (total * factor * gain[...]).astype(low_type)
        grad_normed[...] = jnp.zeros_like(grad_normed)

    lifted = dot_wide(normed[...], weight[...])
    square = lifted * lifted
    bent = jnp.tanh(gelu_scale * (lifted * (1.0 + gelu_cubic * square)))
    half_up = 0.5 * (1.0 + bent)
    both_active[...] = (lifted * half_up).astype(low_type)
    slope = half_up + (0.5 * gelu_scale) * lifted * (1.0 - bent * bent) * (1.0 + 3.0 * gelu_cubic * square)
    grad_lifted = (grad_active[...].astype(wide_type) * slope).astype(low_type)
    both_grad[...] = grad_lifted
    grad_normed[...] += dot_columns(grad_lifted, weight[...])


def feed_forward(first, own, came, gain, weight, grad_active):
    rows, width = first.shape
    hidden = weight.shape[1]
    block = 512
    still = pl.BlockSpec((rows, width), lambda j: (0, 0))
    moving = pl.BlockSpec((rows, block), lambda j: (0, j))
    return pl.pallas_call(
        feed_forward_kernel,
        grid=(hidden // block,),
        in_specs=[
            still,
            still,
            still,
            pl.BlockSpec((1, width), lambda j: (0, 0)),
            pl.BlockSpec((width, block), lambda j: (0, j)),
            moving,
        ],
        out_specs=[still, still, moving, moving, still],
        out_shape=[
            jax.ShapeDtypeStruct((rows, width), wide_type),
            jax.ShapeDtypeStruct((rows, width), low_type),
            jax.ShapeDtypeStruct((rows, hidden), low_type),
            jax.ShapeDtypeStruct((rows, hidden), low_type),
            jax.ShapeDtypeStruct((rows, width), wide_type),
        ],
        compiler_params=pltpu.CompilerParams(vmem_limit_bytes=vmem_budget),
        cost_estimate=heavy,
        name="feed_forward",
    )(first, own, came, gain, weight, grad_active)


def feed_close_kernel(
    second, own, came, gain, grad_out, weight, crossed_t, grad_second, gain_grad, grad_cross, heads_out,
    heads_out_t, inner, *, heads,
):
    values = second[...]
    incoming = (own[...] + came[...]).astype(low_type).astype(wide_type)
    factor = lax.rsqrt(jnp.mean(values * values, axis=-1, keepdims=True) + norm_eps)
    scaled = incoming * gain[...]
    inward = factor * scaled - values * (factor * factor * factor) * jnp.mean(
        scaled * values, axis=-1, keepdims=True
    )
    gain_grad[...] = jnp.broadcast_to(
        jnp.sum(incoming * values * factor, axis=0, keepdims=True), gain_grad.shape
    )
    total = inward + grad_out[...].astype(wide_type)
    grad_second[...] = total
    low = total.astype(low_type)
    grad_cross[...] = low
    made = dot_columns(low, weight[...])
    made_low = made.astype(low_type)
    made_t = made_low.astype(wide_type).T
    low_t = made_t.astype(low_type)
    left = lax.broadcasted_iota(jnp.int32, (made.shape[0], 128), 1) < HD
    inner[...] = jnp.zeros_like(inner)
    for head in range(heads):
        pair = made_low[:, head // 2 * 128 : head // 2 * 128 + 128]
        keep = left if head % 2 == 0 else jnp.logical_not(left)
        heads_out[head] = jnp.where(keep, pair, jnp.zeros_like(pair))
        rows = slice(head * HD, head * HD + HD)
        own_rows = slice(head % 2 * HD, head % 2 * HD + HD)
        other_rows = slice((1 - head % 2) * HD, (1 - head % 2) * HD + HD)
        heads_out_t[head, own_rows, :] = low_t[rows, :]
        heads_out_t[head, other_rows, :] = jnp.zeros_like(low_t[rows, :])
        inner[head : head + 1, :] = jnp.sum(made_t[rows, :] * crossed_t[rows, :], axis=0, keepdims=True)


def feed_close(second, own, came, gain, grad_out, weight, crossed_t):
    rows, width = second.shape
    half = weight.shape[0]
    heads = half // HD
    return pl.pallas_call(
        partial(feed_close_kernel, heads=heads),
        out_shape=[
            jax.ShapeDtypeStruct((rows, width), wide_type),
            jax.ShapeDtypeStruct((8, width), wide_type),
            jax.ShapeDtypeStruct((rows, width), low_type),
            jax.ShapeDtypeStruct((heads, rows, 128), low_type),
            jax.ShapeDtypeStruct((heads, 128, rows), low_type),
            jax.ShapeDtypeStruct((8, rows), wide_type),
        ],
        compiler_params=pltpu.CompilerParams(vmem_limit_bytes=vmem_budget),
        cost_estimate=heavy,
        name="feed_close",
    )(second, own, came, gain, grad_out, weight, crossed_t)


def feed_weights_kernel(normed, grad_out, grad_cross, grad_lifted, active, crossed, left, middle, right):
    third = left.shape[1]
    rest = grad_lifted.shape[1] - third
    left[...] = dot_rows(normed[...], grad_lifted[:, :third]).astype(low_type)
    middle[:, :rest] = dot_rows(normed[...], grad_lifted[:, third:]).astype(low_type)
    middle[:, rest:] = dot_rows(grad_out[...], active[:, : third - rest]).astype(low_type)
    right[:, : 2 * rest] = dot_rows(grad_out[...], active[:, third - rest :]).astype(low_type)
    right[:, 2 * rest :] = dot_rows(grad_cross[...], crossed[...]).astype(low_type)


def feed_weights(*args):
    width = args[0].shape[1]
    third = (2 * args[3].shape[1] + args[5].shape[1]) // 3
    return pl.pallas_call(
        feed_weights_kernel,
        out_shape=[jax.ShapeDtypeStruct((width, third), low_type)] * 3,
        compiler_params=pltpu.CompilerParams(vmem_limit_bytes=vmem_budget),
        cost_estimate=heavy,
        name="feed_weights",
    )(*args)


def cross_backward_kernel(
    facts, query, query_t, grad, grad_t, log_total, inner, pairs, key_weight, value_weight, pair_grads,
    row_grads, query_grad, held, *, chips, span, first
):
    step = pl.program_id(0)
    width, half = key_weight.shape

    @pl.when(step == 0)
    def _():
        query_grad[...] = jnp.zeros_like(query_grad)

    def work(live):
        block = pairs[...].reshape(chips * span, 2 * half)
        heads = half // HD

        def lanes(head, shift=0):
            return block[:, shift + head // 2 * 128 : shift + head // 2 * 128 + 128]

        def products(head):
            scores = dot_wide(lanes(head), query_t[head])
            if live is not None:
                scores = jnp.where(live, scores, masked_fill)
            return scores, dot_wide(lanes(head, half), grad_t[head])

        following = products(0)
        for pair in range(heads // 2):
            lows, low_grads = [], []
            for side in range(2):
                head = pair * 2 + side
                scores, grad_probs = following
                if head + 1 < heads:
                    following = products(head + 1)
                probs = jnp.exp(scores - log_total[head : head + 1, :])
                low_grads.append((probs * (grad_probs - inner[head : head + 1, :])).astype(low_type))
                lows.append(probs.astype(low_type))
                part = dot_rows(lanes(head), low_grads[-1])
                query_grad[head * HD : head * HD + HD, :] += part[side * HD : side * HD + HD, :]
            at = pair * 128
            both = slice(pair * 2, pair * 2 + 2)
            queries = query.shape[1]
            held[:, at : at + 128] = dot_wide(
                jnp.concatenate(low_grads, axis=1), query[both].reshape(2 * queries, 128)
            ).astype(low_type)
            held[:, half + at : half + at + 128] = dot_wide(
                jnp.concatenate(lows, axis=1), grad[both].reshape(2 * queries, 128)
            ).astype(low_type)
        made = held[...]
        pair_grads[...] = made.reshape(chips, span, 2 * half)
        back = dot_columns(made[:, :half], key_weight[...]) + dot_columns(made[:, half:], value_weight[...])
        row_grads[...] = back.astype(row_grads.dtype).reshape(chips, span, width)

    def dead():
        pair_grads[...] = jnp.zeros_like(pair_grads)
        row_grads[...] = jnp.zeros_like(row_grads)

    in_branches(facts, (step + first) * span, chips, span, work, dead)


def cross_backward(facts, query, query_t, grad, grad_t, log_total, inner, pairs, weight, grad_type, first, steps):
    chips, sub, both = pairs.shape
    width = weight.shape[0]
    heads, _, queries = query_t.shape
    span = chunk_of(chips, sub)
    half = both // 2
    rows = steps * span
    pair_block = slab((chips, rows, both), span)
    row_block = slab((chips, rows, width), span)
    return pl.pallas_call(
        partial(cross_backward_kernel, chips=chips, span=span, first=first),
        grid_spec=pltpu.PrefetchScalarGridSpec(
            num_scalar_prefetch=1,
            grid=(steps,),
            in_specs=[
                whole(query.shape),
                whole(query_t.shape),
                whole(grad.shape),
                whole(grad_t.shape),
                whole(log_total.shape),
                whole(inner.shape),
                slab(pairs.shape, span, first),
                pl.BlockSpec((width, half), lambda j, facts: (0, facts[2])),
                pl.BlockSpec((width, half), lambda j, facts: (0, 2 + facts[2])),
            ],
            out_specs=[pair_block, row_block, whole((heads * HD, queries))],
            scratch_shapes=[pltpu.VMEM((chips * span, both), low_type)],
        ),
        out_shape=[
            jax.ShapeDtypeStruct((chips, rows, both), low_type),
            jax.ShapeDtypeStruct((chips, rows, width), grad_type),
            jax.ShapeDtypeStruct((heads * HD, queries), wide_type),
        ],
        compiler_params=pltpu.CompilerParams(vmem_limit_bytes=room(chips)),
        cost_estimate=heavy,
        name="cross_backward",
    )(facts, query, query_t, grad, grad_t, log_total, inner, pairs, weight, weight)


def query_back_kernel(*refs):
    *parts, weight, grad, part = refs
    total = parts[0][...]
    for other in parts[1:]:
        total = total + other[...]
    low = (total * 0.125).T.astype(low_type)
    grad[...] = low
    part[...] = dot_columns(low, weight[...])


def query_back(parts, weight):
    half, rows = parts[0].shape
    return pl.pallas_call(
        query_back_kernel,
        out_shape=[
            jax.ShapeDtypeStruct((rows, half), low_type),
            jax.ShapeDtypeStruct((rows, weight.shape[0]), wide_type),
        ],
        compiler_params=pltpu.CompilerParams(vmem_limit_bytes=vmem_budget),
        cost_estimate=heavy,
        name="query_back",
    )(*parts, weight)


def memory_weights_kernel(facts, *refs, pieces, chips, span, steps):
    rows, other = refs[:2]
    sets = [refs[2 + 4 * piece : 6 + 4 * piece] for piece in range(pieces)]
    pair_out, keep_out, send_out, pair_sum, conv_sum = refs[2 + 4 * pieces :]
    step = pl.program_id(0)
    count = chips * span
    each = steps // pieces

    def flat(ref):
        return ref[...].reshape(count, ref.shape[-1])

    @pl.when(step == 0)
    def _():
        pair_sum[...] = jnp.zeros_like(pair_sum)
        conv_sum[...] = jnp.zeros_like(conv_sum)

    for piece, (hidden, pair_grads, row_grads, other_grads) in enumerate(sets):

        @pl.when((step >= piece * each) & (step < piece * each + each))
        def _(hidden=hidden, pair_grads=pair_grads, row_grads=row_grads, other_grads=other_grads):
            pair_sum[...] += dot_rows(flat(rows), flat(pair_grads)) + dot_rows(flat(other), flat(other_grads))
            conv_sum[...] += dot_rows(flat(hidden), flat(row_grads))

    @pl.when(step == steps - 1)
    def _():
        pair_out[...] = pair_sum[...].astype(low_type)
        half = keep_out.shape[1]
        first = facts[1] == 0
        keep_out[...] = jnp.where(first, conv_sum[:, :half], conv_sum[:, half:])
        send_out[...] = jnp.where(first, conv_sum[:, half:], conv_sum[:, :half]).astype(low_type)


def memory_weights(facts, rows, other, sets):
    chips, sub, width = rows.shape
    span = chunk_of(chips, sub)
    both = sets[0][1].shape[2]
    steps = sub // span
    pieces = len(sets)
    each = steps // pieces

    def piece_block(piece, columns):
        return pl.BlockSpec(
            (chips, span, columns), lambda j, facts: (0, jnp.clip(j - piece * each, 0, each - 1), 0)
        )

    in_specs = [slab(rows.shape, span), slab(other.shape, span)]
    for piece, arrays in enumerate(sets):
        in_specs += [piece_block(piece, array.shape[2]) for array in arrays]
    outs = (((width, both), low_type), ((width, width // 2), wide_type), ((width, width // 2), low_type))
    return pl.pallas_call(
        partial(memory_weights_kernel, pieces=pieces, chips=chips, span=span, steps=steps),
        grid_spec=pltpu.PrefetchScalarGridSpec(
            num_scalar_prefetch=1,
            grid=(steps,),
            in_specs=in_specs,
            out_specs=[whole(shape) for shape, _ in outs],
            scratch_shapes=[pltpu.VMEM((width, both), wide_type), pltpu.VMEM((width, width), wide_type)],
        ),
        out_shape=[jax.ShapeDtypeStruct(shape, kind) for shape, kind in outs],
        compiler_params=pltpu.CompilerParams(vmem_limit_bytes=room(chips)),
        cost_estimate=heavy,
        name="memory_weights",
    )(facts, rows, other, *[array for arrays in sets for array in arrays])


def side_weights_kernel(normed_one, grad_qkv, normed_two, grad_cq, grad_self, attended, first, second):
    half = attended.shape[1]
    cut = first.shape[1]
    first[...] = dot_rows(normed_one[...], grad_qkv[:, :cut]).astype(low_type)
    rest = 3 * half - cut
    second[:, :rest] = dot_rows(normed_one[...], grad_qkv[:, cut:]).astype(low_type)
    second[:, rest : rest + half] = dot_rows(normed_two[...], grad_cq[...]).astype(low_type)
    second[:, rest + half :] = dot_rows(grad_self[...], attended[...]).astype(low_type)


def side_weights(*args):
    width = args[0].shape[1]
    half = args[-1].shape[1]
    cut = 3 * half - 128
    return pl.pallas_call(
        side_weights_kernel,
        out_shape=[
            jax.ShapeDtypeStruct((width, cut), low_type),
            jax.ShapeDtypeStruct((width, 5 * half - cut), low_type),
        ],
        compiler_params=pltpu.CompilerParams(vmem_limit_bytes=vmem_budget),
        cost_estimate=heavy,
        name="side_weights",
    )(*args)


def product_kernel(left, right, out):
    @pl.when(pl.program_id(0) == 0)
    def _():
        out[...] = jnp.zeros_like(out)

    out[...] += dot_wide(left[...], right[...])


def product(left, right):
    rows, depth = left.shape
    width = right.shape[1]
    block = 512
    return pl.pallas_call(
        product_kernel,
        grid=(depth // block,),
        in_specs=[
            pl.BlockSpec((rows, block), lambda j: (0, j)),
            pl.BlockSpec((block, width), lambda j: (j, 0)),
        ],
        out_specs=pl.BlockSpec((rows, width), lambda j: (0, 0)),
        out_shape=jax.ShapeDtypeStruct((rows, width), wide_type),
        compiler_params=pltpu.CompilerParams(vmem_limit_bytes=vmem_budget),
        cost_estimate=heavy,
        name="product",
    )(left, right)


def back_through_norm(values, incoming, gain):
    factor = lax.rsqrt(jnp.mean(values * values, axis=-1, keepdims=True) + norm_eps)
    scaled = incoming * gain
    inward = factor * scaled - values * (factor * factor * factor) * jnp.mean(
        scaled * values, axis=-1, keepdims=True
    )
    return inward, jnp.sum(incoming * values * factor, axis=0, keepdims=True)


def self_forward_kernel(
    facts, rows_in, gain, weight, out_weight, normed_out, triple, attended, log_total, part, *, heads
):
    values = rows_in[...].astype(wide_type)
    factor = lax.rsqrt(jnp.mean(values * values, axis=-1, keepdims=True) + norm_eps)
    normed = (values * factor * gain[...]).astype(low_type)
    normed_out[...] = normed
    rows = values.shape[0]
    half = heads * HD
    for side in range(3):
        triple[:, side * half : side * half + half] = dot_wide(normed, weight[side]).astype(low_type)
    key_pos = lax.broadcasted_iota(jnp.int32, (rows, rows), 0)
    query_pos = lax.broadcasted_iota(jnp.int32, (rows, rows), 1)
    allowed = (key_pos <= query_pos) & (key_pos < facts[0])
    left = lax.broadcasted_iota(jnp.int32, (rows, 128), 1) < HD
    log_total[...] = jnp.zeros_like(log_total)
    for pair in range(heads // 2):
        lanes = slice(pair * 128, pair * 128 + 128)
        query_pair = triple[:, lanes]
        key_pair = triple[:, half + pair * 128 : half + pair * 128 + 128]
        value_pair = triple[:, 2 * half + pair * 128 : 2 * half + pair * 128 + 128]
        parts = []
        for side in range(2):
            head = pair * 2 + side
            keep = left if side == 0 else jnp.logical_not(left)
            query = jnp.where(keep, query_pair, jnp.zeros_like(query_pair))
            scores = jnp.where(allowed, dot_columns(key_pair, query) * 0.125, masked_fill)
            top = jnp.max(scores, axis=0, keepdims=True)
            weights = jnp.exp(scores - top)
            total = jnp.sum(weights, axis=0, keepdims=True)
            log_total[head : head + 1, :] = top + jnp.log(total)
            made = dot_rows(value_pair, (weights / total).astype(low_type))
            parts.append(made[side * HD : side * HD + HD, :])
        attended[:, lanes] = jnp.concatenate(parts).T.astype(low_type)
    part[...] = dot_wide(attended[...], out_weight[...])


def self_forward(facts, rows_in, gain, weight, out_weight):
    rows, width = rows_in.shape
    half = out_weight.shape[0]
    args = (rows_in, gain, weight, out_weight)
    outs = (
        ((rows, width), low_type),
        ((rows, 3 * half), low_type),
        ((rows, half), low_type),
        ((8, rows), wide_type),
        ((rows, width), wide_type),
    )
    return pl.pallas_call(
        partial(self_forward_kernel, heads=half // HD),
        grid_spec=pltpu.PrefetchScalarGridSpec(
            num_scalar_prefetch=1,
            grid=(1,),
            in_specs=[whole(arg.shape) for arg in args],
            out_specs=[whole(shape) for shape, _ in outs],
        ),
        out_shape=[jax.ShapeDtypeStruct(shape, kind) for shape, kind in outs],
        compiler_params=pltpu.CompilerParams(vmem_limit_bytes=vmem_budget),
        cost_estimate=heavy,
        name="self_forward",
    )(facts, *args)


def query_forward_kernel(rows_in, own, came, gain, weight, first, normed_out, heads_out, heads_out_t, *, heads):
    total = rows_in[...].astype(wide_type) + (own[...] + came[...])
    first[...] = total
    factor = lax.rsqrt(jnp.mean(total * total, axis=-1, keepdims=True) + norm_eps)
    normed = (total * factor * gain[...]).astype(low_type)
    normed_out[...] = normed
    query = (dot_wide(normed, weight[...]).astype(low_type).astype(wide_type) * 0.125).astype(low_type)
    turned = query.T
    left = lax.broadcasted_iota(jnp.int32, (query.shape[0], 128), 1) < HD
    for head in range(heads):
        pair = query[:, head // 2 * 128 : head // 2 * 128 + 128]
        keep = left if head % 2 == 0 else jnp.logical_not(left)
        heads_out[head] = jnp.where(keep, pair, jnp.zeros_like(pair))
        own_rows = slice(head % 2 * HD, head % 2 * HD + HD)
        other_rows = slice((1 - head % 2) * HD, (1 - head % 2) * HD + HD)
        mine = turned[head * HD : head * HD + HD, :]
        heads_out_t[head, own_rows, :] = mine
        heads_out_t[head, other_rows, :] = jnp.zeros_like(mine)


def query_forward(rows_in, own, came, gain, weight):
    rows, width = rows_in.shape
    heads = weight.shape[1] // HD
    outs = (
        ((rows, width), wide_type),
        ((rows, width), low_type),
        ((heads, rows, 128), low_type),
        ((heads, 128, rows), low_type),
    )
    return pl.pallas_call(
        partial(query_forward_kernel, heads=heads),
        out_shape=[jax.ShapeDtypeStruct(shape, kind) for shape, kind in outs],
        compiler_params=pltpu.CompilerParams(vmem_limit_bytes=vmem_budget),
        cost_estimate=heavy,
        name="query_forward",
    )(rows_in, own, came, gain, weight)


def self_backward_kernel(
    facts, values, own, came, gain, grad_second, out_weight, triple, log_total, weight,
    grad_first, grad_low, gain_grad, triple_grad, part, *, heads,
):
    rows = triple.shape[0]
    half = heads * HD
    incoming = (own[...] + came[...]).astype(low_type).astype(wide_type)
    inward, gain_row = back_through_norm(values[...], incoming, gain[...])
    gain_grad[...] = jnp.broadcast_to(gain_row, gain_grad.shape)
    total = inward + grad_second[...]
    grad_first[...] = total
    grad_low[...] = total.astype(low_type)
    grad = dot_columns(grad_low[...], out_weight[...]).astype(low_type)
    key_pos = lax.broadcasted_iota(jnp.int32, (rows, rows), 0)
    query_pos = lax.broadcasted_iota(jnp.int32, (rows, rows), 1)
    allowed = (key_pos <= query_pos) & (key_pos < facts[0])
    left = lax.broadcasted_iota(jnp.int32, (rows, 128), 1) < HD
    for pair in range(heads // 2):
        lanes = slice(pair * 128, pair * 128 + 128)
        query_pair = triple[:, lanes]
        key_pair = triple[:, half + pair * 128 : half + pair * 128 + 128]
        value_pair = triple[:, 2 * half + pair * 128 : 2 * half + pair * 128 + 128]
        grad_pair = grad[:, lanes]
        key_sum, value_sum, query_parts = 0.0, 0.0, []
        for side in range(2):
            head = pair * 2 + side
            keep = left if side == 0 else jnp.logical_not(left)
            query = jnp.where(keep, query_pair, jnp.zeros_like(query_pair))
            grad_head = jnp.where(keep, grad_pair, jnp.zeros_like(grad_pair))
            scores = dot_columns(key_pair, query) * 0.125
            probs = jnp.exp(jnp.where(allowed, scores, masked_fill) - log_total[head : head + 1, :])
            grad_probs = dot_columns(value_pair, grad_head)
            inner = jnp.sum(probs * grad_probs, axis=0, keepdims=True)
            grad_scores = (probs * (grad_probs - inner)).astype(low_type)
            value_sum = value_sum + dot_wide(probs.astype(low_type), grad_head)
            key_sum = key_sum + dot_wide(grad_scores, query)
            query_parts.append(dot_rows(key_pair, grad_scores)[side * HD : side * HD + HD, :])
        triple_grad[:, lanes] = (jnp.concatenate(query_parts) * 0.125).T.astype(low_type)
        triple_grad[:, half + pair * 128 : half + pair * 128 + 128] = (key_sum * 0.125).astype(low_type)
        triple_grad[:, 2 * half + pair * 128 : 2 * half + pair * 128 + 128] = value_sum.astype(low_type)
    part[...] = (
        dot_columns(triple_grad[:, :half], weight[0])
        + dot_columns(triple_grad[:, half : 2 * half], weight[1])
        + dot_columns(triple_grad[:, 2 * half :], weight[2])
    )


def self_backward(facts, values, own, came, gain, grad_second, out_weight, triple, log_total, weight):
    rows, wide = triple.shape
    width = weight.shape[1]
    args = (values, own, came, gain, grad_second, out_weight, triple, log_total, weight)
    outs = (
        ((rows, width), wide_type),
        ((rows, width), low_type),
        ((8, width), wide_type),
        ((rows, wide), low_type),
        ((rows, width), wide_type),
    )
    return pl.pallas_call(
        partial(self_backward_kernel, heads=wide // (3 * HD)),
        grid_spec=pltpu.PrefetchScalarGridSpec(
            num_scalar_prefetch=1,
            grid=(1,),
            in_specs=[whole(arg.shape) for arg in args],
            out_specs=[whole(shape) for shape, _ in outs],
        ),
        out_shape=[jax.ShapeDtypeStruct(shape, kind) for shape, kind in outs],
        compiler_params=pltpu.CompilerParams(vmem_limit_bytes=vmem_budget),
        cost_estimate=heavy,
        name="self_backward",
    )(facts, *args)


def input_back_kernel(
    values, own, came, gain, grad_first, second, result_own, result_came, act_sums, cross_gain_grad,
    ffn_gain_grad, input_grad, layer_out, gains_out,
):
    incoming = (own[...] + came[...]).astype(low_type).astype(wide_type)
    inward, gain_row = back_through_norm(values[...].astype(wide_type), incoming, gain[...])
    input_grad[...] = inward + grad_first[...]
    layer_out[...] = (second[...] + (result_own[...] + result_came[...])).astype(low_type)
    width = values.shape[1]
    gains = jnp.concatenate(
        (
            act_sums[1:2, :],
            act_sums[0:1, :],
            0.5 * gain_row,
            0.5 * cross_gain_grad[0:1, :],
            0.5 * ffn_gain_grad[0:1, :],
            jnp.zeros((3, width), wide_type),
        )
    )
    for tile in range(width // 128):
        gains_out[tile] = gains[:, tile * 128 : tile * 128 + 128]


def input_back(*args):
    rows, width = args[0].shape
    outs = (((rows, width), wide_type), ((rows, width), low_type), ((width // 128, 8, 128), wide_type))
    return pl.pallas_call(
        input_back_kernel,
        out_shape=[jax.ShapeDtypeStruct(shape, kind) for shape, kind in outs],
        compiler_params=pltpu.CompilerParams(vmem_limit_bytes=vmem_budget),
        cost_estimate=heavy,
        name="input_back",
    )(*args)


def assemble_kernel(
    facts, memory, memory_came, own, other, left, middle, right, gains, conv, cross_kv,
    cross_out, self_qkv, cross_query, self_out, ffn_in, ffn_out, *gain_outs,
):
    width = conv.shape[1]
    half = width // 2
    third = left.shape[1]
    hidden = ffn_in.shape[1]
    first = facts[1] == 0
    conv[:, :half] = jnp.where(first, memory[:, width:], memory_came[:, width:])
    conv[:, half:] = jnp.where(first, memory_came[:, width:], memory[:, width:])
    for side in range(2):
        mine = memory[:, side * half : side * half + half]
        theirs = memory_came[:, side * half : side * half + half]
        cross_kv[:, side, :half] = jnp.where(first, mine, theirs)
        cross_kv[:, side, half:] = jnp.where(first, theirs, mine)
    rest = 3 * half - own.shape[1]
    self_qkv[0] = own[:, :half]
    self_qkv[1] = own[:, half : 2 * half]
    self_qkv[2, :, : half - rest] = own[:, 2 * half :]
    self_qkv[2, :, half - rest :] = other[:, :rest]
    cross_query[...] = other[:, rest : rest + half]
    self_out[...] = other[:, rest + half :]
    ffn_in[:, :third] = left[...]
    ffn_in[:, third:] = middle[:, : hidden - third]
    ffn_out[:, : 2 * third - hidden] = middle[:, hidden - third :]
    ffn_out[:, 2 * third - hidden :] = right[:, : 2 * hidden - 2 * third]
    cross_out[...] = right[:, 2 * hidden - 2 * third :]
    share = conv.shape[0]
    picked = (
        lax.broadcasted_iota(jnp.int32, (width, share), 0)
        == lax.broadcasted_iota(jnp.int32, (width, share), 1) + facts[0] * share
    ).astype(wide_type)
    first_tile = gains.shape[0] - width // 128
    rows_of = jnp.concatenate([gains[first_tile + tile] for tile in range(width // 128)], axis=1)
    mine = jnp.dot(rows_of, picked, precision=lax.Precision.HIGHEST)
    for number, out in enumerate(gain_outs):
        out[...] = mine[number : number + 1, :]


def assemble(facts, *args):
    share = args[0].shape[0]
    width = 2 * args[0].shape[1] // 3
    half = width // 2
    hidden = (3 * args[4].shape[1] - half) // 2
    outs = (
        (share, width),
        (share, 2, width),
        (share, half),
        (3, share, half),
        (share, half),
        (share, half),
        (share, hidden),
        (share, hidden),
    ) + ((1, share),) * 5
    return pl.pallas_call(
        assemble_kernel,
        grid_spec=pltpu.PrefetchScalarGridSpec(
            num_scalar_prefetch=1,
            grid=(1,),
            in_specs=[whole(arg.shape) for arg in args],
            out_specs=[whole(shape) for shape in outs],
        ),
        out_shape=[jax.ShapeDtypeStruct(shape, wide_type) for shape in outs],
        compiler_params=pltpu.CompilerParams(vmem_limit_bytes=vmem_budget),
        cost_estimate=heavy,
        name="assemble",
    )(facts, *args)


def shards(
    dec_input,
    out_grad,
    enc_feats,
    mem_lengths,
    dec_lengths,
    doc_owner,
    group_gain,
    group_bias,
    conv_weight,
    cross_kv,
    self_gain,
    self_qkv,
    self_out,
    cross_gain,
    cross_query,
    cross_out,
    ffn_gain,
    ffn_in,
    ffn_out,
):
    chips = lax.axis_size("dp")
    chip_index = lax.axis_index("dp")
    core_index = lax.axis_index("mp")
    memory_in = enc_feats[0, 0]
    docs, sub, width = memory_in.shape
    per_group = width // GROUPS
    half = width // 2
    heads = half // HD
    rows_here = docs * sub
    share = width // chips
    bits = chips.bit_length() - 1
    rest = tuple(range(4, bits))
    order_sets = {
        "stats": (0, 1, 2, 3),
        "left": (2, 3, 0, 1),
        "middle": (0, 2, 3, 1),
        "right": (1, 0, 2, 3),
        "first": (0, 1, 2, 3),
        "second": (2, 0, 1, 3),
        "memory": (1, 2, 0, 3),
    }
    orders = {
        name: order + rest if bits >= 4 else tuple(range(bits)) for name, order in order_sets.items()
    }

    outgoing = gather_docs(memory_in, doc_owner)
    features = lax.all_to_all(outgoing, "dp", split_axis=0, concat_axis=0, tiled=True)
    outgoing, dec_input = tie((outgoing, dec_input))
    dec_rows = DEC
    dec_rows_in = dec_input.reshape(dec_rows, width)
    self_facts = dec_lengths[chip_index][None]
    self_weight = self_qkv.transpose(1, 0, 2)
    normed_one, qkv_self, attended, self_totals, part = self_forward(
        self_facts, dec_rows_in, self_gain[None], self_weight, self_out
    )
    part_came = other_core(part)
    memory_here, part = tie((memory_in, part))
    wide_in = memory_here.astype(wide_type)
    slot_pos = lax.broadcasted_iota(jnp.int32, (docs, sub), 1)
    live_in = ((slot_pos * 2 + core_index) * chips + chip_index < mem_lengths[:, None])[:, :, None]
    masked_in = jnp.where(live_in, wide_in, 0.0)
    channel_sums = jnp.stack((jnp.sum(masked_in, axis=1), jnp.sum(masked_in * wide_in, axis=1)), axis=1)
    group_of = (
        lax.broadcasted_iota(jnp.int32, (width, GROUPS), 0) // per_group
        == lax.broadcasted_iota(jnp.int32, (width, GROUPS), 1)
    ).astype(wide_type)

    def group_sums(channels):
        return jnp.dot(channels, group_of, precision=lax.Precision.HIGHEST)

    def to_channels(groups):
        return jnp.dot(groups, group_of.T, precision=lax.Precision.HIGHEST)

    sums_here = group_sums(channel_sums.reshape(docs * 2, width)).reshape(docs, 2 * GROUPS)
    sums_here = jnp.take(sums_here, doc_owner, axis=0, mode="clip")
    stat_sums = ScatterSums([core_total(sums_here)], [orders["stats"]], chip_index)
    stat_sums.begin()

    def next_step(sums, value):
        value = sums.behind(value)
        sums.merge()
        if sums.orders[0]:
            sums.begin()
            value = sums.ahead_of(value)
            sums.send()
        return value

    part_came = stat_sums.ahead_of(part_came)
    stat_sums.send()
    first_out, normed_two, query_heads, query_heads_t = query_forward(
        dec_rows_in, part, part_came, cross_gain[None], cross_query
    )
    cross_kv, query_heads = next_step(stat_sums, (cross_kv, query_heads))
    pair_weight = prepare_weights(cross_kv)
    pair_weight, query_heads = next_step(stat_sums, (pair_weight, query_heads))
    grad_low, query_heads, pair_weight = tie((out_grad.reshape(DEC, width), query_heads, pair_weight))
    grad_active = dot_columns(grad_low, ffn_out).astype(low_type)
    document = doc_owner[chip_index]
    length = mem_lengths[document]
    facts_own = jnp.stack((length, core_index, core_index, 1)).astype(jnp.int32)
    facts_other = jnp.stack((length, 1 - core_index, core_index, 0)).astype(jnp.int32)
    grad_active, query_heads, facts_own, facts_other = tie((grad_active, query_heads, facts_own, facts_other))
    while stat_sums.orders[0]:
        query_heads = next_step(stat_sums, query_heads)
    sums_all = stat_sums.current[0]

    entries = (length * per_group).astype(wide_type)
    center = sums_all[:GROUPS] / entries
    spread = lax.rsqrt(sums_all[GROUPS:] / entries - center * center + group_eps)
    channel_stats = to_channels(jnp.stack((center, spread)))
    stats = jnp.concatenate(
        (channel_stats, group_gain[None], group_bias[None], jnp.zeros((4, width), wide_type))
    )

    features, stats, query_heads, query_heads_t = tie((features, stats, query_heads, query_heads_t))
    memory_own = memory_forward(facts_own, features, stats, conv_weight)
    memory_other = other_core(memory_own)

    carry = (
        jnp.full((8, dec_rows), -1e30, wide_type),
        jnp.zeros((8, dec_rows), wide_type),
        jnp.zeros((half, dec_rows), wide_type),
    )
    pairs_own, *carry = cross_forward(
        facts_own, query_heads_t, memory_own, pair_weight, carry
    )
    pairs_other, top, total, gathered = cross_forward(
        facts_other, query_heads_t, memory_other, pair_weight, carry
    )
    crossed, crossed_t, log_total, part = cross_close(gathered, top, total, cross_out)

    second_out, normed_three, grad_lifted, active, part = feed_forward(
        first_out, part, other_core(part), ffn_gain[None], ffn_in, grad_active
    )
    part_came = other_core(part)
    result_part = product(active, ffn_out)
    part_came, result_part = tie((part_came, result_part))
    result_came = other_core(result_part)
    grad_second, ffn_gain_grad, grad_cross, grad_heads, grad_heads_t, inner = feed_close(
        second_out, part, part_came, ffn_gain[None], grad_low, cross_out, crossed_t
    )
    feed_grads = feed_weights(normed_three, grad_low, grad_cross, grad_lifted, active, crossed)
    feed_sums = Sums.of(
        [grad.reshape(chips, share, grad.shape[1]) for grad in feed_grads],
        [orders["left"], orders["middle"], orders["right"]],
        chip_index,
    )
    inner = feed_sums.start(inner)

    steps = sub // chunk_of(chips, sub)
    place = jnp.concatenate((jnp.stack((chip_index, core_index)).astype(jnp.int32), mem_lengths))
    pair_other, row_other, query_other = cross_backward(
        facts_other, query_heads, query_heads_t, grad_heads, grad_heads_t, log_total, inner, pairs_other, pair_weight,
        low_type, 0, steps,
    )
    facts_two, query_other = feed_sums.round((facts_own, query_other))
    row_came = other_core(row_other)
    pair_own, row_own, query_own = cross_backward(
        facts_two, query_heads, query_heads_t, grad_heads, grad_heads_t, log_total, inner, pairs_own, pair_weight,
        wide_type, 0, steps,
    )

    facts_three, query_own = feed_sums.round((facts_own, query_own))
    grad_memory, hidden, base, act_sums, groups = memory_backward(
        facts_three, features, row_own, row_came, stats, conv_weight, jnp.zeros((8, width), wide_type), 0
    )
    queries, sets = (query_other, query_own), [(hidden, pair_own, grad_memory, pair_other)]

    def dp_hop(value, bit):
        return lax.ppermute(value, "dp", [(chip, chip ^ (1 << bit)) for chip in range(chips)])

    feed_came, base, queries = tie(([part.came for part in feed_sums.parts], base, queries))
    for part, arrived in zip(feed_sums.parts, feed_came):
        part.came = arrived
    returned = [lax.all_to_all(base, "dp", split_axis=0, concat_axis=0, tiled=True)]

    def when_live(work):
        return lax.cond(length > 0, work, nothing_like(work))

    def self_work():
        own_slot = lax.broadcasted_iota(jnp.int32, (chips, 1, 1), 0) == chip_index
        document_groups = jnp.where(own_slot, core_total(groups)[None], 0.0)

        grad_cq, part = query_back(queries, cross_query)
        part_came = other_core(part)
        grad_first, grad_self, cross_gain_grad, grad_qkv, part_one = self_backward(
            self_facts, first_out, part, part_came, cross_gain[None], grad_second, self_out, qkv_self, self_totals,
            self_weight,
        )
        part_one_came = other_core(part_one)
        first_part, second_part = side_weights(normed_one, grad_qkv, normed_two, grad_cq, grad_self, attended)
        part_one_came, first_part = tie((part_one_came, first_part))
        return grad_first, cross_gain_grad, part_one, part_one_came, document_groups, (first_part, second_part)

    queries = feed_sums.round(queries)
    early_feed, late_feed = Sums(feed_sums.parts[:2], chip_index), Sums(feed_sums.parts[2:], chip_index)
    grad_first, cross_gain_grad, part_one, part_one_came, document_groups, late_parts = when_live(self_work)
    while early_feed.going:
        document_groups = early_feed.round(document_groups)
    late_sums = Sums.of(
        [part.reshape(chips, share, -1) for part in late_parts], [orders["first"], orders["second"]], chip_index
    )
    document_groups = late_sums.start(document_groups)

    def memory_work():
        pair_part, conv_keep, conv_send = memory_weights(place, memory_own, memory_other, sets)
        conv_came = other_core(conv_send)
        came, conv_keep = tie((part_one_came, conv_keep))
        input_grad, layer_out, gains = input_back(
            dec_rows_in, part_one, came, self_gain[None], grad_first, second_out, result_part, result_came, act_sums,
            cross_gain_grad, ffn_gain_grad,
        )
        gains, conv_came = tie((gains, conv_came))
        conv_part = (conv_keep + conv_came.astype(wide_type)).astype(low_type)
        return input_grad, layer_out, core_total(gains), jnp.concatenate((pair_part, conv_part), axis=1)

    input_grad, layer_out, small, memory_part = when_live(memory_work)

    memory_sums = Sums.of([memory_part.reshape(chips, share, -1)], [orders["memory"]], chip_index)
    small = memory_sums.start(small)
    late_sums = late_sums.joined(memory_sums)
    all_sums = late_feed.joined(late_sums)
    hop = 0
    moved = memory_grad = None
    while all_sums.going:
        small_came = dp_hop(small, hop) if hop < bits else None
        for bit in ((0,), (1, 2), range(3, bits))[hop] if hop < 3 else ():
            document_groups = document_groups + dp_hop(document_groups, bit)
        value = (small_came, document_groups)
        if hop == 2:
            moved = moved_rows(doc_owner, place, memory_in, document_groups)
            value = (small_came, moved)
        if hop == 3:
            memory_grad = spread_docs(returned, moved, doc_owner)
            value = (small_came, memory_grad)
        if hop == 0:
            returned, small_came = tie((returned, small_came))
            value = (small_came, document_groups)
        small_came, value = all_sums.round(value)
        if hop < bits:
            small = small + small_came
        if hop < 2:
            document_groups = value
        elif hop == 2:
            moved = value
        elif hop == 3:
            memory_grad = value
        hop += 1
    while hop < bits:
        small = small + dp_hop(small, hop)
        hop += 1
    if moved is None:
        moved = moved_rows(doc_owner, place, memory_in, document_groups)
    if memory_grad is None:
        memory_grad = spread_docs(returned, moved, doc_owner)
    first_total, second_total, memory_total = late_sums.totals
    memory_came = other_core(memory_total)
    weight_grads = assemble(
        place, memory_total, memory_came, first_total, second_total, *feed_sums.totals, small
    )
    conv_grad, cross_kv_grad, cross_out_grad, self_qkv_grad, cross_query_grad, self_out_grad = weight_grads[:6]
    ffn_in_grad, ffn_out_grad = weight_grads[6:8]
    gains = [gain.reshape(share) for gain in weight_grads[8:]]
    return (
        layer_out.reshape(1, DEC, width),
        input_grad.reshape(1, DEC, width),
        memory_grad.reshape(1, 1, docs, sub, width),
        gains[0],
        gains[1],
        conv_grad,
        cross_kv_grad,
        gains[2],
        self_qkv_grad.transpose(1, 0, 2),
        self_out_grad.T,
        gains[3],
        cross_query_grad,
        cross_out_grad.T,
        gains[4],
        ffn_in_grad,
        ffn_out_grad.T,
    )


def solution(mesh):
    placed = (
        P("dp", None, None),
        P("dp", None, None),
        P("dp", "mp", None, None, None),
        P(),
        P(),
        P(),
        P(),
        P(),
        P(),
        P(),
        P(),
        P(None, None, "mp"),
        P("mp", None),
        P(),
        P(None, "mp"),
        P("mp", None),
        P(),
        P(None, "mp"),
        P("mp", None),
    )
    return jax.shard_map(
        shards,
        mesh=mesh,
        in_specs=placed,
        out_specs=(
            P("dp", None, None),
            P("dp", None, None),
            P("dp", "mp", None, None, None),
            P("dp"),
            P("dp"),
            P("dp", None),
            P("dp", None, None),
            P("dp"),
            P("dp", None, "mp"),
            P("mp", "dp"),
            P("dp"),
            P("dp", "mp"),
            P("mp", "dp"),
            P("dp"),
            P("dp", "mp"),
            P("mp", "dp"),
        ),
        check_vma=False,
    )
```

```python
from functools import partial

import jax
import jax.numpy as jnp
from jax import lax
from jax.experimental import pallas as pl
from jax.experimental.pallas import tpu as pltpu
from jax.sharding import PartitionSpec as P

HD = 64
GROUPS = 32
DEC = 512


norm_eps = 1e-06
group_eps = 1e-05
masked_fill = -1000000000.0
largest_sum = 1e17
vmem_budget = 16 * 1024 * 1024
vmem_large = 48 * 1024 * 1024


def room(chips):
    return vmem_budget if chips <= 16 else vmem_large


heavy = pl.CostEstimate(flops=10**10, bytes_accessed=10**7, transcendentals=10**7)
low_type = jnp.bfloat16
wide_type = jnp.float32


def dot_wide(left, right):
    return jnp.dot(left, right, preferred_element_type=wide_type)


def dot_rows(left, right):
    return lax.dot_general(left, right, (((0,), (0,)), ((), ())), preferred_element_type=wide_type)


def dot_columns(left, right):
    return lax.dot_general(left, right, (((1,), (1,)), ((), ())), preferred_element_type=wide_type)


def norm_rows(values, gain):
    factor = lax.rsqrt(jnp.mean(values * values, axis=-1, keepdims=True) + norm_eps)
    return (values * factor * gain, factor)


def norm_rows_back(values, factor, gain, incoming):
    scaled = incoming * gain
    inward = factor * scaled - values * factor * factor * factor * jnp.mean(
        scaled * values, axis=-1, keepdims=True
    )
    gain_grad = jnp.sum(incoming * values * factor, axis=0)
    return (inward, gain_grad)


def other_core(values):
    return lax.ppermute(values, "mp", [(0, 1), (1, 0)])


def core_total(partial_sum):
    return partial_sum + other_core(partial_sum)


tie = lax.optimization_barrier


class ScatterSums:
    def __init__(self, arrays, orders, chip_index):
        chips = arrays[0].shape[0]
        self.chip_index = chip_index
        self.bits = chips.bit_length() - 1
        self.orders = [list(order) for order in orders]
        self.left = [list(range(self.bits - 1, -1, -1)) for _ in arrays]
        self.current = [array.reshape((2,) * self.bits + array.shape[1:]) for array in arrays]
        self.kept = self.sent = self.came = None

    def copied(self):
        other = object.__new__(ScatterSums)
        other.chip_index, other.bits = self.chip_index, self.bits
        other.orders = [list(order) for order in self.orders]
        other.left = [list(left) for left in self.left]
        other.current, other.kept, other.sent, other.came = self.current, self.kept, self.sent, self.came
        return other

    def begin(self):
        self.kept, self.sent = [], []
        for number, order in enumerate(self.orders):
            axis = self.left[number].index(order[0])
            mine = (self.chip_index >> order[0]) & 1
            self.sent.append(lax.dynamic_index_in_dim(self.current[number], 1 - mine, axis, False))
            self.kept.append(lax.dynamic_index_in_dim(self.current[number], mine, axis, False))
            self.left[number].pop(axis)

    def ahead_of(self, value):
        self.sent, value = tie((self.sent, value))
        return value

    def send(self):
        chips = 1 << self.bits
        self.came = [
            lax.ppermute(sent, "dp", [(chip, chip ^ (1 << order[0])) for chip in range(chips)])
            for sent, order in zip(self.sent, self.orders)
        ]

    def behind(self, value):
        self.came, value = tie((self.came, value))
        return value

    def merge(self):
        merged = []
        for number, order in enumerate(self.orders):
            total = self.kept[number].astype(wide_type) + self.came[number].astype(wide_type)
            order.pop(0)
            merged.append(total.astype(self.current[number].dtype) if order else total)
        self.current = merged

    def step(self):
        self.begin()
        self.send()
        self.merge()

    def finish(self):
        while self.orders[0]:
            self.step()
        return self.current


def merge_kernel(facts, *refs, plans):
    count = len(plans)
    outs = list(refs[2 * count :])
    for plan, kept, came in zip(plans, refs[:count], refs[count : 2 * count]):
        entries, after, turn = plan["entries"], plan["after"], plan["turn"]

        def total(entry, kept=kept, came=came, after=after):
            own = kept[entry] if after is None else kept[entry >> after, 0, entry & ((1 << after) - 1)]
            return own.astype(wide_type) + came[entry].astype(wide_type)

        if turn is None:
            outs.pop(0)[...] = total(0)
            continue
        sent_out, kept_out = outs.pop(0), outs.pop(0)
        bit, behind = turn
        mine = (facts[0] >> bit) & 1
        for place in range(entries // 2):
            base = (place >> behind << (behind + 1)) | (place & ((1 << behind) - 1))
            kept_out[place] = total(base + (mine << behind)).astype(low_type)
            sent_out[place] = total(base + ((1 - mine) << behind)).astype(low_type)


class Part:
    def __init__(self, array, order):
        self.kept, self.order = array, order
        self.sent = self.came = self.total = None
        self.step = 0
        self.left = tuple(range(len(order) - 1, -1, -1))

    def copied(self):
        other = object.__new__(Part)
        other.__dict__.update(self.__dict__)
        return other


class Sums:
    def __init__(self, parts, chip_index):
        self.parts, self.chip_index = parts, chip_index

    @staticmethod
    def of(arrays, orders, chip_index):
        return Sums([Part(array, order) for array, order in zip(arrays, orders)], chip_index)

    def copied(self):
        return Sums([part.copied() for part in self.parts], self.chip_index)

    def joined(self, *others):
        return Sums([part for sums in (self, *others) for part in sums.parts], self.chip_index)

    def state(self):
        return [(part.kept, part.came) for part in self.parts]

    def stepped(self):
        other = self.copied()
        for part in other.parts:
            part.left = tuple(bit for bit in part.left if bit != part.order[part.step])
            part.step += 1
        return other

    def with_state(self, state):
        other = self.copied()
        for part, (kept, came) in zip(other.parts, state):
            part.kept, part.came = kept, came
        return other

    @property
    def going(self):
        return [part for part in self.parts if part.total is None]

    @property
    def totals(self):
        return [part.total for part in self.parts]

    def start(self, value):
        for part in self.parts:
            chips = part.kept.shape[0]
            behind = part.order[0]
            ahead = len(part.order) - 1 - behind
            view = part.kept.reshape((1 << ahead, 2, 1 << behind) + part.kept.shape[1:])
            mine = (self.chip_index >> behind) & 1
            sent = lax.dynamic_index_in_dim(view, 1 - mine, 1, False)
            part.sent = sent.reshape((chips // 2,) + part.kept.shape[1:])
            part.kept = view
        return self.leave(self.parts, value)

    def leave(self, parts, value):
        sent, value = tie(([part.sent for part in parts], value))
        for part, leaving in zip(parts, sent):
            chips = 1 << len(part.order)
            bit = part.order[part.step]
            part.came = lax.ppermute(leaving, "dp", [(chip, chip ^ (1 << bit)) for chip in range(chips)])
        return value

    def round(self, value):
        parts = self.going
        came, value = tie(([part.came for part in parts], value))
        plans, in_specs, out_specs, out_shape = [], [], [], []
        for part, arrived in zip(parts, came):
            part.came = arrived
            entries, rows, columns = arrived.shape
            kept, bit = part.kept, part.order[part.step]
            if part.step == 0:
                in_specs.append(
                    pl.BlockSpec(
                        (kept.shape[0], 1) + kept.shape[2:],
                        lambda j, facts, bit=bit: (0, (facts[0] >> bit) & 1, 0, 0, 0),
                    )
                )
            else:
                in_specs.append(whole(kept.shape))
            plan = {"entries": entries, "after": bit if part.step == 0 else None, "turn": None}
            part.left = tuple(other for other in part.left if other != bit)
            if part.left:
                following = part.order[part.step + 1]
                plan["turn"] = (following, len(part.left) - 1 - part.left.index(following))
                half = (entries // 2, rows, columns)
                out_specs += [whole(half)] * 2
                out_shape += [jax.ShapeDtypeStruct(half, low_type)] * 2
            else:
                out_specs.append(whole((rows, columns)))
                out_shape.append(jax.ShapeDtypeStruct((rows, columns), wide_type))
            plans.append(plan)
        in_specs += [whole(part.came.shape) for part in parts]
        made = pl.pallas_call(
            partial(merge_kernel, plans=plans),
            grid_spec=pltpu.PrefetchScalarGridSpec(
                num_scalar_prefetch=1, grid=(1,), in_specs=in_specs, out_specs=out_specs
            ),
            out_shape=out_shape,
            compiler_params=pltpu.CompilerParams(vmem_limit_bytes=room(1 << len(parts[0].order))),
            cost_estimate=heavy,
            name="merge_sums",
        )(
            self.chip_index[None].astype(jnp.int32),
            *[part.kept for part in parts],
            *[part.came for part in parts],
        )
        made = list(made)
        for part in parts:
            part.step += 1
            if part.left:
                part.sent, part.kept = made.pop(0), made.pop(0)
            else:
                part.total = made.pop(0)
        parts = [part for part in parts if part.left]
        return self.leave(parts, value) if parts else value


def nothing_like(work):
    def nothing():
        return jax.tree.map(lambda leaf: jnp.zeros(leaf.shape, leaf.dtype), jax.eval_shape(work))

    return nothing


def gather_kernel(owner, rows, out, done, *, docs):
    copies = [pltpu.make_async_copy(rows.at[owner[slot]], out.at[slot], done.at[slot]) for slot in range(docs)]
    for copy in copies:
        copy.start()
    for copy in copies:
        copy.wait()


def gather_docs(memory_in, doc_owner):
    docs = memory_in.shape[0]
    return pl.pallas_call(
        partial(gather_kernel, docs=docs),
        grid_spec=pltpu.PrefetchScalarGridSpec(
            num_scalar_prefetch=1,
            grid=(),
            in_specs=[pl.BlockSpec(memory_space=pltpu.VMEM)],
            out_specs=pl.BlockSpec(memory_space=pl.ANY),
            scratch_shapes=[pltpu.SemaphoreType.DMA((docs,))],
        ),
        out_shape=pltpu.HBM(memory_in.shape, low_type),
        compiler_params=pltpu.CompilerParams(vmem_limit_bytes=vmem_budget),
        cost_estimate=heavy,
        name="gather_docs",
    )(doc_owner, memory_in)


def prepare_kernel(cross_kv, pair):
    width = cross_kv.shape[0]
    for side in range(2):
        pair[:, side * width : side * width + width] = cross_kv[:, side, :]


def prepare_weights(cross_kv):
    width = cross_kv.shape[0]
    return pl.pallas_call(
        prepare_kernel,
        out_shape=jax.ShapeDtypeStruct((width, 2 * width), low_type),
        compiler_params=pltpu.CompilerParams(vmem_limit_bytes=vmem_budget),
        cost_estimate=heavy,
        name="prepare_weights",
    )(cross_kv)


def moved_kernel(owner, facts, features, groups, out, stats, *, chips, count):
    step = pl.program_id(0)
    sub, width = features.shape[1:]

    @pl.when(step == 0)
    def _():
        own_group = (
            lax.broadcasted_iota(jnp.int32, (128, width), 1) // (width // GROUPS)
            == lax.broadcasted_iota(jnp.int32, (128, width), 0)
        ).astype(wide_type)
        stats[...] = jnp.dot(
            groups[0:chips].reshape(chips * 8, 128), own_group, precision=lax.Precision.HIGHEST
        ).reshape(chips, 8, width)

    position = (lax.broadcasted_iota(jnp.int32, (sub, 1), 0) * 2 + facts[1]) * chips + facts[0]

    def one(place, carry):
        slot = step * count + place
        document = owner[slot]
        normed = (features[document].astype(wide_type) - stats[slot, 0:1, :]) * stats[slot, 1:2, :]
        moved = stats[slot, 1:2, :] * (stats[slot, 2:3, :] + normed * stats[slot, 3:4, :])
        out[place] = jnp.where(position < facts[2 + document], moved, 0.0).astype(low_type)
        return carry

    lax.fori_loop(0, count, one, 0)


def moved_rows(doc_owner, facts, features, groups):
    docs, sub, width = features.shape
    count = max(docs // 4, 1)
    return pl.pallas_call(
        partial(moved_kernel, chips=docs, count=count),
        grid_spec=pltpu.PrefetchScalarGridSpec(
            num_scalar_prefetch=2,
            grid=(docs // count,),
            in_specs=[
                pl.BlockSpec(features.shape, lambda j, owner, facts: (0, 0, 0)),
                pl.BlockSpec(groups.shape, lambda j, owner, facts: (0, 0, 0)),
            ],
            out_specs=pl.BlockSpec((count, sub, width), lambda j, owner, facts: (j, 0, 0)),
            scratch_shapes=[pltpu.VMEM((docs, 8, width), wide_type)],
        ),
        out_shape=jax.ShapeDtypeStruct(features.shape, low_type),
        compiler_params=pltpu.CompilerParams(vmem_limit_bytes=room(docs)),
        cost_estimate=heavy,
        name="moved_rows",
    )(doc_owner, facts, features, groups)


def spread_kernel(owner, *refs, docs, pieces):
    rows = refs[:pieces]
    moved, out, held, taken, wide, came, also, gone = refs[pieces:]
    each = rows[0].shape[1]
    loads = [
        [
            pltpu.make_async_copy(
                piece.at[slot], held.at[slot, pl.ds(number * each, each)], came.at[slot * pieces + number]
            )
            for number, piece in enumerate(rows)
        ]
        for slot in range(docs)
    ]
    takes = [pltpu.make_async_copy(moved.at[slot], taken.at[slot], also.at[slot]) for slot in range(docs)]
    stores = [pltpu.make_async_copy(wide.at[slot], out.at[owner[slot]], gone.at[slot]) for slot in range(docs)]
    for slot in range(docs):
        for load in loads[slot]:
            load.start()
        takes[slot].start()
    for slot in range(docs):
        for load in loads[slot]:
            load.wait()
        takes[slot].wait()
        wide[slot] = held[slot].astype(wide_type) - taken[slot].astype(wide_type)
        stores[slot].start()
    for store in stores:
        store.wait()


def spread_docs(rows, moved, doc_owner):
    docs = moved.shape[0]
    pieces = len(rows)
    return pl.pallas_call(
        partial(spread_kernel, docs=docs, pieces=pieces),
        grid_spec=pltpu.PrefetchScalarGridSpec(
            num_scalar_prefetch=1,
            grid=(),
            in_specs=[pl.BlockSpec(memory_space=pl.ANY)] * (pieces + 1),
            out_specs=pl.BlockSpec(memory_space=pl.ANY),
            scratch_shapes=[
                pltpu.VMEM(moved.shape, low_type),
                pltpu.VMEM(moved.shape, low_type),
                pltpu.VMEM(moved.shape, wide_type),
                pltpu.SemaphoreType.DMA((docs * pieces,)),
                pltpu.SemaphoreType.DMA((docs,)),
                pltpu.SemaphoreType.DMA((docs,)),
            ],
        ),
        out_shape=jax.ShapeDtypeStruct(moved.shape, wide_type),
        compiler_params=pltpu.CompilerParams(vmem_limit_bytes=vmem_large),
        cost_estimate=heavy,
        name="spread_docs",
    )(doc_owner, *rows, moved)


def chunk_of(chips, sub):
    return min(sub, max(16, 512 // chips))


def live_rows(facts, start, chips, span):
    row = lax.broadcasted_iota(jnp.int32, (chips * span, 1), 0)
    chip, step = row // span, row % span
    return ((start + step) * 2 + facts[1]) * chips + chip < facts[0]


def in_branches(facts, start, chips, span, work, dead=None):
    first = (start * 2 + facts[1]) * chips
    last = ((start + span - 1) * 2 + facts[1]) * chips + chips - 1
    full = last < facts[0]
    none = first >= facts[0]

    @pl.when(full)
    def _():
        work(None)

    @pl.when(jnp.logical_not(full) & jnp.logical_not(none))
    def _():
        work(live_rows(facts, start, chips, span))

    if dead is not None:
        pl.when(none)(dead)


def whole(shape):
    return pl.BlockSpec(shape, lambda j, facts: (0,) * len(shape))


def slab(shape, span, first=0):
    return pl.BlockSpec((shape[0], span, shape[2]), lambda j, facts: (0, j + first, 0))


def memory_forward_kernel(facts, rows, stats, weight, out, *, chips, span):
    width = rows.shape[-1]
    wide = rows[...].reshape(chips * span, width).astype(wide_type)
    drive = (wide - stats[0:1, :]) * stats[1:2, :] * stats[2:3, :] + stats[3:4, :]
    hidden = (drive * (0.5 + 0.5 * jnp.tanh(0.5 * drive))).astype(low_type)
    made = wide + dot_wide(hidden, weight[...])
    out[...] = made.astype(low_type).reshape(chips, span, width)


def memory_forward(facts, rows, stats, weight):
    chips, sub, width = rows.shape
    span = chunk_of(chips, sub)
    return pl.pallas_call(
        partial(memory_forward_kernel, chips=chips, span=span),
        grid_spec=pltpu.PrefetchScalarGridSpec(
            num_scalar_prefetch=1,
            grid=(sub // span,),
            in_specs=[slab(rows.shape, span), whole(stats.shape), whole(weight.shape)],
            out_specs=slab(rows.shape, span),
        ),
        out_shape=pltpu.HBM(rows.shape, low_type),
        compiler_params=pltpu.CompilerParams(vmem_limit_bytes=room(chips)),
        cost_estimate=heavy,
        name="memory_forward",
    )(facts, rows, stats, weight)


def memory_backward_kernel(
    facts, rows, own, came, stats, weight, sums_in, grad_out, hidden_out, base_out, sums, groups, *, chips, span, steps
):
    step = pl.program_id(0)
    width = rows.shape[-1]
    count = chips * span

    @pl.when(step == 0)
    def _():
        sums[...] = sums_in[...]

    wide = rows[...].reshape(count, width).astype(wide_type)
    normed = (wide - stats[0:1, :]) * stats[1:2, :]
    drive = normed * stats[2:3, :] + stats[3:4, :]
    gate = 0.5 + 0.5 * jnp.tanh(0.5 * drive)
    hidden_out[...] = (drive * gate).astype(low_type).reshape(chips, span, width)
    grad = (own[...].reshape(count, width) + came[...].reshape(count, width).astype(wide_type)).astype(low_type)
    grad_out[...] = grad.reshape(chips, span, width)
    grad_act = dot_columns(grad, weight[...]) * (gate * (1.0 + drive * (1.0 - gate)))
    sums[0:1, :] += jnp.sum(grad_act, axis=0, keepdims=True)
    sums[1:2, :] += jnp.sum(grad_act * normed, axis=0, keepdims=True)
    base = grad.astype(wide_type) + grad_act * (stats[1:2, :] * stats[2:3, :])
    base_out[...] = base.astype(low_type).reshape(chips, span, width)

    @pl.when(step == steps - 1)
    def _():
        per_group = width // GROUPS
        group_of = (
            lax.broadcasted_iota(jnp.int32, (width, 128), 0) // per_group
            == lax.broadcasted_iota(jnp.int32, (width, 128), 1)
        ).astype(wide_type)
        entries = (facts[0] * per_group).astype(wide_type)
        rows_of = jnp.concatenate(
            (
                stats[0:2, :] * (0.5 / per_group),
                sums[0:2, :] * stats[2:3, :] / entries,
                jnp.zeros((4, width), wide_type),
            )
        )
        groups[...] = jnp.dot(rows_of, group_of, precision=lax.Precision.HIGHEST)


def memory_backward(facts, rows, own, came, stats, weight, sums_in, first):
    chips, sub, width = own.shape
    span = chunk_of(chips, rows.shape[1])
    block = slab(own.shape, span)
    return pl.pallas_call(
        partial(memory_backward_kernel, chips=chips, span=span, steps=sub // span),
        grid_spec=pltpu.PrefetchScalarGridSpec(
            num_scalar_prefetch=1,
            grid=(sub // span,),
            in_specs=[
                slab(rows.shape, span, first),
                block,
                block,
                whole(stats.shape),
                whole(weight.shape),
                whole(sums_in.shape),
            ],
            out_specs=[block, block, block, whole(stats.shape), whole((8, 128))],
        ),
        out_shape=[
            jax.ShapeDtypeStruct(own.shape, low_type),
            jax.ShapeDtypeStruct(own.shape, low_type),
            pltpu.HBM(own.shape, low_type),
            jax.ShapeDtypeStruct(stats.shape, wide_type),
            jax.ShapeDtypeStruct((8, 128), wide_type),
        ],
        compiler_params=pltpu.CompilerParams(vmem_limit_bytes=room(chips)),
        cost_estimate=heavy,
        name="memory_backward",
    )(facts, rows, own, came, stats, weight, sums_in)


def cross_forward_kernel(
    facts, query_t, rows, key_weight, value_weight, top_in, total_in, sum_in, pairs, top, total, gathered,
    total_here, sum_here, held, *, chips, span
):
    step = pl.program_id(0)
    half = key_weight.shape[1]
    width = rows.shape[-1]

    @pl.when(step == 0)
    def _():
        top[...] = top_in[...]
        total[...] = total_in[...]
        gathered[...] = sum_in[...]

    def work(live):
        block = rows[...].reshape(chips * span, width)
        keys = dot_wide(block, key_weight[...]).astype(low_type)
        values = dot_wide(block, value_weight[...]).astype(low_type)
        pairs[:, :, :half] = keys.reshape(chips, span, half)
        pairs[:, :, half:] = values.reshape(chips, span, half)
        heads = half // HD

        def score(head):
            made = dot_wide(keys[:, head // 2 * 128 : head // 2 * 128 + 128], query_t[head])
            return made if live is None else jnp.where(live, made, masked_fill)

        def part_of(head, weights):
            part = dot_rows(values[:, head // 2 * 128 : head // 2 * 128 + 128], weights.astype(low_type))
            return part[head % 2 * HD : head % 2 * HD + HD, :]

        def plain():
            following = score(0)
            for head in range(heads):
                scores = following
                if head + 1 < heads:
                    following = score(head + 1)
                weights = jnp.exp(scores - top[head : head + 1, :])
                total_here[head : head + 1, :] = jnp.sum(weights, axis=0, keepdims=True)
                sum_here[head * HD : head * HD + HD, :] = part_of(head, weights)

        def shifted():
            following = score(0)
            for head in range(heads):
                scores = following
                if head + 1 < heads:
                    following = score(head + 1)
                old_top = top[head : head + 1, :]
                new_top = jnp.maximum(old_top, jnp.max(scores, axis=0, keepdims=True))
                weights = jnp.exp(scores - new_top)
                shrink = jnp.exp(old_top - new_top)
                total[head : head + 1, :] = total[head : head + 1, :] * shrink + jnp.sum(
                    weights, axis=0, keepdims=True
                )
                rows_of = slice(head * HD, head * HD + HD)
                gathered[rows_of, :] = gathered[rows_of, :] * shrink + part_of(head, weights)
                top[head : head + 1, :] = new_top

        fresh = (facts[3] == 1) & (step == 0)
        held[0] = jnp.where(fresh, 1, 0)

        @pl.when(jnp.logical_not(fresh))
        def _():
            plain()
            small = jnp.max(total_here[0:heads, :]) < largest_sum
            held[0] = jnp.where(small, 0, 1)

            @pl.when(small)
            def _():
                total[0:heads, :] += total_here[0:heads, :]
                gathered[...] += sum_here[...]

        pl.when(held[0] == 1)(shifted)

    def dead():
        pairs[...] = jnp.zeros_like(pairs)

    in_branches(facts, step * span, chips, span, work, dead)


def cross_forward(facts, query_t, rows, weight, carry):
    chips, sub, width = rows.shape
    heads, _, queries = query_t.shape
    half = heads * HD
    span = chunk_of(chips, sub)
    stat = (8, queries)
    summed = (half, queries)
    return pl.pallas_call(
        partial(cross_forward_kernel, chips=chips, span=span),
        grid_spec=pltpu.PrefetchScalarGridSpec(
            num_scalar_prefetch=1,
            grid=(sub // span,),
            in_specs=[
                whole(query_t.shape),
                slab(rows.shape, span),
                pl.BlockSpec((width, half), lambda j, facts: (0, facts[2])),
                pl.BlockSpec((width, half), lambda j, facts: (0, 2 + facts[2])),
                whole(stat),
                whole(stat),
                whole(summed),
            ],
            out_specs=[slab((chips, sub, 2 * half), span), whole(stat), whole(stat), whole(summed)],
            scratch_shapes=[
                pltpu.VMEM(stat, wide_type),
                pltpu.VMEM(summed, wide_type),
                pltpu.SMEM((1,), jnp.int32),
            ],
        ),
        out_shape=[
            jax.ShapeDtypeStruct((chips, sub, 2 * half), low_type),
            jax.ShapeDtypeStruct(stat, wide_type),
            jax.ShapeDtypeStruct(stat, wide_type),
            jax.ShapeDtypeStruct(summed, wide_type),
        ],
        compiler_params=pltpu.CompilerParams(vmem_limit_bytes=room(chips)),
        cost_estimate=heavy,
        name="cross_forward",
    )(facts, query_t, rows, weight, weight, *carry)


def cross_close_kernel(gathered, top, total, weight, crossed, crossed_t, log_total, part, *, heads):
    log_total[...] = top[...] + jnp.log(jnp.maximum(total[...], 1e-30))
    for head in range(heads):
        rows = slice(head * HD, head * HD + HD)
        crossed_t[rows, :] = gathered[rows, :] / total[head : head + 1, :]
    low = crossed_t[...].T.astype(low_type)
    crossed[...] = low
    part[...] = dot_wide(low, weight[...])


def cross_close(gathered, top, total, weight):
    half, queries = gathered.shape
    return pl.pallas_call(
        partial(cross_close_kernel, heads=half // HD),
        out_shape=[
            jax.ShapeDtypeStruct((queries, half), low_type),
            jax.ShapeDtypeStruct((half, queries), wide_type),
            jax.ShapeDtypeStruct(top.shape, wide_type),
            jax.ShapeDtypeStruct((queries, weight.shape[1]), wide_type),
        ],
        compiler_params=pltpu.CompilerParams(vmem_limit_bytes=vmem_budget),
        cost_estimate=heavy,
        name="cross_close",
    )(gathered, top, total, weight)


gelu_scale = 0.7978845608028654
gelu_cubic = 0.044715


def feed_forward_kernel(
    first, own, came, gain, weight, grad_active, second, normed, both_grad, both_active, grad_normed
):
    step = pl.program_id(0)

    @pl.when(step == 0)
    def _():
        total = first[...] + (own[...] + came[...])
        second[...] = total
        factor = lax.rsqrt(jnp.mean(total * total, axis=-1, keepdims=True) + norm_eps)
        normed[...] = (total * factor * gain[...]).astype(low_type)
        grad_normed[...] = jnp.zeros_like(grad_normed)

    lifted = dot_wide(normed[...], weight[...])
    square = lifted * lifted
    bent = jnp.tanh(gelu_scale * (lifted * (1.0 + gelu_cubic * square)))
    half_up = 0.5 * (1.0 + bent)
    both_active[...] = (lifted * half_up).astype(low_type)
    slope = half_up + (0.5 * gelu_scale) * lifted * (1.0 - bent * bent) * (1.0 + 3.0 * gelu_cubic * square)
    grad_lifted = (grad_active[...].astype(wide_type) * slope).astype(low_type)
    both_grad[...] = grad_lifted
    grad_normed[...] += dot_columns(grad_lifted, weight[...])


def feed_forward(first, own, came, gain, weight, grad_active):
    rows, width = first.shape
    hidden = weight.shape[1]
    block = 512
    still = pl.BlockSpec((rows, width), lambda j: (0, 0))
    moving = pl.BlockSpec((rows, block), lambda j: (0, j))
    return pl.pallas_call(
        feed_forward_kernel,
        grid=(hidden // block,),
        in_specs=[
            still,
            still,
            still,
            pl.BlockSpec((1, width), lambda j: (0, 0)),
            pl.BlockSpec((width, block), lambda j: (0, j)),
            moving,
        ],
        out_specs=[still, still, moving, moving, still],
        out_shape=[
            jax.ShapeDtypeStruct((rows, width), wide_type),
            jax.ShapeDtypeStruct((rows, width), low_type),
            jax.ShapeDtypeStruct((rows, hidden), low_type),
            jax.ShapeDtypeStruct((rows, hidden), low_type),
            jax.ShapeDtypeStruct((rows, width), wide_type),
        ],
        compiler_params=pltpu.CompilerParams(vmem_limit_bytes=vmem_budget),
        cost_estimate=heavy,
        name="feed_forward",
    )(first, own, came, gain, weight, grad_active)


def feed_close_kernel(
    second, own, came, gain, grad_out, weight, crossed_t, grad_second, gain_grad, grad_cross, heads_out,
    heads_out_t, inner, *, heads,
):
    values = second[...]
    incoming = (own[...] + came[...]).astype(low_type).astype(wide_type)
    factor = lax.rsqrt(jnp.mean(values * values, axis=-1, keepdims=True) + norm_eps)
    scaled = incoming * gain[...]
    inward = factor * scaled - values * (factor * factor * factor) * jnp.mean(
        scaled * values, axis=-1, keepdims=True
    )
    gain_grad[...] = jnp.broadcast_to(
        jnp.sum(incoming * values * factor, axis=0, keepdims=True), gain_grad.shape
    )
    total = inward + grad_out[...].astype(wide_type)
    grad_second[...] = total
    low = total.astype(low_type)
    grad_cross[...] = low
    made = dot_columns(low, weight[...])
    made_low = made.astype(low_type)
    made_t = made_low.astype(wide_type).T
    low_t = made_t.astype(low_type)
    left = lax.broadcasted_iota(jnp.int32, (made.shape[0], 128), 1) < HD
    inner[...] = jnp.zeros_like(inner)
    for head in range(heads):
        pair = made_low[:, head // 2 * 128 : head // 2 * 128 + 128]
        keep = left if head % 2 == 0 else jnp.logical_not(left)
        heads_out[head] = jnp.where(keep, pair, jnp.zeros_like(pair))
        rows = slice(head * HD, head * HD + HD)
        own_rows = slice(head % 2 * HD, head % 2 * HD + HD)
        other_rows = slice((1 - head % 2) * HD, (1 - head % 2) * HD + HD)
        heads_out_t[head, own_rows, :] = low_t[rows, :]
        heads_out_t[head, other_rows, :] = jnp.zeros_like(low_t[rows, :])
        inner[head : head + 1, :] = jnp.sum(made_t[rows, :] * crossed_t[rows, :], axis=0, keepdims=True)


def feed_close(second, own, came, gain, grad_out, weight, crossed_t):
    rows, width = second.shape
    half = weight.shape[0]
    heads = half // HD
    return pl.pallas_call(
        partial(feed_close_kernel, heads=heads),
        out_shape=[
            jax.ShapeDtypeStruct((rows, width), wide_type),
            jax.ShapeDtypeStruct((8, width), wide_type),
            jax.ShapeDtypeStruct((rows, width), low_type),
            jax.ShapeDtypeStruct((heads, rows, 128), low_type),
            jax.ShapeDtypeStruct((heads, 128, rows), low_type),
            jax.ShapeDtypeStruct((8, rows), wide_type),
        ],
        compiler_params=pltpu.CompilerParams(vmem_limit_bytes=vmem_budget),
        cost_estimate=heavy,
        name="feed_close",
    )(second, own, came, gain, grad_out, weight, crossed_t)


def feed_weights_kernel(normed, grad_out, grad_cross, grad_lifted, active, crossed, left, middle, right):
    third = left.shape[1]
    rest = grad_lifted.shape[1] - third
    left[...] = dot_rows(normed[...], grad_lifted[:, :third]).astype(low_type)
    middle[:, :rest] = dot_rows(normed[...], grad_lifted[:, third:]).astype(low_type)
    middle[:, rest:] = dot_rows(grad_out[...], active[:, : third - rest]).astype(low_type)
    right[:, : 2 * rest] = dot_rows(grad_out[...], active[:, third - rest :]).astype(low_type)
    right[:, 2 * rest :] = dot_rows(grad_cross[...], crossed[...]).astype(low_type)


def feed_weights(*args):
    width = args[0].shape[1]
    third = (2 * args[3].shape[1] + args[5].shape[1]) // 3
    return pl.pallas_call(
        feed_weights_kernel,
        out_shape=[jax.ShapeDtypeStruct((width, third), low_type)] * 3,
        compiler_params=pltpu.CompilerParams(vmem_limit_bytes=vmem_budget),
        cost_estimate=heavy,
        name="feed_weights",
    )(*args)


def cross_backward_kernel(
    facts, query, query_t, grad, grad_t, log_total, inner, pairs, key_weight, value_weight, pair_grads,
    row_grads, query_grad, held, *, chips, span, first
):
    step = pl.program_id(0)
    width, half = key_weight.shape

    @pl.when(step == 0)
    def _():
        query_grad[...] = jnp.zeros_like(query_grad)

    def work(live):
        block = pairs[...].reshape(chips * span, 2 * half)
        heads = half // HD

        def lanes(head, shift=0):
            return block[:, shift + head // 2 * 128 : shift + head // 2 * 128 + 128]

        def products(head):
            scores = dot_wide(lanes(head), query_t[head])
            if live is not None:
                scores = jnp.where(live, scores, masked_fill)
            return scores, dot_wide(lanes(head, half), grad_t[head])

        following = products(0)
        for pair in range(heads // 2):
            lows, low_grads = [], []
            for side in range(2):
                head = pair * 2 + side
                scores, grad_probs = following
                if head + 1 < heads:
                    following = products(head + 1)
                probs = jnp.exp(scores - log_total[head : head + 1, :])
                low_grads.append((probs * (grad_probs - inner[head : head + 1, :])).astype(low_type))
                lows.append(probs.astype(low_type))
                part = dot_rows(lanes(head), low_grads[-1])
                query_grad[head * HD : head * HD + HD, :] += part[side * HD : side * HD + HD, :]
            at = pair * 128
            both = slice(pair * 2, pair * 2 + 2)
            queries = query.shape[1]
            held[:, at : at + 128] = dot_wide(
                jnp.concatenate(low_grads, axis=1), query[both].reshape(2 * queries, 128)
            ).astype(low_type)
            held[:, half + at : half + at + 128] = dot_wide(
                jnp.concatenate(lows, axis=1), grad[both].reshape(2 * queries, 128)
            ).astype(low_type)
        made = held[...]
        pair_grads[...] = made.reshape(chips, span, 2 * half)
        back = dot_columns(made[:, :half], key_weight[...]) + dot_columns(made[:, half:], value_weight[...])
        row_grads[...] = back.astype(row_grads.dtype).reshape(chips, span, width)

    def dead():
        pair_grads[...] = jnp.zeros_like(pair_grads)
        row_grads[...] = jnp.zeros_like(row_grads)

    in_branches(facts, (step + first) * span, chips, span, work, dead)


def cross_backward(facts, query, query_t, grad, grad_t, log_total, inner, pairs, weight, grad_type, first, steps):
    chips, sub, both = pairs.shape
    width = weight.shape[0]
    heads, _, queries = query_t.shape
    span = chunk_of(chips, sub)
    half = both // 2
    rows = steps * span
    pair_block = slab((chips, rows, both), span)
    row_block = slab((chips, rows, width), span)
    return pl.pallas_call(
        partial(cross_backward_kernel, chips=chips, span=span, first=first),
        grid_spec=pltpu.PrefetchScalarGridSpec(
            num_scalar_prefetch=1,
            grid=(steps,),
            in_specs=[
                whole(query.shape),
                whole(query_t.shape),
                whole(grad.shape),
                whole(grad_t.shape),
                whole(log_total.shape),
                whole(inner.shape),
                slab(pairs.shape, span, first),
                pl.BlockSpec((width, half), lambda j, facts: (0, facts[2])),
                pl.BlockSpec((width, half), lambda j, facts: (0, 2 + facts[2])),
            ],
            out_specs=[pair_block, row_block, whole((heads * HD, queries))],
            scratch_shapes=[pltpu.VMEM((chips * span, both), low_type)],
        ),
        out_shape=[
            jax.ShapeDtypeStruct((chips, rows, both), low_type),
            jax.ShapeDtypeStruct((chips, rows, width), grad_type),
            jax.ShapeDtypeStruct((heads * HD, queries), wide_type),
        ],
        compiler_params=pltpu.CompilerParams(vmem_limit_bytes=room(chips)),
        cost_estimate=heavy,
        name="cross_backward",
    )(facts, query, query_t, grad, grad_t, log_total, inner, pairs, weight, weight)


def query_back_kernel(*refs):
    *parts, weight, grad, part = refs
    total = parts[0][...]
    for other in parts[1:]:
        total = total + other[...]
    low = (total * 0.125).T.astype(low_type)
    grad[...] = low
    part[...] = dot_columns(low, weight[...])


def query_back(parts, weight):
    half, rows = parts[0].shape
    return pl.pallas_call(
        query_back_kernel,
        out_shape=[
            jax.ShapeDtypeStruct((rows, half), low_type),
            jax.ShapeDtypeStruct((rows, weight.shape[0]), wide_type),
        ],
        compiler_params=pltpu.CompilerParams(vmem_limit_bytes=vmem_budget),
        cost_estimate=heavy,
        name="query_back",
    )(*parts, weight)


def memory_weights_kernel(facts, *refs, pieces, chips, span, steps):
    rows, other = refs[:2]
    sets = [refs[2 + 4 * piece : 6 + 4 * piece] for piece in range(pieces)]
    pair_out, keep_out, send_out, pair_sum, conv_sum = refs[2 + 4 * pieces :]
    step = pl.program_id(0)
    count = chips * span
    each = steps // pieces

    def flat(ref):
        return ref[...].reshape(count, ref.shape[-1])

    @pl.when(step == 0)
    def _():
        pair_sum[...] = jnp.zeros_like(pair_sum)
        conv_sum[...] = jnp.zeros_like(conv_sum)

    for piece, (hidden, pair_grads, row_grads, other_grads) in enumerate(sets):

        @pl.when((step >= piece * each) & (step < piece * each + each))
        def _(hidden=hidden, pair_grads=pair_grads, row_grads=row_grads, other_grads=other_grads):
            pair_sum[...] += dot_rows(flat(rows), flat(pair_grads)) + dot_rows(flat(other), flat(other_grads))
            conv_sum[...] += dot_rows(flat(hidden), flat(row_grads))

    @pl.when(step == steps - 1)
    def _():
        pair_out[...] = pair_sum[...].astype(low_type)
        half = keep_out.shape[1]
        first = facts[1] == 0
        keep_out[...] = jnp.where(first, conv_sum[:, :half], conv_sum[:, half:])
        send_out[...] = jnp.where(first, conv_sum[:, half:], conv_sum[:, :half]).astype(low_type)


def memory_weights(facts, rows, other, sets):
    chips, sub, width = rows.shape
    span = chunk_of(chips, sub)
    both = sets[0][1].shape[2]
    steps = sub // span
    pieces = len(sets)
    each = steps // pieces

    def piece_block(piece, columns):
        return pl.BlockSpec(
            (chips, span, columns), lambda j, facts: (0, jnp.clip(j - piece * each, 0, each - 1), 0)
        )

    in_specs = [slab(rows.shape, span), slab(other.shape, span)]
    for piece, arrays in enumerate(sets):
        in_specs += [piece_block(piece, array.shape[2]) for array in arrays]
    outs = (((width, both), low_type), ((width, width // 2), wide_type), ((width, width // 2), low_type))
    return pl.pallas_call(
        partial(memory_weights_kernel, pieces=pieces, chips=chips, span=span, steps=steps),
        grid_spec=pltpu.PrefetchScalarGridSpec(
            num_scalar_prefetch=1,
            grid=(steps,),
            in_specs=in_specs,
            out_specs=[whole(shape) for shape, _ in outs],
            scratch_shapes=[pltpu.VMEM((width, both), wide_type), pltpu.VMEM((width, width), wide_type)],
        ),
        out_shape=[jax.ShapeDtypeStruct(shape, kind) for shape, kind in outs],
        compiler_params=pltpu.CompilerParams(vmem_limit_bytes=room(chips)),
        cost_estimate=heavy,
        name="memory_weights",
    )(facts, rows, other, *[array for arrays in sets for array in arrays])


def side_weights_kernel(normed_one, grad_qkv, normed_two, grad_cq, grad_self, attended, first, second):
    half = attended.shape[1]
    cut = first.shape[1]
    first[...] = dot_rows(normed_one[...], grad_qkv[:, :cut]).astype(low_type)
    rest = 3 * half - cut
    second[:, :rest] = dot_rows(normed_one[...], grad_qkv[:, cut:]).astype(low_type)
    second[:, rest : rest + half] = dot_rows(normed_two[...], grad_cq[...]).astype(low_type)
    second[:, rest + half :] = dot_rows(grad_self[...], attended[...]).astype(low_type)


def side_weights(*args):
    width = args[0].shape[1]
    half = args[-1].shape[1]
    cut = 3 * half - 128
    return pl.pallas_call(
        side_weights_kernel,
        out_shape=[
            jax.ShapeDtypeStruct((width, cut), low_type),
            jax.ShapeDtypeStruct((width, 5 * half - cut), low_type),
        ],
        compiler_params=pltpu.CompilerParams(vmem_limit_bytes=vmem_budget),
        cost_estimate=heavy,
        name="side_weights",
    )(*args)


def product_kernel(left, right, out):
    @pl.when(pl.program_id(0) == 0)
    def _():
        out[...] = jnp.zeros_like(out)

    out[...] += dot_wide(left[...], right[...])


def product(left, right):
    rows, depth = left.shape
    width = right.shape[1]
    block = 512
    return pl.pallas_call(
        product_kernel,
        grid=(depth // block,),
        in_specs=[
            pl.BlockSpec((rows, block), lambda j: (0, j)),
            pl.BlockSpec((block, width), lambda j: (j, 0)),
        ],
        out_specs=pl.BlockSpec((rows, width), lambda j: (0, 0)),
        out_shape=jax.ShapeDtypeStruct((rows, width), wide_type),
        compiler_params=pltpu.CompilerParams(vmem_limit_bytes=vmem_budget),
        cost_estimate=heavy,
        name="product",
    )(left, right)


def back_through_norm(values, incoming, gain):
    factor = lax.rsqrt(jnp.mean(values * values, axis=-1, keepdims=True) + norm_eps)
    scaled = incoming * gain
    inward = factor * scaled - values * (factor * factor * factor) * jnp.mean(
        scaled * values, axis=-1, keepdims=True
    )
    return inward, jnp.sum(incoming * values * factor, axis=0, keepdims=True)


def self_forward_kernel(
    facts, rows_in, gain, weight, out_weight, normed_out, triple, attended, log_total, part, *, heads
):
    values = rows_in[...].astype(wide_type)
    factor = lax.rsqrt(jnp.mean(values * values, axis=-1, keepdims=True) + norm_eps)
    normed = (values * factor * gain[...]).astype(low_type)
    normed_out[...] = normed
    rows = values.shape[0]
    half = heads * HD
    for side in range(3):
        triple[:, side * half : side * half + half] = dot_wide(normed, weight[side]).astype(low_type)
    key_pos = lax.broadcasted_iota(jnp.int32, (rows, rows), 0)
    query_pos = lax.broadcasted_iota(jnp.int32, (rows, rows), 1)
    allowed = (key_pos <= query_pos) & (key_pos < facts[0])
    left = lax.broadcasted_iota(jnp.int32, (rows, 128), 1) < HD
    log_total[...] = jnp.zeros_like(log_total)
    for pair in range(heads // 2):
        lanes = slice(pair * 128, pair * 128 + 128)
        query_pair = triple[:, lanes]
        key_pair = triple[:, half + pair * 128 : half + pair * 128 + 128]
        value_pair = triple[:, 2 * half + pair * 128 : 2 * half + pair * 128 + 128]
        parts = []
        for side in range(2):
            head = pair * 2 + side
            keep = left if side == 0 else jnp.logical_not(left)
            query = jnp.where(keep, query_pair, jnp.zeros_like(query_pair))
            scores = jnp.where(allowed, dot_columns(key_pair, query) * 0.125, masked_fill)
            top = jnp.max(scores, axis=0, keepdims=True)
            weights = jnp.exp(scores - top)
            total = jnp.sum(weights, axis=0, keepdims=True)
            log_total[head : head + 1, :] = top + jnp.log(total)
            made = dot_rows(value_pair, (weights / total).astype(low_type))
            parts.append(made[side * HD : side * HD + HD, :])
        attended[:, lanes] = jnp.concatenate(parts).T.astype(low_type)
    part[...] = dot_wide(attended[...], out_weight[...])


def self_forward(facts, rows_in, gain, weight, out_weight):
    rows, width = rows_in.shape
    half = out_weight.shape[0]
    args = (rows_in, gain, weight, out_weight)
    outs = (
        ((rows, width), low_type),
        ((rows, 3 * half), low_type),
        ((rows, half), low_type),
        ((8, rows), wide_type),
        ((rows, width), wide_type),
    )
    return pl.pallas_call(
        partial(self_forward_kernel, heads=half // HD),
        grid_spec=pltpu.PrefetchScalarGridSpec(
            num_scalar_prefetch=1,
            grid=(1,),
            in_specs=[whole(arg.shape) for arg in args],
            out_specs=[whole(shape) for shape, _ in outs],
        ),
        out_shape=[jax.ShapeDtypeStruct(shape, kind) for shape, kind in outs],
        compiler_params=pltpu.CompilerParams(vmem_limit_bytes=vmem_budget),
        cost_estimate=heavy,
        name="self_forward",
    )(facts, *args)


def query_forward_kernel(rows_in, own, came, gain, weight, first, normed_out, heads_out, heads_out_t, *, heads):
    total = rows_in[...].astype(wide_type) + (own[...] + came[...])
    first[...] = total
    factor = lax.rsqrt(jnp.mean(total * total, axis=-1, keepdims=True) + norm_eps)
    normed = (total * factor * gain[...]).astype(low_type)
    normed_out[...] = normed
    query = (dot_wide(normed, weight[...]).astype(low_type).astype(wide_type) * 0.125).astype(low_type)
    turned = query.T
    left = lax.broadcasted_iota(jnp.int32, (query.shape[0], 128), 1) < HD
    for head in range(heads):
        pair = query[:, head // 2 * 128 : head // 2 * 128 + 128]
        keep = left if head % 2 == 0 else jnp.logical_not(left)
        heads_out[head] = jnp.where(keep, pair, jnp.zeros_like(pair))
        own_rows = slice(head % 2 * HD, head % 2 * HD + HD)
        other_rows = slice((1 - head % 2) * HD, (1 - head % 2) * HD + HD)
        mine = turned[head * HD : head * HD + HD, :]
        heads_out_t[head, own_rows, :] = mine
        heads_out_t[head, other_rows, :] = jnp.zeros_like(mine)


def query_forward(rows_in, own, came, gain, weight):
    rows, width = rows_in.shape
    heads = weight.shape[1] // HD
    outs = (
        ((rows, width), wide_type),
        ((rows, width), low_type),
        ((heads, rows, 128), low_type),
        ((heads, 128, rows), low_type),
    )
    return pl.pallas_call(
        partial(query_forward_kernel, heads=heads),
        out_shape=[jax.ShapeDtypeStruct(shape, kind) for shape, kind in outs],
        compiler_params=pltpu.CompilerParams(vmem_limit_bytes=vmem_budget),
        cost_estimate=heavy,
        name="query_forward",
    )(rows_in, own, came, gain, weight)


def self_backward_kernel(
    facts, values, own, came, gain, grad_second, out_weight, triple, log_total, weight,
    grad_first, grad_low, gain_grad, triple_grad, part, *, heads,
):
    rows = triple.shape[0]
    half = heads * HD
    incoming = (own[...] + came[...]).astype(low_type).astype(wide_type)
    inward, gain_row = back_through_norm(values[...], incoming, gain[...])
    gain_grad[...] = jnp.broadcast_to(gain_row, gain_grad.shape)
    total = inward + grad_second[...]
    grad_first[...] = total
    grad_low[...] = total.astype(low_type)
    grad = dot_columns(grad_low[...], out_weight[...]).astype(low_type)
    key_pos = lax.broadcasted_iota(jnp.int32, (rows, rows), 0)
    query_pos = lax.broadcasted_iota(jnp.int32, (rows, rows), 1)
    allowed = (key_pos <= query_pos) & (key_pos < facts[0])
    left = lax.broadcasted_iota(jnp.int32, (rows, 128), 1) < HD
    for pair in range(heads // 2):
        lanes = slice(pair * 128, pair * 128 + 128)
        query_pair = triple[:, lanes]
        key_pair = triple[:, half + pair * 128 : half + pair * 128 + 128]
        value_pair = triple[:, 2 * half + pair * 128 : 2 * half + pair * 128 + 128]
        grad_pair = grad[:, lanes]
        key_sum, value_sum, query_parts = 0.0, 0.0, []
        for side in range(2):
            head = pair * 2 + side
            keep = left if side == 0 else jnp.logical_not(left)
            query = jnp.where(keep, query_pair, jnp.zeros_like(query_pair))
            grad_head = jnp.where(keep, grad_pair, jnp.zeros_like(grad_pair))
            scores = dot_columns(key_pair, query) * 0.125
            probs = jnp.exp(jnp.where(allowed, scores, masked_fill) - log_total[head : head + 1, :])
            grad_probs = dot_columns(value_pair, grad_head)
            inner = jnp.sum(probs * grad_probs, axis=0, keepdims=True)
            grad_scores = (probs * (grad_probs - inner)).astype(low_type)
            value_sum = value_sum + dot_wide(probs.astype(low_type), grad_head)
            key_sum = key_sum + dot_wide(grad_scores, query)
            query_parts.append(dot_rows(key_pair, grad_scores)[side * HD : side * HD + HD, :])
        triple_grad[:, lanes] = (jnp.concatenate(query_parts) * 0.125).T.astype(low_type)
        triple_grad[:, half + pair * 128 : half + pair * 128 + 128] = (key_sum * 0.125).astype(low_type)
        triple_grad[:, 2 * half + pair * 128 : 2 * half + pair * 128 + 128] = value_sum.astype(low_type)
    part[...] = (
        dot_columns(triple_grad[:, :half], weight[0])
        + dot_columns(triple_grad[:, half : 2 * half], weight[1])
        + dot_columns(triple_grad[:, 2 * half :], weight[2])
    )


def self_backward(facts, values, own, came, gain, grad_second, out_weight, triple, log_total, weight):
    rows, wide = triple.shape
    width = weight.shape[1]
    args = (values, own, came, gain, grad_second, out_weight, triple, log_total, weight)
    outs = (
        ((rows, width), wide_type),
        ((rows, width), low_type),
        ((8, width), wide_type),
        ((rows, wide), low_type),
        ((rows, width), wide_type),
    )
    return pl.pallas_call(
        partial(self_backward_kernel, heads=wide // (3 * HD)),
        grid_spec=pltpu.PrefetchScalarGridSpec(
            num_scalar_prefetch=1,
            grid=(1,),
            in_specs=[whole(arg.shape) for arg in args],
            out_specs=[whole(shape) for shape, _ in outs],
        ),
        out_shape=[jax.ShapeDtypeStruct(shape, kind) for shape, kind in outs],
        compiler_params=pltpu.CompilerParams(vmem_limit_bytes=vmem_budget),
        cost_estimate=heavy,
        name="self_backward",
    )(facts, *args)


def input_back_kernel(
    values, own, came, gain, grad_first, second, result_own, result_came, act_sums, cross_gain_grad,
    ffn_gain_grad, input_grad, layer_out, gains_out,
):
    incoming = (own[...] + came[...]).astype(low_type).astype(wide_type)
    inward, gain_row = back_through_norm(values[...].astype(wide_type), incoming, gain[...])
    input_grad[...] = inward + grad_first[...]
    layer_out[...] = (second[...] + (result_own[...] + result_came[...])).astype(low_type)
    width = values.shape[1]
    gains = jnp.concatenate(
        (
            act_sums[1:2, :],
            act_sums[0:1, :],
            0.5 * gain_row,
            0.5 * cross_gain_grad[0:1, :],
            0.5 * ffn_gain_grad[0:1, :],
            jnp.zeros((3, width), wide_type),
        )
    )
    for tile in range(width // 128):
        gains_out[tile] = gains[:, tile * 128 : tile * 128 + 128]


def input_back(*args):
    rows, width = args[0].shape
    outs = (((rows, width), wide_type), ((rows, width), low_type), ((width // 128, 8, 128), wide_type))
    return pl.pallas_call(
        input_back_kernel,
        out_shape=[jax.ShapeDtypeStruct(shape, kind) for shape, kind in outs],
        compiler_params=pltpu.CompilerParams(vmem_limit_bytes=vmem_budget),
        cost_estimate=heavy,
        name="input_back",
    )(*args)


def assemble_kernel(
    facts, memory, memory_came, own, other, left, middle, right, gains, conv, cross_kv,
    cross_out, self_qkv, cross_query, self_out, ffn_in, ffn_out, *gain_outs,
):
    width = conv.shape[1]
    half = width // 2
    third = left.shape[1]
    hidden = ffn_in.shape[1]
    first = facts[1] == 0
    conv[:, :half] = jnp.where(first, memory[:, width:], memory_came[:, width:])
    conv[:, half:] = jnp.where(first, memory_came[:, width:], memory[:, width:])
    for side in range(2):
        mine = memory[:, side * half : side * half + half]
        theirs = memory_came[:, side * half : side * half + half]
        cross_kv[:, side, :half] = jnp.where(first, mine, theirs)
        cross_kv[:, side, half:] = jnp.where(first, theirs, mine)
    rest = 3 * half - own.shape[1]
    self_qkv[0] = own[:, :half]
    self_qkv[1] = own[:, half : 2 * half]
    self_qkv[2, :, : half - rest] = own[:, 2 * half :]
    self_qkv[2, :, half - rest :] = other[:, :rest]
    cross_query[...] = other[:, rest : rest + half]
    self_out[...] = other[:, rest + half :]
    ffn_in[:, :third] = left[...]
    ffn_in[:, third:] = middle[:, : hidden - third]
    ffn_out[:, : 2 * third - hidden] = middle[:, hidden - third :]
    ffn_out[:, 2 * third - hidden :] = right[:, : 2 * hidden - 2 * third]
    cross_out[...] = right[:, 2 * hidden - 2 * third :]
    share = conv.shape[0]
    picked = (
        lax.broadcasted_iota(jnp.int32, (width, share), 0)
        == lax.broadcasted_iota(jnp.int32, (width, share), 1) + facts[0] * share
    ).astype(wide_type)
    first_tile = gains.shape[0] - width // 128
    rows_of = jnp.concatenate([gains[first_tile + tile] for tile in range(width // 128)], axis=1)
    mine = jnp.dot(rows_of, picked, precision=lax.Precision.HIGHEST)
    for number, out in enumerate(gain_outs):
        out[...] = mine[number : number + 1, :]


def assemble(facts, *args):
    share = args[0].shape[0]
    width = 2 * args[0].shape[1] // 3
    half = width // 2
    hidden = (3 * args[4].shape[1] - half) // 2
    outs = (
        (share, width),
        (share, 2, width),
        (share, half),
        (3, share, half),
        (share, half),
        (share, half),
        (share, hidden),
        (share, hidden),
    ) + ((1, share),) * 5
    return pl.pallas_call(
        assemble_kernel,
        grid_spec=pltpu.PrefetchScalarGridSpec(
            num_scalar_prefetch=1,
            grid=(1,),
            in_specs=[whole(arg.shape) for arg in args],
            out_specs=[whole(shape) for shape in outs],
        ),
        out_shape=[jax.ShapeDtypeStruct(shape, wide_type) for shape in outs],
        compiler_params=pltpu.CompilerParams(vmem_limit_bytes=vmem_budget),
        cost_estimate=heavy,
        name="assemble",
    )(facts, *args)


def shards(
    dec_input,
    out_grad,
    enc_feats,
    mem_lengths,
    dec_lengths,
    doc_owner,
    group_gain,
    group_bias,
    conv_weight,
    cross_kv,
    self_gain,
    self_qkv,
    self_out,
    cross_gain,
    cross_query,
    cross_out,
    ffn_gain,
    ffn_in,
    ffn_out,
):
    chips = lax.axis_size("dp")
    chip_index = lax.axis_index("dp")
    core_index = lax.axis_index("mp")
    memory_in = enc_feats[0, 0]
    docs, sub, width = memory_in.shape
    per_group = width // GROUPS
    half = width // 2
    heads = half // HD
    rows_here = docs * sub
    share = width // chips
    bits = chips.bit_length() - 1
    rest = tuple(range(4, bits))
    order_sets = {
        "stats": (0, 1, 2, 3),
        "left": (2, 3, 0, 1),
        "middle": (0, 2, 3, 1),
        "right": (1, 0, 2, 3),
        "first": (0, 1, 2, 3),
        "second": (2, 0, 1, 3),
        "memory": (1, 2, 0, 3),
    }
    orders = {
        name: order + rest if bits >= 4 else tuple(range(bits)) for name, order in order_sets.items()
    }

    outgoing = gather_docs(memory_in, doc_owner)
    features = lax.all_to_all(outgoing, "dp", split_axis=0, concat_axis=0, tiled=True)
    outgoing, dec_input = tie((outgoing, dec_input))
    dec_rows = DEC
    dec_rows_in = dec_input.reshape(dec_rows, width)
    self_facts = dec_lengths[chip_index][None]
    self_weight = self_qkv.transpose(1, 0, 2)
    normed_one, qkv_self, attended, self_totals, part = self_forward(
        self_facts, dec_rows_in, self_gain[None], self_weight, self_out
    )
    part_came = other_core(part)
    memory_here, part = tie((memory_in, part))
    wide_in = memory_here.astype(wide_type)
    slot_pos = lax.broadcasted_iota(jnp.int32, (docs, sub), 1)
    live_in = ((slot_pos * 2 + core_index) * chips + chip_index < mem_lengths[:, None])[:, :, None]
    masked_in = jnp.where(live_in, wide_in, 0.0)
    channel_sums = jnp.stack((jnp.sum(masked_in, axis=1), jnp.sum(masked_in * wide_in, axis=1)), axis=1)
    group_of = (
        lax.broadcasted_iota(jnp.int32, (width, GROUPS), 0) // per_group
        == lax.broadcasted_iota(jnp.int32, (width, GROUPS), 1)
    ).astype(wide_type)

    def group_sums(channels):
        return jnp.dot(channels, group_of, precision=lax.Precision.HIGHEST)

    def to_channels(groups):
        return jnp.dot(groups, group_of.T, precision=lax.Precision.HIGHEST)

    sums_here = group_sums(channel_sums.reshape(docs * 2, width)).reshape(docs, 2 * GROUPS)
    sums_here = jnp.take(sums_here, doc_owner, axis=0, mode="clip")
    stat_sums = ScatterSums([core_total(sums_here)], [orders["stats"]], chip_index)
    stat_sums.begin()

    def next_step(sums, value):
        value = sums.behind(value)
        sums.merge()
        if sums.orders[0]:
            sums.begin()
            value = sums.ahead_of(value)
            sums.send()
        return value

    part_came = stat_sums.ahead_of(part_came)
    stat_sums.send()
    first_out, normed_two, query_heads, query_heads_t = query_forward(
        dec_rows_in, part, part_came, cross_gain[None], cross_query
    )
    cross_kv, query_heads = next_step(stat_sums, (cross_kv, query_heads))
    pair_weight = prepare_weights(cross_kv)
    pair_weight, query_heads = next_step(stat_sums, (pair_weight, query_heads))
    grad_low, query_heads, pair_weight = tie((out_grad.reshape(DEC, width), query_heads, pair_weight))
    grad_active = dot_columns(grad_low, ffn_out).astype(low_type)
    document = doc_owner[chip_index]
    length = mem_lengths[document]
    facts_own = jnp.stack((length, core_index, core_index, 1)).astype(jnp.int32)
    facts_other = jnp.stack((length, 1 - core_index, core_index, 0)).astype(jnp.int32)
    grad_active, query_heads, facts_own, facts_other = tie((grad_active, query_heads, facts_own, facts_other))
    while stat_sums.orders[0]:
        query_heads = next_step(stat_sums, query_heads)
    sums_all = stat_sums.current[0]

    entries = (length * per_group).astype(wide_type)
    center = sums_all[:GROUPS] / entries
    spread = lax.rsqrt(sums_all[GROUPS:] / entries - center * center + group_eps)
    channel_stats = to_channels(jnp.stack((center, spread)))
    stats = jnp.concatenate(
        (channel_stats, group_gain[None], group_bias[None], jnp.zeros((4, width), wide_type))
    )

    features, stats, query_heads, query_heads_t = tie((features, stats, query_heads, query_heads_t))
    memory_own = memory_forward(facts_own, features, stats, conv_weight)
    memory_other = other_core(memory_own)

    carry = (
        jnp.full((8, dec_rows), -1e30, wide_type),
        jnp.zeros((8, dec_rows), wide_type),
        jnp.zeros((half, dec_rows), wide_type),
    )
    pairs_own, *carry = cross_forward(
        facts_own, query_heads_t, memory_own, pair_weight, carry
    )
    pairs_other, top, total, gathered = cross_forward(
        facts_other, query_heads_t, memory_other, pair_weight, carry
    )
    crossed, crossed_t, log_total, part = cross_close(gathered, top, total, cross_out)

    second_out, normed_three, grad_lifted, active, part = feed_forward(
        first_out, part, other_core(part), ffn_gain[None], ffn_in, grad_active
    )
    part_came = other_core(part)
    result_part = product(active, ffn_out)
    part_came, result_part = tie((part_came, result_part))
    result_came = other_core(result_part)
    grad_second, ffn_gain_grad, grad_cross, grad_heads, grad_heads_t, inner = feed_close(
        second_out, part, part_came, ffn_gain[None], grad_low, cross_out, crossed_t
    )
    feed_grads = feed_weights(normed_three, grad_low, grad_cross, grad_lifted, active, crossed)
    feed_sums = Sums.of(
        [grad.reshape(chips, share, grad.shape[1]) for grad in feed_grads],
        [orders["left"], orders["middle"], orders["right"]],
        chip_index,
    )
    inner = feed_sums.start(inner)

    steps = sub // chunk_of(chips, sub)
    place = jnp.concatenate((jnp.stack((chip_index, core_index)).astype(jnp.int32), mem_lengths))
    pair_other, row_other, query_other = cross_backward(
        facts_other, query_heads, query_heads_t, grad_heads, grad_heads_t, log_total, inner, pairs_other, pair_weight,
        low_type, 0, steps,
    )
    facts_two, query_other = feed_sums.round((facts_own, query_other))
    row_came = other_core(row_other)
    pair_own, row_own, query_own = cross_backward(
        facts_two, query_heads, query_heads_t, grad_heads, grad_heads_t, log_total, inner, pairs_own, pair_weight,
        low_type, 0, steps,
    )

    facts_three, query_own = feed_sums.round((facts_own, query_own))
    grad_memory, hidden, base, act_sums, groups = memory_backward(
        facts_three, features, row_own, row_came, stats, conv_weight, jnp.zeros((8, width), wide_type), 0
    )
    queries, sets = (query_other, query_own), [(hidden, pair_own, grad_memory, pair_other)]

    def dp_hop(value, bit):
        return lax.ppermute(value, "dp", [(chip, chip ^ (1 << bit)) for chip in range(chips)])

    feed_came, base, queries = tie(([part.came for part in feed_sums.parts], base, queries))
    for part, arrived in zip(feed_sums.parts, feed_came):
        part.came = arrived
    returned = [lax.all_to_all(base, "dp", split_axis=0, concat_axis=0, tiled=True)]

    def when_live(work):
        return lax.cond(length > 0, work, nothing_like(work))

    def self_work():
        own_slot = lax.broadcasted_iota(jnp.int32, (chips, 1, 1), 0) == chip_index
        document_groups = jnp.where(own_slot, core_total(groups)[None], 0.0)

        grad_cq, part = query_back(queries, cross_query)
        part_came = other_core(part)
        grad_first, grad_self, cross_gain_grad, grad_qkv, part_one = self_backward(
            self_facts, first_out, part, part_came, cross_gain[None], grad_second, self_out, qkv_self, self_totals,
            self_weight,
        )
        part_one_came = other_core(part_one)
        first_part, second_part = side_weights(normed_one, grad_qkv, normed_two, grad_cq, grad_self, attended)
        part_one_came, first_part = tie((part_one_came, first_part))
        return grad_first, cross_gain_grad, part_one, part_one_came, document_groups, (first_part, second_part)

    queries = feed_sums.round(queries)
    early_feed, late_feed = Sums(feed_sums.parts[:2], chip_index), Sums(feed_sums.parts[2:], chip_index)
    grad_first, cross_gain_grad, part_one, part_one_came, document_groups, late_parts = when_live(self_work)
    while early_feed.going:
        document_groups = early_feed.round(document_groups)
    late_sums = Sums.of(
        [part.reshape(chips, share, -1) for part in late_parts], [orders["first"], orders["second"]], chip_index
    )
    document_groups = late_sums.start(document_groups)

    def memory_work():
        pair_part, conv_keep, conv_send = memory_weights(place, memory_own, memory_other, sets)
        conv_came = other_core(conv_send)
        came, conv_keep = tie((part_one_came, conv_keep))
        input_grad, layer_out, gains = input_back(
            dec_rows_in, part_one, came, self_gain[None], grad_first, second_out, result_part, result_came, act_sums,
            cross_gain_grad, ffn_gain_grad,
        )
        gains, conv_came = tie((gains, conv_came))
        conv_part = (conv_keep + conv_came.astype(wide_type)).astype(low_type)
        return input_grad, layer_out, core_total(gains), jnp.concatenate((pair_part, conv_part), axis=1)

    input_grad, layer_out, small, memory_part = when_live(memory_work)

    memory_sums = Sums.of([memory_part.reshape(chips, share, -1)], [orders["memory"]], chip_index)
    small = memory_sums.start(small)
    late_sums = late_sums.joined(memory_sums)
    all_sums = late_feed.joined(late_sums)
    hop = 0
    moved = memory_grad = None
    while all_sums.going:
        small_came = dp_hop(small, hop) if hop < bits else None
        for bit in ((0,), (1, 2), range(3, bits))[hop] if hop < 3 else ():
            document_groups = document_groups + dp_hop(document_groups, bit)
        value = (small_came, document_groups)
        if hop == 2:
            moved = moved_rows(doc_owner, place, memory_in, document_groups)
            value = (small_came, moved)
        if hop == 3:
            memory_grad = spread_docs(returned, moved, doc_owner)
            value = (small_came, memory_grad)
        if hop == 0:
            returned, small_came = tie((returned, small_came))
            value = (small_came, document_groups)
        small_came, value = all_sums.round(value)
        if hop < bits:
            small = small + small_came
        if hop < 2:
            document_groups = value
        elif hop == 2:
            moved = value
        elif hop == 3:
            memory_grad = value
        hop += 1
    while hop < bits:
        small = small + dp_hop(small, hop)
        hop += 1
    if moved is None:
        moved = moved_rows(doc_owner, place, memory_in, document_groups)
    if memory_grad is None:
        memory_grad = spread_docs(returned, moved, doc_owner)
    first_total, second_total, memory_total = late_sums.totals
    memory_came = other_core(memory_total)
    weight_grads = assemble(
        place, memory_total, memory_came, first_total, second_total, *feed_sums.totals, small
    )
    conv_grad, cross_kv_grad, cross_out_grad, self_qkv_grad, cross_query_grad, self_out_grad = weight_grads[:6]
    ffn_in_grad, ffn_out_grad = weight_grads[6:8]
    gains = [gain.reshape(share) for gain in weight_grads[8:]]
    return (
        layer_out.reshape(1, DEC, width),
        input_grad.reshape(1, DEC, width),
        memory_grad.reshape(1, 1, docs, sub, width),
        gains[0],
        gains[1],
        conv_grad,
        cross_kv_grad,
        gains[2],
        self_qkv_grad.transpose(1, 0, 2),
        self_out_grad.T,
        gains[3],
        cross_query_grad,
        cross_out_grad.T,
        gains[4],
        ffn_in_grad,
        ffn_out_grad.T,
    )


def solution(mesh):
    placed = (
        P("dp", None, None),
        P("dp", None, None),
        P("dp", "mp", None, None, None),
        P(),
        P(),
        P(),
        P(),
        P(),
        P(),
        P(),
        P(),
        P(None, None, "mp"),
        P("mp", None),
        P(),
        P(None, "mp"),
        P("mp", None),
        P(),
        P(None, "mp"),
        P("mp", None),
    )
    return jax.shard_map(
        shards,
        mesh=mesh,
        in_specs=placed,
        out_specs=(
            P("dp", None, None),
            P("dp", None, None),
            P("dp", "mp", None, None, None),
            P("dp"),
            P("dp"),
            P("dp", None),
            P("dp", None, None),
            P("dp"),
            P("dp", None, "mp"),
            P("mp", "dp"),
            P("dp"),
            P("dp", "mp"),
            P("mp", "dp"),
            P("dp"),
            P("dp", "mp"),
            P("mp", "dp"),
        ),
        check_vma=False,
    )
```
